32 devices in a mesh: grp: 4 (over y, x), sfc: 8 (over z, core).
Axes of the slice: x: 2, y: 2, z: 4, core: 2. Of those that a mesh axis runs over, the one named last changes fastest.
Arguments:
- flow_fields: float32 [4, 5, 2048, 128], P('grp', None, 'sfc'), may hold values from -6 to 6
- mean_velocity: float32 [4, 3, 2048, 128], P('grp', None, 'sfc'), may hold values from -3 to 3
- cell_eddy_viscosity: float32 [4, 2048, 128], P('grp', 'sfc'), may hold values from 0.01 to 0.08
- tile_links: int32 [4, 4, 2048], P('grp', None, 'sfc'), may hold values from -1 to 2047, as said below
- tile_target: int32 [4, 2048], P('grp', 'sfc'), may hold values from 0 to 2047, as said below
- projector: float32 [64, 128], replicated, may hold values from -0.5 to 0.5
- acoustic_state: float32 [4, 4, 64, 2048], P('grp', None, None, 'sfc'), may hold values from -6 to 6
- element_face_neighbours: int32 [4, 6, 2048], P('grp', None, 'sfc'), may hold values from -1 to 2047, as said below
- face_codes: int32 [4, 6, 2048], P('grp', None, 'sfc'), may hold values from 0 to 3
Outputs:
- flow_out: float32 [4, 5, 2048, 128], P('grp', None, 'sfc')
- mean_velocity_output: float32 [4, 3, 2048, 128], P('grp', None, 'sfc')
- acoustic_out: float32 [4, 4, 64, 2048], P('grp', None, None, 'sfc')
The draws below stay inside these ranges and needn't reach their ends.
Inputs may be any that keep to these rules, and one draw needn't show every extreme that they name: `tile_links`: each entry is -1 or a tile of the same grp index whose position differs from the tile's own by at most 16. `tile_target`: element e lies on acoustic device e // 256. A tile held at sfc index s targets an element of acoustic device s or s + 1; one flow device sends at most 160 tiles to device s + 1, and in every draw some flow device sends exactly 160. Entries of grp index 3 are not read. `element_face_neighbours`: each entry is -1 or an element whose index differs from the element's own by at most 16.
All inputs are finite; a program needn't handle non-finite values.
Results may differ from the reference program's by a relative error of at most 0.0008.
Values may be sent and summed in bfloat16 or wider, within the bound.
No kernel may reach another device: no remote copies, remote signals or barrier semaphores. Data moves between devices by JAX's collectives and lax.ppermute only.
A program may use at most 128 MiB of HBM per device.

```python
import math
import jax
import jax.numpy as jnp
import numpy as np
from jax import lax

FT = 256
CELLS = 128
HW = 16
E_DEV = 256
HE = 16
NP = 64
TILES = 2048
ELEMS = 2048
CAP = 160
N_GRP = 4
N_SFC = 8


def draw_tile_links(key, part):
    positions = jnp.arange(TILES, dtype=jnp.int32)
    reach = jax.random.randint(jax.random.fold_in(key, 11), (N_GRP, 4, TILES), 1, HW + 1)
    sign = jax.random.randint(jax.random.fold_in(key, 12), (N_GRP, 4, TILES), 0, 2) * 2 - 1
    trial_option = positions[None, None, :] + reach * sign
    return jnp.where((trial_option < 0) | (trial_option >= TILES), -1, trial_option).astype(jnp.int32)


def draw_element_face_neighbours(key, part):
    positions = jnp.arange(ELEMS, dtype=jnp.int32)
    reach = jax.random.randint(jax.random.fold_in(key, 21), (N_GRP, 6, ELEMS), 1, HE + 1)
    sign = jax.random.randint(jax.random.fold_in(key, 22), (N_GRP, 6, ELEMS), 0, 2) * 2 - 1
    trial_option = positions[None, None, :] + reach * sign
    return jnp.where((trial_option < 0) | (trial_option >= ELEMS), -1, trial_option).astype(jnp.int32)


def draw_tile_target(key, part):
    devices = N_GRP * N_SFC
    serial = jnp.arange(devices, dtype=jnp.int32)
    column = serial % N_SFC
    counts = jax.random.randint(jax.random.fold_in(key, 31), (devices,), FT - CAP, CAP + 1)
    pick = jax.random.randint(jax.random.fold_in(key, 32), (), 0, (N_GRP - 1) * (N_SFC - 1))
    chosen = pick // (N_SFC - 1) * N_SFC + pick % (N_SFC - 1)
    counts = jnp.where(serial == chosen, FT - CAP, counts)
    counts = jnp.where(column == N_SFC - 1, FT, counts)
    positions = jnp.arange(FT, dtype=jnp.int32)
    owner = column[:, None] + (positions[None, :] >= counts[:, None]).astype(jnp.int32)
    local = jax.random.randint(jax.random.fold_in(key, 33), (devices, FT), 0, E_DEV)
    return (owner * E_DEV + local).reshape(N_GRP, TILES).astype(jnp.int32)


def plant(values, stream_key, low, high):
    place = [jax.random.randint(jax.random.fold_in(stream_key, axis), (), 0, length) for axis, length in enumerate(values.shape)]
    widest = values.shape.index(max(values.shape))
    neighbour = place[:widest] + [(place[widest] + 1) % values.shape[widest]] + place[widest + 1:]
    return values.at[tuple(place)].set(low).at[tuple(neighbour)].set(high)


def steps_of(own_key, dims, split, smallest, high):
    level = 1.0
    for axis_at, blocks in split:
        draws = jax.random.uniform(jax.random.fold_in(jax.random.fold_in(own_key, 6), axis_at), (blocks,), jnp.float32, smallest / len(split), high / len(split))
        level = level * jnp.repeat(jnp.exp(draws), dims[axis_at] // blocks).reshape((-1,) + (1,) * (len(dims) - 1 - axis_at))
    return level


def centred(stream_key, dims, scale, bound, shards=(), held_as=jnp.bfloat16):
    level = steps_of(stream_key, dims, shards, -0.22, 0.18) if shards else 1.0
    entries = jax.random.normal(stream_key, dims, jnp.float32) * scale * level
    return jnp.minimum(jnp.maximum(entries, -bound), bound).astype(held_as)


def setup_inputs(seed: int = 0) -> dict:
    splits = jax.random.split(jax.random.key(seed), 10)
    return {
        "flow_fields": centred(splits[0], (N_GRP, 5, TILES, CELLS), 1.0, 6.0, ((0, 4), (2, 8)), jnp.float32),
        "mean_velocity": centred(splits[1], (N_GRP, 3, TILES, CELLS), 0.5, 3.0, ((0, 4), (2, 8)), jnp.float32),
        "cell_eddy_viscosity": jnp.clip(jnp.exp(math.log(0.08) - 2.0794415 * jax.random.uniform(splits[2], (N_GRP, TILES, CELLS), jnp.float32) ** steps_of(splits[2], (N_GRP, TILES, CELLS), ((0, 4), (1, 8)), -0.2, 0.2)), 0.01, 0.08),
        "tile_links": draw_tile_links(jax.random.fold_in(splits[9], 71), 0),
        "tile_target": draw_tile_target(jax.random.fold_in(splits[9], 71), 0),
        "projector": centred(splits[5], (NP, CELLS), CELLS ** -0.5, 0.5, (), jnp.float32),
        "acoustic_state": centred(splits[6], (N_GRP, 4, NP, ELEMS), 1.0, 6.0, ((0, 4), (3, 8)), jnp.float32),
        "element_face_neighbours": draw_element_face_neighbours(jax.random.fold_in(splits[9], 71), 0),
        "face_codes": plant(jax.random.randint(splits[8], (N_GRP, 6, ELEMS), 0, 4), jax.random.fold_in(splits[8], 1), 0, 3).astype(jnp.int32),
    }


ADVECT = 0.1
RELAX = 0.1
PENALTY = 1.5
ACOUSTIC_STEP = 0.08

def derivative_operators():
    points = np.array([-1.0, -1.0 / np.sqrt(5.0), 1.0 / np.sqrt(5.0), 1.0])
    weights = np.array([1.0 / np.prod([points[col] - points[other] for other in range(4) if other != col]) for col in range(4)])
    derivative_matrix = np.zeros((4, 4))
    for line in range(4):
        for col in range(4):
            if line != col:
                derivative_matrix[line, col] = weights[col] / weights[line] / (points[line] - points[col])
        derivative_matrix[line, line] = -derivative_matrix[line].sum()
    identity = np.eye(4)
    return np.stack([np.kron(identity, np.kron(identity, derivative_matrix)), np.kron(identity, np.kron(derivative_matrix, identity)), np.kron(derivative_matrix, np.kron(identity, identity))]).astype(np.float32)

def face_tables():
    faces = []
    for face in range(6):
        axis_id = face // 2
        level = 3 * (face % 2)
        members = []
        for second in range(4):
            for first in range(4):
                coords = [first, second]
                coords.insert(axis_id, level)
                members.append(coords[0] + 4 * coords[1] + 16 * coords[2])
        faces.append(members)
    turns = []
    for turn in range(4):
        mapping = []
        for second in range(4):
            for first in range(4):
                if turn == 0:
                    source = (first, second)
                elif turn == 1:
                    source = (3 - second, first)
                elif turn == 2:
                    source = (3 - first, 3 - second)
                else:
                    source = (second, 3 - first)
                mapping.append(source[0] + 4 * source[1])
        turns.append(mapping)
    return (np.array(faces), np.array(turns))

def flow_advance(solver_state, own_rows, links, viscosity):
    center = jnp.take(solver_state, own_rows, axis=1)
    north = jnp.take(solver_state, links[0], axis=1)
    south = jnp.take(solver_state, links[1], axis=1)
    upper = jnp.take(solver_state, links[2], axis=1)
    lower = jnp.take(solver_state, links[3], axis=1)
    east = jnp.roll(center, -1, axis=2)
    west = jnp.roll(center, 1, axis=2)
    laplace = east + west + north + south + upper + lower - 6.0 * center
    advection = center[1] * (east - west) * 0.5 + center[2] * (north - south) * 0.5 + center[3] * (upper - lower) * 0.5
    return center + viscosity * laplace - ADVECT * advection

def lamb_vector(solver_state, own_rows, links):
    velocity = solver_state[1:4]
    center = jnp.take(velocity, own_rows, axis=1)
    east = jnp.roll(center, -1, axis=2)
    west = jnp.roll(center, 1, axis=2)
    along_x = (east - west) * 0.5
    along_y = (jnp.take(velocity, links[0], axis=1) - jnp.take(velocity, links[1], axis=1)) * 0.5
    along_z = (jnp.take(velocity, links[2], axis=1) - jnp.take(velocity, links[3], axis=1)) * 0.5
    vort_x = along_y[2] - along_z[1]
    vort_y = along_z[0] - along_x[2]
    vort_z = along_x[1] - along_y[0]
    return jnp.stack([vort_y * center[2] - vort_z * center[1], vort_z * center[0] - vort_x * center[2], vort_x * center[1] - vort_y * center[0]])

def project(lamb, average, projector):
    packed = jnp.concatenate([lamb, average], 0)
    mapped = jnp.einsum('ctm,nm->tcn', packed, projector, precision=lax.Precision.HIGHEST)
    return mapped.reshape(mapped.shape[0], -1).astype(jnp.bfloat16)

def acoustic_advance(solver_state, wide, links, valid, codes, source):
    derivative_matrix = jnp.asarray(derivative_operators())
    faces, turns = face_tables()
    gradient_fields = jnp.einsum('yws,lsb->ylwb', derivative_matrix, solver_state, precision=lax.Precision.HIGHEST)
    lamb_src = source[0:3]
    mean_flow = source[3:6]
    convect = mean_flow[0][None] * gradient_fields[0] + mean_flow[1][None] * gradient_fields[1] + mean_flow[2][None] * gradient_fields[2]
    rhs_parts = [-(gradient_fields[0, 1] + gradient_fields[1, 2] + gradient_fields[2, 3]) - convect[0]]
    for direction in range(3):
        rhs_parts.append(-gradient_fields[direction, 0] - convect[1 + direction] - lamb_src[direction])
    rhs = jnp.stack(rhs_parts)
    for face in range(6):
        facing = wide[:, faces[face ^ 1], :]
        remote = jnp.take(facing, links[face], axis=2)
        turned = jnp.zeros_like(remote)
        for turn in range(4):
            turned = turned + jnp.where(codes[face][None, None, :] == turn, remote[:, turns[turn], :], jnp.float32(0.0))
        jump = jnp.where(valid[face][None, None, :], turned - solver_state[:, faces[face], :], jnp.float32(0.0))
        rhs = rhs.at[:, faces[face], :].add(PENALTY * jump)
    return solver_state + ACOUSTIC_STEP * rhs

def gather_sources(rows, ids, count):
    index = jnp.where(ids < 0, count, ids).astype(jnp.int32)
    sums = jnp.zeros((count + 1, rows.shape[1]), jnp.float32).at[index].add(rows.astype(jnp.float32))
    counts = jnp.zeros((count + 1,), jnp.float32).at[index].add(jnp.where(ids < 0, jnp.float32(0.0), jnp.float32(1.0)))
    source = sums[:count] / jnp.maximum(counts[:count], 1.0)[:, None]
    return jnp.transpose(source.reshape(count, 6, -1), (1, 2, 0))

def reference(flow_fields, mean_velocity, cell_eddy_viscosity, tile_links, tile_target, projector, acoustic_state, element_face_neighbours, face_codes):

    def flow_row(solver_state, average, viscosity, neighbours):
        total = solver_state.shape[1]
        own_rows = jnp.arange(total, dtype=jnp.int32)
        links = jnp.where(neighbours < 0, own_rows[None, :], neighbours).astype(jnp.int32)
        payloads = []
        for turn in range(2):
            solver_state = flow_advance(solver_state, own_rows, links, viscosity)
            lamb = lamb_vector(solver_state, own_rows, links)
            average = (1.0 - RELAX) * average + RELAX * solver_state[1:4]
            payloads.append(project(lamb, average, projector))
        return (solver_state, average, jnp.stack(payloads))
    new_fields, new_mean, payloads = jax.vmap(flow_row)(flow_fields, mean_velocity, cell_eddy_viscosity, tile_links)
    flow_rows = N_GRP - 1
    targets = tile_target[:flow_rows].reshape(-1)
    last = N_GRP - 1
    solver_state = acoustic_state[last]
    neighbours = element_face_neighbours[last]
    valid = neighbours >= 0
    links = jnp.where(valid, neighbours, 0).astype(jnp.int32)
    for turn in range(2):
        rows = payloads[:flow_rows, turn].reshape(-1, payloads.shape[-1])
        source = gather_sources(rows, targets, solver_state.shape[2])
        solver_state = acoustic_advance(solver_state, solver_state, links, valid, face_codes[last], source)
    is_flow = (jnp.arange(N_GRP) < flow_rows)[:, None, None, None]
    flow_out = jnp.where(is_flow, new_fields, flow_fields)
    mean_velocity_output = jnp.where(is_flow, new_mean, mean_velocity)
    acoustic_out = acoustic_state.at[last].set(solver_state)
    return (flow_out, mean_velocity_output, acoustic_out)
```

```python
import jax
import jax.numpy as jnp
import numpy as np
from jax import lax
from jax.experimental import pallas as pl
from jax.experimental.pallas import tpu as pltpu
from jax.sharding import PartitionSpec as P

HW = 16
HE = 16

ADVECT = 0.1
RELAX = 0.1
PENALTY = 1.5
ACOUSTIC_STEP = 0.08

LANES = 128
EDGE = 3 * HW
FIELD_ORDER = (1, 2, 3, 0, 4)
BASE = 32.0
EXTRA = 16
VMEM_LIMIT = 48 * 1024 * 1024

F32 = jnp.float32
BF16 = jnp.bfloat16


def lobatto_matrix():
    points = np.array([-1.0, -1.0 / np.sqrt(5.0), 1.0 / np.sqrt(5.0), 1.0])
    weights = np.array(
        [
            1.0 / np.prod([points[col] - points[other] for other in range(4) if other != col])
            for col in range(4)
        ]
    )
    matrix = np.zeros((4, 4))
    for line in range(4):
        for col in range(4):
            if line != col:
                matrix[line, col] = weights[col] / weights[line] / (points[line] - points[col])
        matrix[line, line] = -matrix[line].sum()
    return matrix.astype(np.float32)


def face_nodes(face):
    axis, level = face // 2, 3 * (face % 2)
    nodes = []
    for second in range(4):
        for first in range(4):
            coords = [first, second]
            coords.insert(axis, level)
            nodes.append(coords[0] + 4 * coords[1] + 16 * coords[2])
    return nodes


def turned_position(turn, position):
    a, b = position % 4, position // 4
    a, b = ((a, b), (3 - b, a), (3 - a, 3 - b), (b, 3 - a))[turn]
    return a + 4 * b


def split_parts(x):
    high = x.astype(BF16)
    return high, (x - high.astype(F32)).astype(BF16)


def dot(a, b):
    return jnp.dot(a, b, preferred_element_type=F32)


def dot_t(a, b):
    return lax.dot_general(a, b, (((1,), (1,)), ((), ())), preferred_element_type=F32)


def pack_kernel(meta, flow, visc, links, sound, first_out, last_out):
    is_flow, even = meta[0] == 1, meta[1] == 1
    tiles = flow.shape[1]
    elements = sound.shape[2]
    nodes = sound.shape[1]
    off_a = pl.multiple_of(jnp.where(even, 0, tiles - EDGE), 8)
    off_b = pl.multiple_of(jnp.where(even, tiles - EDGE, 0), 8)

    @pl.when(is_flow)
    def _():
        for out, off in ((first_out, off_a), (last_out, off_b)):
            for place, f in enumerate(FIELD_ORDER):
                out[place * EDGE : (place + 1) * EDGE, :] = flow[f, pl.ds(off, EDGE), :]
            out[5 * EDGE : 6 * EDGE, :] = visc[pl.ds(off, EDGE), :]
        low = links[:, :LANES].astype(F32)
        high = links[:, tiles - LANES :].astype(F32)
        first_out[6 * EDGE : 6 * EDGE + 4, :] = jnp.where(even, low, high)
        last_out[6 * EDGE : 6 * EDGE + 4, :] = jnp.where(even, high, low)
        pad = jnp.zeros((4, LANES), F32)
        first_out[6 * EDGE + 4 : 6 * EDGE + 8, :] = pad
        last_out[6 * EDGE + 4 : 6 * EDGE + 8, :] = pad

    @pl.when(jnp.logical_not(is_flow))
    def _():
        for v in range(4):
            low = sound[v, :, :LANES]
            high = sound[v, :, elements - LANES :]
            first_out[v * nodes : (v + 1) * nodes, :] = jnp.where(even, low, high)
            last_out[v * nodes : (v + 1) * nodes, :] = jnp.where(even, high, low)
        rest = jnp.zeros((first_out.shape[0] - 4 * nodes, LANES), F32)
        first_out[4 * nodes :, :] = rest
        last_out[4 * nodes :, :] = rest


def flow_kernel(
    meta, flow, mean, visc, links, target, projector, part_a, part_b,
    flow_out, mean_out, own_one, own_two, next_one, next_two,
    state, high0, low0, high1, low1, vwide, lcol, square, mats, packed, pay,
):
    is_flow, even = meta[0] == 1, meta[1] == 1
    tiles = flow.shape[1]
    wide = tiles + 2 * EDGE
    elements = own_one.shape[1]
    nodes = projector.shape[0]
    band = tiles + 4 * HW
    blocks = 4
    rows = band // blocks
    span = rows + 2 * HW

    @pl.when(jnp.logical_not(is_flow))
    def _():
        flow_out[...] = flow[...]
        mean_out[...] = mean[...]
        own_one[...] = jnp.zeros_like(own_one)
        own_two[...] = jnp.zeros_like(own_two)
        next_one[...] = jnp.zeros_like(next_one)
        next_two[...] = jnp.zeros_like(next_two)

    @pl.when(is_flow)
    def _():
        first_tile = meta[2]
        first_element = meta[3]

        def pick(at, size):
            a, b = part_a[at : at + size, :], part_b[at : at + size, :]
            return jnp.where(even, a, b), jnp.where(even, b, a)

        def put(high, low, at, size, place, value):
            columns = slice(place * LANES, (place + 1) * LANES)
            h, l = split_parts(value)
            high[at : at + size, columns] = h
            low[at : at + size, columns] = l

        for place, f in enumerate(FIELD_ORDER):
            columns = slice(place * LANES, (place + 1) * LANES)
            before, after = pick(place * EDGE, EDGE)
            center = flow[f]
            state[:EDGE, columns] = before
            state[EDGE : EDGE + tiles, columns] = center
            state[EDGE + tiles :, columns] = after
            put(high0, low0, 0, EDGE, place, before)
            put(high0, low0, EDGE, tiles, place, center)
            put(high0, low0, EDGE + tiles, EDGE, place, after)
        before, after = pick(5 * EDGE, EDGE)
        vwide[:EDGE, :] = before
        vwide[EDGE : EDGE + tiles, :] = visc[...]
        vwide[EDGE + tiles :, :] = after
        for ref in (high1, low1):
            ref[:HW, :] = jnp.zeros((HW, ref.shape[1]), BF16)
            ref[wide - HW :, :] = jnp.zeros((HW, ref.shape[1]), BF16)

        before, after = pick(6 * EDGE, 8)
        square[...] = jnp.zeros_like(square)
        square[:8, :] = before
        lcol[:EDGE, :] = square[...].T[LANES - EDGE :, :]
        square[:8, :] = after
        lcol[EDGE + tiles :, :] = square[...].T[:EDGE, :]
        for part in range(tiles // LANES):
            square[:4, :] = links[:, part * LANES : (part + 1) * LANES].astype(F32)
            lcol[EDGE + part * LANES : EDGE + (part + 1) * LANES, :] = square[...].T

        lane = lax.broadcasted_iota(jnp.int32, (rows, 2 * span), 1)
        lane = jnp.where(lane >= span, lane - span, lane)
        for b in range(blocks):
            at = HW + b * rows
            own = (
                first_tile - EDGE + at + lax.broadcasted_iota(jnp.int32, (rows, LANES), 0)
            ).astype(F32)
            given = lcol[at : at + rows, :]
            place = jnp.where(given < 0, own, given).astype(jnp.int32) - (
                first_tile - EDGE + b * rows
            )
            hot = [jnp.where(place[:, k : k + 1] == lane, F32(1.0), F32(0.0)) for k in range(4)]
            mats[b, :rows, :] = (hot[0] + hot[1] + hot[2] + hot[3]).astype(BF16)
            mats[b, rows : 2 * rows, :] = (hot[0] - hot[1]).astype(BF16)
            mats[b, 2 * rows :, :] = (hot[2] - hot[3]).astype(BF16)

        def gathered(high, low, b, columns, at_row):
            at = b * rows
            both = jnp.concatenate([high[at : at + span, columns], low[at : at + span, columns]], 0)
            return dot(mats[b, at_row:, :], both)

        def east_west(x):
            return pltpu.roll(x, LANES - 1, 1), pltpu.roll(x, 1, 1)

        def lamb_block(b, center, shift, dy, dz, average):
            d1 = [(east - west) * 0.5 for east, west in shift]
            d2 = [y * 0.5 for y in dy]
            d3 = [z * 0.5 for z in dz]
            vx = d2[2] - d3[1]
            vy = d3[0] - d1[2]
            vz = d1[1] - d2[0]
            lamb = (
                vy * center[2] - vz * center[1],
                vz * center[0] - vx * center[2],
                vx * center[1] - vy * center[0],
            )
            at = HW + b * rows - EDGE
            low = max(0, -at)
            top = min(rows, tiles - at)
            for i in range(3):
                packed[i, at + low : at + top, :] = lamb[i][low:top]
                mixed = (1.0 - RELAX) * average[i, at + low : at + top, :] + RELAX * center[i][low:top]
                mean_out[i, at + low : at + top, :] = mixed
                packed[3 + i, at + low : at + top, :] = mixed

        def advance(b, high, low, high_next, low_next, average):
            at = HW + b * rows
            center = [state[at : at + rows, k * LANES : (k + 1) * LANES] for k in range(3)]
            scaled = [(0.5 * ADVECT) * c for c in center]
            v = vwide[at : at + rows, :]
            shift, dys, dzs = [], [], []
            for pair in (slice(0, 2), slice(2, 4), slice(4, 5)):
                got = gathered(high, low, b, slice(pair.start * LANES, pair.stop * LANES), 0)
                for place in range(pair.start, pair.stop):
                    inner = slice((place - pair.start) * LANES, (place - pair.start + 1) * LANES)
                    total, dy, dz = (
                        got[:rows, inner],
                        got[rows : 2 * rows, inner],
                        got[2 * rows :, inner],
                    )
                    c = (
                        center[place]
                        if place < 3
                        else state[at : at + rows, place * LANES : (place + 1) * LANES]
                    )
                    east, west = east_west(c)
                    if place < 3:
                        shift.append((east, west))
                        dys.append(dy)
                        dzs.append(dz)
                    new = (
                        c
                        + v * (east + west + total - 6.0 * c)
                        - (scaled[0] * (east - west) + scaled[1] * dy + scaled[2] * dz)
                    )
                    state[at : at + rows, place * LANES : (place + 1) * LANES] = new
                    if place < 3 or average is None:
                        put(high_next, low_next, at, rows, place, new)
            if average is not None:
                lamb_block(b, center, shift, dys, dzs, average)

        proj_high, proj_low = split_parts(projector[...])
        proj_both = jnp.concatenate([proj_high, proj_low], 0)
        local = target[...] - first_element
        hits = jnp.where(
            lax.broadcasted_iota(jnp.int32, (2 * elements, tiles), 0) == local, F32(1.0), F32(0.0)
        ).astype(BF16)

        def send(own_ref, next_ref):
            for c in range(6):
                x_high, x_low = split_parts(packed[c])
                main = dot_t(proj_both, x_high)
                mapped = main[:nodes] + main[nodes:] + dot_t(proj_high, x_low)
                pay[c * nodes : (c + 1) * nodes, :] = mapped.astype(BF16)
            count = own_ref.shape[0]
            sums = dot_t(pay[:count, :], hits)
            if count > 6 * nodes:
                body = sums[: 6 * nodes]
                tail = sums[6 * nodes :]
                line = lax.broadcasted_iota(jnp.int32, tail.shape, 0)
                big = jnp.floor(tail * (1.0 / BASE))
                tail = jnp.where(line == 0, tail - BASE * big, jnp.where(line == 1, big, 0.0))
                own_ref[6 * nodes :, :] = tail[:, :elements]
                next_ref[6 * nodes :, :] = tail[:, elements:].astype(BF16)
            else:
                body = sums
            own_ref[: 6 * nodes, :] = body[:, :elements]
            next_ref[: 6 * nodes, :] = body[:, elements:].astype(BF16)

        pay[6 * nodes :, :] = jnp.ones((EXTRA, tiles), BF16)
        for b in range(blocks):
            advance(b, high0, low0, high1, low1, None)
        for b in range(blocks):
            advance(b, high1, low1, high0, low0, mean)
        send(own_one, next_one)
        for place, f in enumerate(FIELD_ORDER):
            flow_out[f] = state[EDGE : EDGE + tiles, place * LANES : (place + 1) * LANES]
        for b in range(blocks):
            at = HW + b * rows
            center = [state[at : at + rows, k * LANES : (k + 1) * LANES] for k in range(3)]
            first = gathered(high0, low0, b, slice(0, 2 * LANES), rows)
            second = gathered(high0, low0, b, slice(2 * LANES, 3 * LANES), rows)
            all_d = jnp.concatenate([first, second], 1)
            dys = [all_d[:rows, k * LANES : (k + 1) * LANES] for k in range(3)]
            dzs = [all_d[rows:, k * LANES : (k + 1) * LANES] for k in range(3)]
            lamb_block(b, center, [east_west(c) for c in center], dys, dzs, mean_out)
        send(own_two, next_two)


def acoustic_kernel(
    first_step, meta, sound, part_a, part_b, neighbours, codes, source_a, source_b, *refs
):
    if first_step:
        (out, scale_out, edge_a, edge_b, wide, facing, remote, node, rhs, lamb, mean, flat) = refs
    else:
        (scale, out, wide, facing, remote, node, rhs, lamb, mean, flat) = refs
    is_flow, even = meta[0] == 1, meta[1] == 1
    nodes = sound.shape[1]
    elements = sound.shape[2]
    halves = elements // LANES
    matrix = lobatto_matrix()
    block = 4 * nodes

    @pl.when(is_flow)
    def _():
        out[...] = sound[...]
        if first_step:
            scale_out[...] = jnp.zeros_like(scale_out)
            edge_a[...] = jnp.zeros_like(edge_a)
            edge_b[...] = jnp.zeros_like(edge_b)

    @pl.when(jnp.logical_not(is_flow))
    def _():
        first_element = meta[3]
        for v in range(4):
            for h in range(halves):
                wide[h * block + v * nodes : h * block + (v + 1) * nodes, :] = sound[
                    v, :, h * LANES : (h + 1) * LANES
                ]
        a, b = part_a[:block, :].astype(F32), part_b[:block, :].astype(F32)
        wide[halves * block : (halves + 1) * block, :] = jnp.where(even, a, b)
        wide[(halves + 1) * block : (halves + 2) * block, :] = jnp.where(even, b, a)
        for n in range(nodes):
            node[n] = wide[pl.ds(n, 8, stride=nodes), :]

        for face in range(6):
            other = face ^ 1
            axis, level = other // 2, 3 * (other % 2)
            for part in range(halves + 2):
                base = part * block
                if axis == 0:
                    facing[face, part] = wide[pl.ds(base + level, 64, stride=4), :]
                elif axis == 1:
                    for i in range(4):
                        facing[face, part, pl.ds(i, 16, stride=4), :] = wide[
                            pl.ds(base + i + 4 * level, 16, stride=16), :
                        ]
                else:
                    for v in range(4):
                        facing[face, part, v * 16 : (v + 1) * 16, :] = wide[
                            base + v * nodes + 16 * level : base + v * nodes + 16 * level + 16, :
                        ]

        key = lax.broadcasted_iota(jnp.int32, ((halves + 2) * LANES, elements), 0)
        for face in range(6):
            link = neighbours[face : face + 1, :]
            near = link - first_element
            place = jnp.where(
                near < 0, elements + LANES + near, jnp.where(near < elements, near, near + LANES)
            )
            place = jnp.where(link < 0, -1, place)
            hot = jnp.where(key == place, F32(1.0), F32(0.0)).astype(BF16)
            x = jnp.concatenate([facing[face, part] for part in range(halves + 2)], 1)
            high, low = split_parts(x)
            got = dot(jnp.concatenate([high, low], 0), hot)
            got = got[:64] + got[64:]
            for h in range(halves):
                remote[face, h * 64 : (h + 1) * 64, :] = got[:, h * LANES : (h + 1) * LANES]

        total = source_a[...].astype(F32) + source_b[...].astype(F32)
        if first_step:
            count = total[6 * nodes : 6 * nodes + 1] + BASE * total[6 * nodes + 1 : 6 * nodes + 2]
            inverse = 1.0 / jnp.maximum(count, 1.0)
            scale_out[...] = jnp.broadcast_to(inverse, scale_out.shape)
        else:
            inverse = scale[0:1, :]
        total = total[: 6 * nodes] * inverse
        for h in range(halves):
            columns = slice(h * LANES, (h + 1) * LANES)
            lamb[h * block : h * block + nodes, :] = jnp.zeros((nodes, LANES), F32)
            for d in range(3):
                at = h * block + (1 + d) * nodes
                lamb[at : at + nodes, :] = total[d * nodes : (d + 1) * nodes, columns]
                value = total[(3 + d) * nodes : (4 + d) * nodes, columns]
                for v in range(4):
                    at = h * block + v * nodes
                    mean[d, at : at + nodes, :] = value

        line = lax.broadcasted_iota(jnp.int32, (8, LANES), 0)
        component = line % 4
        is_v = [component == v for v in range(4)]
        for n in range(nodes):
            i, j, k = n % 4, n // 4 % 4, n // 16
            lines = (
                [m + 4 * j + 16 * k for m in range(4)],
                [i + 4 * m + 16 * k for m in range(4)],
                [i + 4 * j + 16 * m for m in range(4)],
            )
            grads = []
            for d, at in enumerate((i, j, k)):
                total_d = None
                for m in range(4):
                    if abs(matrix[at, m]) > 1e-12:
                        term = F32(matrix[at, m]) * node[lines[d][m]]
                        total_d = term if total_d is None else total_d + term
                grads.append(total_d)
            div = sum(pltpu.roll(grads[d], 8 - (1 + d), 0) for d in range(3))
            coupled = jnp.where(is_v[0], div, 0.0)
            for d in range(3):
                coupled = jnp.where(is_v[1 + d], pltpu.roll(grads[d], 1 + d, 0), coupled)
            convect = sum(mean[d, pl.ds(n, 8, stride=nodes), :] * grads[d] for d in range(3))
            rhs[n] = -coupled - convect - lamb[pl.ds(n, 8, stride=nodes), :]

        upper = line >= 4
        for face in range(6):
            link = neighbours[face : face + 1, :]
            code = codes[face : face + 1, :]

            def both(row):
                return jnp.where(
                    upper,
                    jnp.broadcast_to(row[:, LANES:], (8, LANES)),
                    jnp.broadcast_to(row[:, :LANES], (8, LANES)),
                )

            valid = both(link) >= 0
            code = both(code)
            is_turn = [code == t for t in range(4)]
            planes = [remote[face, pl.ds(p, 8, stride=16), :] for p in range(16)]
            for p, n in enumerate(face_nodes(face)):
                turned = planes[turned_position(3, p)]
                for t in range(3):
                    turned = jnp.where(is_turn[t], planes[turned_position(t, p)], turned)
                jump = jnp.where(valid, turned - node[n], 0.0)
                rhs[n] = rhs[n] + PENALTY * jump

        for n in range(nodes):
            flat[pl.ds(n, 8, stride=nodes), :] = node[n] + ACOUSTIC_STEP * rhs[n]
        for v in range(4):
            for h in range(halves):
                out[v, :, h * LANES : (h + 1) * LANES] = flat[
                    h * block + v * nodes : h * block + (v + 1) * nodes, :
                ]
        if first_step:
            off_a = pl.multiple_of(jnp.where(even, 0, block), 8)
            off_b = pl.multiple_of(jnp.where(even, block, 0), 8)
            edge_a[...] = flat[pl.ds(off_a, block), :]
            edge_b[...] = flat[pl.ds(off_b, block), :]


def call(kernel, outs, scratch, operands, flops=1e8):
    vmem = pl.BlockSpec(memory_space=pltpu.VMEM)
    moved = sum(int(np.prod(x.shape)) * x.dtype.itemsize for x in (*operands, *outs))
    return pl.pallas_call(
        kernel,
        out_shape=tuple(outs),
        in_specs=[pl.BlockSpec(memory_space=pltpu.SMEM)] + [vmem] * (len(operands) - 1),
        out_specs=tuple([vmem] * len(outs)),
        scratch_shapes=scratch,
        compiler_params=pltpu.CompilerParams(vmem_limit_bytes=VMEM_LIMIT),
        cost_estimate=pl.CostEstimate(flops=int(flops), bytes_accessed=moved, transcendentals=0),
    )(*operands)


def acoustic_step(first_step, meta, sound, parts, neighbours, codes, sources, scale=None):
    _, nodes, elements = sound.shape
    halves = elements // LANES
    block = 4 * nodes
    shape = jax.ShapeDtypeStruct
    outs = [shape(sound.shape, F32)]
    if first_step:
        outs += [shape((8, elements), F32), shape((block, LANES), F32), shape((block, LANES), F32)]
    scratch = [
        pltpu.VMEM(((halves + 2) * block, LANES), F32),
        pltpu.VMEM((6, halves + 2, 64, LANES), F32),
        pltpu.VMEM((6, halves * 64, LANES), F32),
        pltpu.VMEM((nodes, 8, LANES), F32),
        pltpu.VMEM((nodes, 8, LANES), F32),
        pltpu.VMEM((halves * block, LANES), F32),
        pltpu.VMEM((3, halves * block, LANES), F32),
        pltpu.VMEM((halves * block, LANES), F32),
    ]
    operands = [meta, sound, *parts, neighbours, codes, *sources]
    if not first_step:
        operands.append(scale)

    def kernel(*refs):
        acoustic_kernel(first_step, *refs)

    return call(kernel, outs, scratch, operands)


def body(
    flow_fields,
    mean_velocity,
    cell_eddy_viscosity,
    tile_links,
    tile_target,
    projector,
    acoustic_state,
    element_face_neighbours,
    face_codes,
):
    groups = lax.axis_size("grp")
    count = lax.axis_size("sfc")
    group_index = lax.axis_index("grp")
    column = lax.axis_index("sfc")
    flow = flow_fields[0]
    mean = mean_velocity[0]
    visc = cell_eddy_viscosity[0]
    links = tile_links[0]
    sound = acoustic_state[0]
    neighbours = element_face_neighbours[0]
    codes = face_codes[0]
    tiles = flow.shape[1]
    _, nodes, elements = sound.shape
    shape = jax.ShapeDtypeStruct
    meta = jnp.stack(
        [
            (group_index < groups - 1).astype(jnp.int32),
            (column % 2 == 0).astype(jnp.int32),
            (column * tiles).astype(jnp.int32),
            (column * elements).astype(jnp.int32),
        ]
    )

    pairs_a = [p for i in range(1, count - 1, 2) for p in ((i, i + 1), (i + 1, i))]
    pairs_b = [p for i in range(0, count - 1, 2) for p in ((i, i + 1), (i + 1, i))]

    edge_rows = 6 * EDGE + 8
    pack_a, pack_b = call(
        pack_kernel,
        [shape((edge_rows, LANES), F32)] * 2,
        [],
        [meta, flow, visc, links, sound],
    )
    part_a = lax.ppermute(pack_a, "sfc", pairs_a)
    part_b = lax.ppermute(pack_b, "sfc", pairs_b)

    wide = tiles + 2 * EDGE
    band = tiles + 4 * HW
    rows = band // 4
    columns = 5 * LANES
    count_one, count_two = 6 * nodes + EXTRA, 6 * nodes
    flow_out, mean_out, own_one, own_two, next_one, next_two = call(
        flow_kernel,
        [
            shape(flow.shape, F32),
            shape(mean.shape, F32),
            shape((count_one, elements), F32),
            shape((count_two, elements), F32),
            shape((count_one, elements), BF16),
            shape((count_two, elements), BF16),
        ],
        [
            pltpu.VMEM((wide, columns), F32),
            pltpu.VMEM((wide, columns), BF16),
            pltpu.VMEM((wide, columns), BF16),
            pltpu.VMEM((wide, columns), BF16),
            pltpu.VMEM((wide, columns), BF16),
            pltpu.VMEM((wide, LANES), F32),
            pltpu.VMEM((wide, LANES), F32),
            pltpu.VMEM((LANES, LANES), F32),
            pltpu.VMEM((4, 3 * rows, 2 * (rows + 2 * HW)), BF16),
            pltpu.VMEM((6, tiles, LANES), F32),
            pltpu.VMEM((count_one, tiles), BF16),
        ],
        [meta, flow, mean, visc, links, tile_target, projector, part_a, part_b],
        flops=2e9,
    )

    up = [(i, i + 1) for i in range(count - 1)]
    flow_groups = range(groups - 1)

    def climb(x):
        chosen = [(g * count + i, g * count + j) for g in flow_groups for i, j in up]
        return lax.ppermute(x, ("grp", "sfc"), chosen)

    def combined(*xs):
        total = xs[0]
        for x in xs[1:]:
            total = total + x.astype(F32)
        return total.astype(BF16)

    got_one, got_two = climb(next_one), climb(next_two)
    x_one = lax.ppermute(combined(own_one, got_one), "grp", [(0, 1), (2, 3)])
    y_two = lax.ppermute(combined(own_two, got_two), "grp", [(0, 2), (1, 3)])
    y_one = lax.ppermute(combined(own_one, got_one, x_one), "grp", [(1, 3)])
    x_two = lax.ppermute(combined(own_two, got_two, y_two), "grp", [(2, 3)])

    sound, scale, edge_a, edge_b = acoustic_step(
        True, meta, sound, (part_a, part_b), neighbours, codes, (x_one, y_one)
    )
    base = (groups - 1) * count
    part_a = lax.ppermute(edge_a, ("grp", "sfc"), [(base + i, base + j) for i, j in pairs_a])
    part_b = lax.ppermute(edge_b, ("grp", "sfc"), [(base + i, base + j) for i, j in pairs_b])
    (sound,) = acoustic_step(
        False, meta, sound, (part_a, part_b), neighbours, codes, (y_two, x_two), scale
    )
    return flow_out[None], mean_out[None], sound[None]


def solution(mesh):
    placed = (
        P("grp", None, "sfc", None),
        P("grp", None, "sfc", None),
        P("grp", "sfc", None),
        P("grp", None, "sfc"),
        P("grp", "sfc"),
        P(),
        P("grp", None, None, "sfc"),
        P("grp", None, "sfc"),
        P("grp", None, "sfc"),
    )
    return jax.shard_map(
        body,
        mesh=mesh,
        in_specs=placed,
        out_specs=(
            P("grp", None, "sfc", None),
            P("grp", None, "sfc", None),
            P("grp", None, None, "sfc"),
        ),
        check_vma=False,
    )
```

```python
import jax
import jax.numpy as jnp
import numpy as np
from jax import lax
from jax.experimental import pallas as pl
from jax.experimental.pallas import tpu as pltpu
from jax.sharding import PartitionSpec as P

HW = 16
HE = 16

ADVECT = 0.1
RELAX = 0.1
PENALTY = 1.5
ACOUSTIC_STEP = 0.08

LANES = 128
EDGE = 3 * HW
FIELD_ORDER = (1, 2, 3, 0, 4)
BASE = 32.0
EXTRA = 16
VMEM_LIMIT = 48 * 1024 * 1024
PACK_LIMIT = 63 * 1024 * 1024

F32 = jnp.float32
BF16 = jnp.bfloat16


def lobatto_matrix():
    points = np.array([-1.0, -1.0 / np.sqrt(5.0), 1.0 / np.sqrt(5.0), 1.0])
    weights = np.array(
        [
            1.0 / np.prod([points[col] - points[other] for other in range(4) if other != col])
            for col in range(4)
        ]
    )
    matrix = np.zeros((4, 4))
    for line in range(4):
        for col in range(4):
            if line != col:
                matrix[line, col] = weights[col] / weights[line] / (points[line] - points[col])
        matrix[line, line] = -matrix[line].sum()
    return matrix.astype(np.float32)


def face_nodes(face):
    axis, level = face // 2, 3 * (face % 2)
    nodes = []
    for second in range(4):
        for first in range(4):
            coords = [first, second]
            coords.insert(axis, level)
            nodes.append(coords[0] + 4 * coords[1] + 16 * coords[2])
    return nodes


def turned_position(turn, position):
    a, b = position % 4, position // 4
    a, b = ((a, b), (3 - b, a), (3 - a, 3 - b), (b, 3 - a))[turn]
    return a + 4 * b


def split_parts(x):
    high = x.astype(BF16)
    return high, (x - high.astype(F32)).astype(BF16)


def dot(a, b):
    return jnp.dot(a, b, preferred_element_type=F32)


def dot_t(a, b):
    return lax.dot_general(a, b, (((1,), (1,)), ((), ())), preferred_element_type=F32)


def pack_kernel(meta, flow, visc, links, sound, out_a, out_b, links_in, sems, link_sem):
    is_flow, even = meta[0] == 1, meta[1] == 1
    tiles = flow.shape[1]
    _, nodes, elements = sound.shape
    outs = (out_a, out_b)

    @pl.when(is_flow)
    def _():
        fetch = pltpu.make_async_copy(links, links_in, link_sem)
        fetch.start()
        copies = []
        for side, out in enumerate(outs):
            off = pl.multiple_of(jnp.where(even == (side == 0), 0, tiles - EDGE), 8)
            for place, f in enumerate(FIELD_ORDER):
                copies.append(
                    pltpu.make_async_copy(
                        flow.at[f, pl.ds(off, EDGE), :],
                        out.at[pl.ds(place * EDGE, EDGE), :],
                        sems.at[side, place],
                    )
                )
            copies.append(
                pltpu.make_async_copy(
                    visc.at[pl.ds(off, EDGE), :], out.at[pl.ds(5 * EDGE, EDGE), :], sems.at[side, 5]
                )
            )
        for copy in copies:
            copy.start()
        fetch.wait()
        low = links_in[:, :LANES].astype(F32)
        high = links_in[:, tiles - LANES :].astype(F32)
        pad = jnp.zeros((4, LANES), F32)
        out_a[6 * EDGE : 6 * EDGE + 4, :] = jnp.where(even, low, high)
        out_b[6 * EDGE : 6 * EDGE + 4, :] = jnp.where(even, high, low)
        out_a[6 * EDGE + 4 :, :] = pad
        out_b[6 * EDGE + 4 :, :] = pad
        for copy in copies:
            copy.wait()

    @pl.when(jnp.logical_not(is_flow))
    def _():
        copies = []
        for side, out in enumerate(outs):
            off = pl.multiple_of(jnp.where(even == (side == 0), 0, elements - LANES), LANES)
            for v in range(4):
                copies.append(
                    pltpu.make_async_copy(
                        sound.at[v, :, pl.ds(off, LANES)],
                        out.at[pl.ds(v * nodes, nodes), :],
                        sems.at[side, v],
                    )
                )
        for copy in copies:
            copy.start()
        rest = jnp.zeros((out_a.shape[0] - 4 * nodes, LANES), F32)
        out_a[4 * nodes :, :] = rest
        out_b[4 * nodes :, :] = rest
        for copy in copies:
            copy.wait()


class FlowPlan:
    def __init__(self, tiles):
        self.tiles = tiles
        self.wide = tiles + 2 * EDGE
        self.blocks = 4
        self.rows = (tiles + 4 * HW) // self.blocks
        self.span = self.rows + 2 * HW

    def at(self, b):
        return HW + b * self.rows

    def inner(self):
        return range(1, self.blocks - 1)


def columns_of(place):
    return slice(place * LANES, (place + 1) * LANES)


def rows_between(parts, low, high, columns):
    taken = []
    for start, ref in parts:
        a, b = max(low, start), min(high, start + ref.shape[0])
        if a < b:
            taken.append(ref[a - start : b - start, columns])
    return taken[0] if len(taken) == 1 else jnp.concatenate(taken, 0)


def put(high, low, at, place, value):
    h, l = split_parts(value)
    high[at : at + value.shape[0], columns_of(place)] = h
    low[at : at + value.shape[0], columns_of(place)] = l


def east_west(x):
    return pltpu.roll(x, LANES - 1, 1), pltpu.roll(x, 1, 1)


def link_matrix(plan, b, first_tile, given, mat):
    rows, span = plan.rows, plan.span
    lane = lax.broadcasted_iota(jnp.int32, (rows, 2 * span), 1)
    lane = jnp.where(lane >= span, lane - span, lane)
    own = first_tile - EDGE + plan.at(b) + lax.broadcasted_iota(jnp.int32, (rows, LANES), 0)
    place = jnp.where(given < 0, own, given.astype(jnp.int32)) - (first_tile - EDGE + b * rows)
    hot = [jnp.where(place[:, k : k + 1] == lane, F32(1.0), F32(0.0)) for k in range(4)]
    mat[:rows, :] = (hot[0] + hot[1] + hot[2] + hot[3]).astype(BF16)
    mat[rows : 2 * rows, :] = (hot[0] - hot[1]).astype(BF16)
    mat[2 * rows :, :] = (hot[2] - hot[3]).astype(BF16)


def gathered(plan, mat, high, low, b, columns, at_row):
    at = b * plan.rows
    both = [rows_between(x, at, at + plan.span, columns) for x in (high, low)]
    return dot(mat[at_row:, :], jnp.concatenate(both, 0))


def advance(plan, b, mat, high, low, state, v, new_state, new_high, new_low, new_at, wanted):
    rows = plan.rows
    center = [state(k) for k in range(3)]
    scaled = [(0.5 * ADVECT) * c for c in center]
    for first, last in ((0, 2), (2, 4), (4, 5)):
        got = gathered(plan, mat, high, low, b, slice(first * LANES, last * LANES), 0)
        for place in range(first, last):
            inner = columns_of(place - first)
            total, dy, dz = got[:rows, inner], got[rows : 2 * rows, inner], got[2 * rows :, inner]
            c = center[place] if place < 3 else state(place)
            east, west = east_west(c)
            new = (
                c
                + v * (east + west + total - 6.0 * c)
                - (scaled[0] * (east - west) + scaled[1] * dy + scaled[2] * dz)
            )
            new_state[new_at : new_at + rows, columns_of(place)] = new
            if place < wanted:
                put(new_high, new_low, new_at, place, new)


def lamb_block(plan, b, mat, high, low, state, average, average_out, packed):
    rows = plan.rows
    center = [state(k) for k in range(3)]
    got = [
        gathered(plan, mat, high, low, b, slice(0, 2 * LANES), rows),
        gathered(plan, mat, high, low, b, slice(2 * LANES, 3 * LANES), rows),
    ]
    d1, d2, d3 = [], [], []
    for k in range(3):
        east, west = east_west(center[k])
        d1.append((east - west) * 0.5)
        inner = columns_of(k % 2)
        d2.append(got[k // 2][:rows, inner] * 0.5)
        d3.append(got[k // 2][rows:, inner] * 0.5)
    vx = d2[2] - d3[1]
    vy = d3[0] - d1[2]
    vz = d1[1] - d2[0]
    lamb = (
        vy * center[2] - vz * center[1],
        vz * center[0] - vx * center[2],
        vx * center[1] - vy * center[0],
    )
    to = plan.at(b) - EDGE
    low_row, top_row = max(0, -to), min(rows, plan.tiles - to)
    own = slice(to + low_row, to + top_row)
    for i in range(3):
        packed[i, own, :] = lamb[i][low_row:top_row]
        mixed = (1.0 - RELAX) * average[i, own, :] + RELAX * center[i][low_row:top_row]
        average_out[i, own, :] = mixed
        packed[3 + i, own, :] = mixed


def element_sums(projector, packed, hits, pay, own_ref, next_ref):
    nodes = projector.shape[0]
    count, elements = own_ref.shape
    proj_high, proj_low = split_parts(projector[...])
    proj_both = jnp.concatenate([proj_high, proj_low], 0)
    for c in range(6):
        x_high, x_low = split_parts(packed[c])
        main = dot_t(proj_both, x_high)
        mapped = main[:nodes] + main[nodes:] + dot_t(proj_high, x_low)
        pay[c * nodes : (c + 1) * nodes, :] = mapped.astype(BF16)
    if count > 6 * nodes:
        pay[6 * nodes :, :] = jnp.ones((count - 6 * nodes, pay.shape[1]), BF16)
    sums = dot_t(pay[...], hits[...])
    if count > 6 * nodes:
        tail = sums[6 * nodes :]
        line = lax.broadcasted_iota(jnp.int32, tail.shape, 0)
        big = jnp.floor(tail * (1.0 / BASE))
        tail = jnp.where(line == 0, tail - BASE * big, jnp.where(line == 1, big, 0.0))
        sums = jnp.concatenate([sums[: 6 * nodes], tail], 0)
    own_ref[...] = sums[:, :elements]
    next_ref[...] = sums[:, elements:].astype(BF16)


def inner_kernel(
    meta, flow, visc, links, target,
    inner_state, inner_high, inner_low, lcol, inner_mats, hits, high0, low0, square,
):
    plan = FlowPlan(flow.shape[1])
    tiles, rows = plan.tiles, plan.rows

    @pl.when(meta[0] == 1)
    def _():
        first_tile, first_element = meta[2], meta[3]
        for place, f in enumerate(FIELD_ORDER):
            put(high0, low0, 0, place, flow[f])
        square[...] = jnp.zeros_like(square)
        for part in range(tiles // LANES):
            square[:4, :] = links[:, part * LANES : (part + 1) * LANES].astype(F32)
            lcol[part * LANES : (part + 1) * LANES, :] = square[...].T
        local = target[...] - first_element
        hits[...] = jnp.where(
            lax.broadcasted_iota(jnp.int32, hits.shape, 0) == local, F32(1.0), F32(0.0)
        ).astype(BF16)
        for at, b in enumerate(plan.inner()):
            own = slice(plan.at(b) - EDGE, plan.at(b) - EDGE + rows)
            link_matrix(plan, b, first_tile, lcol[own, :], inner_mats.at[at])
            advance(
                plan, b, inner_mats.at[at], [(EDGE, high0)], [(EDGE, low0)],
                lambda place, own=own: flow[FIELD_ORDER[place], own, :],
                visc[own, :], inner_state, inner_high, inner_low, at * rows, 5,
            )


def band_parts(plan, edge, inner):
    rows, last = plan.rows, plan.blocks - 1
    return [
        (plan.at(0), edge.at[:rows]),
        (plan.at(1), inner),
        (plan.at(last), edge.at[rows:]),
    ]


def band_state(plan, b, edge, inner):
    at = plan.at(b)
    parts = band_parts(plan, edge, inner)
    return lambda place: rows_between(parts, at, at + plan.rows, columns_of(place))


def closed(plan, parts, zero):
    return [(0, zero), *parts, (plan.wide - HW, zero)]


def mats_of(plan, b, edge_mats, inner_mats):
    if b in plan.inner():
        return inner_mats.at[b - 1]
    return edge_mats.at[0 if b == 0 else 1]


def first_kernel(
    meta, flow, visc, mean, projector, part_a, part_b, sound, neighbours, codes,
    inner_state, inner_high, inner_low, lcol, inner_mats, hits,
    own_one, next_one, mean_one, base, grads,
    edge_state, edge_high, edge_low, edge_mats, edge_visc,
    square, state0, high0, low0, zero, packed, pay, rows_of, facing, remote, rhs,
):
    is_flow, even = meta[0] == 1, meta[1] == 1
    plan = FlowPlan(packed.shape[1])
    tiles, rows, span = plan.tiles, plan.rows, plan.span
    own_rows = span - EDGE

    @pl.when(is_flow)
    def _():
        first_tile = meta[2]

        def pick(at, size):
            a, b = part_a[at : at + size, :], part_b[at : at + size, :]
            return jnp.where(even, a, b), jnp.where(even, b, a)

        zero[...] = jnp.zeros_like(zero)
        for place, f in enumerate(FIELD_ORDER):
            before, after = pick(place * EDGE, EDGE)
            ends = (
                jnp.concatenate([before, flow[f, :own_rows, :]], 0),
                jnp.concatenate([flow[f, tiles - own_rows :, :], after], 0),
            )
            for side in range(2):
                state0[side, :, columns_of(place)] = ends[side]
                put(high0.at[side], low0.at[side], 0, place, ends[side])
        before, after = pick(5 * EDGE, EDGE)
        edge_visc[:rows, :] = jnp.concatenate([before[HW:], visc[: rows - EDGE + HW, :]], 0)
        edge_visc[rows:, :] = jnp.concatenate(
            [visc[tiles - (rows - EDGE + HW) :, :], after[: EDGE - HW]], 0
        )
        before, after = pick(6 * EDGE, 8)
        given = []
        for side, block in enumerate((before, after)):
            square[...] = jnp.zeros_like(square)
            square[:8, :] = block
            turned = square[...].T
            given.append(
                jnp.concatenate([turned[LANES - EDGE + HW :], lcol[: rows - EDGE + HW, :]], 0)
                if side == 0
                else jnp.concatenate(
                    [lcol[tiles - (rows - EDGE + HW) :, :], turned[: EDGE - HW]], 0
                )
            )
        for side, b in enumerate((0, plan.blocks - 1)):
            link_matrix(plan, b, first_tile, given[side], edge_mats.at[side])
            advance(
                plan, b, edge_mats.at[side],
                [(b * rows, high0.at[side])], [(b * rows, low0.at[side])],
                lambda place, side=side: state0[side, HW : HW + rows, columns_of(place)],
                edge_visc[side * rows : (side + 1) * rows, :],
                edge_state, edge_high, edge_low, side * rows, 5,
            )
        high1 = closed(plan, band_parts(plan, edge_high, inner_high), zero)
        low1 = closed(plan, band_parts(plan, edge_low, inner_low), zero)
        for b in range(plan.blocks):
            lamb_block(
                plan, b, mats_of(plan, b, edge_mats, inner_mats), high1, low1,
                band_state(plan, b, edge_state, inner_state), mean, mean_one, packed,
            )
        element_sums(projector, packed, hits, pay, own_one, next_one)

    @pl.when(jnp.logical_not(is_flow))
    def _():
        own_one[...] = jnp.zeros_like(own_one)
        next_one[...] = jnp.zeros_like(next_one)
        nodes, elements = sound.shape[1:]
        halves = elements // LANES
        block = 4 * nodes
        for v in range(4):
            for h in range(halves):
                rows_of[h * block + v * nodes : h * block + (v + 1) * nodes, :] = sound[
                    v, :, h * LANES : (h + 1) * LANES
                ]
        a, b = part_a[:block, :], part_b[:block, :]
        rows_of[halves * block : (halves + 1) * block, :] = jnp.where(even, a, b)
        rows_of[(halves + 1) * block : (halves + 2) * block, :] = jnp.where(even, b, a)
        for face in range(6):
            for part in range(halves + 2):
                facing_rows(rows_of, part * block, nodes, face ^ 1, facing.at[face, part])
            hot = hot_links(neighbours, face, meta[3], elements, True, True)
            remote_rows([facing[face, part] for part in range(halves + 2)], hot, remote, face)
        derivatives(rows_of, nodes, grads, rhs)
        add_faces(rows_of, nodes, remote, neighbours, codes, rhs, True)
        for n in range(nodes):
            base[n] = rows_of[pl.ds(n, 8, stride=nodes), :] + ACOUSTIC_STEP * rhs[n]


def second_kernel(
    meta, flow, visc, inner_state, inner_high, inner_low, inner_mats,
    edge_state, edge_high, edge_low, edge_mats, edge_visc,
    flow_out, state, high, low, passive, zero,
):
    plan = FlowPlan(flow.shape[1])
    rows = plan.rows
    is_flow = meta[0] == 1

    @pl.when(jnp.logical_not(is_flow))
    def _():
        flow_out[...] = flow[...]

    @pl.when(is_flow)
    def _():
        zero[...] = jnp.zeros_like(zero)
        high1 = closed(plan, band_parts(plan, edge_high, inner_high), zero)
        low1 = closed(plan, band_parts(plan, edge_low, inner_low), zero)
        for b in range(plan.blocks):
            if b in plan.inner():
                v = visc[plan.at(b) - EDGE : plan.at(b) - EDGE + rows, :]
            else:
                v = edge_visc[:rows, :] if b == 0 else edge_visc[rows:, :]
            advance(
                plan, b, mats_of(plan, b, edge_mats, inner_mats), high1, low1,
                band_state(plan, b, edge_state, inner_state), v,
                passive, high, low, b * rows, 3,
            )
        own = slice(EDGE - HW, EDGE - HW + plan.tiles)
        state[...] = passive[:, : state.shape[1]]
        for place, f in enumerate(FIELD_ORDER):
            flow_out[f] = passive[own, columns_of(place)]


def sums_kernel(
    meta, mean, mean_one, projector, inner_mats, edge_mats, hits, state, high, low,
    mean_out, own_two, next_two, zero, packed, pay,
):
    plan = FlowPlan(packed.shape[1])
    rows = plan.rows
    is_flow = meta[0] == 1

    @pl.when(jnp.logical_not(is_flow))
    def _():
        mean_out[...] = mean[...]
        own_two[...] = jnp.zeros_like(own_two)
        next_two[...] = jnp.zeros_like(next_two)

    @pl.when(is_flow)
    def _():
        zero[...] = jnp.zeros_like(zero)
        for b in range(plan.blocks):
            lamb_block(
                plan, b, mats_of(plan, b, edge_mats, inner_mats),
                closed(plan, [(HW, high)], zero), closed(plan, [(HW, low)], zero),
                lambda place, b=b: state[b * rows : (b + 1) * rows, columns_of(place)],
                mean_one, mean_out, packed,
            )
        element_sums(projector, packed, hits, pay, own_two, next_two)


def facing_rows(rows_of, base, nodes, face, to):
    axis, level = face // 2, 3 * (face % 2)
    if axis == 0:
        to[...] = rows_of[pl.ds(base + level, 64, stride=4), :]
    elif axis == 1:
        for i in range(4):
            to[pl.ds(i, 16, stride=4), :] = rows_of[pl.ds(base + i + 4 * level, 16, stride=16), :]
    else:
        for v in range(4):
            at = base + v * nodes + 16 * level
            to[v * 16 : (v + 1) * 16, :] = rows_of[at : at + 16, :]


def hot_links(neighbours, face, first_element, elements, own, beside):
    link = neighbours[face : face + 1, :]
    near = link - first_element
    size = (elements if own else 0) + (2 * LANES if beside else 0)
    start = elements if own else 0
    place = jnp.where(near < 0, start + LANES + near, near - elements + start + LANES)
    inside = (near >= 0) & (near < elements)
    place = jnp.where(inside, near if own else -1, place if beside else -1)
    place = jnp.where(link < 0, -1, place)
    key = lax.broadcasted_iota(jnp.int32, (size, elements), 0)
    return jnp.where(key == place, F32(1.0), F32(0.0)).astype(BF16)


def remote_rows(parts, hot, remote, face):
    x = jnp.concatenate(parts, 1)
    if x.dtype == BF16:
        got = dot(x, hot)
    else:
        high, low = split_parts(x)
        got = dot(jnp.concatenate([high, low], 0), hot)
        got = got[:64] + got[64:]
    for h in range(got.shape[1] // LANES):
        remote[face, h * 64 : (h + 1) * 64, :] = got[:, h * LANES : (h + 1) * LANES]


def derivatives(rows_of, nodes, grads_out, rhs):
    matrix = lobatto_matrix()
    line = lax.broadcasted_iota(jnp.int32, (8, LANES), 0)
    is_v = [line % 4 == v for v in range(4)]
    node = [rows_of[pl.ds(n, 8, stride=nodes), :] for n in range(nodes)]
    for n in range(nodes):
        i, j, k = n % 4, n // 4 % 4, n // 16
        lines = (
            [m + 4 * j + 16 * k for m in range(4)],
            [i + 4 * m + 16 * k for m in range(4)],
            [i + 4 * j + 16 * m for m in range(4)],
        )
        grads = []
        for d, at in enumerate((i, j, k)):
            total = None
            for m in range(4):
                if abs(matrix[at, m]) > 1e-12:
                    term = F32(matrix[at, m]) * node[lines[d][m]]
                    total = term if total is None else total + term
            grads.append(total)
            grads_out[d, n] = total
        div = sum(pltpu.roll(grads[d], 8 - (1 + d), 0) for d in range(3))
        coupled = jnp.where(is_v[0], div, 0.0)
        for d in range(3):
            coupled = jnp.where(is_v[1 + d], pltpu.roll(grads[d], 1 + d, 0), coupled)
        rhs[n] = -coupled


def add_faces(rows_of, nodes, remote, neighbours, codes, rhs, own):
    upper = lax.broadcasted_iota(jnp.int32, (8, LANES), 0) >= 4
    for face in range(6):

        def both(row):
            return jnp.where(
                upper,
                jnp.broadcast_to(row[:, LANES:], (8, LANES)),
                jnp.broadcast_to(row[:, :LANES], (8, LANES)),
            )

        code = both(codes[face : face + 1, :])
        valid = both(neighbours[face : face + 1, :]) >= 0
        is_turn = [code == t for t in range(4)]
        planes = [remote[face, pl.ds(p, 8, stride=16), :] for p in range(16)]
        for p, n in enumerate(face_nodes(face)):
            jump = planes[turned_position(3, p)]
            for t in range(3):
                jump = jnp.where(is_turn[t], planes[turned_position(t, p)], jump)
            if own:
                jump = jnp.where(valid, jump - rows_of[pl.ds(n, 8, stride=nodes), :], 0.0)
            rhs[n] = rhs[n] + PENALTY * jump


def source_rows(total, nodes, lamb, mean):
    block = 4 * nodes
    for h in range(total.shape[1] // LANES):
        columns = slice(h * LANES, (h + 1) * LANES)
        lamb[h * block : h * block + nodes, :] = jnp.zeros((nodes, LANES), F32)
        for d in range(3):
            at = h * block + (1 + d) * nodes
            lamb[at : at + nodes, :] = total[d * nodes : (d + 1) * nodes, columns]
            value = total[(3 + d) * nodes : (4 + d) * nodes, columns]
            for v in range(4):
                at = h * block + v * nodes
                mean[d, at : at + nodes, :] = value


def source_terms(nodes, grads, lamb, mean, n):
    total = lamb[pl.ds(n, 8, stride=nodes), :]
    for d in range(3):
        total = total + mean[d, pl.ds(n, 8, stride=nodes), :] * grads[d, n]
    return total


def sound_one_kernel(
    meta, base, grads, source_a, source_b, rows_of, scale_out, edge_a, edge_b, lamb, mean
):
    is_flow, even = meta[0] == 1, meta[1] == 1
    nodes = base.shape[0]
    block = 4 * nodes

    @pl.when(jnp.logical_not(is_flow))
    def _():
        total = source_a[...].astype(F32) + source_b[...].astype(F32)
        count = total[6 * nodes : 6 * nodes + 1] + BASE * total[6 * nodes + 1 : 6 * nodes + 2]
        inverse = 1.0 / jnp.maximum(count, 1.0)
        scale_out[...] = jnp.broadcast_to(inverse, scale_out.shape)
        source_rows(total[: 6 * nodes] * inverse, nodes, lamb, mean)
        for n in range(nodes):
            rows_of[pl.ds(n, 8, stride=nodes), :] = base[n] - ACOUSTIC_STEP * source_terms(
                nodes, grads, lamb, mean, n
            )
        off_a = pl.multiple_of(jnp.where(even, 0, block), 16)
        off_b = pl.multiple_of(jnp.where(even, block, 0), 16)
        edge_a[...] = rows_of[pl.ds(off_a, block), :].astype(BF16)
        edge_b[...] = rows_of[pl.ds(off_b, block), :].astype(BF16)


def sound_inner_kernel(
    meta, rows_of, neighbours, codes, base, grads, hot_beside, facing, remote, rhs
):
    nodes = base.shape[0]
    elements = neighbours.shape[1]
    halves = elements // LANES
    block = 4 * nodes

    @pl.when(meta[0] == 0)
    def _():
        for face in range(6):
            for part in range(halves):
                facing_rows(rows_of, part * block, nodes, face ^ 1, facing.at[face, part])
            hot = hot_links(neighbours, face, meta[3], elements, True, False)
            remote_rows([facing[face, part] for part in range(halves)], hot, remote, face)
            hot_beside[face] = hot_links(neighbours, face, meta[3], elements, False, True)
        derivatives(rows_of, nodes, grads, rhs)
        add_faces(rows_of, nodes, remote, neighbours, codes, rhs, True)
        for n in range(nodes):
            base[n] = rows_of[pl.ds(n, 8, stride=nodes), :] + ACOUSTIC_STEP * rhs[n]


def sound_two_kernel(
    meta, sound, base, grads, hot_beside, neighbours, codes, scale, source_a, source_b,
    part_a, part_b,
    out, rows_of, facing, remote, rhs, lamb, mean,
):
    is_flow, even = meta[0] == 1, meta[1] == 1
    nodes = base.shape[0]
    elements = sound.shape[2]
    halves = elements // LANES
    block = 4 * nodes

    @pl.when(is_flow)
    def _():
        out[...] = sound[...]

    @pl.when(jnp.logical_not(is_flow))
    def _():
        total = source_a[...].astype(F32) + source_b[...].astype(F32)
        source_rows(total * scale[0:1, :], nodes, lamb, mean)
        a, b = part_a[...].astype(F32), part_b[...].astype(F32)
        rows_of[:block, :] = jnp.where(even, a, b)
        rows_of[block:, :] = jnp.where(even, b, a)
        for face in range(6):
            for part in range(2):
                facing_rows(rows_of, part * block, nodes, face ^ 1, facing.at[face, part])
            remote_rows(
                [facing[face, part].astype(BF16) for part in range(2)], hot_beside[face], remote, face
            )
        for n in range(nodes):
            rhs[n] = -source_terms(nodes, grads, lamb, mean, n)
        add_faces(rows_of, nodes, remote, neighbours, codes, rhs, False)
        for n in range(nodes):
            rows_of[pl.ds(n, 8, stride=nodes), :] = base[n] + ACOUSTIC_STEP * rhs[n]
        for v in range(4):
            for h in range(halves):
                out[v, :, h * LANES : (h + 1) * LANES] = rows_of[
                    h * block + v * nodes : h * block + (v + 1) * nodes, :
                ]


def call(kernel, outs, scratch, operands, flops=1e8, in_hbm=(), limit=VMEM_LIMIT):
    spaces = [pltpu.SMEM] + [
        pltpu.HBM if at in in_hbm else pltpu.VMEM for at in range(1, len(operands))
    ]
    moved = sum(int(np.prod(x.shape)) * x.dtype.itemsize for x in (*operands, *outs))
    return pl.pallas_call(
        kernel,
        out_shape=tuple(outs),
        in_specs=[pl.BlockSpec(memory_space=space) for space in spaces],
        out_specs=tuple([pl.BlockSpec(memory_space=pltpu.VMEM)] * len(outs)),
        scratch_shapes=scratch,
        compiler_params=pltpu.CompilerParams(vmem_limit_bytes=limit),
        cost_estimate=pl.CostEstimate(flops=int(flops), bytes_accessed=moved, transcendentals=0),
    )(*operands)


def body(
    flow_fields,
    mean_velocity,
    cell_eddy_viscosity,
    tile_links,
    tile_target,
    projector,
    acoustic_state,
    element_face_neighbours,
    face_codes,
):
    groups = lax.axis_size("grp")
    count = lax.axis_size("sfc")
    group_index = lax.axis_index("grp")
    column = lax.axis_index("sfc")
    flow = flow_fields[0]
    mean = mean_velocity[0]
    visc = cell_eddy_viscosity[0]
    links = tile_links[0]
    sound = acoustic_state[0]
    neighbours = element_face_neighbours[0]
    codes = face_codes[0]
    tiles = flow.shape[1]
    _, nodes, elements = sound.shape
    halves = elements // LANES
    block = 4 * nodes
    plan = FlowPlan(tiles)
    shape = jax.ShapeDtypeStruct
    vmem = pltpu.VMEM
    meta = jnp.stack(
        [
            (group_index < groups - 1).astype(jnp.int32),
            (column % 2 == 0).astype(jnp.int32),
            (column * tiles).astype(jnp.int32),
            (column * elements).astype(jnp.int32),
        ]
    )

    pairs_a = [p for i in range(1, count - 1, 2) for p in ((i, i + 1), (i + 1, i))]
    pairs_b = [p for i in range(0, count - 1, 2) for p in ((i, i + 1), (i + 1, i))]

    edge_rows = 6 * EDGE + 8
    pack_a, pack_b = call(
        pack_kernel,
        [shape((edge_rows, LANES), F32)] * 2,
        [
            vmem(links.shape, jnp.int32),
            pltpu.SemaphoreType.DMA((2, 6)),
            pltpu.SemaphoreType.DMA,
        ],
        [meta, flow, visc, links, sound],
        in_hbm=(1, 2, 3, 4),
        limit=PACK_LIMIT,
    )
    part_a = lax.ppermute(pack_a, "sfc", pairs_a)
    part_b = lax.ppermute(pack_b, "sfc", pairs_b)

    fields = 5 * LANES
    rows, span = plan.rows, plan.span
    inner_rows = (plan.blocks - 2) * rows
    square = vmem((LANES, LANES), F32)
    packed = vmem((6, tiles, LANES), F32)
    inner_state, inner_high, inner_low, lcol, inner_mats, hits = call(
        inner_kernel,
        [
            shape((inner_rows, fields), F32),
            shape((inner_rows, fields), BF16),
            shape((inner_rows, fields), BF16),
            shape((tiles, LANES), F32),
            shape((plan.blocks - 2, 3 * rows, 2 * span), BF16),
            shape((2 * elements, tiles), BF16),
        ],
        [vmem((tiles, fields), BF16), vmem((tiles, fields), BF16), square],
        [meta, flow, visc, links, tile_target],
        flops=1e9,
    )
    lines = 6 * nodes + EXTRA
    by_node = shape((nodes, 8, LANES), F32)
    by_node_3 = shape((3, nodes, 8, LANES), F32)
    node_rows = vmem((nodes, 8, LANES), F32)
    (
        own_one, next_one, mean_one, base, grads,
        edge_state, edge_high, edge_low, edge_mats, edge_visc,
    ) = call(
        first_kernel,
        [
            shape((lines, elements), F32),
            shape((lines, elements), BF16),
            shape(mean.shape, F32),
            by_node,
            by_node_3,
            shape((2 * rows, fields), F32),
            shape((2 * rows, fields), BF16),
            shape((2 * rows, fields), BF16),
            shape((2, 3 * rows, 2 * span), BF16),
            shape((2 * rows, LANES), F32),
        ],
        [
            square,
            vmem((2, span, fields), F32),
            vmem((2, span, fields), BF16),
            vmem((2, span, fields), BF16),
            vmem((HW, fields), BF16),
            packed,
            vmem((lines, tiles), BF16),
            vmem(((halves + 2) * block, LANES), F32),
            vmem((6, halves + 2, 64, LANES), F32),
            vmem((6, halves * 64, LANES), F32),
            node_rows,
        ],
        [
            meta, flow, visc, mean, projector, part_a, part_b, sound, neighbours, codes,
            inner_state, inner_high, inner_low, lcol, inner_mats, hits,
        ],
        flops=1e9,
    )

    up = [(i, i + 1) for i in range(count - 1)]

    def climb(x):
        chosen = [(g * count + i, g * count + j) for g in range(groups - 1) for i, j in up]
        return lax.ppermute(x, ("grp", "sfc"), chosen)

    def combined(*xs):
        total = xs[0]
        for x in xs[1:]:
            total = total + x.astype(F32)
        return total.astype(BF16)

    got_one = climb(next_one)
    velocity = 3 * LANES
    band = plan.blocks * rows
    flow_out, state2, high2, low2 = call(
        second_kernel,
        [
            shape(flow.shape, F32),
            shape((band, velocity), F32),
            shape((band, velocity), BF16),
            shape((band, velocity), BF16),
        ],
        [vmem((band, fields), F32), vmem((HW, fields), BF16)],
        [
            meta, flow, visc, inner_state, inner_high, inner_low, inner_mats,
            edge_state, edge_high, edge_low, edge_mats, edge_visc,
        ],
        flops=1e9,
    )
    sum_one, high2 = lax.optimization_barrier((combined(own_one, got_one), high2))
    x_one = lax.ppermute(sum_one, "grp", [(0, 1), (2, 3)])
    mean_out, own_two, next_two = call(
        sums_kernel,
        [
            shape(mean.shape, F32),
            shape((6 * nodes, elements), F32),
            shape((6 * nodes, elements), BF16),
        ],
        [vmem((HW, velocity), BF16), packed, vmem((6 * nodes, tiles), BF16)],
        [meta, mean, mean_one, projector, inner_mats, edge_mats, hits, state2, high2, low2],
        flops=1e9,
    )
    got_two = climb(next_two)
    sum_one = combined(own_one, got_one, x_one)
    sum_one, own_two = lax.optimization_barrier((sum_one, own_two))
    sum_two = lax.optimization_barrier(combined(own_two, got_two))
    padded = jnp.pad(sum_two, ((0, EXTRA), (0, 0)))
    cross = lax.ppermute(jnp.where(group_index == 0, padded, sum_one), "grp", [(0, 2), (1, 3)])
    y_two = lax.ppermute(sum_two, "grp", [(1, 3)])

    sound_rows, scale, edge_a, edge_b = call(
        sound_one_kernel,
        [
            shape((halves * block, LANES), F32),
            shape((8, elements), F32),
            shape((block, LANES), BF16),
            shape((block, LANES), BF16),
        ],
        [vmem((halves * block, LANES), F32), vmem((3, halves * block, LANES), F32)],
        [meta, base, grads, x_one, cross],
    )
    last = (groups - 1) * count
    part_a = lax.ppermute(edge_a, ("grp", "sfc"), [(last + i, last + j) for i, j in pairs_a])
    part_b = lax.ppermute(edge_b, ("grp", "sfc"), [(last + i, last + j) for i, j in pairs_b])
    base, grads, hot_beside = call(
        sound_inner_kernel,
        [by_node, by_node_3, shape((6, 2 * LANES, elements), BF16)],
        [
            vmem((6, halves, 64, LANES), F32),
            vmem((6, halves * 64, LANES), F32),
            node_rows,
        ],
        [meta, sound_rows, neighbours, codes],
    )
    x_two = lax.ppermute(combined(own_two, got_two, cross[: 6 * nodes]), "grp", [(2, 3)])
    (sound_out,) = call(
        sound_two_kernel,
        [shape(sound.shape, F32)],
        [
            vmem((halves * block, LANES), F32),
            vmem((6, 2, 64, LANES), F32),
            vmem((6, halves * 64, LANES), F32),
            node_rows,
            vmem((halves * block, LANES), F32),
            vmem((3, halves * block, LANES), F32),
        ],
        [
            meta, sound, base, grads, hot_beside, neighbours, codes, scale,
            x_two, y_two, part_a, part_b,
        ],
    )
    return flow_out[None], mean_out[None], sound_out[None]


def solution(mesh):
    placed = (
        P("grp", None, "sfc", None),
        P("grp", None, "sfc", None),
        P("grp", "sfc", None),
        P("grp", None, "sfc"),
        P("grp", "sfc"),
        P(),
        P("grp", None, None, "sfc"),
        P("grp", None, "sfc"),
        P("grp", None, "sfc"),
    )
    return jax.shard_map(
        body,
        mesh=mesh,
        in_specs=placed,
        out_specs=(
            P("grp", None, "sfc", None),
            P("grp", None, "sfc", None),
            P("grp", None, None, "sfc"),
        ),
        check_vma=False,
    )
```

```python
import jax
import jax.numpy as jnp
import numpy as np
from jax import lax
from jax.experimental import pallas as pl
from jax.experimental.pallas import tpu as pltpu
from jax.sharding import PartitionSpec as P

HW = 16
HE = 16

ADVECT = 0.1
RELAX = 0.1
PENALTY = 1.5
ACOUSTIC_STEP = 0.08

LANES = 128
EDGE = 3 * HW
FIELD_ORDER = (1, 2, 3, 0, 4)
BASE = 32.0
EXTRA = 16
VMEM_LIMIT = 20 * 1024 * 1024
PACK_LIMIT = 64 * 1024 * 1024 - 256 * 1024

F32 = jnp.float32
BF16 = jnp.bfloat16


def lobatto_matrix():
    points = np.array([-1.0, -1.0 / np.sqrt(5.0), 1.0 / np.sqrt(5.0), 1.0])
    weights = np.array(
        [
            1.0 / np.prod([points[col] - points[other] for other in range(4) if other != col])
            for col in range(4)
        ]
    )
    matrix = np.zeros((4, 4))
    for line in range(4):
        for col in range(4):
            if line != col:
                matrix[line, col] = weights[col] / weights[line] / (points[line] - points[col])
        matrix[line, line] = -matrix[line].sum()
    return matrix.astype(np.float32)


def face_nodes(face):
    axis, level = face // 2, 3 * (face % 2)
    nodes = []
    for second in range(4):
        for first in range(4):
            coords = [first, second]
            coords.insert(axis, level)
            nodes.append(coords[0] + 4 * coords[1] + 16 * coords[2])
    return nodes


def turned_position(turn, position):
    a, b = position % 4, position // 4
    a, b = ((a, b), (3 - b, a), (3 - a, 3 - b), (b, 3 - a))[turn]
    return a + 4 * b


def split_parts(x):
    high = x.astype(BF16)
    return high, (x - high.astype(F32)).astype(BF16)


def dot(a, b):
    return jnp.dot(a, b, preferred_element_type=F32)


def dot_t(a, b):
    return lax.dot_general(a, b, (((1,), (1,)), ((), ())), preferred_element_type=F32)


def pack_kernel(meta, flow, visc, links, sound, out_a, out_b, links_in, staged, sems, link_sem):
    is_flow, even = meta[0] == 1, meta[1] == 1
    tiles = flow.shape[1]
    _, nodes, elements = sound.shape
    outs = (out_a, out_b)

    @pl.when(is_flow)
    def _():
        fetch = pltpu.make_async_copy(links, links_in, link_sem)
        fetch.start()
        copies = []
        for side in range(2):
            off = pl.multiple_of(jnp.where(even == (side == 0), 0, tiles - EDGE), 8)
            for place, f in enumerate(FIELD_ORDER):
                copies.append(
                    pltpu.make_async_copy(
                        flow.at[f, pl.ds(off, EDGE), :],
                        staged.at[side, pl.ds(place * EDGE, EDGE), :],
                        sems.at[side, place],
                    )
                )
            copies.append(
                pltpu.make_async_copy(
                    visc.at[pl.ds(off, EDGE), :],
                    staged.at[side, pl.ds(5 * EDGE, EDGE), :],
                    sems.at[side, 5],
                )
            )
        for copy in copies:
            copy.start()
        fetch.wait()
        given = links_in[...]
        own = meta[2] + lax.broadcasted_iota(jnp.int32, given.shape, 1)
        offset = jnp.where(given < 0, 0, given - own).astype(F32)
        low, high = offset[:, :LANES], offset[:, tiles - LANES :]
        pad = jnp.zeros((EXTRA - 4, LANES), F32)
        for side, (a, b) in enumerate(((low, high), (high, low))):
            block = jnp.concatenate([jnp.where(even, a, b), pad], 0)
            outs[side][6 * EDGE :, :] = block.astype(BF16)
        for copy in copies:
            copy.wait()
        for side in range(2):
            outs[side][: 6 * EDGE, :] = staged[side].astype(BF16)

    @pl.when(jnp.logical_not(is_flow))
    def _():
        copies = []
        for side in range(2):
            off = pl.multiple_of(jnp.where(even == (side == 0), 0, elements - LANES), LANES)
            for v in range(4):
                copies.append(
                    pltpu.make_async_copy(
                        sound.at[v, :, pl.ds(off, LANES)],
                        staged.at[side, pl.ds(v * nodes, nodes), :],
                        sems.at[side, v],
                    )
                )
        for copy in copies:
            copy.start()
        for copy in copies:
            copy.wait()
        for side, out in enumerate(outs):
            out[: 4 * nodes, :] = staged[side, : 4 * nodes, :].astype(BF16)
            out[4 * nodes :, :] = jnp.zeros((out.shape[0] - 4 * nodes, LANES), BF16)


class FlowPlan:
    def __init__(self, tiles):
        self.tiles = tiles
        self.wide = tiles + 2 * EDGE
        self.blocks = 4
        self.rows = (tiles + 4 * HW) // self.blocks
        self.span = self.rows + 2 * HW

    def at(self, b):
        return HW + b * self.rows

    def inner(self):
        return range(1, self.blocks - 1)


def columns_of(place):
    return slice(place * LANES, (place + 1) * LANES)


def rows_between(parts, low, high, columns):
    taken = []
    for start, ref in parts:
        a, b = max(low, start), min(high, start + ref.shape[0])
        if a < b:
            taken.append(ref[a - start : b - start, columns])
    return taken[0] if len(taken) == 1 else jnp.concatenate(taken, 0)


def put(high, low, at, place, value):
    h, l = split_parts(value)
    high[at : at + value.shape[0], columns_of(place)] = h
    low[at : at + value.shape[0], columns_of(place)] = l


def east_west(x):
    return pltpu.roll(x, LANES - 1, 1), pltpu.roll(x, 1, 1)


def link_matrix(plan, offset, mat):
    rows, span = plan.rows, plan.span
    lane = lax.broadcasted_iota(jnp.int32, (rows, 2 * span), 1)
    lane = jnp.where(lane >= span, lane - span, lane)
    place = HW + lax.broadcasted_iota(jnp.int32, (rows, LANES), 0) + offset.astype(jnp.int32)
    hot = [jnp.where(place[:, k : k + 1] == lane, F32(1.0), F32(0.0)) for k in range(4)]
    mat[:rows, :] = (hot[0] + hot[1] + hot[2] + hot[3]).astype(BF16)
    mat[rows : 2 * rows, :] = (hot[0] - hot[1]).astype(BF16)
    mat[2 * rows :, :] = (hot[2] - hot[3]).astype(BF16)


def gathered(plan, mat, high, low, b, columns, at_row):
    at = b * plan.rows
    both = [rows_between(x, at, at + plan.span, columns) for x in (high, low)]
    return dot(mat[at_row:, :], jnp.concatenate(both, 0))


def advance(plan, b, mat, high, low, state, v, new_state, new_high, new_low, new_at, wanted):
    rows = plan.rows
    center = [state(k) for k in range(3)]
    scaled = [(0.5 * ADVECT) * c for c in center]
    for first, last in ((0, 2), (2, 4), (4, 5)):
        got = gathered(plan, mat, high, low, b, slice(first * LANES, last * LANES), 0)
        for place in range(first, last):
            inner = columns_of(place - first)
            total, dy, dz = got[:rows, inner], got[rows : 2 * rows, inner], got[2 * rows :, inner]
            c = center[place] if place < 3 else state(place)
            east, west = east_west(c)
            new = (
                c
                + v * (east + west + total - 6.0 * c)
                - (scaled[0] * (east - west) + scaled[1] * dy + scaled[2] * dz)
            )
            new_state[new_at : new_at + rows, columns_of(place)] = new
            if place < wanted:
                put(new_high, new_low, new_at, place, new)


def lamb_block(plan, b, mat, high, low, state, average, average_out, packed):
    rows = plan.rows
    center = [state(k) for k in range(3)]
    got = [
        gathered(plan, mat, high, low, b, slice(0, 2 * LANES), rows),
        gathered(plan, mat, high, low, b, slice(2 * LANES, 3 * LANES), rows),
    ]
    d1, d2, d3 = [], [], []
    for k in range(3):
        east, west = east_west(center[k])
        d1.append((east - west) * 0.5)
        inner = columns_of(k % 2)
        d2.append(got[k // 2][:rows, inner] * 0.5)
        d3.append(got[k // 2][rows:, inner] * 0.5)
    vx = d2[2] - d3[1]
    vy = d3[0] - d1[2]
    vz = d1[1] - d2[0]
    lamb = (
        vy * center[2] - vz * center[1],
        vz * center[0] - vx * center[2],
        vx * center[1] - vy * center[0],
    )
    to = plan.at(b) - EDGE
    low_row, top_row = max(0, -to), min(rows, plan.tiles - to)
    own = slice(to + low_row, to + top_row)
    for i in range(3):
        packed[i, own, :] = lamb[i][low_row:top_row]
        mixed = (1.0 - RELAX) * average[i, own, :] + RELAX * center[i][low_row:top_row]
        average_out[i, own, :] = mixed
        packed[3 + i, own, :] = mixed


def element_sums(projector, packed, hits, pay, own_ref, next_ref):
    nodes = projector.shape[0]
    count, elements = own_ref.shape
    proj_high, proj_low = split_parts(projector[...])
    proj_both = jnp.concatenate([proj_high, proj_low], 0)
    for c in range(6):
        x_high, x_low = split_parts(packed[c])
        main = dot_t(proj_both, x_high)
        mapped = main[:nodes] + main[nodes:] + dot_t(proj_high, x_low)
        pay[c * nodes : (c + 1) * nodes, :] = mapped.astype(BF16)
    if count > 6 * nodes:
        pay[6 * nodes :, :] = jnp.ones((count - 6 * nodes, pay.shape[1]), BF16)
    sums = dot_t(pay[...], hits[...])
    if count > 6 * nodes:
        tail = sums[6 * nodes :]
        line = lax.broadcasted_iota(jnp.int32, tail.shape, 0)
        big = jnp.floor(tail * (1.0 / BASE))
        tail = jnp.where(line == 0, tail - BASE * big, jnp.where(line == 1, big, 0.0))
        sums = jnp.concatenate([sums[: 6 * nodes], tail], 0)
    own_ref[...] = sums[:, :elements]
    next_ref[...] = sums[:, elements:].astype(BF16)


def inner_kernel(
    meta, flow, visc, links, target,
    inner_state, inner_high, inner_low, lcol, inner_mats, hits, high0, low0, square,
):
    plan = FlowPlan(flow.shape[1])
    tiles, rows = plan.tiles, plan.rows

    @pl.when(meta[0] == 1)
    def _():
        first_tile, first_element = meta[2], meta[3]
        for place, f in enumerate(FIELD_ORDER):
            put(high0, low0, 0, place, flow[f])
        square[...] = jnp.zeros_like(square)
        own_tile = first_tile + lax.broadcasted_iota(jnp.int32, links.shape, 1)
        offset = jnp.where(links[...] < 0, 0, links[...] - own_tile).astype(F32)
        for part in range(tiles // LANES):
            square[:4, :] = offset[:, part * LANES : (part + 1) * LANES]
            lcol[part * LANES : (part + 1) * LANES, :] = square[...].T
        local = target[...] - first_element
        hits[...] = jnp.where(
            lax.broadcasted_iota(jnp.int32, hits.shape, 0) == local, F32(1.0), F32(0.0)
        ).astype(BF16)
        for at, b in enumerate(plan.inner()):
            own = slice(plan.at(b) - EDGE, plan.at(b) - EDGE + rows)
            link_matrix(plan, lcol[own, :], inner_mats.at[at])
            advance(
                plan, b, inner_mats.at[at], [(EDGE, high0)], [(EDGE, low0)],
                lambda place, own=own: flow[FIELD_ORDER[place], own, :],
                visc[own, :], inner_state, inner_high, inner_low, at * rows, 5,
            )


def band_parts(plan, edge, inner):
    rows, last = plan.rows, plan.blocks - 1
    return [
        (plan.at(0), edge.at[:rows]),
        (plan.at(1), inner),
        (plan.at(last), edge.at[rows:]),
    ]


def band_state(plan, b, edge, inner):
    at = plan.at(b)
    parts = band_parts(plan, edge, inner)
    return lambda place: rows_between(parts, at, at + plan.rows, columns_of(place))


def closed(plan, parts, zero):
    return [(0, zero), *parts, (plan.wide - HW, zero)]


def mats_of(plan, b, edge_mats, inner_mats):
    if b in plan.inner():
        return inner_mats.at[b - 1]
    return edge_mats.at[0 if b == 0 else 1]


def first_kernel(
    meta, flow, visc, mean, projector, part_a, part_b, sound, neighbours, codes,
    inner_state, inner_high, inner_low, lcol, inner_mats, hits,
    own_one, next_one, mean_one, base, grads,
    edge_state, edge_high, edge_low, edge_mats, edge_visc,
    square, state0, high0, low0, zero, packed, pay, rows_of, facing, remote, rhs,
):
    is_flow, even = meta[0] == 1, meta[1] == 1
    plan = FlowPlan(packed.shape[1])
    tiles, rows, span = plan.tiles, plan.rows, plan.span
    own_rows = span - EDGE

    @pl.when(is_flow)
    def _():
        def pick(at, size):
            a, b = part_a[at : at + size, :].astype(F32), part_b[at : at + size, :].astype(F32)
            return jnp.where(even, a, b), jnp.where(even, b, a)

        zero[...] = jnp.zeros_like(zero)
        for place, f in enumerate(FIELD_ORDER):
            before, after = pick(place * EDGE, EDGE)
            ends = (
                jnp.concatenate([before, flow[f, :own_rows, :]], 0),
                jnp.concatenate([flow[f, tiles - own_rows :, :], after], 0),
            )
            for side in range(2):
                state0[side, :, columns_of(place)] = ends[side]
                put(high0.at[side], low0.at[side], 0, place, ends[side])
        before, after = pick(5 * EDGE, EDGE)
        edge_visc[:rows, :] = jnp.concatenate([before[HW:], visc[: rows - EDGE + HW, :]], 0)
        edge_visc[rows:, :] = jnp.concatenate(
            [visc[tiles - (rows - EDGE + HW) :, :], after[: EDGE - HW]], 0
        )
        before, after = pick(6 * EDGE, EXTRA)
        given = []
        for side, block in enumerate((before, after)):
            square[...] = jnp.zeros_like(square)
            square[:EXTRA, :] = block
            turned = square[...].T
            given.append(
                jnp.concatenate([turned[LANES - EDGE + HW :], lcol[: rows - EDGE + HW, :]], 0)
                if side == 0
                else jnp.concatenate(
                    [lcol[tiles - (rows - EDGE + HW) :, :], turned[: EDGE - HW]], 0
                )
            )
        for side, b in enumerate((0, plan.blocks - 1)):
            link_matrix(plan, given[side], edge_mats.at[side])
            advance(
                plan, b, edge_mats.at[side],
                [(b * rows, high0.at[side])], [(b * rows, low0.at[side])],
                lambda place, side=side: state0[side, HW : HW + rows, columns_of(place)],
                edge_visc[side * rows : (side + 1) * rows, :],
                edge_state, edge_high, edge_low, side * rows, 5,
            )
        high1 = closed(plan, band_parts(plan, edge_high, inner_high), zero)
        low1 = closed(plan, band_parts(plan, edge_low, inner_low), zero)
        for b in range(plan.blocks):
            lamb_block(
                plan, b, mats_of(plan, b, edge_mats, inner_mats), high1, low1,
                band_state(plan, b, edge_state, inner_state), mean, mean_one, packed,
            )
        element_sums(projector, packed, hits, pay, own_one, next_one)

    @pl.when(jnp.logical_not(is_flow))
    def _():
        own_one[...] = jnp.zeros_like(own_one)
        next_one[...] = jnp.zeros_like(next_one)
        nodes, elements = sound.shape[1:]
        halves = elements // LANES
        block = 4 * nodes
        for v in range(4):
            for h in range(halves):
                rows_of[h * block + v * nodes : h * block + (v + 1) * nodes, :] = sound[
                    v, :, h * LANES : (h + 1) * LANES
                ]
        a, b = part_a[:block, :].astype(F32), part_b[:block, :].astype(F32)
        rows_of[halves * block : (halves + 1) * block, :] = jnp.where(even, a, b)
        rows_of[(halves + 1) * block : (halves + 2) * block, :] = jnp.where(even, b, a)
        for face in range(6):
            for part in range(halves + 2):
                facing_rows(rows_of, part * block, nodes, face ^ 1, facing.at[face, part])
            hot = hot_links(neighbours, face, meta[3], elements, True, True)
            remote_rows([facing[face, part] for part in range(halves + 2)], hot, remote, face)
        derivatives(rows_of, nodes, grads, rhs)
        add_faces(rows_of, nodes, remote, neighbours, codes, rhs, True)
        for n in range(nodes):
            base[n] = rows_of[pl.ds(n, 8, stride=nodes), :] + ACOUSTIC_STEP * rhs[n]


def second_kernel(
    meta, flow, visc, mean, mean_one, projector,
    inner_state, inner_high, inner_low, inner_mats, hits,
    edge_state, edge_high, edge_low, edge_mats, edge_visc,
    flow_out, mean_out, own_two, next_two,
    state, high, low, zero, packed, pay,
):
    plan = FlowPlan(packed.shape[1])
    rows = plan.rows
    is_flow = meta[0] == 1

    @pl.when(jnp.logical_not(is_flow))
    def _():
        flow_out[...] = flow[...]
        mean_out[...] = mean[...]
        own_two[...] = jnp.zeros_like(own_two)
        next_two[...] = jnp.zeros_like(next_two)

    @pl.when(is_flow)
    def _():
        zero[...] = jnp.zeros_like(zero)
        high1 = closed(plan, band_parts(plan, edge_high, inner_high), zero)
        low1 = closed(plan, band_parts(plan, edge_low, inner_low), zero)
        for b in range(plan.blocks):
            if b in plan.inner():
                v = visc[plan.at(b) - EDGE : plan.at(b) - EDGE + rows, :]
            else:
                v = edge_visc[:rows, :] if b == 0 else edge_visc[rows:, :]
            advance(
                plan, b, mats_of(plan, b, edge_mats, inner_mats), high1, low1,
                band_state(plan, b, edge_state, inner_state), v,
                state, high, low, b * rows, 3,
            )
        own = slice(EDGE - HW, EDGE - HW + plan.tiles)
        for place, f in enumerate(FIELD_ORDER):
            flow_out[f] = state[own, columns_of(place)]
        for b in range(plan.blocks):
            lamb_block(
                plan, b, mats_of(plan, b, edge_mats, inner_mats),
                closed(plan, [(HW, high)], zero), closed(plan, [(HW, low)], zero),
                lambda place, b=b: state[b * rows : (b + 1) * rows, columns_of(place)],
                mean_one, mean_out, packed,
            )
        element_sums(projector, packed, hits, pay, own_two, next_two)


def facing_rows(rows_of, base, nodes, face, to):
    axis, level = face // 2, 3 * (face % 2)
    if axis == 0:
        to[...] = rows_of[pl.ds(base + level, 64, stride=4), :]
    elif axis == 1:
        for i in range(4):
            to[pl.ds(i, 16, stride=4), :] = rows_of[pl.ds(base + i + 4 * level, 16, stride=16), :]
    else:
        for v in range(4):
            at = base + v * nodes + 16 * level
            to[v * 16 : (v + 1) * 16, :] = rows_of[at : at + 16, :]


def hot_links(neighbours, face, first_element, elements, own, beside):
    link = neighbours[face : face + 1, :]
    near = link - first_element
    size = (elements if own else 0) + (2 * LANES if beside else 0)
    start = elements if own else 0
    place = jnp.where(near < 0, start + LANES + near, near - elements + start + LANES)
    inside = (near >= 0) & (near < elements)
    place = jnp.where(inside, near if own else -1, place if beside else -1)
    place = jnp.where(link < 0, -1, place)
    key = lax.broadcasted_iota(jnp.int32, (size, elements), 0)
    return jnp.where(key == place, F32(1.0), F32(0.0)).astype(BF16)


def remote_rows(parts, hot, remote, face):
    x = jnp.concatenate(parts, 1)
    if x.dtype == BF16:
        got = dot(x, hot)
    else:
        high, low = split_parts(x)
        got = dot(jnp.concatenate([high, low], 0), hot)
        got = got[:64] + got[64:]
    for h in range(got.shape[1] // LANES):
        remote[face, h * 64 : (h + 1) * 64, :] = got[:, h * LANES : (h + 1) * LANES]


def derivatives(rows_of, nodes, grads_out, rhs):
    matrix = lobatto_matrix()
    line = lax.broadcasted_iota(jnp.int32, (8, LANES), 0)
    is_v = [line % 4 == v for v in range(4)]
    node = [rows_of[pl.ds(n, 8, stride=nodes), :] for n in range(nodes)]
    for n in range(nodes):
        i, j, k = n % 4, n // 4 % 4, n // 16
        lines = (
            [m + 4 * j + 16 * k for m in range(4)],
            [i + 4 * m + 16 * k for m in range(4)],
            [i + 4 * j + 16 * m for m in range(4)],
        )
        grads = []
        for d, at in enumerate((i, j, k)):
            total = None
            for m in range(4):
                if abs(matrix[at, m]) > 1e-12:
                    term = F32(matrix[at, m]) * node[lines[d][m]]
                    total = term if total is None else total + term
            grads.append(total)
            grads_out[d, n] = total
        div = sum(pltpu.roll(grads[d], 8 - (1 + d), 0) for d in range(3))
        coupled = jnp.where(is_v[0], div, 0.0)
        for d in range(3):
            coupled = jnp.where(is_v[1 + d], pltpu.roll(grads[d], 1 + d, 0), coupled)
        rhs[n] = -coupled


def add_faces(rows_of, nodes, remote, neighbours, codes, rhs, own):
    upper = lax.broadcasted_iota(jnp.int32, (8, LANES), 0) >= 4
    for face in range(6):

        def both(row):
            return jnp.where(
                upper,
                jnp.broadcast_to(row[:, LANES:], (8, LANES)),
                jnp.broadcast_to(row[:, :LANES], (8, LANES)),
            )

        code = both(codes[face : face + 1, :])
        valid = both(neighbours[face : face + 1, :]) >= 0
        is_turn = [code == t for t in range(4)]
        planes = [remote[face, pl.ds(p, 8, stride=16), :] for p in range(16)]
        for p, n in enumerate(face_nodes(face)):
            jump = planes[turned_position(3, p)]
            for t in range(3):
                jump = jnp.where(is_turn[t], planes[turned_position(t, p)], jump)
            if own:
                jump = jnp.where(valid, jump - rows_of[pl.ds(n, 8, stride=nodes), :], 0.0)
            rhs[n] = rhs[n] + PENALTY * jump


def source_rows(total, nodes, lamb, mean):
    block = 4 * nodes
    for h in range(total.shape[1] // LANES):
        columns = slice(h * LANES, (h + 1) * LANES)
        lamb[h * block : h * block + nodes, :] = jnp.zeros((nodes, LANES), F32)
        for d in range(3):
            at = h * block + (1 + d) * nodes
            lamb[at : at + nodes, :] = total[d * nodes : (d + 1) * nodes, columns]
            value = total[(3 + d) * nodes : (4 + d) * nodes, columns]
            for v in range(4):
                at = h * block + v * nodes
                mean[d, at : at + nodes, :] = value


def source_terms(nodes, grads, lamb, mean, n):
    total = lamb[pl.ds(n, 8, stride=nodes), :]
    for d in range(3):
        total = total + mean[d, pl.ds(n, 8, stride=nodes), :] * grads[d, n]
    return total


def sound_one_kernel(
    meta, base, grads, source_a, source_b, rows_of, scale_out, edge_a, edge_b, lamb, mean
):
    is_flow, even = meta[0] == 1, meta[1] == 1
    nodes = base.shape[0]
    block = 4 * nodes

    @pl.when(jnp.logical_not(is_flow))
    def _():
        total = source_a[...].astype(F32) + source_b[...].astype(F32)
        count = total[6 * nodes : 6 * nodes + 1] + BASE * total[6 * nodes + 1 : 6 * nodes + 2]
        inverse = 1.0 / jnp.maximum(count, 1.0)
        scale_out[...] = jnp.broadcast_to(inverse, scale_out.shape)
        source_rows(total[: 6 * nodes] * inverse, nodes, lamb, mean)
        for n in range(nodes):
            rows_of[pl.ds(n, 8, stride=nodes), :] = base[n] - ACOUSTIC_STEP * source_terms(
                nodes, grads, lamb, mean, n
            )
        off_a = pl.multiple_of(jnp.where(even, 0, block), 16)
        off_b = pl.multiple_of(jnp.where(even, block, 0), 16)
        edge_a[...] = rows_of[pl.ds(off_a, block), :].astype(BF16)
        edge_b[...] = rows_of[pl.ds(off_b, block), :].astype(BF16)


def sound_inner_kernel(
    meta, rows_of, neighbours, codes, base, grads, hot_beside, facing, remote, rhs
):
    nodes = base.shape[0]
    elements = neighbours.shape[1]
    halves = elements // LANES
    block = 4 * nodes

    @pl.when(meta[0] == 0)
    def _():
        for face in range(6):
            for part in range(halves):
                facing_rows(rows_of, part * block, nodes, face ^ 1, facing.at[face, part])
            hot = hot_links(neighbours, face, meta[3], elements, True, False)
            remote_rows([facing[face, part] for part in range(halves)], hot, remote, face)
            hot_beside[face] = hot_links(neighbours, face, meta[3], elements, False, True)
        derivatives(rows_of, nodes, grads, rhs)
        add_faces(rows_of, nodes, remote, neighbours, codes, rhs, True)
        for n in range(nodes):
            base[n] = rows_of[pl.ds(n, 8, stride=nodes), :] + ACOUSTIC_STEP * rhs[n]


def sound_two_kernel(
    meta, sound, base, grads, hot_beside, neighbours, codes, scale, source_a, source_b,
    part_a, part_b,
    out, rows_of, facing, remote, rhs, lamb, mean,
):
    is_flow, even = meta[0] == 1, meta[1] == 1
    nodes = base.shape[0]
    elements = sound.shape[2]
    halves = elements // LANES
    block = 4 * nodes

    @pl.when(is_flow)
    def _():
        out[...] = sound[...]

    @pl.when(jnp.logical_not(is_flow))
    def _():
        total = source_a[...].astype(F32) + source_b[...].astype(F32)
        source_rows(total * scale[0:1, :], nodes, lamb, mean)
        a, b = part_a[...].astype(F32), part_b[...].astype(F32)
        rows_of[:block, :] = jnp.where(even, a, b)
        rows_of[block:, :] = jnp.where(even, b, a)
        for face in range(6):
            for part in range(2):
                facing_rows(rows_of, part * block, nodes, face ^ 1, facing.at[face, part])
            remote_rows(
                [facing[face, part].astype(BF16) for part in range(2)], hot_beside[face], remote, face
            )
        for n in range(nodes):
            rhs[n] = -source_terms(nodes, grads, lamb, mean, n)
        add_faces(rows_of, nodes, remote, neighbours, codes, rhs, False)
        for n in range(nodes):
            rows_of[pl.ds(n, 8, stride=nodes), :] = base[n] + ACOUSTIC_STEP * rhs[n]
        for v in range(4):
            for h in range(halves):
                out[v, :, h * LANES : (h + 1) * LANES] = rows_of[
                    h * block + v * nodes : h * block + (v + 1) * nodes, :
                ]


def call(kernel, outs, scratch, operands, in_hbm=(), limit=VMEM_LIMIT):
    spaces = [pltpu.SMEM] + [
        pltpu.HBM if at in in_hbm else pltpu.VMEM for at in range(1, len(operands))
    ]
    moved = sum(int(np.prod(x.shape)) * x.dtype.itemsize for x in (*operands, *outs))
    return pl.pallas_call(
        kernel,
        out_shape=tuple(outs),
        in_specs=[pl.BlockSpec(memory_space=space) for space in spaces],
        out_specs=tuple([pl.BlockSpec(memory_space=pltpu.VMEM)] * len(outs)),
        scratch_shapes=scratch,
        compiler_params=pltpu.CompilerParams(vmem_limit_bytes=limit),
        cost_estimate=pl.CostEstimate(flops=10**8, bytes_accessed=moved, transcendentals=0),
    )(*operands)


def body(
    flow_fields,
    mean_velocity,
    cell_eddy_viscosity,
    tile_links,
    tile_target,
    projector,
    acoustic_state,
    element_face_neighbours,
    face_codes,
):
    groups = lax.axis_size("grp")
    count = lax.axis_size("sfc")
    group_index = lax.axis_index("grp")
    column = lax.axis_index("sfc")
    flow = flow_fields[0]
    mean = mean_velocity[0]
    visc = cell_eddy_viscosity[0]
    links = tile_links[0]
    sound = acoustic_state[0]
    neighbours = element_face_neighbours[0]
    codes = face_codes[0]
    tiles = flow.shape[1]
    _, nodes, elements = sound.shape
    halves = elements // LANES
    block = 4 * nodes
    plan = FlowPlan(tiles)
    shape = jax.ShapeDtypeStruct
    vmem = pltpu.VMEM
    meta = jnp.stack(
        [
            (group_index < groups - 1).astype(jnp.int32),
            (column % 2 == 0).astype(jnp.int32),
            (column * tiles).astype(jnp.int32),
            (column * elements).astype(jnp.int32),
        ]
    )

    pairs_a = [p for i in range(1, count - 1, 2) for p in ((i, i + 1), (i + 1, i))]
    pairs_b = [p for i in range(0, count - 1, 2) for p in ((i, i + 1), (i + 1, i))]

    edge_rows = 6 * EDGE + EXTRA
    pack_a, pack_b = call(
        pack_kernel,
        [shape((edge_rows, LANES), BF16)] * 2,
        [
            vmem(links.shape, jnp.int32),
            vmem((2, 6 * EDGE, LANES), F32),
            pltpu.SemaphoreType.DMA((2, 6)),
            pltpu.SemaphoreType.DMA,
        ],
        [meta, flow, visc, links, sound],
        in_hbm=(1, 2, 3, 4),
        limit=PACK_LIMIT,
    )
    part_a = lax.ppermute(pack_a, "sfc", pairs_a)
    part_b = lax.ppermute(pack_b, "sfc", pairs_b)

    fields = 5 * LANES
    rows, span = plan.rows, plan.span
    inner_rows = (plan.blocks - 2) * rows
    square = vmem((LANES, LANES), F32)
    packed = vmem((6, tiles, LANES), F32)
    inner_state, inner_high, inner_low, lcol, inner_mats, hits = call(
        inner_kernel,
        [
            shape((inner_rows, fields), F32),
            shape((inner_rows, fields), BF16),
            shape((inner_rows, fields), BF16),
            shape((tiles, LANES), F32),
            shape((plan.blocks - 2, 3 * rows, 2 * span), BF16),
            shape((2 * elements, tiles), BF16),
        ],
        [vmem((tiles, fields), BF16), vmem((tiles, fields), BF16), square],
        [meta, flow, visc, links, tile_target],
    )
    lines = 6 * nodes + EXTRA
    by_node = shape((nodes, 8, LANES), F32)
    by_node_3 = shape((3, nodes, 8, LANES), F32)
    node_rows = vmem((nodes, 8, LANES), F32)
    (
        own_one, next_one, mean_one, base, grads,
        edge_state, edge_high, edge_low, edge_mats, edge_visc,
    ) = call(
        first_kernel,
        [
            shape((lines, elements), F32),
            shape((lines, elements), BF16),
            shape(mean.shape, F32),
            by_node,
            by_node_3,
            shape((2 * rows, fields), F32),
            shape((2 * rows, fields), BF16),
            shape((2 * rows, fields), BF16),
            shape((2, 3 * rows, 2 * span), BF16),
            shape((2 * rows, LANES), F32),
        ],
        [
            square,
            vmem((2, span, fields), F32),
            vmem((2, span, fields), BF16),
            vmem((2, span, fields), BF16),
            vmem((HW, fields), BF16),
            packed,
            vmem((lines, tiles), BF16),
            vmem(((halves + 2) * block, LANES), F32),
            vmem((6, halves + 2, 64, LANES), F32),
            vmem((6, halves * 64, LANES), F32),
            node_rows,
        ],
        [
            meta, flow, visc, mean, projector, part_a, part_b, sound, neighbours, codes,
            inner_state, inner_high, inner_low, lcol, inner_mats, hits,
        ],
    )

    up = [(i, i + 1) for i in range(count - 1)]

    def climb(x):
        chosen = [(g * count + i, g * count + j) for g in range(groups - 1) for i, j in up]
        return lax.ppermute(x, ("grp", "sfc"), chosen)

    def combined(*xs):
        total = xs[0]
        for x in xs[1:]:
            total = total + x.astype(F32)
        return total.astype(BF16)

    got_one = climb(next_one)
    band = plan.blocks * rows
    velocity = 3 * LANES
    flow_out, mean_out, own_two, next_two = call(
        second_kernel,
        [
            shape(flow.shape, F32),
            shape(mean.shape, F32),
            shape((6 * nodes, elements), F32),
            shape((6 * nodes, elements), BF16),
        ],
        [
            vmem((band, fields), F32),
            vmem((band, velocity), BF16),
            vmem((band, velocity), BF16),
            vmem((HW, fields), BF16),
            packed,
            vmem((6 * nodes, tiles), BF16),
        ],
        [
            meta, flow, visc, mean, mean_one, projector,
            inner_state, inner_high, inner_low, inner_mats, hits,
            edge_state, edge_high, edge_low, edge_mats, edge_visc,
        ],
    )
    sum_one, next_two, own_two = lax.optimization_barrier(
        (combined(own_one, got_one), next_two, own_two)
    )
    x_one = lax.ppermute(sum_one, "grp", [(0, 1), (2, 3)])
    got_two = climb(next_two)
    sum_one, own_two = lax.optimization_barrier((combined(own_one, got_one, x_one), own_two))
    sum_two = lax.optimization_barrier(combined(own_two, got_two))
    padded = jnp.pad(sum_two, ((0, EXTRA), (0, 0)))
    cross = lax.ppermute(jnp.where(group_index == 0, padded, sum_one), "grp", [(0, 2), (1, 3)])
    last_two, sum_two = lax.optimization_barrier(
        (combined(own_two, got_two, cross[: 6 * nodes]), sum_two)
    )
    x_two = lax.ppermute(last_two, "grp", [(2, 3)])
    y_two = lax.ppermute(sum_two, "grp", [(1, 3)])

    sound_rows, scale, edge_a, edge_b = call(
        sound_one_kernel,
        [
            shape((halves * block, LANES), F32),
            shape((8, elements), F32),
            shape((block, LANES), BF16),
            shape((block, LANES), BF16),
        ],
        [vmem((halves * block, LANES), F32), vmem((3, halves * block, LANES), F32)],
        [meta, base, grads, x_one, cross],
    )
    last = (groups - 1) * count
    part_a = lax.ppermute(edge_a, ("grp", "sfc"), [(last + i, last + j) for i, j in pairs_a])
    part_b = lax.ppermute(edge_b, ("grp", "sfc"), [(last + i, last + j) for i, j in pairs_b])
    base, grads, hot_beside = call(
        sound_inner_kernel,
        [by_node, by_node_3, shape((6, 2 * LANES, elements), BF16)],
        [
            vmem((6, halves, 64, LANES), F32),
            vmem((6, halves * 64, LANES), F32),
            node_rows,
        ],
        [meta, sound_rows, neighbours, codes],
    )
    (sound_out,) = call(
        sound_two_kernel,
        [shape(sound.shape, F32)],
        [
            vmem((halves * block, LANES), F32),
            vmem((6, 2, 64, LANES), F32),
            vmem((6, halves * 64, LANES), F32),
            node_rows,
            vmem((halves * block, LANES), F32),
            vmem((3, halves * block, LANES), F32),
        ],
        [
            meta, sound, base, grads, hot_beside, neighbours, codes, scale,
            x_two, y_two, part_a, part_b,
        ],
    )
    return flow_out[None], mean_out[None], sound_out[None]


def solution(mesh):
    placed = (
        P("grp", None, "sfc", None),
        P("grp", None, "sfc", None),
        P("grp", "sfc", None),
        P("grp", None, "sfc"),
        P("grp", "sfc"),
        P(),
        P("grp", None, None, "sfc"),
        P("grp", None, "sfc"),
        P("grp", None, "sfc"),
    )
    return jax.shard_map(
        body,
        mesh=mesh,
        in_specs=placed,
        out_specs=(
            P("grp", None, "sfc", None),
            P("grp", None, "sfc", None),
            P("grp", None, None, "sfc"),
        ),
        check_vma=False,
    )
```

```python
import jax
import jax.numpy as jnp
import numpy as np
from jax import lax
from jax.experimental import pallas as pl
from jax.experimental.pallas import tpu as pltpu
from jax.sharding import PartitionSpec as P

HW = 16
HE = 16

ADVECT = 0.1
RELAX = 0.1
PENALTY = 1.5
ACOUSTIC_STEP = 0.08

LANES = 128
EDGE = 3 * HW
FIELD_ORDER = (1, 2, 3, 0, 4)
BASE = 32.0
EXTRA = 16
VMEM_LIMIT = 20 * 1024 * 1024
PACK_LIMIT = 64 * 1024 * 1024 - 256 * 1024

F32 = jnp.float32
BF16 = jnp.bfloat16


def lobatto_matrix():
    points = np.array([-1.0, -1.0 / np.sqrt(5.0), 1.0 / np.sqrt(5.0), 1.0])
    weights = np.array(
        [
            1.0 / np.prod([points[col] - points[other] for other in range(4) if other != col])
            for col in range(4)
        ]
    )
    matrix = np.zeros((4, 4))
    for line in range(4):
        for col in range(4):
            if line != col:
                matrix[line, col] = weights[col] / weights[line] / (points[line] - points[col])
        matrix[line, line] = -matrix[line].sum()
    return matrix.astype(np.float32)


def face_nodes(face):
    axis, level = face // 2, 3 * (face % 2)
    nodes = []
    for second in range(4):
        for first in range(4):
            coords = [first, second]
            coords.insert(axis, level)
            nodes.append(coords[0] + 4 * coords[1] + 16 * coords[2])
    return nodes


def turned_position(turn, position):
    a, b = position % 4, position // 4
    a, b = ((a, b), (3 - b, a), (3 - a, 3 - b), (b, 3 - a))[turn]
    return a + 4 * b


def split_parts(x):
    high = x.astype(BF16)
    return high, (x - high.astype(F32)).astype(BF16)


def dot(a, b):
    return jnp.dot(a, b, preferred_element_type=F32)


def dot_t(a, b):
    return lax.dot_general(a, b, (((1,), (1,)), ((), ())), preferred_element_type=F32)


def pack_kernel(meta, flow, visc, links, sound, out_a, out_b, links_in, staged, sems, link_sem):
    is_flow, even = meta[0] == 1, meta[1] == 1
    tiles = flow.shape[1]
    _, nodes, elements = sound.shape
    outs = (out_a, out_b)

    @pl.when(is_flow)
    def _():
        fetch = pltpu.make_async_copy(links, links_in, link_sem)
        fetch.start()
        copies = []
        for side in range(2):
            off = pl.multiple_of(jnp.where(even == (side == 0), 0, tiles - EDGE), 8)
            for place, f in enumerate(FIELD_ORDER):
                copies.append(
                    pltpu.make_async_copy(
                        flow.at[f, pl.ds(off, EDGE), :],
                        staged.at[side, pl.ds(place * EDGE, EDGE), :],
                        sems.at[side, place],
                    )
                )
            copies.append(
                pltpu.make_async_copy(
                    visc.at[pl.ds(off, EDGE), :],
                    staged.at[side, pl.ds(5 * EDGE, EDGE), :],
                    sems.at[side, 5],
                )
            )
        for copy in copies:
            copy.start()
        fetch.wait()
        given = links_in[...]
        own = meta[2] + lax.broadcasted_iota(jnp.int32, given.shape, 1)
        offset = jnp.where(given < 0, 0, given - own).astype(F32)
        low, high = offset[:, :LANES], offset[:, tiles - LANES :]
        pad = jnp.zeros((EXTRA - 4, LANES), F32)
        for side, (a, b) in enumerate(((low, high), (high, low))):
            block = jnp.concatenate([jnp.where(even, a, b), pad], 0)
            outs[side][6 * EDGE :, :] = block.astype(BF16)
        for copy in copies:
            copy.wait()
        for side in range(2):
            outs[side][: 6 * EDGE, :] = staged[side].astype(BF16)

    @pl.when(jnp.logical_not(is_flow))
    def _():
        copies = []
        for side in range(2):
            off = pl.multiple_of(jnp.where(even == (side == 0), 0, elements - LANES), LANES)
            for v in range(4):
                copies.append(
                    pltpu.make_async_copy(
                        sound.at[v, :, pl.ds(off, LANES)],
                        staged.at[side, pl.ds(v * nodes, nodes), :],
                        sems.at[side, v],
                    )
                )
        for copy in copies:
            copy.start()
        for copy in copies:
            copy.wait()
        for side, out in enumerate(outs):
            out[: 4 * nodes, :] = staged[side, : 4 * nodes, :].astype(BF16)
            out[4 * nodes :, :] = jnp.zeros((out.shape[0] - 4 * nodes, LANES), BF16)


class FlowPlan:
    def __init__(self, tiles):
        self.tiles = tiles
        self.wide = tiles + 2 * EDGE
        self.blocks = 4
        self.rows = (tiles + 4 * HW) // self.blocks
        self.span = self.rows + 2 * HW

    def at(self, b):
        return HW + b * self.rows

    def inner(self):
        return range(1, self.blocks - 1)


def columns_of(place):
    return slice(place * LANES, (place + 1) * LANES)


def rows_between(parts, low, high, columns):
    taken = []
    for start, ref in parts:
        a, b = max(low, start), min(high, start + ref.shape[0])
        if a < b:
            taken.append(ref[a - start : b - start, columns])
    return taken[0] if len(taken) == 1 else jnp.concatenate(taken, 0)


def put(high, low, at, place, value):
    h, l = split_parts(value)
    high[at : at + value.shape[0], columns_of(place)] = h
    low[at : at + value.shape[0], columns_of(place)] = l


def east_west(x):
    return pltpu.roll(x, LANES - 1, 1), pltpu.roll(x, 1, 1)


def link_matrix(plan, offset, mat):
    rows, span = plan.rows, plan.span
    lane = lax.broadcasted_iota(jnp.int32, (rows, 2 * span), 1)
    lane = jnp.where(lane >= span, lane - span, lane)
    place = HW + lax.broadcasted_iota(jnp.int32, (rows, LANES), 0) + offset.astype(jnp.int32)
    hot = [jnp.where(place[:, k : k + 1] == lane, F32(1.0), F32(0.0)) for k in range(4)]
    mat[:rows, :] = (hot[0] + hot[1] + hot[2] + hot[3]).astype(BF16)
    mat[rows : 2 * rows, :] = (hot[0] - hot[1]).astype(BF16)
    mat[2 * rows :, :] = (hot[2] - hot[3]).astype(BF16)


def gathered(plan, mat, high, low, b, columns, at_row):
    at = b * plan.rows
    both = [rows_between(x, at, at + plan.span, columns) for x in (high, low)]
    return dot(mat[at_row:, :], jnp.concatenate(both, 0))


def advance(plan, b, mat, high, low, state, v, new_state, new_high, new_low, new_at, wanted):
    rows = plan.rows
    center = [state(k) for k in range(3)]
    scaled = [(0.5 * ADVECT) * c for c in center]
    for first, last in ((0, 2), (2, 4), (4, 5)):
        got = gathered(plan, mat, high, low, b, slice(first * LANES, last * LANES), 0)
        for place in range(first, last):
            inner = columns_of(place - first)
            total, dy, dz = got[:rows, inner], got[rows : 2 * rows, inner], got[2 * rows :, inner]
            c = center[place] if place < 3 else state(place)
            east, west = east_west(c)
            new = (
                c
                + v * (east + west + total - 6.0 * c)
                - (scaled[0] * (east - west) + scaled[1] * dy + scaled[2] * dz)
            )
            new_state[new_at : new_at + rows, columns_of(place)] = new
            if place < wanted:
                put(new_high, new_low, new_at, place, new)


def lamb_block(plan, b, mat, high, low, state, average, average_out, packed):
    rows = plan.rows
    center = [state(k) for k in range(3)]
    got = [
        gathered(plan, mat, high, low, b, slice(0, 2 * LANES), rows),
        gathered(plan, mat, high, low, b, slice(2 * LANES, 3 * LANES), rows),
    ]
    d1, d2, d3 = [], [], []
    for k in range(3):
        east, west = east_west(center[k])
        d1.append((east - west) * 0.5)
        inner = columns_of(k % 2)
        d2.append(got[k // 2][:rows, inner] * 0.5)
        d3.append(got[k // 2][rows:, inner] * 0.5)
    vx = d2[2] - d3[1]
    vy = d3[0] - d1[2]
    vz = d1[1] - d2[0]
    lamb = (
        vy * center[2] - vz * center[1],
        vz * center[0] - vx * center[2],
        vx * center[1] - vy * center[0],
    )
    to = plan.at(b) - EDGE
    low_row, top_row = max(0, -to), min(rows, plan.tiles - to)
    own = slice(to + low_row, to + top_row)
    for i in range(3):
        packed[i, own, :] = lamb[i][low_row:top_row]
        mixed = (1.0 - RELAX) * average[i, own, :] + RELAX * center[i][low_row:top_row]
        average_out[i, own, :] = mixed
        packed[3 + i, own, :] = mixed


def element_sums(projector, packed, hits, pay, own_ref, next_ref):
    nodes = projector.shape[0]
    count, elements = own_ref.shape
    proj_high, proj_low = split_parts(projector[...])
    proj_both = jnp.concatenate([proj_high, proj_low], 0)
    for c in range(6):
        x_high, x_low = split_parts(packed[c])
        main = dot_t(proj_both, x_high)
        mapped = main[:nodes] + main[nodes:] + dot_t(proj_high, x_low)
        pay[c * nodes : (c + 1) * nodes, :] = mapped.astype(BF16)
    if count > 6 * nodes:
        pay[6 * nodes :, :] = jnp.ones((count - 6 * nodes, pay.shape[1]), BF16)
    sums = dot_t(pay[...], hits[...])
    if count > 6 * nodes:
        tail = sums[6 * nodes :]
        line = lax.broadcasted_iota(jnp.int32, tail.shape, 0)
        big = jnp.floor(tail * (1.0 / BASE))
        tail = jnp.where(line == 0, tail - BASE * big, jnp.where(line == 1, big, 0.0))
        sums = jnp.concatenate([sums[: 6 * nodes], tail], 0)
    own_ref[...] = sums[:, :elements]
    next_ref[...] = sums[:, elements:].astype(BF16)


def inner_kernel(
    meta, flow, visc, links, target,
    inner_state, inner_high, inner_low, lcol, inner_mats, hits, high0, low0, square,
):
    plan = FlowPlan(flow.shape[1])
    tiles, rows = plan.tiles, plan.rows

    @pl.when(meta[0] == 1)
    def _():
        first_tile, first_element = meta[2], meta[3]
        for place, f in enumerate(FIELD_ORDER):
            put(high0, low0, 0, place, flow[f])
        square[...] = jnp.zeros_like(square)
        own_tile = first_tile + lax.broadcasted_iota(jnp.int32, links.shape, 1)
        offset = jnp.where(links[...] < 0, 0, links[...] - own_tile).astype(F32)
        for part in range(tiles // LANES):
            square[:4, :] = offset[:, part * LANES : (part + 1) * LANES]
            lcol[part * LANES : (part + 1) * LANES, :] = square[...].T
        local = target[...] - first_element
        hits[...] = jnp.where(
            lax.broadcasted_iota(jnp.int32, hits.shape, 0) == local, F32(1.0), F32(0.0)
        ).astype(BF16)
        for at, b in enumerate(plan.inner()):
            own = slice(plan.at(b) - EDGE, plan.at(b) - EDGE + rows)
            link_matrix(plan, lcol[own, :], inner_mats.at[at])
            advance(
                plan, b, inner_mats.at[at], [(EDGE, high0)], [(EDGE, low0)],
                lambda place, own=own: flow[FIELD_ORDER[place], own, :],
                visc[own, :], inner_state, inner_high, inner_low, at * rows, 5,
            )


def band_parts(plan, edge, inner):
    rows, last = plan.rows, plan.blocks - 1
    return [
        (plan.at(0), edge.at[:rows]),
        (plan.at(1), inner),
        (plan.at(last), edge.at[rows:]),
    ]


def band_state(plan, b, edge, inner):
    at = plan.at(b)
    parts = band_parts(plan, edge, inner)
    return lambda place: rows_between(parts, at, at + plan.rows, columns_of(place))


def closed(plan, parts, zero):
    return [(0, zero), *parts, (plan.wide - HW, zero)]


def mats_of(plan, b, edge_mats, inner_mats):
    if b in plan.inner():
        return inner_mats.at[b - 1]
    return edge_mats.at[0 if b == 0 else 1]


def first_kernel(
    meta, flow, visc, mean, projector, part_a, part_b, sound, neighbours, codes,
    inner_state, inner_high, inner_low, lcol, inner_mats, hits,
    own_one, next_one, mean_one, base, grads,
    edge_state, edge_high, edge_low, edge_mats, edge_visc,
    square, state0, high0, low0, zero, packed, pay, rows_of, facing, remote, rhs,
):
    is_flow, even = meta[0] == 1, meta[1] == 1
    plan = FlowPlan(packed.shape[1])
    tiles, rows, span = plan.tiles, plan.rows, plan.span
    own_rows = span - EDGE

    @pl.when(is_flow)
    def _():
        def pick(at, size):
            a, b = part_a[at : at + size, :].astype(F32), part_b[at : at + size, :].astype(F32)
            return jnp.where(even, a, b), jnp.where(even, b, a)

        zero[...] = jnp.zeros_like(zero)
        for place, f in enumerate(FIELD_ORDER):
            before, after = pick(place * EDGE, EDGE)
            ends = (
                jnp.concatenate([before, flow[f, :own_rows, :]], 0),
                jnp.concatenate([flow[f, tiles - own_rows :, :], after], 0),
            )
            for side in range(2):
                state0[side, :, columns_of(place)] = ends[side]
                put(high0.at[side], low0.at[side], 0, place, ends[side])
        before, after = pick(5 * EDGE, EDGE)
        edge_visc[:rows, :] = jnp.concatenate([before[HW:], visc[: rows - EDGE + HW, :]], 0)
        edge_visc[rows:, :] = jnp.concatenate(
            [visc[tiles - (rows - EDGE + HW) :, :], after[: EDGE - HW]], 0
        )
        before, after = pick(6 * EDGE, EXTRA)
        given = []
        for side, block in enumerate((before, after)):
            square[...] = jnp.zeros_like(square)
            square[:EXTRA, :] = block
            turned = square[...].T
            given.append(
                jnp.concatenate([turned[LANES - EDGE + HW :], lcol[: rows - EDGE + HW, :]], 0)
                if side == 0
                else jnp.concatenate(
                    [lcol[tiles - (rows - EDGE + HW) :, :], turned[: EDGE - HW]], 0
                )
            )
        for side, b in enumerate((0, plan.blocks - 1)):
            link_matrix(plan, given[side], edge_mats.at[side])
            advance(
                plan, b, edge_mats.at[side],
                [(b * rows, high0.at[side])], [(b * rows, low0.at[side])],
                lambda place, side=side: state0[side, HW : HW + rows, columns_of(place)],
                edge_visc[side * rows : (side + 1) * rows, :],
                edge_state, edge_high, edge_low, side * rows, 5,
            )
        high1 = closed(plan, band_parts(plan, edge_high, inner_high), zero)
        low1 = closed(plan, band_parts(plan, edge_low, inner_low), zero)
        for b in range(plan.blocks):
            lamb_block(
                plan, b, mats_of(plan, b, edge_mats, inner_mats), high1, low1,
                band_state(plan, b, edge_state, inner_state), mean, mean_one, packed,
            )
        element_sums(projector, packed, hits, pay, own_one, next_one)

    @pl.when(jnp.logical_not(is_flow))
    def _():
        own_one[...] = jnp.zeros_like(own_one)
        next_one[...] = jnp.zeros_like(next_one)
        nodes, elements = sound.shape[1:]
        halves = elements // LANES
        block = 4 * nodes
        for v in range(4):
            for h in range(halves):
                rows_of[h * block + v * nodes : h * block + (v + 1) * nodes, :] = sound[
                    v, :, h * LANES : (h + 1) * LANES
                ]
        a, b = part_a[:block, :].astype(F32), part_b[:block, :].astype(F32)
        rows_of[halves * block : (halves + 1) * block, :] = jnp.where(even, a, b)
        rows_of[(halves + 1) * block : (halves + 2) * block, :] = jnp.where(even, b, a)
        for face in range(6):
            for part in range(halves + 2):
                facing_rows(rows_of, part * block, nodes, face ^ 1, facing.at[face, part])
            hot = hot_links(neighbours, face, meta[3], elements, True, True)
            remote_rows([facing[face, part] for part in range(halves + 2)], hot, remote, face)
        derivatives(rows_of, nodes, grads, rhs)
        add_faces(rows_of, nodes, remote, neighbours, codes, rhs, True)
        for n in range(nodes):
            base[n] = rows_of[pl.ds(n, 8, stride=nodes), :] + ACOUSTIC_STEP * rhs[n]


def second_kernel(
    meta, flow, visc, mean, mean_one, projector,
    inner_state, inner_high, inner_low, inner_mats, hits,
    edge_state, edge_high, edge_low, edge_mats, edge_visc,
    flow_out, mean_out, own_two, next_two,
    state, high, low, zero, packed, pay,
):
    plan = FlowPlan(packed.shape[1])
    rows = plan.rows
    is_flow = meta[0] == 1

    @pl.when(jnp.logical_not(is_flow))
    def _():
        flow_out[...] = flow[...]
        mean_out[...] = mean[...]
        own_two[...] = jnp.zeros_like(own_two)
        next_two[...] = jnp.zeros_like(next_two)

    @pl.when(is_flow)
    def _():
        zero[...] = jnp.zeros_like(zero)
        high1 = closed(plan, band_parts(plan, edge_high, inner_high), zero)
        low1 = closed(plan, band_parts(plan, edge_low, inner_low), zero)
        for b in range(plan.blocks):
            if b in plan.inner():
                v = visc[plan.at(b) - EDGE : plan.at(b) - EDGE + rows, :]
            else:
                v = edge_visc[:rows, :] if b == 0 else edge_visc[rows:, :]
            advance(
                plan, b, mats_of(plan, b, edge_mats, inner_mats), high1, low1,
                band_state(plan, b, edge_state, inner_state), v,
                state, high, low, b * rows, 3,
            )
        own = slice(EDGE - HW, EDGE - HW + plan.tiles)
        for place, f in enumerate(FIELD_ORDER):
            flow_out[f] = state[own, columns_of(place)]
        for b in range(plan.blocks):
            lamb_block(
                plan, b, mats_of(plan, b, edge_mats, inner_mats),
                closed(plan, [(HW, high)], zero), closed(plan, [(HW, low)], zero),
                lambda place, b=b: state[b * rows : (b + 1) * rows, columns_of(place)],
                mean_one, mean_out, packed,
            )
        element_sums(projector, packed, hits, pay, own_two, next_two)


def facing_rows(rows_of, base, nodes, face, to):
    axis, level = face // 2, 3 * (face % 2)
    if axis == 0:
        to[...] = rows_of[pl.ds(base + level, 64, stride=4), :]
    elif axis == 1:
        for i in range(4):
            to[pl.ds(i, 16, stride=4), :] = rows_of[pl.ds(base + i + 4 * level, 16, stride=16), :]
    else:
        for v in range(4):
            at = base + v * nodes + 16 * level
            to[v * 16 : (v + 1) * 16, :] = rows_of[at : at + 16, :]


def hot_links(neighbours, face, first_element, elements, own, beside):
    link = neighbours[face : face + 1, :]
    near = link - first_element
    size = (elements if own else 0) + (2 * LANES if beside else 0)
    start = elements if own else 0
    place = jnp.where(near < 0, start + LANES + near, near - elements + start + LANES)
    inside = (near >= 0) & (near < elements)
    place = jnp.where(inside, near if own else -1, place if beside else -1)
    place = jnp.where(link < 0, -1, place)
    key = lax.broadcasted_iota(jnp.int32, (size, elements), 0)
    return jnp.where(key == place, F32(1.0), F32(0.0)).astype(BF16)


def remote_rows(parts, hot, remote, face):
    x = jnp.concatenate(parts, 1)
    if x.dtype == BF16:
        got = dot(x, hot)
    else:
        high, low = split_parts(x)
        got = dot(jnp.concatenate([high, low], 0), hot)
        got = got[:64] + got[64:]
    for h in range(got.shape[1] // LANES):
        remote[face, h * 64 : (h + 1) * 64, :] = got[:, h * LANES : (h + 1) * LANES]


def derivatives(rows_of, nodes, grads_out, rhs):
    matrix = lobatto_matrix()
    line = lax.broadcasted_iota(jnp.int32, (8, LANES), 0)
    is_v = [line % 4 == v for v in range(4)]
    node = [rows_of[pl.ds(n, 8, stride=nodes), :] for n in range(nodes)]
    for n in range(nodes):
        i, j, k = n % 4, n // 4 % 4, n // 16
        lines = (
            [m + 4 * j + 16 * k for m in range(4)],
            [i + 4 * m + 16 * k for m in range(4)],
            [i + 4 * j + 16 * m for m in range(4)],
        )
        grads = []
        for d, at in enumerate((i, j, k)):
            total = None
            for m in range(4):
                if abs(matrix[at, m]) > 1e-12:
                    term = F32(matrix[at, m]) * node[lines[d][m]]
                    total = term if total is None else total + term
            grads.append(total)
            grads_out[d, n] = total
        div = sum(pltpu.roll(grads[d], 8 - (1 + d), 0) for d in range(3))
        coupled = jnp.where(is_v[0], div, 0.0)
        for d in range(3):
            coupled = jnp.where(is_v[1 + d], pltpu.roll(grads[d], 1 + d, 0), coupled)
        rhs[n] = -coupled


def add_faces(rows_of, nodes, remote, neighbours, codes, rhs, own):
    upper = lax.broadcasted_iota(jnp.int32, (8, LANES), 0) >= 4
    for face in range(6):

        def both(row):
            return jnp.where(
                upper,
                jnp.broadcast_to(row[:, LANES:], (8, LANES)),
                jnp.broadcast_to(row[:, :LANES], (8, LANES)),
            )

        code = both(codes[face : face + 1, :])
        valid = both(neighbours[face : face + 1, :]) >= 0
        is_turn = [code == t for t in range(4)]
        planes = [remote[face, pl.ds(p, 8, stride=16), :] for p in range(16)]
        for p, n in enumerate(face_nodes(face)):
            jump = planes[turned_position(3, p)]
            for t in range(3):
                jump = jnp.where(is_turn[t], planes[turned_position(t, p)], jump)
            if own:
                jump = jnp.where(valid, jump - rows_of[pl.ds(n, 8, stride=nodes), :], 0.0)
            rhs[n] = rhs[n] + PENALTY * jump


def source_rows(total, nodes, lamb, mean):
    block = 4 * nodes
    for h in range(total.shape[1] // LANES):
        columns = slice(h * LANES, (h + 1) * LANES)
        lamb[h * block : h * block + nodes, :] = jnp.zeros((nodes, LANES), F32)
        for d in range(3):
            at = h * block + (1 + d) * nodes
            lamb[at : at + nodes, :] = total[d * nodes : (d + 1) * nodes, columns]
            value = total[(3 + d) * nodes : (4 + d) * nodes, columns]
            for v in range(4):
                at = h * block + v * nodes
                mean[d, at : at + nodes, :] = value


def source_terms(nodes, grads, lamb, mean, n):
    total = lamb[pl.ds(n, 8, stride=nodes), :]
    for d in range(3):
        total = total + mean[d, pl.ds(n, 8, stride=nodes), :] * grads[d, n]
    return total


def sound_one_kernel(
    meta, base, grads, source_a, source_b, rows_of, scale_out, edge_a, edge_b, lamb, mean
):
    is_flow, even = meta[0] == 1, meta[1] == 1
    nodes = base.shape[0]
    block = 4 * nodes

    @pl.when(jnp.logical_not(is_flow))
    def _():
        total = source_a[...].astype(F32) + source_b[...].astype(F32)
        count = total[6 * nodes : 6 * nodes + 1] + BASE * total[6 * nodes + 1 : 6 * nodes + 2]
        inverse = 1.0 / jnp.maximum(count, 1.0)
        scale_out[...] = jnp.broadcast_to(inverse, scale_out.shape)
        source_rows(total[: 6 * nodes] * inverse, nodes, lamb, mean)
        for n in range(nodes):
            rows_of[pl.ds(n, 8, stride=nodes), :] = base[n] - ACOUSTIC_STEP * source_terms(
                nodes, grads, lamb, mean, n
            )
        off_a = pl.multiple_of(jnp.where(even, 0, block), 16)
        off_b = pl.multiple_of(jnp.where(even, block, 0), 16)
        edge_a[...] = rows_of[pl.ds(off_a, block), :].astype(BF16)
        edge_b[...] = rows_of[pl.ds(off_b, block), :].astype(BF16)


def sound_inner_kernel(
    meta, rows_of, neighbours, codes, base, grads, hot_beside, facing, remote, rhs
):
    nodes = base.shape[0]
    elements = neighbours.shape[1]
    halves = elements // LANES
    block = 4 * nodes

    @pl.when(meta[0] == 0)
    def _():
        for face in range(6):
            for part in range(halves):
                facing_rows(rows_of, part * block, nodes, face ^ 1, facing.at[face, part])
            hot = hot_links(neighbours, face, meta[3], elements, True, False)
            remote_rows([facing[face, part] for part in range(halves)], hot, remote, face)
            hot_beside[face] = hot_links(neighbours, face, meta[3], elements, False, True)
        derivatives(rows_of, nodes, grads, rhs)
        add_faces(rows_of, nodes, remote, neighbours, codes, rhs, True)
        for n in range(nodes):
            base[n] = rows_of[pl.ds(n, 8, stride=nodes), :] + ACOUSTIC_STEP * rhs[n]


def sound_two_kernel(
    meta, sound, base, grads, hot_beside, neighbours, codes, scale, source_a, source_b,
    part_a, part_b,
    out, rows_of, facing, remote, rhs, lamb, mean,
):
    is_flow, even = meta[0] == 1, meta[1] == 1
    nodes = base.shape[0]
    elements = sound.shape[2]
    halves = elements // LANES
    block = 4 * nodes

    @pl.when(is_flow)
    def _():
        out[...] = sound[...]

    @pl.when(jnp.logical_not(is_flow))
    def _():
        total = source_a[...].astype(F32) + source_b[...].astype(F32)
        source_rows(total * scale[0:1, :], nodes, lamb, mean)
        a, b = part_a[...].astype(F32), part_b[...].astype(F32)
        rows_of[:block, :] = jnp.where(even, a, b)
        rows_of[block:, :] = jnp.where(even, b, a)
        for face in range(6):
            for part in range(2):
                facing_rows(rows_of, part * block, nodes, face ^ 1, facing.at[face, part])
            remote_rows(
                [facing[face, part].astype(BF16) for part in range(2)], hot_beside[face], remote, face
            )
        for n in range(nodes):
            rhs[n] = -source_terms(nodes, grads, lamb, mean, n)
        add_faces(rows_of, nodes, remote, neighbours, codes, rhs, False)
        for n in range(nodes):
            rows_of[pl.ds(n, 8, stride=nodes), :] = base[n] + ACOUSTIC_STEP * rhs[n]
        for v in range(4):
            for h in range(halves):
                out[v, :, h * LANES : (h + 1) * LANES] = rows_of[
                    h * block + v * nodes : h * block + (v + 1) * nodes, :
                ]


def call(kernel, outs, scratch, operands, in_hbm=(), limit=VMEM_LIMIT):
    spaces = [pltpu.SMEM] + [
        pltpu.HBM if at in in_hbm else pltpu.VMEM for at in range(1, len(operands))
    ]
    moved = sum(int(np.prod(x.shape)) * x.dtype.itemsize for x in (*operands, *outs))
    return pl.pallas_call(
        kernel,
        out_shape=tuple(outs),
        in_specs=[pl.BlockSpec(memory_space=space) for space in spaces],
        out_specs=tuple([pl.BlockSpec(memory_space=pltpu.VMEM)] * len(outs)),
        scratch_shapes=scratch,
        compiler_params=pltpu.CompilerParams(vmem_limit_bytes=limit),
        cost_estimate=pl.CostEstimate(flops=10**8, bytes_accessed=moved, transcendentals=0),
    )(*operands)


def body(
    flow_fields,
    mean_velocity,
    cell_eddy_viscosity,
    tile_links,
    tile_target,
    projector,
    acoustic_state,
    element_face_neighbours,
    face_codes,
):
    groups = lax.axis_size("grp")
    count = lax.axis_size("sfc")
    group_index = lax.axis_index("grp")
    column = lax.axis_index("sfc")
    flow = flow_fields[0]
    mean = mean_velocity[0]
    visc = cell_eddy_viscosity[0]
    links = tile_links[0]
    sound = acoustic_state[0]
    neighbours = element_face_neighbours[0]
    codes = face_codes[0]
    tiles = flow.shape[1]
    _, nodes, elements = sound.shape
    halves = elements // LANES
    block = 4 * nodes
    plan = FlowPlan(tiles)
    shape = jax.ShapeDtypeStruct
    vmem = pltpu.VMEM
    meta = jnp.stack(
        [
            (group_index < groups - 1).astype(jnp.int32),
            (column % 2 == 0).astype(jnp.int32),
            (column * tiles).astype(jnp.int32),
            (column * elements).astype(jnp.int32),
        ]
    )

    pairs_a = [p for i in range(1, count - 1, 2) for p in ((i, i + 1), (i + 1, i))]
    pairs_b = [p for i in range(0, count - 1, 2) for p in ((i, i + 1), (i + 1, i))]

    edge_rows = 6 * EDGE + EXTRA
    pack_a, pack_b = call(
        pack_kernel,
        [shape((edge_rows, LANES), BF16)] * 2,
        [
            vmem(links.shape, jnp.int32),
            vmem((2, 6 * EDGE, LANES), F32),
            pltpu.SemaphoreType.DMA((2, 6)),
            pltpu.SemaphoreType.DMA,
        ],
        [meta, flow, visc, links, sound],
        in_hbm=(1, 2, 3, 4),
        limit=PACK_LIMIT,
    )
    part_a = lax.ppermute(pack_a, "sfc", pairs_a)
    part_b = lax.ppermute(pack_b, "sfc", pairs_b)

    fields = 5 * LANES
    rows, span = plan.rows, plan.span
    inner_rows = (plan.blocks - 2) * rows
    square = vmem((LANES, LANES), F32)
    packed = vmem((6, tiles, LANES), F32)
    inner_state, inner_high, inner_low, lcol, inner_mats, hits = call(
        inner_kernel,
        [
            shape((inner_rows, fields), F32),
            shape((inner_rows, fields), BF16),
            shape((inner_rows, fields), BF16),
            shape((tiles, LANES), F32),
            shape((plan.blocks - 2, 3 * rows, 2 * span), BF16),
            shape((2 * elements, tiles), BF16),
        ],
        [vmem((tiles, fields), BF16), vmem((tiles, fields), BF16), square],
        [meta, flow, visc, links, tile_target],
    )
    lines = 6 * nodes + EXTRA
    by_node = shape((nodes, 8, LANES), F32)
    by_node_3 = shape((3, nodes, 8, LANES), F32)
    node_rows = vmem((nodes, 8, LANES), F32)
    (
        own_one, next_one, mean_one, base, grads,
        edge_state, edge_high, edge_low, edge_mats, edge_visc,
    ) = call(
        first_kernel,
        [
            shape((lines, elements), F32),
            shape((lines, elements), BF16),
            shape(mean.shape, F32),
            by_node,
            by_node_3,
            shape((2 * rows, fields), F32),
            shape((2 * rows, fields), BF16),
            shape((2 * rows, fields), BF16),
            shape((2, 3 * rows, 2 * span), BF16),
            shape((2 * rows, LANES), F32),
        ],
        [
            square,
            vmem((2, span, fields), F32),
            vmem((2, span, fields), BF16),
            vmem((2, span, fields), BF16),
            vmem((HW, fields), BF16),
            packed,
            vmem((lines, tiles), BF16),
            vmem(((halves + 2) * block, LANES), F32),
            vmem((6, halves + 2, 64, LANES), F32),
            vmem((6, halves * 64, LANES), F32),
            node_rows,
        ],
        [
            meta, flow, visc, mean, projector, part_a, part_b, sound, neighbours, codes,
            inner_state, inner_high, inner_low, lcol, inner_mats, hits,
        ],
    )

    up = [(i, i + 1) for i in range(count - 1)]

    def climb(x):
        chosen = [(g * count + i, g * count + j) for g in range(groups - 1) for i, j in up]
        return lax.ppermute(x, ("grp", "sfc"), chosen)

    def combined(*xs):
        total = xs[0]
        for x in xs[1:]:
            total = total + x.astype(F32)
        return total.astype(BF16)

    got_one = climb(next_one)
    band = plan.blocks * rows
    velocity = 3 * LANES
    flow_out, mean_out, own_two, next_two = call(
        second_kernel,
        [
            shape(flow.shape, F32),
            shape(mean.shape, F32),
            shape((6 * nodes, elements), F32),
            shape((6 * nodes, elements), BF16),
        ],
        [
            vmem((band, fields), F32),
            vmem((band, velocity), BF16),
            vmem((band, velocity), BF16),
            vmem((HW, fields), BF16),
            packed,
            vmem((6 * nodes, tiles), BF16),
        ],
        [
            meta, flow, visc, mean, mean_one, projector,
            inner_state, inner_high, inner_low, inner_mats, hits,
            edge_state, edge_high, edge_low, edge_mats, edge_visc,
        ],
    )
    got_two = climb(next_two)
    x_one = lax.ppermute(combined(own_one, got_one), "grp", [(0, 1), (2, 3)])
    y_two = lax.ppermute(combined(own_two, got_two), "grp", [(0, 2), (1, 3)])
    y_one = lax.ppermute(combined(own_one, got_one, x_one), "grp", [(1, 3)])
    x_two = lax.ppermute(combined(own_two, got_two, y_two), "grp", [(2, 3)])

    sound_rows, scale, edge_a, edge_b = call(
        sound_one_kernel,
        [
            shape((halves * block, LANES), F32),
            shape((8, elements), F32),
            shape((block, LANES), BF16),
            shape((block, LANES), BF16),
        ],
        [vmem((halves * block, LANES), F32), vmem((3, halves * block, LANES), F32)],
        [meta, base, grads, x_one, y_one],
    )
    last = (groups - 1) * count
    part_a = lax.ppermute(edge_a, ("grp", "sfc"), [(last + i, last + j) for i, j in pairs_a])
    part_b = lax.ppermute(edge_b, ("grp", "sfc"), [(last + i, last + j) for i, j in pairs_b])
    base, grads, hot_beside = call(
        sound_inner_kernel,
        [by_node, by_node_3, shape((6, 2 * LANES, elements), BF16)],
        [
            vmem((6, halves, 64, LANES), F32),
            vmem((6, halves * 64, LANES), F32),
            node_rows,
        ],
        [meta, sound_rows, neighbours, codes],
    )
    (sound_out,) = call(
        sound_two_kernel,
        [shape(sound.shape, F32)],
        [
            vmem((halves * block, LANES), F32),
            vmem((6, 2, 64, LANES), F32),
            vmem((6, halves * 64, LANES), F32),
            node_rows,
            vmem((halves * block, LANES), F32),
            vmem((3, halves * block, LANES), F32),
        ],
        [
            meta, sound, base, grads, hot_beside, neighbours, codes, scale,
            x_two, y_two, part_a, part_b,
        ],
    )
    return flow_out[None], mean_out[None], sound_out[None]


def solution(mesh):
    placed = (
        P("grp", None, "sfc", None),
        P("grp", None, "sfc", None),
        P("grp", "sfc", None),
        P("grp", None, "sfc"),
        P("grp", "sfc"),
        P(),
        P("grp", None, None, "sfc"),
        P("grp", None, "sfc"),
        P("grp", None, "sfc"),
    )
    return jax.shard_map(
        body,
        mesh=mesh,
        in_specs=placed,
        out_specs=(
            P("grp", None, "sfc", None),
            P("grp", None, "sfc", None),
            P("grp", None, None, "sfc"),
        ),
        check_vma=False,
    )
```

```python
import jax
import jax.numpy as jnp
import numpy as np
from jax import lax
from jax.experimental import pallas as pl
from jax.experimental.pallas import tpu as pltpu
from jax.sharding import PartitionSpec as P

HW = 16
HE = 16

ADVECT = 0.1
RELAX = 0.1
PENALTY = 1.5
ACOUSTIC_STEP = 0.08

LANES = 128
EDGE = 3 * HW
FIELD_ORDER = (1, 2, 3, 0, 4)
ALL_FIELDS = ((0, 2), (2, 4), (4, 5))
BASE = 32.0
EXTRA = 16
VMEM_LIMIT = 20 * 1024 * 1024
PACK_LIMIT = 62 * 1024 * 1024

F32 = jnp.float32
BF16 = jnp.bfloat16


def lobatto_matrix():
    points = np.array([-1.0, -1.0 / np.sqrt(5.0), 1.0 / np.sqrt(5.0), 1.0])
    weights = np.array(
        [
            1.0 / np.prod([points[col] - points[other] for other in range(4) if other != col])
            for col in range(4)
        ]
    )
    matrix = np.zeros((4, 4))
    for line in range(4):
        for col in range(4):
            if line != col:
                matrix[line, col] = weights[col] / weights[line] / (points[line] - points[col])
        matrix[line, line] = -matrix[line].sum()
    return matrix.astype(np.float32)


def face_nodes(face):
    axis, level = face // 2, 3 * (face % 2)
    nodes = []
    for second in range(4):
        for first in range(4):
            coords = [first, second]
            coords.insert(axis, level)
            nodes.append(coords[0] + 4 * coords[1] + 16 * coords[2])
    return nodes


def turned_position(turn, position):
    a, b = position % 4, position // 4
    a, b = ((a, b), (3 - b, a), (3 - a, 3 - b), (b, 3 - a))[turn]
    return a + 4 * b


def split_parts(x):
    high = x.astype(BF16)
    return high, (x - high.astype(F32)).astype(BF16)


def dot(a, b):
    return jnp.dot(a, b, preferred_element_type=F32)


def dot_t(a, b):
    return lax.dot_general(a, b, (((1,), (1,)), ((), ())), preferred_element_type=F32)


def on_flow_row():
    return lax.axis_index("grp") < lax.axis_size("grp") - 1


def on_even_column():
    return lax.rem(lax.axis_index("sfc"), 2) == 0


def pack_kernel(flow, visc, links, sound, out_a, out_b, links_in, staged, sems, link_sem):
    is_flow, even = on_flow_row(), on_even_column()
    tiles = flow.shape[1]
    _, nodes, elements = sound.shape
    outs = (out_a, out_b)

    @pl.when(is_flow)
    def _():
        fetch = pltpu.make_async_copy(links, links_in, link_sem)
        fetch.start()
        copies = []
        for side in range(2):
            off = pl.multiple_of(jnp.where(even == (side == 0), 0, tiles - EDGE), 8)
            for place, f in enumerate(FIELD_ORDER):
                copies.append(
                    pltpu.make_async_copy(
                        flow.at[f, pl.ds(off, EDGE), :],
                        staged.at[side, pl.ds(place * EDGE, EDGE), :],
                        sems.at[side, place],
                    )
                )
            copies.append(
                pltpu.make_async_copy(
                    visc.at[pl.ds(off, EDGE), :],
                    staged.at[side, pl.ds(5 * EDGE, EDGE), :],
                    sems.at[side, 5],
                )
            )
        for copy in copies:
            copy.start()
        fetch.wait()
        given = links_in[...]
        own = lax.axis_index("sfc") * tiles + lax.broadcasted_iota(jnp.int32, given.shape, 1)
        offset = jnp.where(given < 0, 0, given - own).astype(F32)
        low, high = offset[:, :LANES], offset[:, tiles - LANES :]
        pad = jnp.zeros((EXTRA - 4, LANES), F32)
        for side, (a, b) in enumerate(((low, high), (high, low))):
            block = jnp.concatenate([jnp.where(even, a, b), pad], 0)
            outs[side][6 * EDGE :, :] = block.astype(BF16)
        for copy in copies:
            copy.wait()
        for side in range(2):
            outs[side][: 6 * EDGE, :] = staged[side].astype(BF16)

    @pl.when(jnp.logical_not(is_flow))
    def _():
        copies = []
        for side in range(2):
            off = pl.multiple_of(jnp.where(even == (side == 0), 0, elements - LANES), LANES)
            for v in range(4):
                copies.append(
                    pltpu.make_async_copy(
                        sound.at[v, :, pl.ds(off, LANES)],
                        staged.at[side, pl.ds(v * nodes, nodes), :],
                        sems.at[side, v],
                    )
                )
        for copy in copies:
            copy.start()
        for copy in copies:
            copy.wait()
        for side, out in enumerate(outs):
            out[: 4 * nodes, :] = staged[side, : 4 * nodes, :].astype(BF16)
            out[4 * nodes :, :] = jnp.zeros((out.shape[0] - 4 * nodes, LANES), BF16)


class FlowPlan:
    def __init__(self, tiles):
        self.tiles = tiles
        self.wide = tiles + 2 * EDGE
        self.blocks = 4
        self.rows = (tiles + 4 * HW) // self.blocks
        self.span = self.rows + 2 * HW

    def at(self, b):
        return HW + b * self.rows

    def inner(self):
        return range(1, self.blocks - 1)


def columns_of(place):
    return slice(place * LANES, (place + 1) * LANES)


def rows_between(parts, low, high, columns):
    taken = []
    for start, ref in parts:
        a, b = max(low, start), min(high, start + ref.shape[0])
        if a < b:
            taken.append(ref[a - start : b - start, columns])
    return taken[0] if len(taken) == 1 else jnp.concatenate(taken, 0)


def put(high, low, at, place, value):
    h, l = split_parts(value)
    high[at : at + value.shape[0], columns_of(place)] = h
    low[at : at + value.shape[0], columns_of(place)] = l


def east_west(x):
    return pltpu.roll(x, LANES - 1, 1), pltpu.roll(x, 1, 1)


def link_matrix(plan, offset, mat):
    rows, span = plan.rows, plan.span
    lane = lax.broadcasted_iota(jnp.int32, (rows, 2 * span), 1)
    lane = jnp.where(lane >= span, lane - span, lane)
    place = HW + lax.broadcasted_iota(jnp.int32, (rows, LANES), 0) + offset.astype(jnp.int32)
    hot = [jnp.where(place[:, k : k + 1] == lane, F32(1.0), F32(0.0)) for k in range(4)]
    mat[:rows, :] = (hot[0] + hot[1] + hot[2] + hot[3]).astype(BF16)
    mat[rows : 2 * rows, :] = (hot[0] - hot[1]).astype(BF16)
    mat[2 * rows :, :] = (hot[2] - hot[3]).astype(BF16)


def gathered(plan, mat, high, low, b, columns, at_row):
    at = b * plan.rows
    both = [rows_between(x, at, at + plan.span, columns) for x in (high, low)]
    return dot(mat[at_row:, :], jnp.concatenate(both, 0))


def advance(plan, b, mat, high, low, state, v, places, new_state, new_high, new_low, new_at, split):
    rows = plan.rows
    center = [state(k) for k in range(3)]
    scaled = [(0.5 * ADVECT) * c for c in center]
    for first, last in places:
        got = gathered(plan, mat, high, low, b, slice(first * LANES, last * LANES), 0)
        for place in range(first, last):
            inner = columns_of(place - first)
            total, dy, dz = got[:rows, inner], got[rows : 2 * rows, inner], got[2 * rows :, inner]
            c = center[place] if place < 3 else state(place)
            east, west = east_west(c)
            new = (
                c
                + v * (east + west + total - 6.0 * c)
                - (scaled[0] * (east - west) + scaled[1] * dy + scaled[2] * dz)
            )
            new_state[new_at : new_at + rows, columns_of(place)] = new
            if split:
                put(new_high, new_low, new_at, place, new)


def lamb_block(plan, b, mat, high, low, state, average, average_out, packed):
    rows = plan.rows
    center = [state(k) for k in range(3)]
    got = [
        gathered(plan, mat, high, low, b, slice(0, 2 * LANES), rows),
        gathered(plan, mat, high, low, b, slice(2 * LANES, 3 * LANES), rows),
    ]
    d1, d2, d3 = [], [], []
    for k in range(3):
        east, west = east_west(center[k])
        d1.append((east - west) * 0.5)
        inner = columns_of(k % 2)
        d2.append(got[k // 2][:rows, inner] * 0.5)
        d3.append(got[k // 2][rows:, inner] * 0.5)
    vx = d2[2] - d3[1]
    vy = d3[0] - d1[2]
    vz = d1[1] - d2[0]
    lamb = (
        vy * center[2] - vz * center[1],
        vz * center[0] - vx * center[2],
        vx * center[1] - vy * center[0],
    )
    to = plan.at(b) - EDGE
    low_row, top_row = max(0, -to), min(rows, plan.tiles - to)
    own = slice(to + low_row, to + top_row)
    for i in range(3):
        packed[i, own, :] = lamb[i][low_row:top_row]
        mixed = (1.0 - RELAX) * average[i, own, :] + RELAX * center[i][low_row:top_row]
        average_out[i, own, :] = mixed
        packed[3 + i, own, :] = mixed


def element_sums(projector, packed, hits, pay, own_ref, next_ref):
    nodes = projector.shape[0]
    count, elements = own_ref.shape
    proj_high, proj_low = split_parts(projector[...])
    proj_both = jnp.concatenate([proj_high, proj_low], 0)
    for c in range(6):
        x_high, x_low = split_parts(packed[c])
        main = dot_t(proj_both, x_high)
        mapped = main[:nodes] + main[nodes:] + dot_t(proj_high, x_low)
        pay[c * nodes : (c + 1) * nodes, :] = mapped.astype(BF16)
    if count > 6 * nodes:
        pay[6 * nodes :, :] = jnp.ones((count - 6 * nodes, pay.shape[1]), BF16)
    sums = dot_t(pay[...], hits[...])
    if count > 6 * nodes:
        tail = sums[6 * nodes :]
        line = lax.broadcasted_iota(jnp.int32, tail.shape, 0)
        big = jnp.floor(tail * (1.0 / BASE))
        tail = jnp.where(line == 0, tail - BASE * big, jnp.where(line == 1, big, 0.0))
        sums = jnp.concatenate([sums[: 6 * nodes], tail], 0)
    own_ref[...] = sums[:, :elements]
    next_ref[...] = sums[:, elements:].astype(BF16)


def inner_kernel(
    flow, visc, links, target,
    inner_state, inner_high, inner_low, lcol, inner_mats, hits, high0, low0, square,
):
    plan = FlowPlan(flow.shape[1])
    tiles, rows = plan.tiles, plan.rows

    @pl.when(on_flow_row())
    def _():
        column = lax.axis_index("sfc")
        first_tile, first_element = column * tiles, column * (hits.shape[0] // 2)
        for place, f in enumerate(FIELD_ORDER):
            put(high0, low0, 0, place, flow[f])
        square[...] = jnp.zeros_like(square)
        own_tile = first_tile + lax.broadcasted_iota(jnp.int32, links.shape, 1)
        offset = jnp.where(links[...] < 0, 0, links[...] - own_tile).astype(F32)
        for part in range(tiles // LANES):
            square[:4, :] = offset[:, part * LANES : (part + 1) * LANES]
            lcol[part * LANES : (part + 1) * LANES, :] = square[...].T
        local = target[...] - first_element
        hits[...] = jnp.where(
            lax.broadcasted_iota(jnp.int32, hits.shape, 0) == local, F32(1.0), F32(0.0)
        ).astype(BF16)
        for at, b in enumerate(plan.inner()):
            own = slice(plan.at(b) - EDGE, plan.at(b) - EDGE + rows)
            link_matrix(plan, lcol[own, :], inner_mats.at[at])
            advance(
                plan, b, inner_mats.at[at], [(EDGE, high0)], [(EDGE, low0)],
                lambda place, own=own: flow[FIELD_ORDER[place], own, :],
                visc[own, :], ALL_FIELDS, inner_state, inner_high, inner_low, at * rows, True,
            )


def band_parts(plan, edge, inner):
    rows, last = plan.rows, plan.blocks - 1
    return [
        (plan.at(0), edge.at[:rows]),
        (plan.at(1), inner),
        (plan.at(last), edge.at[rows:]),
    ]


def band_state(plan, b, edge, inner):
    at = plan.at(b)
    parts = band_parts(plan, edge, inner)
    return lambda place: rows_between(parts, at, at + plan.rows, columns_of(place))


def closed(plan, parts, zero):
    return [(0, zero), *parts, (plan.wide - HW, zero)]


def mats_of(plan, b, edge_mats, inner_mats):
    if b in plan.inner():
        return inner_mats.at[b - 1]
    return edge_mats.at[0 if b == 0 else 1]


def first_kernel(
    flow, visc, mean, projector, part_a, part_b, sound, neighbours, codes,
    inner_state, inner_high, inner_low, lcol, inner_mats, hits,
    own_one, next_one, mean_one, base, grads,
    edge_state, edge_high, edge_low, edge_mats, edge_visc,
    square, state0, high0, low0, zero, packed, pay, rows_of, facing, remote, rhs,
):
    is_flow, even = on_flow_row(), on_even_column()
    plan = FlowPlan(packed.shape[1])
    tiles, rows, span = plan.tiles, plan.rows, plan.span
    own_rows = span - EDGE

    @pl.when(is_flow)
    def _():
        def pick(at, size):
            a, b = part_a[at : at + size, :].astype(F32), part_b[at : at + size, :].astype(F32)
            return jnp.where(even, a, b), jnp.where(even, b, a)

        zero[...] = jnp.zeros_like(zero)
        for place, f in enumerate(FIELD_ORDER):
            before, after = pick(place * EDGE, EDGE)
            ends = (
                jnp.concatenate([before, flow[f, :own_rows, :]], 0),
                jnp.concatenate([flow[f, tiles - own_rows :, :], after], 0),
            )
            for side in range(2):
                state0[side, :, columns_of(place)] = ends[side]
                put(high0.at[side], low0.at[side], 0, place, ends[side])
        before, after = pick(5 * EDGE, EDGE)
        edge_visc[:rows, :] = jnp.concatenate([before[HW:], visc[: rows - EDGE + HW, :]], 0)
        edge_visc[rows:, :] = jnp.concatenate(
            [visc[tiles - (rows - EDGE + HW) :, :], after[: EDGE - HW]], 0
        )
        before, after = pick(6 * EDGE, EXTRA)
        given = []
        for side, block in enumerate((before, after)):
            square[...] = jnp.zeros_like(square)
            square[:EXTRA, :] = block
            turned = square[...].T
            given.append(
                jnp.concatenate([turned[LANES - EDGE + HW :], lcol[: rows - EDGE + HW, :]], 0)
                if side == 0
                else jnp.concatenate(
                    [lcol[tiles - (rows - EDGE + HW) :, :], turned[: EDGE - HW]], 0
                )
            )
        for side, b in enumerate((0, plan.blocks - 1)):
            link_matrix(plan, given[side], edge_mats.at[side])
            advance(
                plan, b, edge_mats.at[side],
                [(b * rows, high0.at[side])], [(b * rows, low0.at[side])],
                lambda place, side=side: state0[side, HW : HW + rows, columns_of(place)],
                edge_visc[side * rows : (side + 1) * rows, :], ALL_FIELDS,
                edge_state, edge_high, edge_low, side * rows, True,
            )
        high1 = closed(plan, band_parts(plan, edge_high, inner_high), zero)
        low1 = closed(plan, band_parts(plan, edge_low, inner_low), zero)
        for b in range(plan.blocks):
            lamb_block(
                plan, b, mats_of(plan, b, edge_mats, inner_mats), high1, low1,
                band_state(plan, b, edge_state, inner_state), mean, mean_one, packed,
            )
        element_sums(projector, packed, hits, pay, own_one, next_one)

    @pl.when(jnp.logical_not(is_flow))
    def _():
        own_one[...] = jnp.zeros_like(own_one)
        next_one[...] = jnp.zeros_like(next_one)
        nodes, elements = sound.shape[1:]
        halves = elements // LANES
        block = 4 * nodes
        for v in range(4):
            for h in range(halves):
                rows_of[h * block + v * nodes : h * block + (v + 1) * nodes, :] = sound[
                    v, :, h * LANES : (h + 1) * LANES
                ]
        a, b = part_a[:block, :].astype(F32), part_b[:block, :].astype(F32)
        rows_of[halves * block : (halves + 1) * block, :] = jnp.where(even, a, b)
        rows_of[(halves + 1) * block : (halves + 2) * block, :] = jnp.where(even, b, a)
        for face in range(6):
            for part in range(halves + 2):
                facing_rows(rows_of, part * block, nodes, face ^ 1, facing.at[face, part])
            hot = hot_links(neighbours, face, elements, True, True)
            remote_rows([facing[face, part] for part in range(halves + 2)], hot, remote, face)
        derivatives(rows_of, nodes, grads, rhs)
        add_faces(rows_of, nodes, remote, neighbours, codes, rhs, True)
        for n in range(nodes):
            base[n] = rows_of[pl.ds(n, 8, stride=nodes), :] + ACOUSTIC_STEP * rhs[n]


def second_block(plan, b, carried, visc, places, new_state, new_parts):
    (inner_state, inner_high, inner_low, inner_mats, edge_state, edge_high, edge_low, edge_mats,
     edge_visc, zero) = carried
    rows = plan.rows
    if b in plan.inner():
        v = visc[plan.at(b) - EDGE : plan.at(b) - EDGE + rows, :]
    else:
        v = edge_visc[:rows, :] if b == 0 else edge_visc[rows:, :]
    advance(
        plan, b, mats_of(plan, b, edge_mats, inner_mats),
        closed(plan, band_parts(plan, edge_high, inner_high), zero),
        closed(plan, band_parts(plan, edge_low, inner_low), zero),
        band_state(plan, b, edge_state, inner_state), v, places,
        new_state, *new_parts, b * rows, new_parts[0] is not None,
    )


def second_kernel(
    visc, mean, mean_one, projector,
    inner_state, inner_high, inner_low, inner_mats, hits,
    edge_state, edge_high, edge_low, edge_mats, edge_visc,
    state, mean_two, own_two, next_two,
    high, low, zero, packed, pay,
):
    plan = FlowPlan(packed.shape[1])
    rows = plan.rows
    is_flow = on_flow_row()

    @pl.when(jnp.logical_not(is_flow))
    def _():
        own_two[...] = jnp.zeros_like(own_two)
        next_two[...] = jnp.zeros_like(next_two)

    @pl.when(is_flow)
    def _():
        zero[...] = jnp.zeros_like(zero)
        carried = (
            inner_state, inner_high, inner_low, inner_mats,
            edge_state, edge_high, edge_low, edge_mats, edge_visc, zero,
        )
        for b in range(plan.blocks):
            second_block(plan, b, carried, visc, ((0, 2), (2, 3)), state, (high, low))
        for b in range(plan.blocks):
            lamb_block(
                plan, b, mats_of(plan, b, edge_mats, inner_mats),
                closed(plan, [(HW, high)], zero), closed(plan, [(HW, low)], zero),
                lambda place, b=b: state[b * rows : (b + 1) * rows, columns_of(place)],
                mean_one, mean_two, packed,
            )
        element_sums(projector, packed, hits, pay, own_two, next_two)


def output_kernel(
    flow, visc, mean, state, mean_two,
    inner_state, inner_high, inner_low, inner_mats,
    edge_state, edge_high, edge_low, edge_mats, edge_visc, after,
    flow_out, mean_out, token, passive, zero,
):
    plan = FlowPlan(flow.shape[1])
    is_flow = on_flow_row()
    token[...] = jnp.zeros_like(token)

    @pl.when(jnp.logical_not(is_flow))
    def _():
        flow_out[...] = flow[...]
        mean_out[...] = mean[...]

    @pl.when(is_flow)
    def _():
        zero[...] = jnp.zeros_like(zero)
        mean_out[...] = mean_two[...]
        carried = (
            inner_state, inner_high, inner_low, inner_mats,
            edge_state, edge_high, edge_low, edge_mats, edge_visc, zero,
        )
        own = slice(EDGE - HW, EDGE - HW + plan.tiles)
        for place in range(3):
            flow_out[FIELD_ORDER[place]] = state[own, columns_of(place)]
        for b in range(plan.blocks):
            second_block(plan, b, carried, visc, ((3, 5),), passive, (None, None))
        for place in (3, 4):
            flow_out[FIELD_ORDER[place]] = passive[own, columns_of(place)]


def facing_rows(rows_of, base, nodes, face, to):
    axis, level = face // 2, 3 * (face % 2)
    if axis == 0:
        to[...] = rows_of[pl.ds(base + level, 64, stride=4), :]
    elif axis == 1:
        for i in range(4):
            to[pl.ds(i, 16, stride=4), :] = rows_of[pl.ds(base + i + 4 * level, 16, stride=16), :]
    else:
        for v in range(4):
            at = base + v * nodes + 16 * level
            to[v * 16 : (v + 1) * 16, :] = rows_of[at : at + 16, :]


def hot_links(neighbours, face, elements, own, beside):
    link = neighbours[face : face + 1, :]
    near = link - lax.axis_index("sfc") * elements
    size = (elements if own else 0) + (2 * LANES if beside else 0)
    start = elements if own else 0
    place = jnp.where(near < 0, start + LANES + near, near - elements + start + LANES)
    inside = (near >= 0) & (near < elements)
    place = jnp.where(inside, near if own else -1, place if beside else -1)
    place = jnp.where(link < 0, -1, place)
    key = lax.broadcasted_iota(jnp.int32, (size, elements), 0)
    return jnp.where(key == place, F32(1.0), F32(0.0)).astype(BF16)


def remote_rows(parts, hot, remote, face):
    x = jnp.concatenate(parts, 1)
    if x.dtype == BF16:
        got = dot(x, hot)
    else:
        high, low = split_parts(x)
        got = dot(jnp.concatenate([high, low], 0), hot)
        got = got[:64] + got[64:]
    for h in range(got.shape[1] // LANES):
        remote[face, h * 64 : (h + 1) * 64, :] = got[:, h * LANES : (h + 1) * LANES]


def derivatives(rows_of, nodes, grads_out, rhs):
    matrix = lobatto_matrix()
    line = lax.broadcasted_iota(jnp.int32, (8, LANES), 0)
    is_v = [line % 4 == v for v in range(4)]
    node = [rows_of[pl.ds(n, 8, stride=nodes), :] for n in range(nodes)]
    for n in range(nodes):
        i, j, k = n % 4, n // 4 % 4, n // 16
        lines = (
            [m + 4 * j + 16 * k for m in range(4)],
            [i + 4 * m + 16 * k for m in range(4)],
            [i + 4 * j + 16 * m for m in range(4)],
        )
        grads = []
        for d, at in enumerate((i, j, k)):
            total = None
            for m in range(4):
                if abs(matrix[at, m]) > 1e-12:
                    term = F32(matrix[at, m]) * node[lines[d][m]]
                    total = term if total is None else total + term
            grads.append(total)
            grads_out[d, n] = total
        div = sum(pltpu.roll(grads[d], 8 - (1 + d), 0) for d in range(3))
        coupled = jnp.where(is_v[0], div, 0.0)
        for d in range(3):
            coupled = jnp.where(is_v[1 + d], pltpu.roll(grads[d], 1 + d, 0), coupled)
        rhs[n] = -coupled


def add_faces(rows_of, nodes, remote, neighbours, codes, rhs, own):
    upper = lax.broadcasted_iota(jnp.int32, (8, LANES), 0) >= 4
    for face in range(6):

        def both(row):
            return jnp.where(
                upper,
                jnp.broadcast_to(row[:, LANES:], (8, LANES)),
                jnp.broadcast_to(row[:, :LANES], (8, LANES)),
            )

        code = both(codes[face : face + 1, :])
        valid = both(neighbours[face : face + 1, :]) >= 0
        is_turn = [code == t for t in range(4)]
        planes = [remote[face, pl.ds(p, 8, stride=16), :] for p in range(16)]
        for p, n in enumerate(face_nodes(face)):
            jump = planes[turned_position(3, p)]
            for t in range(3):
                jump = jnp.where(is_turn[t], planes[turned_position(t, p)], jump)
            if own:
                jump = jnp.where(valid, jump - rows_of[pl.ds(n, 8, stride=nodes), :], 0.0)
            rhs[n] = rhs[n] + PENALTY * jump


def source_rows(total, nodes, lamb, mean):
    block = 4 * nodes
    for h in range(total.shape[1] // LANES):
        columns = slice(h * LANES, (h + 1) * LANES)
        lamb[h * block : h * block + nodes, :] = jnp.zeros((nodes, LANES), F32)
        for d in range(3):
            at = h * block + (1 + d) * nodes
            lamb[at : at + nodes, :] = total[d * nodes : (d + 1) * nodes, columns]
            value = total[(3 + d) * nodes : (4 + d) * nodes, columns]
            for v in range(4):
                at = h * block + v * nodes
                mean[d, at : at + nodes, :] = value


def source_terms(nodes, grads, lamb, mean, n):
    total = lamb[pl.ds(n, 8, stride=nodes), :]
    for d in range(3):
        total = total + mean[d, pl.ds(n, 8, stride=nodes), :] * grads[d, n]
    return total


def sound_one_kernel(
    base, grads, source_a, source_b, rows_of, scale_out, edge_a, edge_b, lamb, mean
):
    is_flow, even = on_flow_row(), on_even_column()
    nodes = base.shape[0]
    block = 4 * nodes

    @pl.when(jnp.logical_not(is_flow))
    def _():
        total = source_a[...].astype(F32) + source_b[...].astype(F32)
        count = total[6 * nodes : 6 * nodes + 1] + BASE * total[6 * nodes + 1 : 6 * nodes + 2]
        inverse = 1.0 / jnp.maximum(count, 1.0)
        scale_out[...] = jnp.broadcast_to(inverse, scale_out.shape)
        source_rows(total[: 6 * nodes] * inverse, nodes, lamb, mean)
        for n in range(nodes):
            rows_of[pl.ds(n, 8, stride=nodes), :] = base[n] - ACOUSTIC_STEP * source_terms(
                nodes, grads, lamb, mean, n
            )
        off_a = pl.multiple_of(jnp.where(even, 0, block), 16)
        off_b = pl.multiple_of(jnp.where(even, block, 0), 16)
        edge_a[...] = rows_of[pl.ds(off_a, block), :].astype(BF16)
        edge_b[...] = rows_of[pl.ds(off_b, block), :].astype(BF16)


def sound_inner_kernel(
    rows_of, neighbours, codes, scale, source_a, source_b,
    base, hot_beside, facing, remote, rhs, grads, lamb, mean,
):
    nodes = base.shape[0]
    elements = neighbours.shape[1]
    halves = elements // LANES
    block = 4 * nodes

    @pl.when(jnp.logical_not(on_flow_row()))
    def _():
        for face in range(6):
            for part in range(halves):
                facing_rows(rows_of, part * block, nodes, face ^ 1, facing.at[face, part])
            hot = hot_links(neighbours, face, elements, True, False)
            remote_rows([facing[face, part] for part in range(halves)], hot, remote, face)
            hot_beside[face] = hot_links(neighbours, face, elements, False, True)
        derivatives(rows_of, nodes, grads, rhs)
        add_faces(rows_of, nodes, remote, neighbours, codes, rhs, True)
        total = source_a[...].astype(F32) + source_b[...].astype(F32)
        source_rows(total * scale[0:1, :], nodes, lamb, mean)
        for n in range(nodes):
            base[n] = rows_of[pl.ds(n, 8, stride=nodes), :] + ACOUSTIC_STEP * (
                rhs[n] - source_terms(nodes, grads, lamb, mean, n)
            )


def sound_two_kernel(
    sound, base, hot_beside, neighbours, codes, part_a, part_b,
    out, rows_of, facing, remote, rhs,
):
    is_flow, even = on_flow_row(), on_even_column()
    nodes = base.shape[0]
    elements = sound.shape[2]
    halves = elements // LANES
    block = 4 * nodes

    @pl.when(is_flow)
    def _():
        out[...] = sound[...]

    @pl.when(jnp.logical_not(is_flow))
    def _():
        a, b = part_a[...].astype(F32), part_b[...].astype(F32)
        rows_of[:block, :] = jnp.where(even, a, b)
        rows_of[block:, :] = jnp.where(even, b, a)
        for face in range(6):
            for part in range(2):
                facing_rows(rows_of, part * block, nodes, face ^ 1, facing.at[face, part])
            remote_rows(
                [facing[face, part].astype(BF16) for part in range(2)], hot_beside[face], remote, face
            )
        rhs[...] = jnp.zeros_like(rhs)
        add_faces(rows_of, nodes, remote, neighbours, codes, rhs, False)
        for n in range(nodes):
            rows_of[pl.ds(n, 8, stride=nodes), :] = base[n] + ACOUSTIC_STEP * rhs[n]
        for v in range(4):
            for h in range(halves):
                out[v, :, h * LANES : (h + 1) * LANES] = rows_of[
                    h * block + v * nodes : h * block + (v + 1) * nodes, :
                ]


def call(kernel, outs, scratch, operands, in_hbm=(), limit=VMEM_LIMIT):
    spaces = [pltpu.HBM if at in in_hbm else pltpu.VMEM for at in range(len(operands))]
    moved = sum(int(np.prod(x.shape)) * x.dtype.itemsize for x in (*operands, *outs))
    return pl.pallas_call(
        kernel,
        out_shape=tuple(outs),
        in_specs=[pl.BlockSpec(memory_space=space) for space in spaces],
        out_specs=tuple([pl.BlockSpec(memory_space=pltpu.VMEM)] * len(outs)),
        scratch_shapes=scratch,
        compiler_params=pltpu.CompilerParams(vmem_limit_bytes=limit),
        cost_estimate=pl.CostEstimate(flops=10**8, bytes_accessed=moved, transcendentals=0),
    )(*operands)


def body(
    flow_fields,
    mean_velocity,
    cell_eddy_viscosity,
    tile_links,
    tile_target,
    projector,
    acoustic_state,
    element_face_neighbours,
    face_codes,
):
    groups = lax.axis_size("grp")
    count = lax.axis_size("sfc")
    flow = flow_fields[0]
    mean = mean_velocity[0]
    visc = cell_eddy_viscosity[0]
    links = tile_links[0]
    sound = acoustic_state[0]
    neighbours = element_face_neighbours[0]
    codes = face_codes[0]
    tiles = flow.shape[1]
    _, nodes, elements = sound.shape
    halves = elements // LANES
    block = 4 * nodes
    plan = FlowPlan(tiles)
    shape = jax.ShapeDtypeStruct
    vmem = pltpu.VMEM
    pairs_a = [p for i in range(1, count - 1, 2) for p in ((i, i + 1), (i + 1, i))]
    pairs_b = [p for i in range(0, count - 1, 2) for p in ((i, i + 1), (i + 1, i))]

    edge_rows = 6 * EDGE + EXTRA
    pack_a, pack_b = call(
        pack_kernel,
        [shape((edge_rows, LANES), BF16)] * 2,
        [
            vmem(links.shape, jnp.int32),
            vmem((2, 6 * EDGE, LANES), F32),
            pltpu.SemaphoreType.DMA((2, 6)),
            pltpu.SemaphoreType.DMA,
        ],
        [flow, visc, links, sound],
        in_hbm=(0, 1, 2, 3),
        limit=PACK_LIMIT,
    )
    part_a = lax.ppermute(pack_a, "sfc", pairs_a)
    part_b = lax.ppermute(pack_b, "sfc", pairs_b)

    fields = 5 * LANES
    rows, span = plan.rows, plan.span
    inner_rows = (plan.blocks - 2) * rows
    square = vmem((LANES, LANES), F32)
    packed = vmem((6, tiles, LANES), F32)
    inner_state, inner_high, inner_low, lcol, inner_mats, hits = call(
        inner_kernel,
        [
            shape((inner_rows, fields), F32),
            shape((inner_rows, fields), BF16),
            shape((inner_rows, fields), BF16),
            shape((tiles, LANES), F32),
            shape((plan.blocks - 2, 3 * rows, 2 * span), BF16),
            shape((2 * elements, tiles), BF16),
        ],
        [vmem((tiles, fields), BF16), vmem((tiles, fields), BF16), square],
        [flow, visc, links, tile_target],
    )
    lines = 6 * nodes + EXTRA
    by_node = shape((nodes, 8, LANES), F32)
    by_node_3 = shape((3, nodes, 8, LANES), F32)
    node_rows = vmem((nodes, 8, LANES), F32)
    (
        own_one, next_one, mean_one, base, grads,
        edge_state, edge_high, edge_low, edge_mats, edge_visc,
    ) = call(
        first_kernel,
        [
            shape((lines, elements), F32),
            shape((lines, elements), BF16),
            shape(mean.shape, F32),
            by_node,
            by_node_3,
            shape((2 * rows, fields), F32),
            shape((2 * rows, fields), BF16),
            shape((2 * rows, fields), BF16),
            shape((2, 3 * rows, 2 * span), BF16),
            shape((2 * rows, LANES), F32),
        ],
        [
            square,
            vmem((2, span, fields), F32),
            vmem((2, span, fields), BF16),
            vmem((2, span, fields), BF16),
            vmem((HW, fields), BF16),
            packed,
            vmem((lines, tiles), BF16),
            vmem(((halves + 2) * block, LANES), F32),
            vmem((6, halves + 2, 64, LANES), F32),
            vmem((6, halves * 64, LANES), F32),
            node_rows,
        ],
        [
            flow, visc, mean, projector, part_a, part_b, sound, neighbours, codes,
            inner_state, inner_high, inner_low, lcol, inner_mats, hits,
        ],
    )

    up = [(i, i + 1) for i in range(count - 1)]

    def climb(x):
        chosen = [(g * count + i, g * count + j) for g in range(groups - 1) for i, j in up]
        return lax.ppermute(x, ("grp", "sfc"), chosen)

    def combined(*xs):
        total = xs[0]
        for x in xs[1:]:
            total = total + x.astype(F32)
        return total.astype(BF16)

    got_one = climb(next_one)
    band = plan.blocks * rows
    velocity = 3 * LANES
    step_one = [inner_state, inner_high, inner_low, inner_mats]
    edges = [edge_state, edge_high, edge_low, edge_mats, edge_visc]
    state_two, mean_two, own_two, next_two = call(
        second_kernel,
        [
            shape((band, velocity), F32),
            shape(mean.shape, F32),
            shape((6 * nodes, elements), F32),
            shape((6 * nodes, elements), BF16),
        ],
        [
            vmem((band, velocity), BF16),
            vmem((band, velocity), BF16),
            vmem((HW, fields), BF16),
            packed,
            vmem((6 * nodes, tiles), BF16),
        ],
        [visc, mean, mean_one, projector, *step_one, hits, *edges],
    )
    got_two = climb(next_two)
    sum_one = combined(own_one, got_one)
    x_one = lax.ppermute(sum_one, "grp", [(0, 1), (2, 3)])
    flow_out, mean_out, token = call(
        output_kernel,
        [shape(flow.shape, F32), shape(mean.shape, F32), shape((8, LANES), F32)],
        [vmem((band, fields), F32), vmem((HW, fields), BF16)],
        [flow, visc, mean, state_two, mean_two, *step_one, *edges, sum_one],
    )
    y_two = lax.ppermute(combined(own_two, got_two, token[0, 0]), "grp", [(0, 2), (1, 3)])
    y_one = lax.ppermute(combined(own_one, got_one, x_one), "grp", [(1, 3)])
    x_two = lax.ppermute(combined(own_two, got_two, y_two), "grp", [(2, 3)])

    sound_rows, scale, edge_a, edge_b = call(
        sound_one_kernel,
        [
            shape((halves * block, LANES), F32),
            shape((8, elements), F32),
            shape((block, LANES), BF16),
            shape((block, LANES), BF16),
        ],
        [vmem((halves * block, LANES), F32), vmem((3, halves * block, LANES), F32)],
        [base, grads, x_one, y_one],
    )
    last = (groups - 1) * count
    part_a = lax.ppermute(edge_a, ("grp", "sfc"), [(last + i, last + j) for i, j in pairs_a])
    part_b = lax.ppermute(edge_b, ("grp", "sfc"), [(last + i, last + j) for i, j in pairs_b])
    base, hot_beside = call(
        sound_inner_kernel,
        [by_node, shape((6, 2 * LANES, elements), BF16)],
        [
            vmem((6, halves, 64, LANES), F32),
            vmem((6, halves * 64, LANES), F32),
            node_rows,
            vmem((3, nodes, 8, LANES), F32),
            vmem((halves * block, LANES), F32),
            vmem((3, halves * block, LANES), F32),
        ],
        [sound_rows, neighbours, codes, scale, x_two, y_two],
    )
    (sound_out,) = call(
        sound_two_kernel,
        [shape(sound.shape, F32)],
        [
            vmem((halves * block, LANES), F32),
            vmem((6, 2, 64, LANES), F32),
            vmem((6, halves * 64, LANES), F32),
            node_rows,
        ],
        [sound, base, hot_beside, neighbours, codes, part_a, part_b],
    )
    return flow_out[None], mean_out[None], sound_out[None]


def solution(mesh):
    placed = (
        P("grp", None, "sfc", None),
        P("grp", None, "sfc", None),
        P("grp", "sfc", None),
        P("grp", None, "sfc"),
        P("grp", "sfc"),
        P(),
        P("grp", None, None, "sfc"),
        P("grp", None, "sfc"),
        P("grp", None, "sfc"),
    )
    return jax.shard_map(
        body,
        mesh=mesh,
        in_specs=placed,
        out_specs=(
            P("grp", None, "sfc", None),
            P("grp", None, "sfc", None),
            P("grp", None, None, "sfc"),
        ),
        check_vma=False,
    )
```

```python
import jax
import jax.numpy as jnp
import numpy as np
from jax import lax
from jax.experimental import pallas as pl
from jax.experimental.pallas import tpu as pltpu
from jax.sharding import PartitionSpec as P

HW = 16
HE = 16

ADVECT = 0.1
RELAX = 0.1
PENALTY = 1.5
ACOUSTIC_STEP = 0.08

LANES = 128
EDGE = 3 * HW
NO_LINK = 64
FIELD_ORDER = (1, 2, 3, 0, 4)
ALL_FIELDS = ((0, 2), (2, 4), (4, 5))
BASE = 32.0
EXTRA = 16
VMEM_LIMIT = 20 * 1024 * 1024
PACK_LIMIT = 60 * 1024 * 1024

F32 = jnp.float32
BF16 = jnp.bfloat16


def lobatto_matrix():
    points = np.array([-1.0, -1.0 / np.sqrt(5.0), 1.0 / np.sqrt(5.0), 1.0])
    weights = np.array(
        [
            1.0 / np.prod([points[col] - points[other] for other in range(4) if other != col])
            for col in range(4)
        ]
    )
    matrix = np.zeros((4, 4))
    for line in range(4):
        for col in range(4):
            if line != col:
                matrix[line, col] = weights[col] / weights[line] / (points[line] - points[col])
        matrix[line, line] = -matrix[line].sum()
    return matrix.astype(np.float32)


def face_nodes(face):
    axis, level = face // 2, 3 * (face % 2)
    nodes = []
    for second in range(4):
        for first in range(4):
            coords = [first, second]
            coords.insert(axis, level)
            nodes.append(coords[0] + 4 * coords[1] + 16 * coords[2])
    return nodes


def turned_position(turn, position):
    a, b = position % 4, position // 4
    a, b = ((a, b), (3 - b, a), (3 - a, 3 - b), (b, 3 - a))[turn]
    return a + 4 * b


def split_parts(x):
    high = x.astype(BF16)
    return high, (x - high.astype(F32)).astype(BF16)


def dot(a, b):
    return jnp.dot(a, b, preferred_element_type=F32)


def dot_t(a, b):
    return lax.dot_general(a, b, (((1,), (1,)), ((), ())), preferred_element_type=F32)


def on_flow_row():
    return lax.axis_index("grp") < lax.axis_size("grp") - 1


def on_even_column():
    return lax.rem(lax.axis_index("sfc"), 2) == 0


def pack_kernel(
    flow, visc, links, sound, neighbours, codes,
    out_a, out_b, links_in, faces_in, staged, sems, link_sems,
):
    is_flow, even = on_flow_row(), on_even_column()
    tiles = flow.shape[1]
    _, nodes, elements = sound.shape
    outs = (out_a, out_b)

    @pl.when(is_flow)
    def _():
        fetch = pltpu.make_async_copy(links, links_in, link_sems.at[0])
        fetch.start()
        copies = []
        for side in range(2):
            off = pl.multiple_of(jnp.where(even == (side == 0), 0, tiles - EDGE), 8)
            for place, f in enumerate(FIELD_ORDER):
                copies.append(
                    pltpu.make_async_copy(
                        flow.at[f, pl.ds(off, EDGE), :],
                        staged.at[side, pl.ds(place * EDGE, EDGE), :],
                        sems.at[side, place],
                    )
                )
            copies.append(
                pltpu.make_async_copy(
                    visc.at[pl.ds(off, EDGE), :],
                    staged.at[side, pl.ds(5 * EDGE, EDGE), :],
                    sems.at[side, 5],
                )
            )
        for copy in copies:
            copy.start()
        fetch.wait()
        given = links_in[...]
        own = lax.axis_index("sfc") * tiles + lax.broadcasted_iota(jnp.int32, given.shape, 1)
        offset = jnp.where(given < 0, 0, given - own).astype(F32)
        low, high = offset[:, :LANES], offset[:, tiles - LANES :]
        pad = jnp.zeros((EXTRA - 4, LANES), F32)
        for side, (a, b) in enumerate(((low, high), (high, low))):
            block = jnp.concatenate([jnp.where(even, a, b), pad], 0)
            outs[side][6 * EDGE :, :] = block.astype(BF16)
        for copy in copies:
            copy.wait()
        for side in range(2):
            outs[side][: 6 * EDGE, :] = staged[side].astype(BF16)

    @pl.when(jnp.logical_not(is_flow))
    def _():
        copies = []
        for side in range(2):
            off = pl.multiple_of(jnp.where(even == (side == 0), 0, elements - LANES), LANES)
            for v in range(4):
                copies.append(
                    pltpu.make_async_copy(
                        sound.at[v, :, pl.ds(off, LANES)],
                        staged.at[side, pl.ds(v * nodes, nodes), :],
                        sems.at[side, v],
                    )
                )
        for at, ref in enumerate((neighbours, codes)):
            copies.append(pltpu.make_async_copy(ref, faces_in.at[at], link_sems.at[at]))
        for copy in copies:
            copy.start()
        for copy in copies:
            copy.wait()
        first = lax.axis_index("sfc") * elements
        own = first + lax.broadcasted_iota(jnp.int32, (1, elements), 1)
        for face in range(6):
            link = faces_in[0, face]
            offset = jnp.where(link < 0, NO_LINK, link - own).astype(F32)
            for at, row in enumerate((offset, faces_in[1, face].astype(F32))):
                line = 4 * nodes + 6 * at + face
                low, high = row[:, :LANES], row[:, elements - LANES :]
                staged[0, line : line + 1, :] = jnp.where(even, low, high)
                staged[1, line : line + 1, :] = jnp.where(even, high, low)
        used = 4 * nodes + 12
        for side, out in enumerate(outs):
            staged[side, used:, :] = jnp.zeros((staged.shape[1] - used, LANES), F32)
            out[: 6 * EDGE, :] = staged[side].astype(BF16)
            out[6 * EDGE :, :] = jnp.zeros((out.shape[0] - 6 * EDGE, LANES), BF16)


class FlowPlan:
    def __init__(self, tiles):
        self.tiles = tiles
        self.wide = tiles + 2 * EDGE
        self.blocks = 4
        self.rows = (tiles + 4 * HW) // self.blocks
        self.span = self.rows + 2 * HW

    def at(self, b):
        return HW + b * self.rows

    def inner(self):
        return range(1, self.blocks - 1)


def columns_of(place):
    return slice(place * LANES, (place + 1) * LANES)


def rows_between(parts, low, high, columns):
    taken = []
    for start, ref in parts:
        a, b = max(low, start), min(high, start + ref.shape[0])
        if a < b:
            taken.append(ref[a - start : b - start, columns])
    return taken[0] if len(taken) == 1 else jnp.concatenate(taken, 0)


def put(high, low, at, place, value):
    h, l = split_parts(value)
    high[at : at + value.shape[0], columns_of(place)] = h
    low[at : at + value.shape[0], columns_of(place)] = l


def east_west(x):
    return pltpu.roll(x, LANES - 1, 1), pltpu.roll(x, 1, 1)


def link_matrix(plan, offset, mat):
    rows, span = plan.rows, plan.span
    lane = lax.broadcasted_iota(jnp.int32, (rows, 2 * span), 1)
    lane = jnp.where(lane >= span, lane - span, lane)
    place = HW + lax.broadcasted_iota(jnp.int32, (rows, LANES), 0) + offset.astype(jnp.int32)
    hot = [jnp.where(place[:, k : k + 1] == lane, F32(1.0), F32(0.0)) for k in range(4)]
    mat[:rows, :] = (hot[0] + hot[1] + hot[2] + hot[3]).astype(BF16)
    mat[rows : 2 * rows, :] = (hot[0] - hot[1]).astype(BF16)
    mat[2 * rows :, :] = (hot[2] - hot[3]).astype(BF16)


def gathered(plan, mat, high, low, b, columns, at_row):
    at = b * plan.rows
    both = [rows_between(x, at, at + plan.span, columns) for x in (high, low)]
    return dot(mat[at_row:, :], jnp.concatenate(both, 0))


def advance(plan, b, mat, high, low, state, v, places, new_state, new_high, new_low, new_at, split):
    rows = plan.rows
    center = [state(k) for k in range(3)]
    scaled = [(0.5 * ADVECT) * c for c in center]
    for first, last in places:
        got = gathered(plan, mat, high, low, b, slice(first * LANES, last * LANES), 0)
        for place in range(first, last):
            inner = columns_of(place - first)
            total, dy, dz = got[:rows, inner], got[rows : 2 * rows, inner], got[2 * rows :, inner]
            c = center[place] if place < 3 else state(place)
            east, west = east_west(c)
            new = (
                c
                + v * (east + west + total - 6.0 * c)
                - (scaled[0] * (east - west) + scaled[1] * dy + scaled[2] * dz)
            )
            new_state[new_at : new_at + rows, columns_of(place)] = new
            if split:
                put(new_high, new_low, new_at, place, new)


def lamb_block(plan, b, mat, high, low, state, average, average_out, packed):
    rows = plan.rows
    center = [state(k) for k in range(3)]
    got = [
        gathered(plan, mat, high, low, b, slice(0, 2 * LANES), rows),
        gathered(plan, mat, high, low, b, slice(2 * LANES, 3 * LANES), rows),
    ]
    d1, d2, d3 = [], [], []
    for k in range(3):
        east, west = east_west(center[k])
        d1.append((east - west) * 0.5)
        inner = columns_of(k % 2)
        d2.append(got[k // 2][:rows, inner] * 0.5)
        d3.append(got[k // 2][rows:, inner] * 0.5)
    vx = d2[2] - d3[1]
    vy = d3[0] - d1[2]
    vz = d1[1] - d2[0]
    lamb = (
        vy * center[2] - vz * center[1],
        vz * center[0] - vx * center[2],
        vx * center[1] - vy * center[0],
    )
    to = plan.at(b) - EDGE
    low_row, top_row = max(0, -to), min(rows, plan.tiles - to)
    own = slice(to + low_row, to + top_row)
    for i in range(3):
        packed[i, own, :] = lamb[i][low_row:top_row]
        mixed = (1.0 - RELAX) * average[i, own, :] + RELAX * center[i][low_row:top_row]
        average_out[i, own, :] = mixed
        packed[3 + i, own, :] = mixed


def element_sums(projector, packed, hits, pay, own_ref, next_ref):
    nodes = projector.shape[0]
    count, elements = own_ref.shape
    proj_high, proj_low = split_parts(projector[...])
    proj_both = jnp.concatenate([proj_high, proj_low], 0)
    for c in range(6):
        x_high, x_low = split_parts(packed[c])
        main = dot_t(proj_both, x_high)
        mapped = main[:nodes] + main[nodes:] + dot_t(proj_high, x_low)
        pay[c * nodes : (c + 1) * nodes, :] = mapped.astype(BF16)
    if count > 6 * nodes:
        pay[6 * nodes :, :] = jnp.ones((count - 6 * nodes, pay.shape[1]), BF16)
    sums = dot_t(pay[...], hits[...])
    if count > 6 * nodes:
        tail = sums[6 * nodes :]
        line = lax.broadcasted_iota(jnp.int32, tail.shape, 0)
        big = jnp.floor(tail * (1.0 / BASE))
        tail = jnp.where(line == 0, tail - BASE * big, jnp.where(line == 1, big, 0.0))
        sums = jnp.concatenate([sums[: 6 * nodes], tail], 0)
    own_ref[...] = sums[:, :elements]
    next_ref[...] = sums[:, elements:].astype(BF16)


def inner_kernel(
    flow, visc, links, target,
    inner_state, inner_high, inner_low, lcol, inner_mats, hits, high0, low0, square,
):
    plan = FlowPlan(flow.shape[1])
    tiles, rows = plan.tiles, plan.rows

    @pl.when(on_flow_row())
    def _():
        column = lax.axis_index("sfc")
        first_tile, first_element = column * tiles, column * (hits.shape[0] // 2)
        for place, f in enumerate(FIELD_ORDER):
            put(high0, low0, 0, place, flow[f])
        square[...] = jnp.zeros_like(square)
        own_tile = first_tile + lax.broadcasted_iota(jnp.int32, links.shape, 1)
        offset = jnp.where(links[...] < 0, 0, links[...] - own_tile).astype(F32)
        for part in range(tiles // LANES):
            square[:4, :] = offset[:, part * LANES : (part + 1) * LANES]
            lcol[part * LANES : (part + 1) * LANES, :] = square[...].T
        local = target[...] - first_element
        hits[...] = jnp.where(
            lax.broadcasted_iota(jnp.int32, hits.shape, 0) == local, F32(1.0), F32(0.0)
        ).astype(BF16)
        for at, b in enumerate(plan.inner()):
            own = slice(plan.at(b) - EDGE, plan.at(b) - EDGE + rows)
            link_matrix(plan, lcol[own, :], inner_mats.at[at])
            advance(
                plan, b, inner_mats.at[at], [(EDGE, high0)], [(EDGE, low0)],
                lambda place, own=own: flow[FIELD_ORDER[place], own, :],
                visc[own, :], ALL_FIELDS, inner_state, inner_high, inner_low, at * rows, True,
            )


def band_parts(plan, edge, inner):
    rows, last = plan.rows, plan.blocks - 1
    return [
        (plan.at(0), edge.at[:rows]),
        (plan.at(1), inner),
        (plan.at(last), edge.at[rows:]),
    ]


def band_state(plan, b, edge, inner):
    at = plan.at(b)
    parts = band_parts(plan, edge, inner)
    return lambda place: rows_between(parts, at, at + plan.rows, columns_of(place))


def closed(plan, parts, zero):
    return [(0, zero), *parts, (plan.wide - HW, zero)]


def mats_of(plan, b, edge_mats, inner_mats):
    if b in plan.inner():
        return inner_mats.at[b - 1]
    return edge_mats.at[0 if b == 0 else 1]


def first_kernel(
    flow, visc, mean, projector, part_a, part_b, sound, neighbours, codes,
    inner_state, inner_high, inner_low, lcol, inner_mats, hits,
    own_one, next_one, mean_one, base, grads, hot_two,
    edge_state, edge_high, edge_low, edge_mats, edge_visc,
    square, state0, high0, low0, zero, packed, pay, rows_of, facing, remote, rhs,
):
    is_flow, even = on_flow_row(), on_even_column()
    plan = FlowPlan(packed.shape[1])
    tiles, rows, span = plan.tiles, plan.rows, plan.span
    own_rows = span - EDGE

    @pl.when(is_flow)
    def _():
        def pick(at, size):
            a, b = part_a[at : at + size, :].astype(F32), part_b[at : at + size, :].astype(F32)
            return jnp.where(even, a, b), jnp.where(even, b, a)

        zero[...] = jnp.zeros_like(zero)
        for place, f in enumerate(FIELD_ORDER):
            before, after = pick(place * EDGE, EDGE)
            ends = (
                jnp.concatenate([before, flow[f, :own_rows, :]], 0),
                jnp.concatenate([flow[f, tiles - own_rows :, :], after], 0),
            )
            for side in range(2):
                state0[side, :, columns_of(place)] = ends[side]
                put(high0.at[side], low0.at[side], 0, place, ends[side])
        before, after = pick(5 * EDGE, EDGE)
        edge_visc[:rows, :] = jnp.concatenate([before[HW:], visc[: rows - EDGE + HW, :]], 0)
        edge_visc[rows:, :] = jnp.concatenate(
            [visc[tiles - (rows - EDGE + HW) :, :], after[: EDGE - HW]], 0
        )
        before, after = pick(6 * EDGE, EXTRA)
        given = []
        for side, block in enumerate((before, after)):
            square[...] = jnp.zeros_like(square)
            square[:EXTRA, :] = block
            turned = square[...].T
            given.append(
                jnp.concatenate([turned[LANES - EDGE + HW :], lcol[: rows - EDGE + HW, :]], 0)
                if side == 0
                else jnp.concatenate(
                    [lcol[tiles - (rows - EDGE + HW) :, :], turned[: EDGE - HW]], 0
                )
            )
        for side, b in enumerate((0, plan.blocks - 1)):
            link_matrix(plan, given[side], edge_mats.at[side])
            advance(
                plan, b, edge_mats.at[side],
                [(b * rows, high0.at[side])], [(b * rows, low0.at[side])],
                lambda place, side=side: state0[side, HW : HW + rows, columns_of(place)],
                edge_visc[side * rows : (side + 1) * rows, :], ALL_FIELDS,
                edge_state, edge_high, edge_low, side * rows, True,
            )
        high1 = closed(plan, band_parts(plan, edge_high, inner_high), zero)
        low1 = closed(plan, band_parts(plan, edge_low, inner_low), zero)
        for b in range(plan.blocks):
            lamb_block(
                plan, b, mats_of(plan, b, edge_mats, inner_mats), high1, low1,
                band_state(plan, b, edge_state, inner_state), mean, mean_one, packed,
            )
        element_sums(projector, packed, hits, pay, own_one, next_one)

    @pl.when(jnp.logical_not(is_flow))
    def _():
        own_one[...] = jnp.zeros_like(own_one)
        next_one[...] = jnp.zeros_like(next_one)
        nodes, elements = sound.shape[1:]
        halves = elements // LANES
        block = 4 * nodes
        for v in range(4):
            for h in range(halves):
                rows_of[h * block + v * nodes : h * block + (v + 1) * nodes, :] = sound[
                    v, :, h * LANES : (h + 1) * LANES
                ]
        a, b = part_a[:block, :].astype(F32), part_b[:block, :].astype(F32)
        before, after = jnp.where(even, a, b), jnp.where(even, b, a)
        lane = lax.broadcasted_iota(jnp.int32, (1, LANES), 1)
        beside = lane < LANES // 2
        rows_of[halves * block : (halves + 1) * block, :] = jnp.where(beside, after, before)
        rows_of[(halves + 1) * block : (halves + 2) * block, :] = jnp.zeros_like(before)
        rows_of[(halves + 2) * block : (halves + 3) * block, :] = before
        rows_of[(halves + 3) * block :, :] = after
        a = part_a[block : block + EXTRA, :].astype(F32)
        b = part_b[block : block + EXTRA, :].astype(F32)
        given = jnp.where(beside, jnp.where(even, b, a), jnp.where(even, a, b)).astype(jnp.int32)
        own_parts = [0, 1, halves + 2, halves + 3]
        first = lax.axis_index("sfc") * elements
        masks = []
        for face in range(6):
            for at, part in enumerate(own_parts):
                facing_rows(rows_of, part * block, nodes, face ^ 1, facing.at[face, at])
            link, code = neighbours[face], codes[face]
            offset, extra_code = given[face : face + 1, :], given[6 + face : 7 + face, :]
            extra = jnp.where(beside, elements + lane, lane - LANES) + offset
            near = jnp.concatenate([link - first, extra], 1)
            valid = jnp.concatenate([link, jnp.where(offset >= NO_LINK, -1, 0)], 1) >= 0
            place = jnp.where(
                near < 0, elements + LANES + near, jnp.where(near < elements, near, near + LANES)
            )
            hot = hot_columns(jnp.where(valid, place, -1), elements + 2 * LANES)
            remote_rows([facing[face, at] for at in range(4)], hot, remote, face)
            near = link - first
            place = jnp.where(near < 0, elements + LANES + near, near)
            hot_two[face] = hot_columns(jnp.where(link < 0, -1, place), elements + LANES)
            masks.append(
                (
                    face_masks(link[:, :LANES], link[:, LANES:], code[:, :LANES], code[:, LANES:]),
                    face_masks(
                        jnp.where(offset >= NO_LINK, -1, 0), jnp.full((1, LANES), -1, jnp.int32),
                        extra_code, extra_code,
                    ),
                )
            )
        for group in range(2):
            start = group * halves * block
            derivatives(rows_of, start, nodes, grads.at[group], rhs)
            add_faces(
                rows_of, start, nodes, remote, group * halves * 64, [m[group] for m in masks], rhs
            )
            for n in range(nodes):
                base[group, n] = node_of(rows_of, start, nodes, n) + ACOUSTIC_STEP * rhs[n]


def second_block(plan, b, carried, visc, places, new_state, new_parts):
    (inner_state, inner_high, inner_low, inner_mats, edge_state, edge_high, edge_low, edge_mats,
     edge_visc, zero) = carried
    rows = plan.rows
    if b in plan.inner():
        v = visc[plan.at(b) - EDGE : plan.at(b) - EDGE + rows, :]
    else:
        v = edge_visc[:rows, :] if b == 0 else edge_visc[rows:, :]
    advance(
        plan, b, mats_of(plan, b, edge_mats, inner_mats),
        closed(plan, band_parts(plan, edge_high, inner_high), zero),
        closed(plan, band_parts(plan, edge_low, inner_low), zero),
        band_state(plan, b, edge_state, inner_state), v, places,
        new_state, *new_parts, b * rows, new_parts[0] is not None,
    )


def second_kernel(
    visc, mean, mean_one, projector,
    inner_state, inner_high, inner_low, inner_mats, hits,
    edge_state, edge_high, edge_low, edge_mats, edge_visc,
    state, mean_two, own_two, next_two,
    high, low, zero, packed, pay,
):
    plan = FlowPlan(packed.shape[1])
    rows = plan.rows
    is_flow = on_flow_row()

    @pl.when(jnp.logical_not(is_flow))
    def _():
        own_two[...] = jnp.zeros_like(own_two)
        next_two[...] = jnp.zeros_like(next_two)

    @pl.when(is_flow)
    def _():
        zero[...] = jnp.zeros_like(zero)
        carried = (
            inner_state, inner_high, inner_low, inner_mats,
            edge_state, edge_high, edge_low, edge_mats, edge_visc, zero,
        )
        for b in range(plan.blocks):
            second_block(plan, b, carried, visc, ((0, 2), (2, 3)), state, (high, low))
        for b in range(plan.blocks):
            lamb_block(
                plan, b, mats_of(plan, b, edge_mats, inner_mats),
                closed(plan, [(HW, high)], zero), closed(plan, [(HW, low)], zero),
                lambda place, b=b: state[b * rows : (b + 1) * rows, columns_of(place)],
                mean_one, mean_two, packed,
            )
        element_sums(projector, packed, hits, pay, own_two, next_two)


def output_kernel(
    flow, visc, mean, state, mean_two,
    inner_state, inner_high, inner_low, inner_mats,
    edge_state, edge_high, edge_low, edge_mats, edge_visc, after, after_up, after_down, own_one,
    flow_out, mean_out, own_one_out, passive, zero,
):
    plan = FlowPlan(flow.shape[1])
    is_flow = on_flow_row()
    own_one_out[...] = own_one[...]

    @pl.when(jnp.logical_not(is_flow))
    def _():
        flow_out[...] = flow[...]
        mean_out[...] = mean[...]

    @pl.when(is_flow)
    def _():
        zero[...] = jnp.zeros_like(zero)
        mean_out[...] = mean_two[...]
        carried = (
            inner_state, inner_high, inner_low, inner_mats,
            edge_state, edge_high, edge_low, edge_mats, edge_visc, zero,
        )
        own = slice(EDGE - HW, EDGE - HW + plan.tiles)
        for place in range(3):
            flow_out[FIELD_ORDER[place]] = state[own, columns_of(place)]
        for b in range(plan.blocks):
            second_block(plan, b, carried, visc, ((3, 5),), passive, (None, None))
        for place in (3, 4):
            flow_out[FIELD_ORDER[place]] = passive[own, columns_of(place)]


def facing_rows(rows_of, base, nodes, face, to):
    axis, level = face // 2, 3 * (face % 2)
    if axis == 0:
        to[...] = rows_of[pl.ds(base + level, 64, stride=4), :]
    elif axis == 1:
        for i in range(4):
            to[pl.ds(i, 16, stride=4), :] = rows_of[pl.ds(base + i + 4 * level, 16, stride=16), :]
    else:
        for v in range(4):
            at = base + v * nodes + 16 * level
            to[v * 16 : (v + 1) * 16, :] = rows_of[at : at + 16, :]


def hot_columns(place, size):
    key = lax.broadcasted_iota(jnp.int32, (size, place.shape[1]), 0)
    return jnp.where(key == place, F32(1.0), F32(0.0)).astype(BF16)


def node_of(rows_of, start, nodes, n):
    return rows_of[pl.ds(start + n, 8, stride=nodes), :]


def remote_rows(parts, hot, remote, face):
    high, low = split_parts(jnp.concatenate(parts, 1))
    got = dot(jnp.concatenate([high, low], 0), hot)
    got = got[:64] + got[64:]
    for h in range(got.shape[1] // LANES):
        remote[face, h * 64 : (h + 1) * 64, :] = got[:, h * LANES : (h + 1) * LANES]


def derivatives(rows_of, start, nodes, grads_out, rhs):
    matrix = lobatto_matrix()
    line = lax.broadcasted_iota(jnp.int32, (8, LANES), 0)
    is_v = [line % 4 == v for v in range(4)]
    node = [node_of(rows_of, start, nodes, n) for n in range(nodes)]
    for n in range(nodes):
        i, j, k = n % 4, n // 4 % 4, n // 16
        lines = (
            [m + 4 * j + 16 * k for m in range(4)],
            [i + 4 * m + 16 * k for m in range(4)],
            [i + 4 * j + 16 * m for m in range(4)],
        )
        grads = []
        for d, at in enumerate((i, j, k)):
            total = None
            for m in range(4):
                if abs(matrix[at, m]) > 1e-12:
                    term = F32(matrix[at, m]) * node[lines[d][m]]
                    total = term if total is None else total + term
            grads.append(total)
            grads_out[d, n] = total
        div = sum(pltpu.roll(grads[d], 8 - (1 + d), 0) for d in range(3))
        coupled = jnp.where(is_v[0], div, 0.0)
        for d in range(3):
            coupled = jnp.where(is_v[1 + d], pltpu.roll(grads[d], 1 + d, 0), coupled)
        rhs[n] = -coupled


def face_masks(link_low, link_high, code_low, code_high):
    upper = lax.broadcasted_iota(jnp.int32, (8, LANES), 0) >= 4

    def both(low, high):
        return jnp.where(
            upper, jnp.broadcast_to(high, (8, LANES)), jnp.broadcast_to(low, (8, LANES))
        )

    code = both(code_low, code_high)
    return both(link_low, link_high) >= 0, [code == t for t in range(3)]


def add_faces(rows_of, start, nodes, remote, remote_start, masks, rhs):
    for face in range(6):
        valid, is_turn = masks[face]
        planes = [remote[face, pl.ds(remote_start + p, 8, stride=16), :] for p in range(16)]
        for p, n in enumerate(face_nodes(face)):
            turned = planes[turned_position(3, p)]
            for t in range(3):
                turned = jnp.where(is_turn[t], planes[turned_position(t, p)], turned)
            jump = jnp.where(valid, turned - node_of(rows_of, start, nodes, n), 0.0)
            rhs[n] = rhs[n] + PENALTY * jump


def source_rows(total, start, nodes, lamb, mean):
    block = 4 * nodes
    for h in range(total.shape[1] // LANES):
        columns = slice(h * LANES, (h + 1) * LANES)
        low = start + h * block
        lamb[low : low + nodes, :] = jnp.zeros((nodes, LANES), F32)
        for d in range(3):
            at = low + (1 + d) * nodes
            lamb[at : at + nodes, :] = total[d * nodes : (d + 1) * nodes, columns]
            value = total[(3 + d) * nodes : (4 + d) * nodes, columns]
            for v in range(4):
                mean[d, low + v * nodes : low + (v + 1) * nodes, :] = value


def source_terms(start, nodes, grads, lamb, mean, n):
    total = node_of(lamb, start, nodes, n)
    for d in range(3):
        total = total + mean[d, pl.ds(start + n, 8, stride=nodes), :] * grads[d, n]
    return total


def border_kernel(sums, up, down):
    nodes_rows = (sums.shape[0] - EXTRA) // (LANES // HE)
    group = lax.broadcasted_iota(jnp.int32, (1, LANES), 1) // HE

    @pl.when(on_flow_row())
    def _():
        for out, tile, shift in ((up, sums.shape[1] - LANES, HE), (down, 0, 0)):
            columns = slice(tile, tile + LANES)
            total = jnp.zeros((nodes_rows, LANES), F32)
            for i in range(LANES // HE):
                x = sums[i * nodes_rows : (i + 1) * nodes_rows, columns].astype(F32)
                turn = (HE * i + shift) % LANES
                x = pltpu.roll(x, turn, 1) if turn else x
                total = jnp.where(group == i, x, total)
            out[:nodes_rows, :] = total.astype(BF16)
            x = sums[sums.shape[0] - EXTRA :, columns].astype(F32)
            x = pltpu.roll(x, shift, 1) if shift else x
            out[nodes_rows:, :] = jnp.where(group == 0, x, 0.0).astype(BF16)


def border_sums(up, down):
    lines = up.shape[0] - EXTRA
    lane = lax.broadcasted_iota(jnp.int32, (1, LANES), 1)
    parts = []
    for i in range(LANES // HE + 1):
        rows = slice(0, lines) if i < LANES // HE else slice(lines, lines + EXTRA)
        at = HE * (i % (LANES // HE))
        x = pltpu.roll(up[rows], (2 * LANES - HE - at) % LANES, 1)
        y = pltpu.roll(down[rows], (LANES - at) % LANES, 1) if at else down[rows]
        parts.append(jnp.where(lane >= LANES - HE, x, jnp.where(lane < HE, y, 0.0)))
    return jnp.concatenate(parts, 0)


def scaled_sums(total, nodes):
    count = total[6 * nodes : 6 * nodes + 1] + BASE * total[6 * nodes + 1 : 6 * nodes + 2]
    inverse = 1.0 / jnp.maximum(count, 1.0)
    return total[: 6 * nodes] * inverse, inverse


def sound_one_kernel(
    base, grads, hot_two, neighbours, codes, source_a, source_b, up_a, up_b, down_a, down_b,
    base_two, grads_two, scale_out, rows_of, facing, remote, rhs, lamb, mean,
):
    nodes = base.shape[1]
    elements = source_a.shape[1]
    halves = elements // LANES
    block = 4 * nodes

    @pl.when(jnp.logical_not(on_flow_row()))
    def _():
        own, inverse = scaled_sums(source_a[...].astype(F32) + source_b[...].astype(F32), nodes)
        scale_out[...] = jnp.broadcast_to(inverse, scale_out.shape)
        source_rows(own, 0, nodes, lamb, mean)
        extra = border_sums(
            up_a[...].astype(F32) + up_b[...].astype(F32),
            down_a[...].astype(F32) + down_b[...].astype(F32),
        )
        extra, _ = scaled_sums(extra, nodes)
        none = (halves + 1) * block
        lamb[none:, :] = jnp.zeros((block, LANES), F32)
        for d in range(3):
            mean[d, none:, :] = jnp.zeros((block, LANES), F32)
        source_rows(extra, halves * block, nodes, lamb, mean)
        for group in range(2):
            start = group * halves * block
            for n in range(nodes):
                rows_of[pl.ds(start + n, 8, stride=nodes), :] = base[
                    group, n
                ] - ACOUSTIC_STEP * source_terms(start, nodes, grads.at[group], lamb, mean, n)
        masks = []
        for face in range(6):
            for part in range(halves + 1):
                facing_rows(rows_of, part * block, nodes, face ^ 1, facing.at[face, part])
            remote_rows(
                [facing[face, part] for part in range(halves + 1)], hot_two[face], remote, face
            )
            link, code = neighbours[face], codes[face]
            masks.append(
                face_masks(link[:, :LANES], link[:, LANES:], code[:, :LANES], code[:, LANES:])
            )
        derivatives(rows_of, 0, nodes, grads_two, rhs)
        add_faces(rows_of, 0, nodes, remote, 0, masks, rhs)
        for n in range(nodes):
            base_two[n] = node_of(rows_of, 0, nodes, n) + ACOUSTIC_STEP * rhs[n]


def sound_two_kernel(
    sound, base, grads, scale, source_a, source_b, out, rows_of, lamb, mean
):
    nodes = base.shape[0]
    halves = sound.shape[2] // LANES
    block = 4 * nodes
    is_flow = on_flow_row()

    @pl.when(is_flow)
    def _():
        out[...] = sound[...]

    @pl.when(jnp.logical_not(is_flow))
    def _():
        total = source_a[...].astype(F32) + source_b[...].astype(F32)
        source_rows(total * scale[0:1, :], 0, nodes, lamb, mean)
        for n in range(nodes):
            rows_of[pl.ds(n, 8, stride=nodes), :] = base[n] - ACOUSTIC_STEP * source_terms(
                0, nodes, grads, lamb, mean, n
            )
        for v in range(4):
            for h in range(halves):
                out[v, :, h * LANES : (h + 1) * LANES] = rows_of[
                    h * block + v * nodes : h * block + (v + 1) * nodes, :
                ]


def call(kernel, outs, scratch, operands, flops=10**8, in_hbm=(), limit=VMEM_LIMIT):
    spaces = [pltpu.HBM if at in in_hbm else pltpu.VMEM for at in range(len(operands))]
    moved = sum(int(np.prod(x.shape)) * x.dtype.itemsize for x in (*operands, *outs))
    return pl.pallas_call(
        kernel,
        out_shape=tuple(outs),
        in_specs=[pl.BlockSpec(memory_space=space) for space in spaces],
        out_specs=tuple([pl.BlockSpec(memory_space=pltpu.VMEM)] * len(outs)),
        scratch_shapes=scratch,
        compiler_params=pltpu.CompilerParams(vmem_limit_bytes=limit),
        cost_estimate=pl.CostEstimate(flops=flops, bytes_accessed=moved, transcendentals=0),
    )(*operands)


def body(
    flow_fields,
    mean_velocity,
    cell_eddy_viscosity,
    tile_links,
    tile_target,
    projector,
    acoustic_state,
    element_face_neighbours,
    face_codes,
):
    groups = lax.axis_size("grp")
    count = lax.axis_size("sfc")
    flow = flow_fields[0]
    mean = mean_velocity[0]
    visc = cell_eddy_viscosity[0]
    links = tile_links[0]
    sound = acoustic_state[0]
    faces, span = element_face_neighbours.shape[1:]
    neighbours = element_face_neighbours.reshape(faces, 1, span)
    codes = face_codes.reshape(faces, 1, span)
    tiles = flow.shape[1]
    _, nodes, elements = sound.shape
    halves = elements // LANES
    block = 4 * nodes
    plan = FlowPlan(tiles)
    shape = jax.ShapeDtypeStruct
    vmem = pltpu.VMEM
    pairs_a = [p for i in range(1, count - 1, 2) for p in ((i, i + 1), (i + 1, i))]
    pairs_b = [p for i in range(0, count - 1, 2) for p in ((i, i + 1), (i + 1, i))]

    edge_rows = 6 * EDGE + EXTRA
    pack_a, pack_b = call(
        pack_kernel,
        [shape((edge_rows, LANES), BF16)] * 2,
        [
            vmem(links.shape, jnp.int32),
            vmem((2, *neighbours.shape), jnp.int32),
            vmem((2, 6 * EDGE, LANES), F32),
            pltpu.SemaphoreType.DMA((2, 6)),
            pltpu.SemaphoreType.DMA((2,)),
        ],
        [flow, visc, links, sound, neighbours, codes],
        in_hbm=(0, 1, 2, 3, 4, 5),
        limit=PACK_LIMIT,
        flops=10**10,
    )
    part_a = lax.ppermute(pack_a, "sfc", pairs_a)
    part_b = lax.ppermute(pack_b, "sfc", pairs_b)

    fields = 5 * LANES
    rows, span = plan.rows, plan.span
    inner_rows = (plan.blocks - 2) * rows
    square = vmem((LANES, LANES), F32)
    packed = vmem((6, tiles, LANES), F32)
    inner_state, inner_high, inner_low, lcol, inner_mats, hits = call(
        inner_kernel,
        [
            shape((inner_rows, fields), F32),
            shape((inner_rows, fields), BF16),
            shape((inner_rows, fields), BF16),
            shape((tiles, LANES), F32),
            shape((plan.blocks - 2, 3 * rows, 2 * span), BF16),
            shape((2 * elements, tiles), BF16),
        ],
        [vmem((tiles, fields), BF16), vmem((tiles, fields), BF16), square],
        [flow, visc, links, tile_target],
    )
    lines = 6 * nodes + EXTRA
    by_node = (nodes, 8, LANES)
    node_rows = vmem((nodes, 8, LANES), F32)
    (
        own_one, next_one, mean_one, base, grads, hot_two,
        edge_state, edge_high, edge_low, edge_mats, edge_visc,
    ) = call(
        first_kernel,
        [
            shape((lines, elements), F32),
            shape((lines, elements), BF16),
            shape(mean.shape, F32),
            shape((2, *by_node), F32),
            shape((2, 3, *by_node), F32),
            shape((6, elements + LANES, elements), BF16),
            shape((2 * rows, fields), F32),
            shape((2 * rows, fields), BF16),
            shape((2 * rows, fields), BF16),
            shape((2, 3 * rows, 2 * span), BF16),
            shape((2 * rows, LANES), F32),
        ],
        [
            square,
            vmem((2, span, fields), F32),
            vmem((2, span, fields), BF16),
            vmem((2, span, fields), BF16),
            vmem((HW, fields), BF16),
            packed,
            vmem((lines, tiles), BF16),
            vmem(((halves + 4) * block, LANES), F32),
            vmem((6, 4, 64, LANES), F32),
            vmem((6, (halves + 2) * 64, LANES), F32),
            node_rows,
        ],
        [
            flow, visc, mean, projector, part_a, part_b, sound, neighbours, codes,
            inner_state, inner_high, inner_low, lcol, inner_mats, hits,
        ],
    )

    up = [(i, i + 1) for i in range(count - 1)]

    def climb(x):
        chosen = [(g * count + i, g * count + j) for g in range(groups - 1) for i, j in up]
        return lax.ppermute(x, ("grp", "sfc"), chosen)

    def combined(*xs):
        total = xs[0]
        for x in xs[1:]:
            total = total + x.astype(F32)
        return total.astype(BF16)

    got_one = climb(next_one)
    band = plan.blocks * rows
    velocity = 3 * LANES
    step_one = [inner_state, inner_high, inner_low, inner_mats]
    edges = [edge_state, edge_high, edge_low, edge_mats, edge_visc]
    state_two, mean_two, own_two, next_two = call(
        second_kernel,
        [
            shape((band, velocity), F32),
            shape(mean.shape, F32),
            shape((6 * nodes, elements), F32),
            shape((6 * nodes, elements), BF16),
        ],
        [
            vmem((band, velocity), BF16),
            vmem((band, velocity), BF16),
            vmem((HW, fields), BF16),
            packed,
            vmem((6 * nodes, tiles), BF16),
        ],
        [visc, mean, mean_one, projector, *step_one, hits, *edges],
    )
    def borders(sums, row):
        lines = 6 * nodes // (LANES // HE) + EXTRA
        up, down = call(border_kernel, [shape((lines, LANES), BF16)] * 2, [], [sums])
        last = (groups - 1) * count
        return [
            lax.ppermute(
                x, ("grp", "sfc"),
                [(row * count + i, last + i + step) for i in range(count) if 0 <= i + step < count],
            )
            for x, step in ((up, 1), (down, -1))
        ]

    got_two = climb(next_two)
    sum_one = combined(own_one, got_one)
    x_one = lax.ppermute(sum_one, "grp", [(0, 1), (2, 3)])
    up_a, down_a = borders(sum_one, 2)
    sum_two = combined(own_two, got_two)
    y_two = lax.ppermute(sum_two, "grp", [(0, 2), (1, 3)])
    flow_out, mean_out, own_one = call(
        output_kernel,
        [shape(flow.shape, F32), shape(mean.shape, F32), shape(own_one.shape, F32)],
        [vmem((band, fields), F32), vmem((HW, fields), BF16)],
        [flow, visc, mean, state_two, mean_two, *step_one, *edges, sum_two, up_a, down_a, own_one],
    )
    sum_one = combined(own_one, got_one, x_one)
    y_one = lax.ppermute(sum_one, "grp", [(1, 3)])
    up_b, down_b = borders(sum_one, 1)
    x_two = lax.ppermute(combined(own_two, got_two, y_two), "grp", [(2, 3)])

    held = vmem(((halves + 2) * block, LANES), F32)
    held_3 = vmem((3, (halves + 2) * block, LANES), F32)
    base, grads, scale = call(
        sound_one_kernel,
        [shape(by_node, F32), shape((3, *by_node), F32), shape((8, elements), F32)],
        [
            held,
            vmem((6, halves + 1, 64, LANES), F32),
            vmem((6, halves * 64, LANES), F32),
            node_rows,
            held,
            held_3,
        ],
        [
            base, grads, hot_two, neighbours, codes, x_one, y_one,
            up_a, up_b, down_a, down_b,
        ],
        flops=10**10,
    )
    (sound_out,) = call(
        sound_two_kernel,
        [shape(sound.shape, F32)],
        [
            vmem((halves * block, LANES), F32),
            vmem((halves * block, LANES), F32),
            vmem((3, halves * block, LANES), F32),
        ],
        [sound, base, grads, scale, x_two, y_two],
    )
    return flow_out[None], mean_out[None], sound_out[None]


def solution(mesh):
    placed = (
        P("grp", None, "sfc", None),
        P("grp", None, "sfc", None),
        P("grp", "sfc", None),
        P("grp", None, "sfc"),
        P("grp", "sfc"),
        P(),
        P("grp", None, None, "sfc"),
        P("grp", None, "sfc"),
        P("grp", None, "sfc"),
    )
    return jax.shard_map(
        body,
        mesh=mesh,
        in_specs=placed,
        out_specs=(
            P("grp", None, "sfc", None),
            P("grp", None, "sfc", None),
            P("grp", None, None, "sfc"),
        ),
        check_vma=False,
    )
```

```python
import jax
import jax.numpy as jnp
import numpy as np
from jax import lax
from jax.experimental import pallas as pl
from jax.experimental.pallas import tpu as pltpu
from jax.sharding import PartitionSpec as P

HW = 16
HE = 16

ADVECT = 0.1
RELAX = 0.1
PENALTY = 1.5
ACOUSTIC_STEP = 0.08

LANES = 128
EDGE = 3 * HW
NO_LINK = 64
FIELD_ORDER = (1, 2, 3, 0, 4)
ALL_FIELDS = ((0, 2), (2, 4), (4, 5))
BASE = 32.0
EXTRA = 16
VMEM_LIMIT = 20 * 1024 * 1024
PACK_LIMIT = 60 * 1024 * 1024

F32 = jnp.float32
BF16 = jnp.bfloat16


def lobatto_matrix():
    points = np.array([-1.0, -1.0 / np.sqrt(5.0), 1.0 / np.sqrt(5.0), 1.0])
    weights = np.array(
        [
            1.0 / np.prod([points[col] - points[other] for other in range(4) if other != col])
            for col in range(4)
        ]
    )
    matrix = np.zeros((4, 4))
    for line in range(4):
        for col in range(4):
            if line != col:
                matrix[line, col] = weights[col] / weights[line] / (points[line] - points[col])
        matrix[line, line] = -matrix[line].sum()
    return matrix.astype(np.float32)


def face_nodes(face):
    axis, level = face // 2, 3 * (face % 2)
    nodes = []
    for second in range(4):
        for first in range(4):
            coords = [first, second]
            coords.insert(axis, level)
            nodes.append(coords[0] + 4 * coords[1] + 16 * coords[2])
    return nodes


def turned_position(turn, position):
    a, b = position % 4, position // 4
    a, b = ((a, b), (3 - b, a), (3 - a, 3 - b), (b, 3 - a))[turn]
    return a + 4 * b


def split_parts(x):
    high = x.astype(BF16)
    return high, (x - high.astype(F32)).astype(BF16)


def dot(a, b):
    return jnp.dot(a, b, preferred_element_type=F32)


def dot_t(a, b):
    return lax.dot_general(a, b, (((1,), (1,)), ((), ())), preferred_element_type=F32)


def on_flow_row():
    return lax.axis_index("grp") < lax.axis_size("grp") - 1


def on_even_column():
    return lax.rem(lax.axis_index("sfc"), 2) == 0


def pack_kernel(
    flow, visc, links, sound, neighbours, codes,
    out_a, out_b, links_in, faces_in, staged, sems, link_sems,
):
    is_flow, even = on_flow_row(), on_even_column()
    tiles = flow.shape[1]
    _, nodes, elements = sound.shape
    outs = (out_a, out_b)

    @pl.when(is_flow)
    def _():
        fetch = pltpu.make_async_copy(links, links_in, link_sems.at[0])
        fetch.start()
        copies = []
        for side in range(2):
            off = pl.multiple_of(jnp.where(even == (side == 0), 0, tiles - EDGE), 8)
            for place, f in enumerate(FIELD_ORDER):
                copies.append(
                    pltpu.make_async_copy(
                        flow.at[f, pl.ds(off, EDGE), :],
                        staged.at[side, pl.ds(place * EDGE, EDGE), :],
                        sems.at[side, place],
                    )
                )
            copies.append(
                pltpu.make_async_copy(
                    visc.at[pl.ds(off, EDGE), :],
                    staged.at[side, pl.ds(5 * EDGE, EDGE), :],
                    sems.at[side, 5],
                )
            )
        for copy in copies:
            copy.start()
        fetch.wait()
        given = links_in[...]
        own = lax.axis_index("sfc") * tiles + lax.broadcasted_iota(jnp.int32, given.shape, 1)
        offset = jnp.where(given < 0, 0, given - own).astype(F32)
        low, high = offset[:, :LANES], offset[:, tiles - LANES :]
        pad = jnp.zeros((EXTRA - 4, LANES), F32)
        for side, (a, b) in enumerate(((low, high), (high, low))):
            block = jnp.concatenate([jnp.where(even, a, b), pad], 0)
            outs[side][6 * EDGE :, :] = block.astype(BF16)
        for copy in copies:
            copy.wait()
        for side in range(2):
            outs[side][: 6 * EDGE, :] = staged[side].astype(BF16)

    @pl.when(jnp.logical_not(is_flow))
    def _():
        copies = []
        for side in range(2):
            off = pl.multiple_of(jnp.where(even == (side == 0), 0, elements - LANES), LANES)
            for v in range(4):
                copies.append(
                    pltpu.make_async_copy(
                        sound.at[v, :, pl.ds(off, LANES)],
                        staged.at[side, pl.ds(v * nodes, nodes), :],
                        sems.at[side, v],
                    )
                )
        for at, ref in enumerate((neighbours, codes)):
            copies.append(pltpu.make_async_copy(ref, faces_in.at[at], link_sems.at[at]))
        for copy in copies:
            copy.start()
        for copy in copies:
            copy.wait()
        first = lax.axis_index("sfc") * elements
        own = first + lax.broadcasted_iota(jnp.int32, (1, elements), 1)
        for face in range(6):
            link = faces_in[0, face]
            offset = jnp.where(link < 0, NO_LINK, link - own).astype(F32)
            for at, row in enumerate((offset, faces_in[1, face].astype(F32))):
                line = 4 * nodes + 6 * at + face
                low, high = row[:, :LANES], row[:, elements - LANES :]
                staged[0, line : line + 1, :] = jnp.where(even, low, high)
                staged[1, line : line + 1, :] = jnp.where(even, high, low)
        used = 4 * nodes + 12
        for side, out in enumerate(outs):
            staged[side, used:, :] = jnp.zeros((staged.shape[1] - used, LANES), F32)
            out[: 6 * EDGE, :] = staged[side].astype(BF16)
            out[6 * EDGE :, :] = jnp.zeros((out.shape[0] - 6 * EDGE, LANES), BF16)


class FlowPlan:
    def __init__(self, tiles):
        self.tiles = tiles
        self.wide = tiles + 2 * EDGE
        self.blocks = 4
        self.rows = (tiles + 4 * HW) // self.blocks
        self.span = self.rows + 2 * HW

    def at(self, b):
        return HW + b * self.rows

    def inner(self):
        return range(1, self.blocks - 1)


def columns_of(place):
    return slice(place * LANES, (place + 1) * LANES)


def rows_between(parts, low, high, columns):
    taken = []
    for start, ref in parts:
        a, b = max(low, start), min(high, start + ref.shape[0])
        if a < b:
            taken.append(ref[a - start : b - start, columns])
    return taken[0] if len(taken) == 1 else jnp.concatenate(taken, 0)


def put(high, low, at, place, value):
    h, l = split_parts(value)
    high[at : at + value.shape[0], columns_of(place)] = h
    low[at : at + value.shape[0], columns_of(place)] = l


def east_west(x):
    return pltpu.roll(x, LANES - 1, 1), pltpu.roll(x, 1, 1)


def link_matrix(plan, offset, mat):
    rows, span = plan.rows, plan.span
    lane = lax.broadcasted_iota(jnp.int32, (rows, 2 * span), 1)
    lane = jnp.where(lane >= span, lane - span, lane)
    place = HW + lax.broadcasted_iota(jnp.int32, (rows, LANES), 0) + offset.astype(jnp.int32)
    hot = [jnp.where(place[:, k : k + 1] == lane, F32(1.0), F32(0.0)) for k in range(4)]
    mat[:rows, :] = (hot[0] + hot[1] + hot[2] + hot[3]).astype(BF16)
    mat[rows : 2 * rows, :] = (hot[0] - hot[1]).astype(BF16)
    mat[2 * rows :, :] = (hot[2] - hot[3]).astype(BF16)


def gathered(plan, mat, high, low, b, columns, at_row):
    at = b * plan.rows
    both = [rows_between(x, at, at + plan.span, columns) for x in (high, low)]
    return dot(mat[at_row:, :], jnp.concatenate(both, 0))


def advance(plan, b, mat, high, low, state, v, places, new_state, new_high, new_low, new_at, split):
    rows = plan.rows
    center = [state(k) for k in range(3)]
    scaled = [(0.5 * ADVECT) * c for c in center]
    for first, last in places:
        got = gathered(plan, mat, high, low, b, slice(first * LANES, last * LANES), 0)
        for place in range(first, last):
            inner = columns_of(place - first)
            total, dy, dz = got[:rows, inner], got[rows : 2 * rows, inner], got[2 * rows :, inner]
            c = center[place] if place < 3 else state(place)
            east, west = east_west(c)
            new = (
                c
                + v * (east + west + total - 6.0 * c)
                - (scaled[0] * (east - west) + scaled[1] * dy + scaled[2] * dz)
            )
            new_state[new_at : new_at + rows, columns_of(place)] = new
            if split:
                put(new_high, new_low, new_at, place, new)


def lamb_block(plan, b, mat, high, low, state, average, average_out, packed):
    rows = plan.rows
    center = [state(k) for k in range(3)]
    got = [
        gathered(plan, mat, high, low, b, slice(0, 2 * LANES), rows),
        gathered(plan, mat, high, low, b, slice(2 * LANES, 3 * LANES), rows),
    ]
    d1, d2, d3 = [], [], []
    for k in range(3):
        east, west = east_west(center[k])
        d1.append((east - west) * 0.5)
        inner = columns_of(k % 2)
        d2.append(got[k // 2][:rows, inner] * 0.5)
        d3.append(got[k // 2][rows:, inner] * 0.5)
    vx = d2[2] - d3[1]
    vy = d3[0] - d1[2]
    vz = d1[1] - d2[0]
    lamb = (
        vy * center[2] - vz * center[1],
        vz * center[0] - vx * center[2],
        vx * center[1] - vy * center[0],
    )
    to = plan.at(b) - EDGE
    low_row, top_row = max(0, -to), min(rows, plan.tiles - to)
    own = slice(to + low_row, to + top_row)
    for i in range(3):
        packed[i, own, :] = lamb[i][low_row:top_row]
        mixed = (1.0 - RELAX) * average[i, own, :] + RELAX * center[i][low_row:top_row]
        average_out[i, own, :] = mixed
        packed[3 + i, own, :] = mixed


def element_sums(projector, packed, hits, pay, own_ref, next_ref):
    nodes = projector.shape[0]
    count, elements = own_ref.shape
    proj_high, proj_low = split_parts(projector[...])
    proj_both = jnp.concatenate([proj_high, proj_low], 0)
    for c in range(6):
        x_high, x_low = split_parts(packed[c])
        main = dot_t(proj_both, x_high)
        mapped = main[:nodes] + main[nodes:] + dot_t(proj_high, x_low)
        pay[c * nodes : (c + 1) * nodes, :] = mapped.astype(BF16)
    if count > 6 * nodes:
        pay[6 * nodes :, :] = jnp.ones((count - 6 * nodes, pay.shape[1]), BF16)
    sums = dot_t(pay[...], hits[...])
    if count > 6 * nodes:
        tail = sums[6 * nodes :]
        line = lax.broadcasted_iota(jnp.int32, tail.shape, 0)
        big = jnp.floor(tail * (1.0 / BASE))
        tail = jnp.where(line == 0, tail - BASE * big, jnp.where(line == 1, big, 0.0))
        sums = jnp.concatenate([sums[: 6 * nodes], tail], 0)
    own_ref[...] = sums[:, :elements]
    next_ref[...] = sums[:, elements:].astype(BF16)


def inner_kernel(
    flow, visc, links, target,
    inner_state, inner_high, inner_low, lcol, inner_mats, hits, high0, low0, square,
):
    plan = FlowPlan(flow.shape[1])
    tiles, rows = plan.tiles, plan.rows

    @pl.when(on_flow_row())
    def _():
        column = lax.axis_index("sfc")
        first_tile, first_element = column * tiles, column * (hits.shape[0] // 2)
        for place, f in enumerate(FIELD_ORDER):
            put(high0, low0, 0, place, flow[f])
        square[...] = jnp.zeros_like(square)
        own_tile = first_tile + lax.broadcasted_iota(jnp.int32, links.shape, 1)
        offset = jnp.where(links[...] < 0, 0, links[...] - own_tile).astype(F32)
        for part in range(tiles // LANES):
            square[:4, :] = offset[:, part * LANES : (part + 1) * LANES]
            lcol[part * LANES : (part + 1) * LANES, :] = square[...].T
        local = target[...] - first_element
        hits[...] = jnp.where(
            lax.broadcasted_iota(jnp.int32, hits.shape, 0) == local, F32(1.0), F32(0.0)
        ).astype(BF16)
        for at, b in enumerate(plan.inner()):
            own = slice(plan.at(b) - EDGE, plan.at(b) - EDGE + rows)
            link_matrix(plan, lcol[own, :], inner_mats.at[at])
            advance(
                plan, b, inner_mats.at[at], [(EDGE, high0)], [(EDGE, low0)],
                lambda place, own=own: flow[FIELD_ORDER[place], own, :],
                visc[own, :], ALL_FIELDS, inner_state, inner_high, inner_low, at * rows, True,
            )


def band_parts(plan, edge, inner):
    rows, last = plan.rows, plan.blocks - 1
    return [
        (plan.at(0), edge.at[:rows]),
        (plan.at(1), inner),
        (plan.at(last), edge.at[rows:]),
    ]


def band_state(plan, b, edge, inner):
    at = plan.at(b)
    parts = band_parts(plan, edge, inner)
    return lambda place: rows_between(parts, at, at + plan.rows, columns_of(place))


def closed(plan, parts, zero):
    return [(0, zero), *parts, (plan.wide - HW, zero)]


def mats_of(plan, b, edge_mats, inner_mats):
    if b in plan.inner():
        return inner_mats.at[b - 1]
    return edge_mats.at[0 if b == 0 else 1]


def first_kernel(
    flow, visc, mean, projector, part_a, part_b, sound, neighbours, codes,
    inner_state, inner_high, inner_low, lcol, inner_mats, hits,
    own_one, next_one, mean_one, base, grads, hot_two,
    edge_state, edge_high, edge_low, edge_mats, edge_visc,
    square, state0, high0, low0, zero, packed, pay, rows_of, facing, remote, rhs,
):
    is_flow, even = on_flow_row(), on_even_column()
    plan = FlowPlan(packed.shape[1])
    tiles, rows, span = plan.tiles, plan.rows, plan.span
    own_rows = span - EDGE

    @pl.when(is_flow)
    def _():
        def pick(at, size):
            a, b = part_a[at : at + size, :].astype(F32), part_b[at : at + size, :].astype(F32)
            return jnp.where(even, a, b), jnp.where(even, b, a)

        zero[...] = jnp.zeros_like(zero)
        for place, f in enumerate(FIELD_ORDER):
            before, after = pick(place * EDGE, EDGE)
            ends = (
                jnp.concatenate([before, flow[f, :own_rows, :]], 0),
                jnp.concatenate([flow[f, tiles - own_rows :, :], after], 0),
            )
            for side in range(2):
                state0[side, :, columns_of(place)] = ends[side]
                put(high0.at[side], low0.at[side], 0, place, ends[side])
        before, after = pick(5 * EDGE, EDGE)
        edge_visc[:rows, :] = jnp.concatenate([before[HW:], visc[: rows - EDGE + HW, :]], 0)
        edge_visc[rows:, :] = jnp.concatenate(
            [visc[tiles - (rows - EDGE + HW) :, :], after[: EDGE - HW]], 0
        )
        before, after = pick(6 * EDGE, EXTRA)
        given = []
        for side, block in enumerate((before, after)):
            square[...] = jnp.zeros_like(square)
            square[:EXTRA, :] = block
            turned = square[...].T
            given.append(
                jnp.concatenate([turned[LANES - EDGE + HW :], lcol[: rows - EDGE + HW, :]], 0)
                if side == 0
                else jnp.concatenate(
                    [lcol[tiles - (rows - EDGE + HW) :, :], turned[: EDGE - HW]], 0
                )
            )
        for side, b in enumerate((0, plan.blocks - 1)):
            link_matrix(plan, given[side], edge_mats.at[side])
            advance(
                plan, b, edge_mats.at[side],
                [(b * rows, high0.at[side])], [(b * rows, low0.at[side])],
                lambda place, side=side: state0[side, HW : HW + rows, columns_of(place)],
                edge_visc[side * rows : (side + 1) * rows, :], ALL_FIELDS,
                edge_state, edge_high, edge_low, side * rows, True,
            )
        high1 = closed(plan, band_parts(plan, edge_high, inner_high), zero)
        low1 = closed(plan, band_parts(plan, edge_low, inner_low), zero)
        for b in range(plan.blocks):
            lamb_block(
                plan, b, mats_of(plan, b, edge_mats, inner_mats), high1, low1,
                band_state(plan, b, edge_state, inner_state), mean, mean_one, packed,
            )
        element_sums(projector, packed, hits, pay, own_one, next_one)

    @pl.when(jnp.logical_not(is_flow))
    def _():
        own_one[...] = jnp.zeros_like(own_one)
        next_one[...] = jnp.zeros_like(next_one)
        nodes, elements = sound.shape[1:]
        halves = elements // LANES
        block = 4 * nodes
        for v in range(4):
            for h in range(halves):
                rows_of[h * block + v * nodes : h * block + (v + 1) * nodes, :] = sound[
                    v, :, h * LANES : (h + 1) * LANES
                ]
        a, b = part_a[:block, :].astype(F32), part_b[:block, :].astype(F32)
        before, after = jnp.where(even, a, b), jnp.where(even, b, a)
        lane = lax.broadcasted_iota(jnp.int32, (1, LANES), 1)
        beside = lane < LANES // 2
        rows_of[halves * block : (halves + 1) * block, :] = jnp.where(beside, after, before)
        rows_of[(halves + 1) * block : (halves + 2) * block, :] = jnp.zeros_like(before)
        rows_of[(halves + 2) * block : (halves + 3) * block, :] = before
        rows_of[(halves + 3) * block :, :] = after
        a = part_a[block : block + EXTRA, :].astype(F32)
        b = part_b[block : block + EXTRA, :].astype(F32)
        given = jnp.where(beside, jnp.where(even, b, a), jnp.where(even, a, b)).astype(jnp.int32)
        own_parts = [0, 1, halves + 2, halves + 3]
        first = lax.axis_index("sfc") * elements
        masks = []
        for face in range(6):
            for at, part in enumerate(own_parts):
                facing_rows(rows_of, part * block, nodes, face ^ 1, facing.at[face, at])
            link, code = neighbours[face], codes[face]
            offset, extra_code = given[face : face + 1, :], given[6 + face : 7 + face, :]
            extra = jnp.where(beside, elements + lane, lane - LANES) + offset
            near = jnp.concatenate([link - first, extra], 1)
            valid = jnp.concatenate([link, jnp.where(offset >= NO_LINK, -1, 0)], 1) >= 0
            place = jnp.where(
                near < 0, elements + LANES + near, jnp.where(near < elements, near, near + LANES)
            )
            hot = hot_columns(jnp.where(valid, place, -1), elements + 2 * LANES)
            remote_rows([facing[face, at] for at in range(4)], hot, remote, face)
            near = link - first
            place = jnp.where(near < 0, elements + LANES + near, near)
            hot_two[face] = hot_columns(jnp.where(link < 0, -1, place), elements + LANES)
            masks.append(
                (
                    face_masks(link[:, :LANES], link[:, LANES:], code[:, :LANES], code[:, LANES:]),
                    face_masks(
                        jnp.where(offset >= NO_LINK, -1, 0), jnp.full((1, LANES), -1, jnp.int32),
                        extra_code, extra_code,
                    ),
                )
            )
        for group in range(2):
            start = group * halves * block
            derivatives(rows_of, start, nodes, grads, rhs)
            add_faces(
                rows_of, start, nodes, remote, group * halves * 64, [m[group] for m in masks], rhs
            )
            for n in range(nodes):
                base[pl.ds(start + n, 8, stride=nodes), :] = (
                    node_of(rows_of, start, nodes, n) + ACOUSTIC_STEP * rhs[n]
                )


def second_block(plan, b, carried, visc, places, new_state, new_parts):
    (inner_state, inner_high, inner_low, inner_mats, edge_state, edge_high, edge_low, edge_mats,
     edge_visc, zero) = carried
    rows = plan.rows
    if b in plan.inner():
        v = visc[plan.at(b) - EDGE : plan.at(b) - EDGE + rows, :]
    else:
        v = edge_visc[:rows, :] if b == 0 else edge_visc[rows:, :]
    advance(
        plan, b, mats_of(plan, b, edge_mats, inner_mats),
        closed(plan, band_parts(plan, edge_high, inner_high), zero),
        closed(plan, band_parts(plan, edge_low, inner_low), zero),
        band_state(plan, b, edge_state, inner_state), v, places,
        new_state, *new_parts, b * rows, new_parts[0] is not None,
    )


def second_kernel(
    visc, mean, mean_one, projector,
    inner_state, inner_high, inner_low, inner_mats, hits,
    edge_state, edge_high, edge_low, edge_mats, edge_visc,
    state, mean_two, own_two, next_two,
    high, low, zero, packed, pay,
):
    plan = FlowPlan(packed.shape[1])
    rows = plan.rows
    is_flow = on_flow_row()

    @pl.when(jnp.logical_not(is_flow))
    def _():
        own_two[...] = jnp.zeros_like(own_two)
        next_two[...] = jnp.zeros_like(next_two)

    @pl.when(is_flow)
    def _():
        zero[...] = jnp.zeros_like(zero)
        carried = (
            inner_state, inner_high, inner_low, inner_mats,
            edge_state, edge_high, edge_low, edge_mats, edge_visc, zero,
        )
        for b in range(plan.blocks):
            second_block(plan, b, carried, visc, ((0, 2), (2, 3)), state, (high, low))
        for b in range(plan.blocks):
            lamb_block(
                plan, b, mats_of(plan, b, edge_mats, inner_mats),
                closed(plan, [(HW, high)], zero), closed(plan, [(HW, low)], zero),
                lambda place, b=b: state[b * rows : (b + 1) * rows, columns_of(place)],
                mean_one, mean_two, packed,
            )
        element_sums(projector, packed, hits, pay, own_two, next_two)


def output_kernel(
    flow, visc, mean, state, mean_two,
    inner_state, inner_high, inner_low, inner_mats,
    edge_state, edge_high, edge_low, edge_mats, edge_visc, after, after_border, own_one,
    flow_out, mean_out, own_one_out, passive, zero,
):
    plan = FlowPlan(flow.shape[1])
    is_flow = on_flow_row()
    own_one_out[...] = own_one[...]

    @pl.when(jnp.logical_not(is_flow))
    def _():
        flow_out[...] = flow[...]
        mean_out[...] = mean[...]

    @pl.when(is_flow)
    def _():
        zero[...] = jnp.zeros_like(zero)
        mean_out[...] = mean_two[...]
        carried = (
            inner_state, inner_high, inner_low, inner_mats,
            edge_state, edge_high, edge_low, edge_mats, edge_visc, zero,
        )
        own = slice(EDGE - HW, EDGE - HW + plan.tiles)
        for place in range(3):
            flow_out[FIELD_ORDER[place]] = state[own, columns_of(place)]
        for b in range(plan.blocks):
            second_block(plan, b, carried, visc, ((3, 5),), passive, (None, None))
        for place in (3, 4):
            flow_out[FIELD_ORDER[place]] = passive[own, columns_of(place)]


def facing_rows(rows_of, base, nodes, face, to):
    axis, level = face // 2, 3 * (face % 2)
    if axis == 0:
        to[...] = rows_of[pl.ds(base + level, 64, stride=4), :]
    elif axis == 1:
        for i in range(4):
            to[pl.ds(i, 16, stride=4), :] = rows_of[pl.ds(base + i + 4 * level, 16, stride=16), :]
    else:
        for v in range(4):
            at = base + v * nodes + 16 * level
            to[v * 16 : (v + 1) * 16, :] = rows_of[at : at + 16, :]


def hot_columns(place, size):
    key = lax.broadcasted_iota(jnp.int32, (size, place.shape[1]), 0)
    return jnp.where(key == place, F32(1.0), F32(0.0)).astype(BF16)


def node_of(rows_of, start, nodes, n):
    return rows_of[pl.ds(start + n, 8, stride=nodes), :]


def remote_rows(parts, hot, remote, face):
    high, low = split_parts(jnp.concatenate(parts, 1))
    got = dot(jnp.concatenate([high, low], 0), hot)
    got = got[:64] + got[64:]
    for h in range(got.shape[1] // LANES):
        remote[face, h * 64 : (h + 1) * 64, :] = got[:, h * LANES : (h + 1) * LANES]


def derivatives(rows_of, start, nodes, grads_out, rhs):
    matrix = lobatto_matrix()
    line = lax.broadcasted_iota(jnp.int32, (8, LANES), 0)
    is_v = [line % 4 == v for v in range(4)]
    node = [node_of(rows_of, start, nodes, n) for n in range(nodes)]
    for n in range(nodes):
        i, j, k = n % 4, n // 4 % 4, n // 16
        lines = (
            [m + 4 * j + 16 * k for m in range(4)],
            [i + 4 * m + 16 * k for m in range(4)],
            [i + 4 * j + 16 * m for m in range(4)],
        )
        grads = []
        for d, at in enumerate((i, j, k)):
            total = None
            for m in range(4):
                if abs(matrix[at, m]) > 1e-12:
                    term = F32(matrix[at, m]) * node[lines[d][m]]
                    total = term if total is None else total + term
            grads.append(total)
            grads_out[d, pl.ds(start + n, 8, stride=nodes), :] = total
        div = sum(pltpu.roll(grads[d], 8 - (1 + d), 0) for d in range(3))
        coupled = jnp.where(is_v[0], div, 0.0)
        for d in range(3):
            coupled = jnp.where(is_v[1 + d], pltpu.roll(grads[d], 1 + d, 0), coupled)
        rhs[n] = -coupled


def face_masks(link_low, link_high, code_low, code_high):
    upper = lax.broadcasted_iota(jnp.int32, (8, LANES), 0) >= 4

    def both(low, high):
        return jnp.where(
            upper, jnp.broadcast_to(high, (8, LANES)), jnp.broadcast_to(low, (8, LANES))
        )

    code = both(code_low, code_high)
    return both(link_low, link_high) >= 0, [code == t for t in range(3)]


def add_faces(rows_of, start, nodes, remote, remote_start, masks, rhs):
    for face in range(6):
        valid, is_turn = masks[face]
        planes = [remote[face, pl.ds(remote_start + p, 8, stride=16), :] for p in range(16)]
        for p, n in enumerate(face_nodes(face)):
            turned = planes[turned_position(3, p)]
            for t in range(3):
                turned = jnp.where(is_turn[t], planes[turned_position(t, p)], turned)
            jump = jnp.where(valid, turned - node_of(rows_of, start, nodes, n), 0.0)
            rhs[n] = rhs[n] + PENALTY * jump


def with_sources(total, columns, block, nodes, base, grads):
    for v in range(4):
        rows = slice(block * 4 * nodes + v * nodes, block * 4 * nodes + (v + 1) * nodes)
        added = total[(v - 1) * nodes : v * nodes, columns] if v else None
        for d in range(3):
            term = total[(3 + d) * nodes : (4 + d) * nodes, columns] * grads[d, rows, :]
            added = term if added is None else added + term
        yield v, rows, base[rows, :] - ACOUSTIC_STEP * added


def border_kernel(sums, *refs):
    *_, up, down = refs
    nodes_rows = (sums.shape[0] - EXTRA) // (LANES // HE)
    group = lax.broadcasted_iota(jnp.int32, (1, LANES), 1) // HE

    @pl.when(on_flow_row())
    def _():
        for out, tile, shift in ((up, sums.shape[1] - LANES, HE), (down, 0, 0)):
            columns = slice(tile, tile + LANES)
            total = jnp.zeros((nodes_rows, LANES), F32)
            for i in range(LANES // HE):
                x = sums[i * nodes_rows : (i + 1) * nodes_rows, columns].astype(F32)
                turn = (HE * i + shift) % LANES
                x = pltpu.roll(x, turn, 1) if turn else x
                total = jnp.where(group == i, x, total)
            out[:nodes_rows, :] = total.astype(BF16)
            x = sums[sums.shape[0] - EXTRA :, columns].astype(F32)
            x = pltpu.roll(x, shift, 1) if shift else x
            out[nodes_rows:, :] = jnp.where(group == 0, x, 0.0).astype(BF16)


def border_sums(up, down):
    lines = up.shape[0] - EXTRA
    lane = lax.broadcasted_iota(jnp.int32, (1, LANES), 1)
    parts = []
    for i in range(LANES // HE + 1):
        rows = slice(0, lines) if i < LANES // HE else slice(lines, lines + EXTRA)
        at = HE * (i % (LANES // HE))
        x = pltpu.roll(up[rows], (2 * LANES - HE - at) % LANES, 1)
        y = pltpu.roll(down[rows], (LANES - at) % LANES, 1) if at else down[rows]
        parts.append(jnp.where(lane >= LANES - HE, x, jnp.where(lane < HE, y, 0.0)))
    return jnp.concatenate(parts, 0)


def scaled_sums(total, nodes):
    count = total[6 * nodes : 6 * nodes + 1] + BASE * total[6 * nodes + 1 : 6 * nodes + 2]
    inverse = 1.0 / jnp.maximum(count, 1.0)
    return total[: 6 * nodes] * inverse, inverse


def sound_one_kernel(
    base, grads, hot_two, neighbours, codes, source_a, source_b, up_a, up_b, down_a, down_b,
    base_two, grads_two, scale_out, rows_of, facing, remote, rhs,
):
    elements = source_a.shape[1]
    halves = elements // LANES
    nodes = base_two.shape[0] // (4 * halves)
    block = 4 * nodes

    @pl.when(jnp.logical_not(on_flow_row()))
    def _():
        own, inverse = scaled_sums(source_a[...].astype(F32) + source_b[...].astype(F32), nodes)
        scale_out[...] = jnp.broadcast_to(inverse, scale_out.shape)
        extra = border_sums(
            up_a[...].astype(F32) + up_b[...].astype(F32),
            down_a[...].astype(F32) + down_b[...].astype(F32),
        )
        extra, _ = scaled_sums(extra, nodes)
        for h in range(halves + 1):
            total, columns = (own, columns_of(h)) if h < halves else (extra, columns_of(0))
            for _, rows, new in with_sources(total, columns, h, nodes, base, grads):
                rows_of[rows, :] = new
        masks = []
        for face in range(6):
            for part in range(halves + 1):
                facing_rows(rows_of, part * block, nodes, face ^ 1, facing.at[face, part])
            remote_rows(
                [facing[face, part] for part in range(halves + 1)], hot_two[face], remote, face
            )
            link, code = neighbours[face], codes[face]
            masks.append(
                face_masks(link[:, :LANES], link[:, LANES:], code[:, :LANES], code[:, LANES:])
            )
        derivatives(rows_of, 0, nodes, grads_two, rhs)
        add_faces(rows_of, 0, nodes, remote, 0, masks, rhs)
        for n in range(nodes):
            base_two[pl.ds(n, 8, stride=nodes), :] = (
                node_of(rows_of, 0, nodes, n) + ACOUSTIC_STEP * rhs[n]
            )


def sound_two_kernel(sound, base, grads, scale, source_a, source_b, out):
    nodes = sound.shape[1]
    is_flow = on_flow_row()

    @pl.when(is_flow)
    def _():
        out[...] = sound[...]

    @pl.when(jnp.logical_not(is_flow))
    def _():
        total = (source_a[...].astype(F32) + source_b[...].astype(F32)) * scale[0:1, :]
        for h in range(sound.shape[2] // LANES):
            for v, _, new in with_sources(total, columns_of(h), h, nodes, base, grads):
                out[v, :, columns_of(h)] = new


def call(kernel, outs, scratch, operands, flops=10**8, in_hbm=(), limit=VMEM_LIMIT):
    spaces = [pltpu.HBM if at in in_hbm else pltpu.VMEM for at in range(len(operands))]
    moved = sum(int(np.prod(x.shape)) * x.dtype.itemsize for x in (*operands, *outs))
    return pl.pallas_call(
        kernel,
        out_shape=tuple(outs),
        in_specs=[pl.BlockSpec(memory_space=space) for space in spaces],
        out_specs=tuple([pl.BlockSpec(memory_space=pltpu.VMEM)] * len(outs)),
        scratch_shapes=scratch,
        compiler_params=pltpu.CompilerParams(vmem_limit_bytes=limit),
        cost_estimate=pl.CostEstimate(flops=flops, bytes_accessed=moved, transcendentals=0),
    )(*operands)


def body(
    flow_fields,
    mean_velocity,
    cell_eddy_viscosity,
    tile_links,
    tile_target,
    projector,
    acoustic_state,
    element_face_neighbours,
    face_codes,
):
    groups = lax.axis_size("grp")
    count = lax.axis_size("sfc")
    flow = flow_fields[0]
    mean = mean_velocity[0]
    visc = cell_eddy_viscosity[0]
    links = tile_links[0]
    sound = acoustic_state[0]
    faces, span = element_face_neighbours.shape[1:]
    neighbours = element_face_neighbours.reshape(faces, 1, span)
    codes = face_codes.reshape(faces, 1, span)
    tiles = flow.shape[1]
    _, nodes, elements = sound.shape
    halves = elements // LANES
    block = 4 * nodes
    plan = FlowPlan(tiles)
    shape = jax.ShapeDtypeStruct
    vmem = pltpu.VMEM
    pairs_a = [p for i in range(1, count - 1, 2) for p in ((i, i + 1), (i + 1, i))]
    pairs_b = [p for i in range(0, count - 1, 2) for p in ((i, i + 1), (i + 1, i))]

    edge_rows = 6 * EDGE + EXTRA
    pack_a, pack_b = call(
        pack_kernel,
        [shape((edge_rows, LANES), BF16)] * 2,
        [
            vmem(links.shape, jnp.int32),
            vmem((2, *neighbours.shape), jnp.int32),
            vmem((2, 6 * EDGE, LANES), F32),
            pltpu.SemaphoreType.DMA((2, 6)),
            pltpu.SemaphoreType.DMA((2,)),
        ],
        [flow, visc, links, sound, neighbours, codes],
        in_hbm=(0, 1, 2, 3, 4, 5),
        limit=PACK_LIMIT,
        flops=10**10,
    )
    part_a = lax.ppermute(pack_a, "sfc", pairs_a)
    part_b = lax.ppermute(pack_b, "sfc", pairs_b)

    fields = 5 * LANES
    rows, span = plan.rows, plan.span
    inner_rows = (plan.blocks - 2) * rows
    square = vmem((LANES, LANES), F32)
    packed = vmem((6, tiles, LANES), F32)
    inner_state, inner_high, inner_low, lcol, inner_mats, hits = call(
        inner_kernel,
        [
            shape((inner_rows, fields), F32),
            shape((inner_rows, fields), BF16),
            shape((inner_rows, fields), BF16),
            shape((tiles, LANES), F32),
            shape((plan.blocks - 2, 3 * rows, 2 * span), BF16),
            shape((2 * elements, tiles), BF16),
        ],
        [vmem((tiles, fields), BF16), vmem((tiles, fields), BF16), square],
        [flow, visc, links, tile_target],
    )
    lines = 6 * nodes + EXTRA
    node_rows = vmem((nodes, 8, LANES), F32)
    (
        own_one, next_one, mean_one, base, grads, hot_two,
        edge_state, edge_high, edge_low, edge_mats, edge_visc,
    ) = call(
        first_kernel,
        [
            shape((lines, elements), F32),
            shape((lines, elements), BF16),
            shape(mean.shape, F32),
            shape(((halves + 2) * block, LANES), F32),
            shape((3, (halves + 2) * block, LANES), F32),
            shape((6, elements + LANES, elements), BF16),
            shape((2 * rows, fields), F32),
            shape((2 * rows, fields), BF16),
            shape((2 * rows, fields), BF16),
            shape((2, 3 * rows, 2 * span), BF16),
            shape((2 * rows, LANES), F32),
        ],
        [
            square,
            vmem((2, span, fields), F32),
            vmem((2, span, fields), BF16),
            vmem((2, span, fields), BF16),
            vmem((HW, fields), BF16),
            packed,
            vmem((lines, tiles), BF16),
            vmem(((halves + 4) * block, LANES), F32),
            vmem((6, 4, 64, LANES), F32),
            vmem((6, (halves + 2) * 64, LANES), F32),
            node_rows,
        ],
        [
            flow, visc, mean, projector, part_a, part_b, sound, neighbours, codes,
            inner_state, inner_high, inner_low, lcol, inner_mats, hits,
        ],
    )

    up = [(i, i + 1) for i in range(count - 1)]

    def climb(x):
        chosen = [(g * count + i, g * count + j) for g in range(groups - 1) for i, j in up]
        return lax.ppermute(x, ("grp", "sfc"), chosen)

    def combined(*xs):
        total = xs[0]
        for x in xs[1:]:
            total = total + x.astype(F32)
        return total.astype(BF16)

    got_one = climb(next_one)
    band = plan.blocks * rows
    velocity = 3 * LANES
    step_one = [inner_state, inner_high, inner_low, inner_mats]
    edges = [edge_state, edge_high, edge_low, edge_mats, edge_visc]
    state_two, mean_two, own_two, next_two = call(
        second_kernel,
        [
            shape((band, velocity), F32),
            shape(mean.shape, F32),
            shape((6 * nodes, elements), F32),
            shape((6 * nodes, elements), BF16),
        ],
        [
            vmem((band, velocity), BF16),
            vmem((band, velocity), BF16),
            vmem((HW, fields), BF16),
            packed,
            vmem((6 * nodes, tiles), BF16),
        ],
        [visc, mean, mean_one, projector, *step_one, hits, *edges],
    )
    def borders(sums, row, after=()):
        lines = 6 * nodes // (LANES // HE) + EXTRA
        up, down = call(border_kernel, [shape((lines, LANES), BF16)] * 2, [], [sums, *after])
        last = (groups - 1) * count
        return up, *[
            lax.ppermute(
                x, ("grp", "sfc"),
                [(row * count + i, last + i + step) for i in range(count) if 0 <= i + step < count],
            )
            for x, step in ((up, 1), (down, -1))
        ]

    got_two = climb(next_two)
    sum_one = combined(own_one, got_one)
    x_one = lax.ppermute(sum_one, "grp", [(0, 1), (2, 3)])
    border, up_a, down_a = borders(sum_one, 2)
    sum_two = combined(own_two, got_two)
    y_two = lax.ppermute(sum_two, "grp", [(0, 2), (1, 3)])
    flow_out, mean_out, own_one = call(
        output_kernel,
        [shape(flow.shape, F32), shape(mean.shape, F32), shape(own_one.shape, F32)],
        [vmem((band, fields), F32), vmem((HW, fields), BF16)],
        [flow, visc, mean, state_two, mean_two, *step_one, *edges, sum_two, border, own_one],
    )
    sum_one = combined(own_one, got_one, x_one)
    y_one = lax.ppermute(sum_one, "grp", [(1, 3)])
    _, up_b, down_b = borders(sum_one, 1, (up_a, down_a))
    x_two = lax.ppermute(combined(own_two, got_two, y_two), "grp", [(2, 3)])

    base, grads, scale = call(
        sound_one_kernel,
        [
            shape((halves * block, LANES), F32),
            shape((3, halves * block, LANES), F32),
            shape((8, elements), F32),
        ],
        [
            vmem(((halves + 1) * block, LANES), F32),
            vmem((6, halves + 1, 64, LANES), F32),
            vmem((6, halves * 64, LANES), F32),
            node_rows,
        ],
        [
            base, grads, hot_two, neighbours, codes, x_one, y_one,
            up_a, up_b, down_a, down_b,
        ],
        flops=10**10,
    )
    (sound_out,) = call(
        sound_two_kernel,
        [shape(sound.shape, F32)],
        [],
        [sound, base, grads, scale, x_two, y_two],
    )
    return flow_out[None], mean_out[None], sound_out[None]


def solution(mesh):
    placed = (
        P("grp", None, "sfc", None),
        P("grp", None, "sfc", None),
        P("grp", "sfc", None),
        P("grp", None, "sfc"),
        P("grp", "sfc"),
        P(),
        P("grp", None, None, "sfc"),
        P("grp", None, "sfc"),
        P("grp", None, "sfc"),
    )
    return jax.shard_map(
        body,
        mesh=mesh,
        in_specs=placed,
        out_specs=(
            P("grp", None, "sfc", None),
            P("grp", None, "sfc", None),
            P("grp", None, None, "sfc"),
        ),
        check_vma=False,
    )
```

```python
import jax
import jax.numpy as jnp
import numpy as np
from jax import lax
from jax.experimental import pallas as pl
from jax.experimental.pallas import tpu as pltpu
from jax.sharding import PartitionSpec as P

HW = 16
HE = 16

ADVECT = 0.1
RELAX = 0.1
PENALTY = 1.5
ACOUSTIC_STEP = 0.08

LANES = 128
EDGE = 3 * HW
NO_LINK = 64
FIELD_ORDER = (1, 2, 3, 0, 4)
ALL_FIELDS = ((0, 2), (2, 4), (4, 5))
BASE = 32.0
EXTRA = 16
PACK_COST, SECOND_COST, OUTPUT_COST, SOUND_COST = 10**10, 10**10, 10**9, 10**9
VMEM_LIMIT = 20 * 1024 * 1024
PACK_LIMIT = 60 * 1024 * 1024

F32 = jnp.float32
BF16 = jnp.bfloat16


def lobatto_matrix():
    points = np.array([-1.0, -1.0 / np.sqrt(5.0), 1.0 / np.sqrt(5.0), 1.0])
    weights = np.array(
        [
            1.0 / np.prod([points[col] - points[other] for other in range(4) if other != col])
            for col in range(4)
        ]
    )
    matrix = np.zeros((4, 4))
    for line in range(4):
        for col in range(4):
            if line != col:
                matrix[line, col] = weights[col] / weights[line] / (points[line] - points[col])
        matrix[line, line] = -matrix[line].sum()
    return matrix.astype(np.float32)


def face_nodes(face):
    axis, level = face // 2, 3 * (face % 2)
    nodes = []
    for second in range(4):
        for first in range(4):
            coords = [first, second]
            coords.insert(axis, level)
            nodes.append(coords[0] + 4 * coords[1] + 16 * coords[2])
    return nodes


def turned_position(turn, position):
    a, b = position % 4, position // 4
    a, b = ((a, b), (3 - b, a), (3 - a, 3 - b), (b, 3 - a))[turn]
    return a + 4 * b


def split_parts(x):
    high = x.astype(BF16)
    return high, (x - high.astype(F32)).astype(BF16)


def dot(a, b):
    return jnp.dot(a, b, preferred_element_type=F32)


def dot_t(a, b):
    return lax.dot_general(a, b, (((1,), (1,)), ((), ())), preferred_element_type=F32)


def on_flow_row():
    return lax.axis_index("grp") < lax.axis_size("grp") - 1


def on_even_column():
    return lax.rem(lax.axis_index("sfc"), 2) == 0


def pack_kernel(
    flow, visc, links, sound, neighbours, codes,
    out_a, out_b, links_in, faces_in, staged, sems, link_sems,
):
    is_flow, even = on_flow_row(), on_even_column()
    tiles = flow.shape[1]
    _, nodes, elements = sound.shape
    outs = (out_a, out_b)

    @pl.when(is_flow)
    def _():
        fetch = pltpu.make_async_copy(links, links_in, link_sems.at[0])
        fetch.start()
        copies = []
        for side in range(2):
            off = pl.multiple_of(jnp.where(even == (side == 0), 0, tiles - EDGE), 8)
            for place, f in enumerate(FIELD_ORDER):
                copies.append(
                    pltpu.make_async_copy(
                        flow.at[f, pl.ds(off, EDGE), :],
                        staged.at[side, pl.ds(place * EDGE, EDGE), :],
                        sems.at[side, place],
                    )
                )
            copies.append(
                pltpu.make_async_copy(
                    visc.at[pl.ds(off, EDGE), :],
                    staged.at[side, pl.ds(5 * EDGE, EDGE), :],
                    sems.at[side, 5],
                )
            )
        for copy in copies:
            copy.start()
        fetch.wait()
        given = links_in[...]
        own = lax.axis_index("sfc") * tiles + lax.broadcasted_iota(jnp.int32, given.shape, 1)
        offset = jnp.where(given < 0, 0, given - own).astype(F32)
        low, high = offset[:, :LANES], offset[:, tiles - LANES :]
        pad = jnp.zeros((EXTRA - 4, LANES), F32)
        for side, (a, b) in enumerate(((low, high), (high, low))):
            block = jnp.concatenate([jnp.where(even, a, b), pad], 0)
            outs[side][6 * EDGE :, :] = block.astype(BF16)
        for copy in copies:
            copy.wait()
        for side in range(2):
            outs[side][: 6 * EDGE, :] = staged[side].astype(BF16)

    @pl.when(jnp.logical_not(is_flow))
    def _():
        copies = []
        for side in range(2):
            off = pl.multiple_of(jnp.where(even == (side == 0), 0, elements - LANES), LANES)
            for v in range(4):
                copies.append(
                    pltpu.make_async_copy(
                        sound.at[v, :, pl.ds(off, LANES)],
                        staged.at[side, pl.ds(v * nodes, nodes), :],
                        sems.at[side, v],
                    )
                )
        for at, ref in enumerate((neighbours, codes)):
            copies.append(pltpu.make_async_copy(ref, faces_in.at[at], link_sems.at[at]))
        for copy in copies:
            copy.start()
        for copy in copies:
            copy.wait()
        first = lax.axis_index("sfc") * elements
        own = first + lax.broadcasted_iota(jnp.int32, (1, elements), 1)
        for face in range(6):
            link = faces_in[0, face]
            offset = jnp.where(link < 0, NO_LINK, link - own).astype(F32)
            for at, row in enumerate((offset, faces_in[1, face].astype(F32))):
                line = 4 * nodes + 6 * at + face
                low, high = row[:, :LANES], row[:, elements - LANES :]
                staged[0, line : line + 1, :] = jnp.where(even, low, high)
                staged[1, line : line + 1, :] = jnp.where(even, high, low)
        used = 4 * nodes + 12
        for side, out in enumerate(outs):
            staged[side, used:, :] = jnp.zeros((staged.shape[1] - used, LANES), F32)
            out[: 6 * EDGE, :] = staged[side].astype(BF16)
            out[6 * EDGE :, :] = jnp.zeros((out.shape[0] - 6 * EDGE, LANES), BF16)


class FlowPlan:
    def __init__(self, tiles):
        self.tiles = tiles
        self.wide = tiles + 2 * EDGE
        self.blocks = 4
        self.rows = (tiles + 4 * HW) // self.blocks
        self.span = self.rows + 2 * HW

    def at(self, b):
        return HW + b * self.rows

    def inner(self):
        return range(1, self.blocks - 1)


def columns_of(place):
    return slice(place * LANES, (place + 1) * LANES)


def rows_between(parts, low, high, columns):
    taken = []
    for start, ref in parts:
        a, b = max(low, start), min(high, start + ref.shape[0])
        if a < b:
            taken.append(ref[a - start : b - start, columns])
    return taken[0] if len(taken) == 1 else jnp.concatenate(taken, 0)


def put(high, low, at, place, value):
    h, l = split_parts(value)
    high[at : at + value.shape[0], columns_of(place)] = h
    low[at : at + value.shape[0], columns_of(place)] = l


def east_west(x):
    return pltpu.roll(x, LANES - 1, 1), pltpu.roll(x, 1, 1)


def link_matrix(plan, offset, mat):
    rows, span = plan.rows, plan.span
    lane = lax.broadcasted_iota(jnp.int32, (rows, 2 * span), 1)
    lane = jnp.where(lane >= span, lane - span, lane)
    place = HW + lax.broadcasted_iota(jnp.int32, (rows, LANES), 0) + offset.astype(jnp.int32)
    hot = [jnp.where(place[:, k : k + 1] == lane, F32(1.0), F32(0.0)) for k in range(4)]
    mat[:rows, :] = (hot[0] + hot[1] + hot[2] + hot[3]).astype(BF16)
    mat[rows : 2 * rows, :] = (hot[0] - hot[1]).astype(BF16)
    mat[2 * rows :, :] = (hot[2] - hot[3]).astype(BF16)


def gathered(plan, mat, high, low, b, columns, at_row):
    at = b * plan.rows
    both = [rows_between(x, at, at + plan.span, columns) for x in (high, low)]
    return dot(mat[at_row:, :], jnp.concatenate(both, 0))


def advance(plan, b, mat, high, low, state, v, places, new_state, new_high, new_low, new_at, split):
    rows = plan.rows
    center = [state(k) for k in range(3)]
    scaled = [(0.5 * ADVECT) * c for c in center]
    for first, last in places:
        got = gathered(plan, mat, high, low, b, slice(first * LANES, last * LANES), 0)
        for place in range(first, last):
            inner = columns_of(place - first)
            total, dy, dz = got[:rows, inner], got[rows : 2 * rows, inner], got[2 * rows :, inner]
            c = center[place] if place < 3 else state(place)
            east, west = east_west(c)
            new = (
                c
                + v * (east + west + total - 6.0 * c)
                - (scaled[0] * (east - west) + scaled[1] * dy + scaled[2] * dz)
            )
            new_state[new_at : new_at + rows, columns_of(place)] = new
            if split:
                put(new_high, new_low, new_at, place, new)


def lamb_block(plan, b, mat, high, low, state, average, average_out, packed):
    rows = plan.rows
    center = [state(k) for k in range(3)]
    got = [
        gathered(plan, mat, high, low, b, slice(0, 2 * LANES), rows),
        gathered(plan, mat, high, low, b, slice(2 * LANES, 3 * LANES), rows),
    ]
    d1, d2, d3 = [], [], []
    for k in range(3):
        east, west = east_west(center[k])
        d1.append((east - west) * 0.5)
        inner = columns_of(k % 2)
        d2.append(got[k // 2][:rows, inner] * 0.5)
        d3.append(got[k // 2][rows:, inner] * 0.5)
    vx = d2[2] - d3[1]
    vy = d3[0] - d1[2]
    vz = d1[1] - d2[0]
    lamb = (
        vy * center[2] - vz * center[1],
        vz * center[0] - vx * center[2],
        vx * center[1] - vy * center[0],
    )
    to = plan.at(b) - EDGE
    low_row, top_row = max(0, -to), min(rows, plan.tiles - to)
    own = slice(to + low_row, to + top_row)
    for i in range(3):
        packed[i, own, :] = lamb[i][low_row:top_row]
        mixed = (1.0 - RELAX) * average[i, own, :] + RELAX * center[i][low_row:top_row]
        average_out[i, own, :] = mixed
        packed[3 + i, own, :] = mixed


def element_sums(projector, packed, hits, pay, own_ref, next_ref):
    nodes = projector.shape[0]
    count, elements = own_ref.shape
    proj_high, proj_low = split_parts(projector[...])
    proj_both = jnp.concatenate([proj_high, proj_low], 0)
    for c in range(6):
        x_high, x_low = split_parts(packed[c])
        main = dot_t(proj_both, x_high)
        mapped = main[:nodes] + main[nodes:] + dot_t(proj_high, x_low)
        pay[c * nodes : (c + 1) * nodes, :] = mapped.astype(BF16)
    if count > 6 * nodes:
        pay[6 * nodes :, :] = jnp.ones((count - 6 * nodes, pay.shape[1]), BF16)
    sums = dot_t(pay[...], hits[...])
    if count > 6 * nodes:
        tail = sums[6 * nodes :]
        line = lax.broadcasted_iota(jnp.int32, tail.shape, 0)
        big = jnp.floor(tail * (1.0 / BASE))
        tail = jnp.where(line == 0, tail - BASE * big, jnp.where(line == 1, big, 0.0))
        sums = jnp.concatenate([sums[: 6 * nodes], tail], 0)
    own_ref[...] = sums[:, :elements]
    next_ref[...] = sums[:, elements:].astype(BF16)


def inner_kernel(
    flow, visc, links, target,
    inner_state, inner_high, inner_low, lcol, inner_mats, hits, high0, low0, square,
):
    plan = FlowPlan(flow.shape[1])
    tiles, rows = plan.tiles, plan.rows

    @pl.when(on_flow_row())
    def _():
        column = lax.axis_index("sfc")
        first_tile, first_element = column * tiles, column * (hits.shape[0] // 2)
        for place, f in enumerate(FIELD_ORDER):
            put(high0, low0, 0, place, flow[f])
        square[...] = jnp.zeros_like(square)
        own_tile = first_tile + lax.broadcasted_iota(jnp.int32, links.shape, 1)
        offset = jnp.where(links[...] < 0, 0, links[...] - own_tile).astype(F32)
        for part in range(tiles // LANES):
            square[:4, :] = offset[:, part * LANES : (part + 1) * LANES]
            lcol[part * LANES : (part + 1) * LANES, :] = square[...].T
        local = target[...] - first_element
        hits[...] = jnp.where(
            lax.broadcasted_iota(jnp.int32, hits.shape, 0) == local, F32(1.0), F32(0.0)
        ).astype(BF16)
        for at, b in enumerate(plan.inner()):
            own = slice(plan.at(b) - EDGE, plan.at(b) - EDGE + rows)
            link_matrix(plan, lcol[own, :], inner_mats.at[at])
            advance(
                plan, b, inner_mats.at[at], [(EDGE, high0)], [(EDGE, low0)],
                lambda place, own=own: flow[FIELD_ORDER[place], own, :],
                visc[own, :], ALL_FIELDS, inner_state, inner_high, inner_low, at * rows, True,
            )


def band_parts(plan, edge, inner):
    rows, last = plan.rows, plan.blocks - 1
    return [
        (plan.at(0), edge.at[:rows]),
        (plan.at(1), inner),
        (plan.at(last), edge.at[rows:]),
    ]


def band_state(plan, b, edge, inner):
    at = plan.at(b)
    parts = band_parts(plan, edge, inner)
    return lambda place: rows_between(parts, at, at + plan.rows, columns_of(place))


def closed(plan, parts, zero):
    return [(0, zero), *parts, (plan.wide - HW, zero)]


def mats_of(plan, b, edge_mats, inner_mats):
    if b in plan.inner():
        return inner_mats.at[b - 1]
    return edge_mats.at[0 if b == 0 else 1]


def first_kernel(
    flow, visc, mean, projector, part_a, part_b, sound, neighbours, codes,
    inner_state, inner_high, inner_low, lcol, inner_mats, hits,
    own_one, next_one, mean_one, base, grads, hot_two,
    edge_state, edge_high, edge_low, edge_mats, edge_visc,
    square, state0, high0, low0, zero, packed, pay, rows_of, facing, remote, rhs,
):
    is_flow, even = on_flow_row(), on_even_column()
    plan = FlowPlan(packed.shape[1])
    tiles, rows, span = plan.tiles, plan.rows, plan.span
    own_rows = span - EDGE

    @pl.when(is_flow)
    def _():
        def pick(at, size):
            a, b = part_a[at : at + size, :].astype(F32), part_b[at : at + size, :].astype(F32)
            return jnp.where(even, a, b), jnp.where(even, b, a)

        zero[...] = jnp.zeros_like(zero)
        for place, f in enumerate(FIELD_ORDER):
            before, after = pick(place * EDGE, EDGE)
            ends = (
                jnp.concatenate([before, flow[f, :own_rows, :]], 0),
                jnp.concatenate([flow[f, tiles - own_rows :, :], after], 0),
            )
            for side in range(2):
                state0[side, :, columns_of(place)] = ends[side]
                put(high0.at[side], low0.at[side], 0, place, ends[side])
        before, after = pick(5 * EDGE, EDGE)
        edge_visc[:rows, :] = jnp.concatenate([before[HW:], visc[: rows - EDGE + HW, :]], 0)
        edge_visc[rows:, :] = jnp.concatenate(
            [visc[tiles - (rows - EDGE + HW) :, :], after[: EDGE - HW]], 0
        )
        before, after = pick(6 * EDGE, EXTRA)
        given = []
        for side, block in enumerate((before, after)):
            square[...] = jnp.zeros_like(square)
            square[:EXTRA, :] = block
            turned = square[...].T
            given.append(
                jnp.concatenate([turned[LANES - EDGE + HW :], lcol[: rows - EDGE + HW, :]], 0)
                if side == 0
                else jnp.concatenate(
                    [lcol[tiles - (rows - EDGE + HW) :, :], turned[: EDGE - HW]], 0
                )
            )
        for side, b in enumerate((0, plan.blocks - 1)):
            link_matrix(plan, given[side], edge_mats.at[side])
            advance(
                plan, b, edge_mats.at[side],
                [(b * rows, high0.at[side])], [(b * rows, low0.at[side])],
                lambda place, side=side: state0[side, HW : HW + rows, columns_of(place)],
                edge_visc[side * rows : (side + 1) * rows, :], ALL_FIELDS,
                edge_state, edge_high, edge_low, side * rows, True,
            )
        high1 = closed(plan, band_parts(plan, edge_high, inner_high), zero)
        low1 = closed(plan, band_parts(plan, edge_low, inner_low), zero)
        for b in range(plan.blocks):
            lamb_block(
                plan, b, mats_of(plan, b, edge_mats, inner_mats), high1, low1,
                band_state(plan, b, edge_state, inner_state), mean, mean_one, packed,
            )
        element_sums(projector, packed, hits, pay, own_one, next_one)

    @pl.when(jnp.logical_not(is_flow))
    def _():
        own_one[...] = jnp.zeros_like(own_one)
        next_one[...] = jnp.zeros_like(next_one)
        nodes, elements = sound.shape[1:]
        halves = elements // LANES
        block = 4 * nodes
        for v in range(4):
            for h in range(halves):
                rows_of[h * block + v * nodes : h * block + (v + 1) * nodes, :] = sound[
                    v, :, h * LANES : (h + 1) * LANES
                ]
        a, b = part_a[:block, :].astype(F32), part_b[:block, :].astype(F32)
        before, after = jnp.where(even, a, b), jnp.where(even, b, a)
        lane = lax.broadcasted_iota(jnp.int32, (1, LANES), 1)
        beside = lane < LANES // 2
        rows_of[halves * block : (halves + 1) * block, :] = jnp.where(beside, after, before)
        rows_of[(halves + 1) * block : (halves + 2) * block, :] = jnp.zeros_like(before)
        rows_of[(halves + 2) * block : (halves + 3) * block, :] = before
        rows_of[(halves + 3) * block :, :] = after
        a = part_a[block : block + EXTRA, :].astype(F32)
        b = part_b[block : block + EXTRA, :].astype(F32)
        given = jnp.where(beside, jnp.where(even, b, a), jnp.where(even, a, b)).astype(jnp.int32)
        own_parts = [0, 1, halves + 2, halves + 3]
        first = lax.axis_index("sfc") * elements
        masks = []
        for face in range(6):
            for at, part in enumerate(own_parts):
                facing_rows(rows_of, part * block, nodes, face ^ 1, facing.at[face, at])
            link, code = neighbours[face], codes[face]
            offset, extra_code = given[face : face + 1, :], given[6 + face : 7 + face, :]
            extra = jnp.where(beside, elements + lane, lane - LANES) + offset
            near = jnp.concatenate([link - first, extra], 1)
            valid = jnp.concatenate([link, jnp.where(offset >= NO_LINK, -1, 0)], 1) >= 0
            place = jnp.where(
                near < 0, elements + LANES + near, jnp.where(near < elements, near, near + LANES)
            )
            hot = hot_columns(jnp.where(valid, place, -1), elements + 2 * LANES)
            remote_rows([facing[face, at] for at in range(4)], hot, remote, face)
            near = link - first
            place = jnp.where(near < 0, elements + LANES + near, near)
            hot_two[face] = hot_columns(jnp.where(link < 0, -1, place), elements + LANES)
            masks.append(
                (
                    face_masks(link[:, :LANES], link[:, LANES:], code[:, :LANES], code[:, LANES:]),
                    face_masks(
                        jnp.where(offset >= NO_LINK, -1, 0), jnp.full((1, LANES), -1, jnp.int32),
                        extra_code, extra_code,
                    ),
                )
            )
        for group in range(2):
            start = group * halves * block
            derivatives(rows_of, start, nodes, grads, rhs)
            add_faces(
                rows_of, start, nodes, remote, group * halves * 64, [m[group] for m in masks], rhs
            )
            for n in range(nodes):
                base[pl.ds(start + n, 8, stride=nodes), :] = (
                    node_of(rows_of, start, nodes, n) + ACOUSTIC_STEP * rhs[n]
                )


def second_block(plan, b, carried, visc, places, new_state, new_parts):
    (inner_state, inner_high, inner_low, inner_mats, edge_state, edge_high, edge_low, edge_mats,
     edge_visc, zero) = carried
    rows = plan.rows
    if b in plan.inner():
        v = visc[plan.at(b) - EDGE : plan.at(b) - EDGE + rows, :]
    else:
        v = edge_visc[:rows, :] if b == 0 else edge_visc[rows:, :]
    advance(
        plan, b, mats_of(plan, b, edge_mats, inner_mats),
        closed(plan, band_parts(plan, edge_high, inner_high), zero),
        closed(plan, band_parts(plan, edge_low, inner_low), zero),
        band_state(plan, b, edge_state, inner_state), v, places,
        new_state, *new_parts, b * rows, new_parts[0] is not None,
    )


def second_kernel(
    visc, mean, mean_one, projector,
    inner_state, inner_high, inner_low, inner_mats, hits,
    edge_state, edge_high, edge_low, edge_mats, edge_visc,
    state, mean_two, own_two, next_two,
    high, low, zero, packed, pay,
):
    plan = FlowPlan(packed.shape[1])
    rows = plan.rows
    is_flow = on_flow_row()

    @pl.when(jnp.logical_not(is_flow))
    def _():
        own_two[...] = jnp.zeros_like(own_two)
        next_two[...] = jnp.zeros_like(next_two)

    @pl.when(is_flow)
    def _():
        zero[...] = jnp.zeros_like(zero)
        carried = (
            inner_state, inner_high, inner_low, inner_mats,
            edge_state, edge_high, edge_low, edge_mats, edge_visc, zero,
        )
        for b in range(plan.blocks):
            second_block(plan, b, carried, visc, ((0, 2), (2, 3)), state, (high, low))
        for b in range(plan.blocks):
            lamb_block(
                plan, b, mats_of(plan, b, edge_mats, inner_mats),
                closed(plan, [(HW, high)], zero), closed(plan, [(HW, low)], zero),
                lambda place, b=b: state[b * rows : (b + 1) * rows, columns_of(place)],
                mean_one, mean_two, packed,
            )
        element_sums(projector, packed, hits, pay, own_two, next_two)


def output_kernel(
    flow, visc, mean, state, mean_two,
    inner_state, inner_high, inner_low, inner_mats,
    edge_state, edge_high, edge_low, edge_mats, edge_visc, after, after_up, after_down, own_one,
    flow_out, mean_out, own_one_out, passive, zero,
):
    plan = FlowPlan(flow.shape[1])
    is_flow = on_flow_row()
    own_one_out[...] = own_one[...]

    @pl.when(jnp.logical_not(is_flow))
    def _():
        flow_out[...] = flow[...]
        mean_out[...] = mean[...]

    @pl.when(is_flow)
    def _():
        zero[...] = jnp.zeros_like(zero)
        mean_out[...] = mean_two[...]
        carried = (
            inner_state, inner_high, inner_low, inner_mats,
            edge_state, edge_high, edge_low, edge_mats, edge_visc, zero,
        )
        own = slice(EDGE - HW, EDGE - HW + plan.tiles)
        for place in range(3):
            flow_out[FIELD_ORDER[place]] = state[own, columns_of(place)]
        for b in range(plan.blocks):
            second_block(plan, b, carried, visc, ((3, 5),), passive, (None, None))
        for place in (3, 4):
            flow_out[FIELD_ORDER[place]] = passive[own, columns_of(place)]


def facing_rows(rows_of, base, nodes, face, to):
    axis, level = face // 2, 3 * (face % 2)
    if axis == 0:
        to[...] = rows_of[pl.ds(base + level, 64, stride=4), :]
    elif axis == 1:
        for i in range(4):
            to[pl.ds(i, 16, stride=4), :] = rows_of[pl.ds(base + i + 4 * level, 16, stride=16), :]
    else:
        for v in range(4):
            at = base + v * nodes + 16 * level
            to[v * 16 : (v + 1) * 16, :] = rows_of[at : at + 16, :]


def hot_columns(place, size):
    key = lax.broadcasted_iota(jnp.int32, (size, place.shape[1]), 0)
    return jnp.where(key == place, F32(1.0), F32(0.0)).astype(BF16)


def node_of(rows_of, start, nodes, n):
    return rows_of[pl.ds(start + n, 8, stride=nodes), :]


def remote_rows(parts, hot, remote, face):
    high, low = split_parts(jnp.concatenate(parts, 1))
    got = dot(jnp.concatenate([high, low], 0), hot)
    got = got[:64] + got[64:]
    for h in range(got.shape[1] // LANES):
        remote[face, h * 64 : (h + 1) * 64, :] = got[:, h * LANES : (h + 1) * LANES]


def derivatives(rows_of, start, nodes, grads_out, rhs):
    matrix = lobatto_matrix()
    line = lax.broadcasted_iota(jnp.int32, (8, LANES), 0)
    is_v = [line % 4 == v for v in range(4)]
    node = [node_of(rows_of, start, nodes, n) for n in range(nodes)]
    for n in range(nodes):
        i, j, k = n % 4, n // 4 % 4, n // 16
        lines = (
            [m + 4 * j + 16 * k for m in range(4)],
            [i + 4 * m + 16 * k for m in range(4)],
            [i + 4 * j + 16 * m for m in range(4)],
        )
        grads = []
        for d, at in enumerate((i, j, k)):
            total = None
            for m in range(4):
                if abs(matrix[at, m]) > 1e-12:
                    term = F32(matrix[at, m]) * node[lines[d][m]]
                    total = term if total is None else total + term
            grads.append(total)
            grads_out[d, pl.ds(start + n, 8, stride=nodes), :] = total
        div = sum(pltpu.roll(grads[d], 8 - (1 + d), 0) for d in range(3))
        coupled = jnp.where(is_v[0], div, 0.0)
        for d in range(3):
            coupled = jnp.where(is_v[1 + d], pltpu.roll(grads[d], 1 + d, 0), coupled)
        rhs[n] = -coupled


def face_masks(link_low, link_high, code_low, code_high):
    upper = lax.broadcasted_iota(jnp.int32, (8, LANES), 0) >= 4

    def both(low, high):
        return jnp.where(
            upper, jnp.broadcast_to(high, (8, LANES)), jnp.broadcast_to(low, (8, LANES))
        )

    code = both(code_low, code_high)
    return both(link_low, link_high) >= 0, [code == t for t in range(3)]


def add_faces(rows_of, start, nodes, remote, remote_start, masks, rhs):
    for face in range(6):
        valid, is_turn = masks[face]
        planes = [remote[face, pl.ds(remote_start + p, 8, stride=16), :] for p in range(16)]
        for p, n in enumerate(face_nodes(face)):
            turned = planes[turned_position(3, p)]
            for t in range(3):
                turned = jnp.where(is_turn[t], planes[turned_position(t, p)], turned)
            jump = jnp.where(valid, turned - node_of(rows_of, start, nodes, n), 0.0)
            rhs[n] = rhs[n] + PENALTY * jump


def with_sources(total, columns, block, nodes, base, grads):
    for v in range(4):
        rows = slice(block * 4 * nodes + v * nodes, block * 4 * nodes + (v + 1) * nodes)
        added = total[(v - 1) * nodes : v * nodes, columns] if v else None
        for d in range(3):
            term = total[(3 + d) * nodes : (4 + d) * nodes, columns] * grads[d, rows, :]
            added = term if added is None else added + term
        yield v, rows, base[rows, :] - ACOUSTIC_STEP * added


def gated_sum_kernel(own, *refs):
    *others, _, out = refs

    @pl.when(on_flow_row())
    def _():
        total = own[...]
        for other in others:
            total = total + other[...].astype(F32)
        out[...] = total.astype(BF16)


def border_kernel(sums, up, down):
    nodes_rows = (sums.shape[0] - EXTRA) // (LANES // HE)
    group = lax.broadcasted_iota(jnp.int32, (1, LANES), 1) // HE
    for out, tile, shift in ((up, sums.shape[1] - LANES, HE), (down, 0, 0)):
        columns = slice(tile, tile + LANES)
        total = jnp.zeros((nodes_rows, LANES), F32)
        for i in range(LANES // HE):
            x = sums[i * nodes_rows : (i + 1) * nodes_rows, columns].astype(F32)
            turn = (HE * i + shift) % LANES
            x = pltpu.roll(x, turn, 1) if turn else x
            total = jnp.where(group == i, x, total)
        out[:nodes_rows, :] = total.astype(BF16)
        x = sums[sums.shape[0] - EXTRA :, columns].astype(F32)
        x = pltpu.roll(x, shift, 1) if shift else x
        out[nodes_rows:, :] = jnp.where(group == 0, x, 0.0).astype(BF16)


def border_sums(up, down):
    lines = up.shape[0] - EXTRA
    lane = lax.broadcasted_iota(jnp.int32, (1, LANES), 1)
    parts = []
    for i in range(LANES // HE + 1):
        rows = slice(0, lines) if i < LANES // HE else slice(lines, lines + EXTRA)
        at = HE * (i % (LANES // HE))
        x = pltpu.roll(up[rows], (2 * LANES - HE - at) % LANES, 1)
        y = pltpu.roll(down[rows], (LANES - at) % LANES, 1) if at else down[rows]
        parts.append(jnp.where(lane >= LANES - HE, x, jnp.where(lane < HE, y, 0.0)))
    return jnp.concatenate(parts, 0)


def scaled_sums(total, nodes):
    count = total[6 * nodes : 6 * nodes + 1] + BASE * total[6 * nodes + 1 : 6 * nodes + 2]
    inverse = 1.0 / jnp.maximum(count, 1.0)
    return total[: 6 * nodes] * inverse, inverse


def sound_one_kernel(
    base, grads, hot_two, neighbours, codes, source_a, source_b, up_a, down_a, up_b, down_b, after,
    base_two, grads_two, scale_out, rows_of, facing, remote, rhs,
):
    elements = source_a.shape[1]
    halves = elements // LANES
    nodes = base_two.shape[0] // (4 * halves)
    block = 4 * nodes

    @pl.when(jnp.logical_not(on_flow_row()))
    def _():
        own, inverse = scaled_sums(source_a[...].astype(F32) + source_b[...].astype(F32), nodes)
        scale_out[...] = jnp.broadcast_to(inverse, scale_out.shape)
        extra = border_sums(
            up_a[...].astype(F32) + up_b[...].astype(F32),
            down_a[...].astype(F32) + down_b[...].astype(F32),
        )
        extra, _ = scaled_sums(extra, nodes)
        for h in range(halves + 1):
            total, columns = (own, columns_of(h)) if h < halves else (extra, columns_of(0))
            for _, rows, new in with_sources(total, columns, h, nodes, base, grads):
                rows_of[rows, :] = new
        masks = []
        for face in range(6):
            for part in range(halves + 1):
                facing_rows(rows_of, part * block, nodes, face ^ 1, facing.at[face, part])
            remote_rows(
                [facing[face, part] for part in range(halves + 1)], hot_two[face], remote, face
            )
            link, code = neighbours[face], codes[face]
            masks.append(
                face_masks(link[:, :LANES], link[:, LANES:], code[:, :LANES], code[:, LANES:])
            )
        derivatives(rows_of, 0, nodes, grads_two, rhs)
        add_faces(rows_of, 0, nodes, remote, 0, masks, rhs)
        for n in range(nodes):
            base_two[pl.ds(n, 8, stride=nodes), :] = (
                node_of(rows_of, 0, nodes, n) + ACOUSTIC_STEP * rhs[n]
            )


def sound_two_kernel(sound, base, grads, scale, source_a, source_b, out):
    nodes = sound.shape[1]
    is_flow = on_flow_row()

    @pl.when(is_flow)
    def _():
        out[...] = sound[...]

    @pl.when(jnp.logical_not(is_flow))
    def _():
        total = (source_a[...].astype(F32) + source_b[...].astype(F32)) * scale[0:1, :]
        for h in range(sound.shape[2] // LANES):
            for v, _, new in with_sources(total, columns_of(h), h, nodes, base, grads):
                out[v, :, columns_of(h)] = new


def call(kernel, outs, scratch, operands, cost=None, in_hbm=(), limit=VMEM_LIMIT):
    spaces = [pltpu.HBM if at in in_hbm else pltpu.VMEM for at in range(len(operands))]
    moved = sum(int(np.prod(x.shape)) * x.dtype.itemsize for x in (*operands, *outs))
    return pl.pallas_call(
        kernel,
        out_shape=tuple(outs),
        in_specs=[pl.BlockSpec(memory_space=space) for space in spaces],
        out_specs=tuple([pl.BlockSpec(memory_space=pltpu.VMEM)] * len(outs)),
        scratch_shapes=scratch,
        compiler_params=pltpu.CompilerParams(vmem_limit_bytes=limit),
        cost_estimate=pl.CostEstimate(flops=10**8 if cost is None else cost, bytes_accessed=moved if cost is None else 0, transcendentals=0),
    )(*operands)


def body(
    flow_fields,
    mean_velocity,
    cell_eddy_viscosity,
    tile_links,
    tile_target,
    projector,
    acoustic_state,
    element_face_neighbours,
    face_codes,
):
    groups = lax.axis_size("grp")
    count = lax.axis_size("sfc")
    flow = flow_fields[0]
    mean = mean_velocity[0]
    visc = cell_eddy_viscosity[0]
    links = tile_links[0]
    sound = acoustic_state[0]
    faces, span = element_face_neighbours.shape[1:]
    neighbours = element_face_neighbours.reshape(faces, 1, span)
    codes = face_codes.reshape(faces, 1, span)
    tiles = flow.shape[1]
    _, nodes, elements = sound.shape
    halves = elements // LANES
    block = 4 * nodes
    plan = FlowPlan(tiles)
    shape = jax.ShapeDtypeStruct
    vmem = pltpu.VMEM
    pairs_a = [p for i in range(1, count - 1, 2) for p in ((i, i + 1), (i + 1, i))]
    pairs_b = [p for i in range(0, count - 1, 2) for p in ((i, i + 1), (i + 1, i))]

    edge_rows = 6 * EDGE + EXTRA
    pack_a, pack_b = call(
        pack_kernel,
        [shape((edge_rows, LANES), BF16)] * 2,
        [
            vmem(links.shape, jnp.int32),
            vmem((2, *neighbours.shape), jnp.int32),
            vmem((2, 6 * EDGE, LANES), F32),
            pltpu.SemaphoreType.DMA((2, 6)),
            pltpu.SemaphoreType.DMA((2,)),
        ],
        [flow, visc, links, sound, neighbours, codes],
        in_hbm=(0, 1, 2, 3, 4, 5),
        limit=PACK_LIMIT,
        cost=PACK_COST,
    )
    part_a = lax.ppermute(pack_a, "sfc", pairs_a)
    part_b = lax.ppermute(pack_b, "sfc", pairs_b)

    fields = 5 * LANES
    rows, span = plan.rows, plan.span
    inner_rows = (plan.blocks - 2) * rows
    square = vmem((LANES, LANES), F32)
    packed = vmem((6, tiles, LANES), F32)
    inner_state, inner_high, inner_low, lcol, inner_mats, hits = call(
        inner_kernel,
        [
            shape((inner_rows, fields), F32),
            shape((inner_rows, fields), BF16),
            shape((inner_rows, fields), BF16),
            shape((tiles, LANES), F32),
            shape((plan.blocks - 2, 3 * rows, 2 * span), BF16),
            shape((2 * elements, tiles), BF16),
        ],
        [vmem((tiles, fields), BF16), vmem((tiles, fields), BF16), square],
        [flow, visc, links, tile_target],
    )
    lines = 6 * nodes + EXTRA
    node_rows = vmem((nodes, 8, LANES), F32)
    (
        own_one, next_one, mean_one, base, grads, hot_two,
        edge_state, edge_high, edge_low, edge_mats, edge_visc,
    ) = call(
        first_kernel,
        [
            shape((lines, elements), F32),
            shape((lines, elements), BF16),
            shape(mean.shape, F32),
            shape(((halves + 2) * block, LANES), F32),
            shape((3, (halves + 2) * block, LANES), F32),
            shape((6, elements + LANES, elements), BF16),
            shape((2 * rows, fields), F32),
            shape((2 * rows, fields), BF16),
            shape((2 * rows, fields), BF16),
            shape((2, 3 * rows, 2 * span), BF16),
            shape((2 * rows, LANES), F32),
        ],
        [
            square,
            vmem((2, span, fields), F32),
            vmem((2, span, fields), BF16),
            vmem((2, span, fields), BF16),
            vmem((HW, fields), BF16),
            packed,
            vmem((lines, tiles), BF16),
            vmem(((halves + 4) * block, LANES), F32),
            vmem((6, 4, 64, LANES), F32),
            vmem((6, (halves + 2) * 64, LANES), F32),
            node_rows,
        ],
        [
            flow, visc, mean, projector, part_a, part_b, sound, neighbours, codes,
            inner_state, inner_high, inner_low, lcol, inner_mats, hits,
        ],
    )

    up = [(i, i + 1) for i in range(count - 1)]

    def climb(x):
        chosen = [(g * count + i, g * count + j) for g in range(groups - 1) for i, j in up]
        return lax.ppermute(x, ("grp", "sfc"), chosen)

    def combined(*xs):
        total = xs[0]
        for x in xs[1:]:
            total = total + x.astype(F32)
        return total.astype(BF16)

    got_one = climb(next_one)
    band = plan.blocks * rows
    velocity = 3 * LANES
    step_one = [inner_state, inner_high, inner_low, inner_mats]
    edges = [edge_state, edge_high, edge_low, edge_mats, edge_visc]
    state_two, mean_two, own_two, next_two = call(
        second_kernel,
        [
            shape((band, velocity), F32),
            shape(mean.shape, F32),
            shape((6 * nodes, elements), F32),
            shape((6 * nodes, elements), BF16),
        ],
        [
            vmem((band, velocity), BF16),
            vmem((band, velocity), BF16),
            vmem((HW, fields), BF16),
            packed,
            vmem((6 * nodes, tiles), BF16),
        ],
        [visc, mean, mean_one, projector, *step_one, hits, *edges],
        cost=SECOND_COST,
    )
    last = (groups - 1) * count
    lines_beside = 6 * nodes // (LANES // HE) + EXTRA

    def borders(sums, row):
        up_border, down_border = call(
            border_kernel, [shape((lines_beside, LANES), BF16)] * 2, [], [sums], cost=0
        )
        start = row * count
        return up_border, [
            lax.ppermute(
                up_border, ("grp", "sfc"), [(start + i, last + i + 1) for i in range(count - 1)]
            ),
            lax.ppermute(
                down_border, ("grp", "sfc"), [(start + i, last + i - 1) for i in range(1, count)]
            ),
        ]

    got_two = climb(next_two)
    sum_one_2 = combined(own_one, got_one)
    one_0_to_1 = lax.ppermute(sum_one_2, "grp", [(0, 1)])
    _, beside_2 = borders(sum_one_2, 2)
    sum_two_1 = combined(own_two, got_two)
    two_0_to_2 = lax.ppermute(sum_two_1, "grp", [(0, 2)])
    one_2_to_3 = lax.ppermute(sum_one_2, "grp", [(2, 3)])
    two_1_to_3 = lax.ppermute(sum_two_1, "grp", [(1, 3)])
    flow_out, mean_out, own_one = call(
        output_kernel,
        [shape(flow.shape, F32), shape(mean.shape, F32), shape(own_one.shape, F32)],
        [vmem((band, fields), F32), vmem((HW, fields), BF16)],
        [flow, visc, mean, state_two, mean_two, *step_one, *edges, sum_two_1, *beside_2, own_one],
        cost=OUTPUT_COST,
    )
    sum_one_1 = combined(own_one, got_one, one_0_to_1)
    one_1_to_3 = lax.ppermute(sum_one_1, "grp", [(1, 3)])
    border, beside_1 = borders(sum_one_1, 1)
    (sum_two_2,) = call(
        gated_sum_kernel,
        [shape(own_two.shape, BF16)],
        [],
        [own_two, got_two, two_0_to_2, border],
        cost=0,
    )
    two_2_to_3 = lax.ppermute(sum_two_2, "grp", [(2, 3)])

    base, grads, scale = call(
        sound_one_kernel,
        [
            shape((halves * block, LANES), F32),
            shape((3, halves * block, LANES), F32),
            shape((8, elements), F32),
        ],
        [
            vmem(((halves + 1) * block, LANES), F32),
            vmem((6, halves + 1, 64, LANES), F32),
            vmem((6, halves * 64, LANES), F32),
            node_rows,
        ],
        [
            base, grads, hot_two, neighbours, codes, one_2_to_3, one_1_to_3,
            *beside_1, *beside_2, two_1_to_3,
        ],
        cost=SOUND_COST,
    )
    (sound_out,) = call(
        sound_two_kernel,
        [shape(sound.shape, F32)],
        [],
        [sound, base, grads, scale, two_2_to_3, two_1_to_3],
    )
    return flow_out[None], mean_out[None], sound_out[None]


def solution(mesh):
    placed = (
        P("grp", None, "sfc", None),
        P("grp", None, "sfc", None),
        P("grp", "sfc", None),
        P("grp", None, "sfc"),
        P("grp", "sfc"),
        P(),
        P("grp", None, None, "sfc"),
        P("grp", None, "sfc"),
        P("grp", None, "sfc"),
    )
    return jax.shard_map(
        body,
        mesh=mesh,
        in_specs=placed,
        out_specs=(
            P("grp", None, "sfc", None),
            P("grp", None, "sfc", None),
            P("grp", None, None, "sfc"),
        ),
        check_vma=False,
    )
```

```python
import jax
import jax.numpy as jnp
import numpy as np
from jax import lax
from jax.experimental import pallas as pl
from jax.experimental.pallas import tpu as pltpu
from jax.sharding import PartitionSpec as P

HW = 16
HE = 16

ADVECT = 0.1
RELAX = 0.1
PENALTY = 1.5
ACOUSTIC_STEP = 0.08

LANES = 128
EDGE = 3 * HW
NO_LINK = 64
FIELD_ORDER = (1, 2, 3, 0, 4)
ALL_FIELDS = ((0, 2), (2, 4), (4, 5))
BASE = 32.0
EXTRA = 16
PACK_COST, SECOND_COST, OUTPUT_COST, SOUND_COST = 10**10, 10**10, 10**9, 2 * 10**9
VMEM_LIMIT = 20 * 1024 * 1024
PACK_LIMIT = 60 * 1024 * 1024

F32 = jnp.float32
BF16 = jnp.bfloat16


def lobatto_matrix():
    points = np.array([-1.0, -1.0 / np.sqrt(5.0), 1.0 / np.sqrt(5.0), 1.0])
    weights = np.array(
        [
            1.0 / np.prod([points[col] - points[other] for other in range(4) if other != col])
            for col in range(4)
        ]
    )
    matrix = np.zeros((4, 4))
    for line in range(4):
        for col in range(4):
            if line != col:
                matrix[line, col] = weights[col] / weights[line] / (points[line] - points[col])
        matrix[line, line] = -matrix[line].sum()
    return matrix.astype(np.float32)


def face_nodes(face):
    axis, level = face // 2, 3 * (face % 2)
    nodes = []
    for second in range(4):
        for first in range(4):
            coords = [first, second]
            coords.insert(axis, level)
            nodes.append(coords[0] + 4 * coords[1] + 16 * coords[2])
    return nodes


def turned_position(turn, position):
    a, b = position % 4, position // 4
    a, b = ((a, b), (3 - b, a), (3 - a, 3 - b), (b, 3 - a))[turn]
    return a + 4 * b


def split_parts(x):
    high = x.astype(BF16)
    return high, (x - high.astype(F32)).astype(BF16)


def dot(a, b):
    return jnp.dot(a, b, preferred_element_type=F32)


def dot_t(a, b):
    return lax.dot_general(a, b, (((1,), (1,)), ((), ())), preferred_element_type=F32)


def on_flow_row():
    return lax.axis_index("grp") < lax.axis_size("grp") - 1


def on_even_column():
    return lax.rem(lax.axis_index("sfc"), 2) == 0


def pack_kernel(
    flow, visc, links, sound, neighbours, codes,
    out_a, out_b, links_in, faces_in, staged, sems, link_sems,
):
    is_flow, even = on_flow_row(), on_even_column()
    tiles = flow.shape[1]
    _, nodes, elements = sound.shape
    outs = (out_a, out_b)

    @pl.when(is_flow)
    def _():
        fetch = pltpu.make_async_copy(links, links_in, link_sems.at[0])
        fetch.start()
        copies = []
        for side in range(2):
            off = pl.multiple_of(jnp.where(even == (side == 0), 0, tiles - EDGE), 8)
            for place, f in enumerate(FIELD_ORDER):
                copies.append(
                    pltpu.make_async_copy(
                        flow.at[f, pl.ds(off, EDGE), :],
                        staged.at[side, pl.ds(place * EDGE, EDGE), :],
                        sems.at[side, place],
                    )
                )
            copies.append(
                pltpu.make_async_copy(
                    visc.at[pl.ds(off, EDGE), :],
                    staged.at[side, pl.ds(5 * EDGE, EDGE), :],
                    sems.at[side, 5],
                )
            )
        for copy in copies:
            copy.start()
        fetch.wait()
        given = links_in[...]
        own = lax.axis_index("sfc") * tiles + lax.broadcasted_iota(jnp.int32, given.shape, 1)
        offset = jnp.where(given < 0, 0, given - own).astype(F32)
        low, high = offset[:, :LANES], offset[:, tiles - LANES :]
        pad = jnp.zeros((EXTRA - 4, LANES), F32)
        for side, (a, b) in enumerate(((low, high), (high, low))):
            block = jnp.concatenate([jnp.where(even, a, b), pad], 0)
            outs[side][6 * EDGE :, :] = block.astype(BF16)
        for copy in copies:
            copy.wait()
        for side in range(2):
            outs[side][: 6 * EDGE, :] = staged[side].astype(BF16)

    @pl.when(jnp.logical_not(is_flow))
    def _():
        copies = []
        for side in range(2):
            off = pl.multiple_of(jnp.where(even == (side == 0), 0, elements - LANES), LANES)
            for v in range(4):
                copies.append(
                    pltpu.make_async_copy(
                        sound.at[v, :, pl.ds(off, LANES)],
                        staged.at[side, pl.ds(v * nodes, nodes), :],
                        sems.at[side, v],
                    )
                )
        for at, ref in enumerate((neighbours, codes)):
            copies.append(pltpu.make_async_copy(ref, faces_in.at[at], link_sems.at[at]))
        for copy in copies:
            copy.start()
        for copy in copies:
            copy.wait()
        first = lax.axis_index("sfc") * elements
        own = first + lax.broadcasted_iota(jnp.int32, (1, elements), 1)
        for face in range(6):
            link = faces_in[0, face]
            offset = jnp.where(link < 0, NO_LINK, link - own).astype(F32)
            for at, row in enumerate((offset, faces_in[1, face].astype(F32))):
                line = 4 * nodes + 6 * at + face
                low, high = row[:, :LANES], row[:, elements - LANES :]
                staged[0, line : line + 1, :] = jnp.where(even, low, high)
                staged[1, line : line + 1, :] = jnp.where(even, high, low)
        used = 4 * nodes + 12
        for side, out in enumerate(outs):
            staged[side, used:, :] = jnp.zeros((staged.shape[1] - used, LANES), F32)
            out[: 6 * EDGE, :] = staged[side].astype(BF16)
            out[6 * EDGE :, :] = jnp.zeros((out.shape[0] - 6 * EDGE, LANES), BF16)


class FlowPlan:
    def __init__(self, tiles):
        self.tiles = tiles
        self.wide = tiles + 2 * EDGE
        self.blocks = 4
        self.rows = (tiles + 4 * HW) // self.blocks
        self.span = self.rows + 2 * HW

    def at(self, b):
        return HW + b * self.rows

    def inner(self):
        return range(1, self.blocks - 1)


def columns_of(place):
    return slice(place * LANES, (place + 1) * LANES)


def rows_between(parts, low, high, columns):
    taken = []
    for start, ref in parts:
        a, b = max(low, start), min(high, start + ref.shape[0])
        if a < b:
            taken.append(ref[a - start : b - start, columns])
    return taken[0] if len(taken) == 1 else jnp.concatenate(taken, 0)


def put(high, low, at, place, value):
    h, l = split_parts(value)
    high[at : at + value.shape[0], columns_of(place)] = h
    low[at : at + value.shape[0], columns_of(place)] = l


def east_west(x):
    return pltpu.roll(x, LANES - 1, 1), pltpu.roll(x, 1, 1)


def link_matrix(plan, offset, mat):
    rows, span = plan.rows, plan.span
    lane = lax.broadcasted_iota(jnp.int32, (rows, 2 * span), 1)
    lane = jnp.where(lane >= span, lane - span, lane)
    place = HW + lax.broadcasted_iota(jnp.int32, (rows, LANES), 0) + offset.astype(jnp.int32)
    hot = [jnp.where(place[:, k : k + 1] == lane, F32(1.0), F32(0.0)) for k in range(4)]
    mat[:rows, :] = (hot[0] + hot[1] + hot[2] + hot[3]).astype(BF16)
    mat[rows : 2 * rows, :] = (hot[0] - hot[1]).astype(BF16)
    mat[2 * rows :, :] = (hot[2] - hot[3]).astype(BF16)


def gathered(plan, mat, high, low, b, columns, at_row):
    at = b * plan.rows
    both = [rows_between(x, at, at + plan.span, columns) for x in (high, low)]
    return dot(mat[at_row:, :], jnp.concatenate(both, 0))


def advance(plan, b, mat, high, low, state, v, places, new_state, new_high, new_low, new_at, split):
    rows = plan.rows
    center = [state(k) for k in range(3)]
    scaled = [(0.5 * ADVECT) * c for c in center]
    for first, last in places:
        got = gathered(plan, mat, high, low, b, slice(first * LANES, last * LANES), 0)
        for place in range(first, last):
            inner = columns_of(place - first)
            total, dy, dz = got[:rows, inner], got[rows : 2 * rows, inner], got[2 * rows :, inner]
            c = center[place] if place < 3 else state(place)
            east, west = east_west(c)
            new = (
                c
                + v * (east + west + total - 6.0 * c)
                - (scaled[0] * (east - west) + scaled[1] * dy + scaled[2] * dz)
            )
            new_state[new_at : new_at + rows, columns_of(place)] = new
            if split:
                put(new_high, new_low, new_at, place, new)


def lamb_block(plan, b, mat, high, low, state, average, average_out, packed):
    rows = plan.rows
    center = [state(k) for k in range(3)]
    got = [
        gathered(plan, mat, high, low, b, slice(0, 2 * LANES), rows),
        gathered(plan, mat, high, low, b, slice(2 * LANES, 3 * LANES), rows),
    ]
    d1, d2, d3 = [], [], []
    for k in range(3):
        east, west = east_west(center[k])
        d1.append((east - west) * 0.5)
        inner = columns_of(k % 2)
        d2.append(got[k // 2][:rows, inner] * 0.5)
        d3.append(got[k // 2][rows:, inner] * 0.5)
    vx = d2[2] - d3[1]
    vy = d3[0] - d1[2]
    vz = d1[1] - d2[0]
    lamb = (
        vy * center[2] - vz * center[1],
        vz * center[0] - vx * center[2],
        vx * center[1] - vy * center[0],
    )
    to = plan.at(b) - EDGE
    low_row, top_row = max(0, -to), min(rows, plan.tiles - to)
    own = slice(to + low_row, to + top_row)
    for i in range(3):
        packed[i, own, :] = lamb[i][low_row:top_row]
        mixed = (1.0 - RELAX) * average[i, own, :] + RELAX * center[i][low_row:top_row]
        average_out[i, own, :] = mixed
        packed[3 + i, own, :] = mixed


def element_sums(projector, packed, hits, pay, own_ref, next_ref):
    nodes = projector.shape[0]
    count, elements = own_ref.shape
    proj_high, proj_low = split_parts(projector[...])
    proj_both = jnp.concatenate([proj_high, proj_low], 0)
    for c in range(6):
        x_high, x_low = split_parts(packed[c])
        main = dot_t(proj_both, x_high)
        mapped = main[:nodes] + main[nodes:] + dot_t(proj_high, x_low)
        pay[c * nodes : (c + 1) * nodes, :] = mapped.astype(BF16)
    if count > 6 * nodes:
        pay[6 * nodes :, :] = jnp.ones((count - 6 * nodes, pay.shape[1]), BF16)
    sums = dot_t(pay[...], hits[...])
    if count > 6 * nodes:
        tail = sums[6 * nodes :]
        line = lax.broadcasted_iota(jnp.int32, tail.shape, 0)
        big = jnp.floor(tail * (1.0 / BASE))
        tail = jnp.where(line == 0, tail - BASE * big, jnp.where(line == 1, big, 0.0))
        sums = jnp.concatenate([sums[: 6 * nodes], tail], 0)
    own_ref[...] = sums[:, :elements]
    next_ref[...] = sums[:, elements:].astype(BF16)


def inner_kernel(
    flow, visc, links, target,
    inner_state, inner_high, inner_low, lcol, inner_mats, hits, high0, low0, square,
):
    plan = FlowPlan(flow.shape[1])
    tiles, rows = plan.tiles, plan.rows

    @pl.when(on_flow_row())
    def _():
        column = lax.axis_index("sfc")
        first_tile, first_element = column * tiles, column * (hits.shape[0] // 2)
        for place, f in enumerate(FIELD_ORDER):
            put(high0, low0, 0, place, flow[f])
        square[...] = jnp.zeros_like(square)
        own_tile = first_tile + lax.broadcasted_iota(jnp.int32, links.shape, 1)
        offset = jnp.where(links[...] < 0, 0, links[...] - own_tile).astype(F32)
        for part in range(tiles // LANES):
            square[:4, :] = offset[:, part * LANES : (part + 1) * LANES]
            lcol[part * LANES : (part + 1) * LANES, :] = square[...].T
        local = target[...] - first_element
        hits[...] = jnp.where(
            lax.broadcasted_iota(jnp.int32, hits.shape, 0) == local, F32(1.0), F32(0.0)
        ).astype(BF16)
        for at, b in enumerate(plan.inner()):
            own = slice(plan.at(b) - EDGE, plan.at(b) - EDGE + rows)
            link_matrix(plan, lcol[own, :], inner_mats.at[at])
            advance(
                plan, b, inner_mats.at[at], [(EDGE, high0)], [(EDGE, low0)],
                lambda place, own=own: flow[FIELD_ORDER[place], own, :],
                visc[own, :], ALL_FIELDS, inner_state, inner_high, inner_low, at * rows, True,
            )


def band_parts(plan, edge, inner):
    rows, last = plan.rows, plan.blocks - 1
    return [
        (plan.at(0), edge.at[:rows]),
        (plan.at(1), inner),
        (plan.at(last), edge.at[rows:]),
    ]


def band_state(plan, b, edge, inner):
    at = plan.at(b)
    parts = band_parts(plan, edge, inner)
    return lambda place: rows_between(parts, at, at + plan.rows, columns_of(place))


def closed(plan, parts, zero):
    return [(0, zero), *parts, (plan.wide - HW, zero)]


def mats_of(plan, b, edge_mats, inner_mats):
    if b in plan.inner():
        return inner_mats.at[b - 1]
    return edge_mats.at[0 if b == 0 else 1]


def first_kernel(
    flow, visc, mean, projector, part_a, part_b, sound, neighbours, codes,
    inner_state, inner_high, inner_low, lcol, inner_mats, hits,
    own_one, next_one, mean_one, base, grads,
    edge_state, edge_high, edge_low, edge_mats, edge_visc,
    square, state0, high0, low0, zero, packed, pay, rows_of, facing, remote, rhs,
):
    is_flow, even = on_flow_row(), on_even_column()
    plan = FlowPlan(packed.shape[1])
    tiles, rows, span = plan.tiles, plan.rows, plan.span
    own_rows = span - EDGE

    @pl.when(is_flow)
    def _():
        def pick(at, size):
            a, b = part_a[at : at + size, :].astype(F32), part_b[at : at + size, :].astype(F32)
            return jnp.where(even, a, b), jnp.where(even, b, a)

        zero[...] = jnp.zeros_like(zero)
        for place, f in enumerate(FIELD_ORDER):
            before, after = pick(place * EDGE, EDGE)
            ends = (
                jnp.concatenate([before, flow[f, :own_rows, :]], 0),
                jnp.concatenate([flow[f, tiles - own_rows :, :], after], 0),
            )
            for side in range(2):
                state0[side, :, columns_of(place)] = ends[side]
                put(high0.at[side], low0.at[side], 0, place, ends[side])
        before, after = pick(5 * EDGE, EDGE)
        edge_visc[:rows, :] = jnp.concatenate([before[HW:], visc[: rows - EDGE + HW, :]], 0)
        edge_visc[rows:, :] = jnp.concatenate(
            [visc[tiles - (rows - EDGE + HW) :, :], after[: EDGE - HW]], 0
        )
        before, after = pick(6 * EDGE, EXTRA)
        given = []
        for side, block in enumerate((before, after)):
            square[...] = jnp.zeros_like(square)
            square[:EXTRA, :] = block
            turned = square[...].T
            given.append(
                jnp.concatenate([turned[LANES - EDGE + HW :], lcol[: rows - EDGE + HW, :]], 0)
                if side == 0
                else jnp.concatenate(
                    [lcol[tiles - (rows - EDGE + HW) :, :], turned[: EDGE - HW]], 0
                )
            )
        for side, b in enumerate((0, plan.blocks - 1)):
            link_matrix(plan, given[side], edge_mats.at[side])
            advance(
                plan, b, edge_mats.at[side],
                [(b * rows, high0.at[side])], [(b * rows, low0.at[side])],
                lambda place, side=side: state0[side, HW : HW + rows, columns_of(place)],
                edge_visc[side * rows : (side + 1) * rows, :], ALL_FIELDS,
                edge_state, edge_high, edge_low, side * rows, True,
            )
        high1 = closed(plan, band_parts(plan, edge_high, inner_high), zero)
        low1 = closed(plan, band_parts(plan, edge_low, inner_low), zero)
        for b in range(plan.blocks):
            lamb_block(
                plan, b, mats_of(plan, b, edge_mats, inner_mats), high1, low1,
                band_state(plan, b, edge_state, inner_state), mean, mean_one, packed,
            )
        element_sums(projector, packed, hits, pay, own_one, next_one)

    @pl.when(jnp.logical_not(is_flow))
    def _():
        own_one[...] = jnp.zeros_like(own_one)
        next_one[...] = jnp.zeros_like(next_one)
        nodes, elements = sound.shape[1:]
        halves = elements // LANES
        block = 4 * nodes
        for v in range(4):
            for h in range(halves):
                rows_of[h * block + v * nodes : h * block + (v + 1) * nodes, :] = sound[
                    v, :, h * LANES : (h + 1) * LANES
                ]
        a, b = part_a[:block, :].astype(F32), part_b[:block, :].astype(F32)
        before, after = jnp.where(even, a, b), jnp.where(even, b, a)
        lane = lax.broadcasted_iota(jnp.int32, (1, LANES), 1)
        beside = lane < LANES // 2
        rows_of[halves * block : (halves + 1) * block, :] = jnp.where(beside, after, before)
        rows_of[(halves + 1) * block : (halves + 2) * block, :] = jnp.zeros_like(before)
        rows_of[(halves + 2) * block : (halves + 3) * block, :] = before
        rows_of[(halves + 3) * block :, :] = after
        a = part_a[block : block + EXTRA, :].astype(F32)
        b = part_b[block : block + EXTRA, :].astype(F32)
        given = jnp.where(beside, jnp.where(even, b, a), jnp.where(even, a, b)).astype(jnp.int32)
        own_parts = [0, 1, halves + 2, halves + 3]
        first = lax.axis_index("sfc") * elements
        masks = []
        for face in range(6):
            for at, part in enumerate(own_parts):
                facing_rows(rows_of, part * block, nodes, face ^ 1, facing.at[face, at])
            link, code = neighbours[face], codes[face]
            offset, extra_code = given[face : face + 1, :], given[6 + face : 7 + face, :]
            extra = jnp.where(beside, elements + lane, lane - LANES) + offset
            near = jnp.concatenate([link - first, extra], 1)
            valid = jnp.concatenate([link, jnp.where(offset >= NO_LINK, -1, 0)], 1) >= 0
            place = jnp.where(
                near < 0, elements + LANES + near, jnp.where(near < elements, near, near + LANES)
            )
            hot = hot_columns(jnp.where(valid, place, -1), elements + 2 * LANES)
            remote_rows([facing[face, at] for at in range(4)], hot, remote, face)
            masks.append(
                (
                    face_masks(link[:, :LANES], link[:, LANES:], code[:, :LANES], code[:, LANES:]),
                    face_masks(
                        jnp.where(offset >= NO_LINK, -1, 0), jnp.full((1, LANES), -1, jnp.int32),
                        extra_code, extra_code,
                    ),
                )
            )
        for group in range(2):
            start = group * halves * block
            derivatives(rows_of, start, nodes, grads, rhs)
            add_faces(
                rows_of, start, nodes, remote, group * halves * 64, [m[group] for m in masks], rhs
            )
            for n in range(nodes):
                base[pl.ds(start + n, 8, stride=nodes), :] = (
                    node_of(rows_of, start, nodes, n) + ACOUSTIC_STEP * rhs[n]
                )


def second_block(plan, b, carried, visc, places, new_state, new_parts):
    (inner_state, inner_high, inner_low, inner_mats, edge_state, edge_high, edge_low, edge_mats,
     edge_visc, zero) = carried
    rows = plan.rows
    if b in plan.inner():
        v = visc[plan.at(b) - EDGE : plan.at(b) - EDGE + rows, :]
    else:
        v = edge_visc[:rows, :] if b == 0 else edge_visc[rows:, :]
    advance(
        plan, b, mats_of(plan, b, edge_mats, inner_mats),
        closed(plan, band_parts(plan, edge_high, inner_high), zero),
        closed(plan, band_parts(plan, edge_low, inner_low), zero),
        band_state(plan, b, edge_state, inner_state), v, places,
        new_state, *new_parts, b * rows, new_parts[0] is not None,
    )


def second_kernel(
    visc, mean, mean_one, projector,
    inner_state, inner_high, inner_low, inner_mats, hits,
    edge_state, edge_high, edge_low, edge_mats, edge_visc,
    state, mean_two, own_two, next_two,
    high, low, zero, packed, pay,
):
    plan = FlowPlan(packed.shape[1])
    rows = plan.rows
    is_flow = on_flow_row()

    @pl.when(jnp.logical_not(is_flow))
    def _():
        own_two[...] = jnp.zeros_like(own_two)
        next_two[...] = jnp.zeros_like(next_two)

    @pl.when(is_flow)
    def _():
        zero[...] = jnp.zeros_like(zero)
        carried = (
            inner_state, inner_high, inner_low, inner_mats,
            edge_state, edge_high, edge_low, edge_mats, edge_visc, zero,
        )
        for b in range(plan.blocks):
            second_block(plan, b, carried, visc, ((0, 2), (2, 3)), state, (high, low))
        for b in range(plan.blocks):
            lamb_block(
                plan, b, mats_of(plan, b, edge_mats, inner_mats),
                closed(plan, [(HW, high)], zero), closed(plan, [(HW, low)], zero),
                lambda place, b=b: state[b * rows : (b + 1) * rows, columns_of(place)],
                mean_one, mean_two, packed,
            )
        element_sums(projector, packed, hits, pay, own_two, next_two)


def output_kernel(
    flow, visc, mean, state, mean_two,
    inner_state, inner_high, inner_low, inner_mats,
    edge_state, edge_high, edge_low, edge_mats, edge_visc, after, after_up, after_down, own_one,
    flow_out, mean_out, own_one_out, passive, zero,
):
    plan = FlowPlan(flow.shape[1])
    is_flow = on_flow_row()
    own_one_out[...] = own_one[...]

    @pl.when(jnp.logical_not(is_flow))
    def _():
        flow_out[...] = flow[...]
        mean_out[...] = mean[...]

    @pl.when(is_flow)
    def _():
        zero[...] = jnp.zeros_like(zero)
        mean_out[...] = mean_two[...]
        carried = (
            inner_state, inner_high, inner_low, inner_mats,
            edge_state, edge_high, edge_low, edge_mats, edge_visc, zero,
        )
        own = slice(EDGE - HW, EDGE - HW + plan.tiles)
        for place in range(3):
            flow_out[FIELD_ORDER[place]] = state[own, columns_of(place)]
        for b in range(plan.blocks):
            second_block(plan, b, carried, visc, ((3, 5),), passive, (None, None))
        for place in (3, 4):
            flow_out[FIELD_ORDER[place]] = passive[own, columns_of(place)]


def facing_rows(rows_of, base, nodes, face, to):
    axis, level = face // 2, 3 * (face % 2)
    if axis == 0:
        to[...] = rows_of[pl.ds(base + level, 64, stride=4), :]
    elif axis == 1:
        for i in range(4):
            to[pl.ds(i, 16, stride=4), :] = rows_of[pl.ds(base + i + 4 * level, 16, stride=16), :]
    else:
        for v in range(4):
            at = base + v * nodes + 16 * level
            to[v * 16 : (v + 1) * 16, :] = rows_of[at : at + 16, :]


def hot_columns(place, size):
    key = lax.broadcasted_iota(jnp.int32, (size, place.shape[1]), 0)
    return jnp.where(key == place, F32(1.0), F32(0.0)).astype(BF16)


def node_of(rows_of, start, nodes, n):
    return rows_of[pl.ds(start + n, 8, stride=nodes), :]


def taken(x, at):
    return jnp.take_along_axis(x, at, axis=1, mode="promise_in_bounds")


def remote_rows(parts, hot, remote, face):
    high, low = split_parts(jnp.concatenate(parts, 1))
    got = dot(jnp.concatenate([high, low], 0), hot)
    got = got[:64] + got[64:]
    for h in range(got.shape[1] // LANES):
        remote[face, h * 64 : (h + 1) * 64, :] = got[:, h * LANES : (h + 1) * LANES]


def derivatives(rows_of, start, nodes, grads_out, rhs):
    matrix = lobatto_matrix()
    line = lax.broadcasted_iota(jnp.int32, (8, LANES), 0)
    is_v = [line % 4 == v for v in range(4)]
    node = [node_of(rows_of, start, nodes, n) for n in range(nodes)]
    for n in range(nodes):
        i, j, k = n % 4, n // 4 % 4, n // 16
        lines = (
            [m + 4 * j + 16 * k for m in range(4)],
            [i + 4 * m + 16 * k for m in range(4)],
            [i + 4 * j + 16 * m for m in range(4)],
        )
        grads = []
        for d, at in enumerate((i, j, k)):
            total = None
            for m in range(4):
                if abs(matrix[at, m]) > 1e-12:
                    term = F32(matrix[at, m]) * node[lines[d][m]]
                    total = term if total is None else total + term
            grads.append(total)
            grads_out[d, pl.ds(start + n, 8, stride=nodes), :] = total
        div = sum(pltpu.roll(grads[d], 8 - (1 + d), 0) for d in range(3))
        coupled = jnp.where(is_v[0], div, 0.0)
        for d in range(3):
            coupled = jnp.where(is_v[1 + d], pltpu.roll(grads[d], 1 + d, 0), coupled)
        rhs[n] = -coupled


def face_masks(link_low, link_high, code_low, code_high):
    upper = lax.broadcasted_iota(jnp.int32, (8, LANES), 0) >= 4

    def both(low, high):
        return jnp.where(
            upper, jnp.broadcast_to(high, (8, LANES)), jnp.broadcast_to(low, (8, LANES))
        )

    code = both(code_low, code_high)
    return both(link_low, link_high) >= 0, [code == t for t in range(3)]


def add_faces(rows_of, start, nodes, remote, remote_start, masks, rhs):
    for face in range(6):
        valid, is_turn = masks[face]
        planes = [remote[face, pl.ds(remote_start + p, 8, stride=16), :] for p in range(16)]
        for p, n in enumerate(face_nodes(face)):
            turned = planes[turned_position(3, p)]
            for t in range(3):
                turned = jnp.where(is_turn[t], planes[turned_position(t, p)], turned)
            jump = jnp.where(valid, turned - node_of(rows_of, start, nodes, n), 0.0)
            rhs[n] = rhs[n] + PENALTY * jump


def with_sources(total, columns, block, nodes, base, grads):
    for v in range(4):
        rows = slice(block * 4 * nodes + v * nodes, block * 4 * nodes + (v + 1) * nodes)
        added = total[(v - 1) * nodes : v * nodes, columns] if v else None
        for d in range(3):
            term = total[(3 + d) * nodes : (4 + d) * nodes, columns] * grads[d, rows, :]
            added = term if added is None else added + term
        yield v, rows, base[rows, :] - ACOUSTIC_STEP * added


def gated_sum_kernel(own, *refs):
    *others, _, out = refs

    @pl.when(on_flow_row())
    def _():
        total = own[...]
        for other in others:
            total = total + other[...].astype(F32)
        out[...] = total.astype(BF16)


def border_kernel(sums, up, down):
    nodes_rows = (sums.shape[0] - EXTRA) // (LANES // HE)
    group = lax.broadcasted_iota(jnp.int32, (1, LANES), 1) // HE
    for out, tile, shift in ((up, sums.shape[1] - LANES, HE), (down, 0, 0)):
        columns = slice(tile, tile + LANES)
        total = jnp.zeros((nodes_rows, LANES), F32)
        for i in range(LANES // HE):
            x = sums[i * nodes_rows : (i + 1) * nodes_rows, columns].astype(F32)
            turn = (HE * i + shift) % LANES
            x = pltpu.roll(x, turn, 1) if turn else x
            total = jnp.where(group == i, x, total)
        out[:nodes_rows, :] = total.astype(BF16)
        x = sums[sums.shape[0] - EXTRA :, columns].astype(F32)
        x = pltpu.roll(x, shift, 1) if shift else x
        out[nodes_rows:, :] = jnp.where(group == 0, x, 0.0).astype(BF16)


def border_sums(up, down):
    lines = up.shape[0] - EXTRA
    lane = lax.broadcasted_iota(jnp.int32, (1, LANES), 1)
    parts = []
    for i in range(LANES // HE + 1):
        rows = slice(0, lines) if i < LANES // HE else slice(lines, lines + EXTRA)
        at = HE * (i % (LANES // HE))
        x = pltpu.roll(up[rows], (2 * LANES - HE - at) % LANES, 1)
        y = pltpu.roll(down[rows], (LANES - at) % LANES, 1) if at else down[rows]
        parts.append(jnp.where(lane >= LANES - HE, x, jnp.where(lane < HE, y, 0.0)))
    return jnp.concatenate(parts, 0)


def scaled_sums(total, nodes):
    count = total[6 * nodes : 6 * nodes + 1] + BASE * total[6 * nodes + 1 : 6 * nodes + 2]
    inverse = 1.0 / jnp.maximum(count, 1.0)
    return total[: 6 * nodes] * inverse, inverse


def sound_one_kernel(
    base, grads, neighbours, codes, source_a, source_b, up_a, down_a, up_b, down_b, after,
    base_two, grads_two, scale_out, rows_of, facing, remote, rhs,
):
    elements = source_a.shape[1]
    halves = elements // LANES
    nodes = base_two.shape[0] // (4 * halves)
    block = 4 * nodes

    @pl.when(jnp.logical_not(on_flow_row()))
    def _():
        own, inverse = scaled_sums(source_a[...].astype(F32) + source_b[...].astype(F32), nodes)
        scale_out[...] = jnp.broadcast_to(inverse, scale_out.shape)
        extra = border_sums(
            up_a[...].astype(F32) + up_b[...].astype(F32),
            down_a[...].astype(F32) + down_b[...].astype(F32),
        )
        extra, _ = scaled_sums(extra, nodes)
        for h in range(halves + 1):
            total, columns = (own, columns_of(h)) if h < halves else (extra, columns_of(0))
            for _, rows, new in with_sources(total, columns, h, nodes, base, grads):
                rows_of[rows, :] = new
        masks = []
        for face in range(6):
            for part in range(halves + 1):
                facing_rows(rows_of, part * block, nodes, face ^ 1, facing.at[face, part])
            link, code = neighbours[face], codes[face]
            near = link - lax.axis_index("sfc") * elements
            for h in range(halves):
                here = near[:, columns_of(h)]
                at = jnp.broadcast_to(here & (LANES - 1), (64, LANES))
                got = taken(facing[face, halves], at)
                for part in range(halves):
                    inside = (here >= part * LANES) & (here < (part + 1) * LANES)
                    got = jnp.where(inside, taken(facing[face, part], at), got)
                remote[face, h * 64 : (h + 1) * 64, :] = got
            masks.append(
                face_masks(link[:, :LANES], link[:, LANES:], code[:, :LANES], code[:, LANES:])
            )
        derivatives(rows_of, 0, nodes, grads_two, rhs)
        add_faces(rows_of, 0, nodes, remote, 0, masks, rhs)
        for n in range(nodes):
            base_two[pl.ds(n, 8, stride=nodes), :] = (
                node_of(rows_of, 0, nodes, n) + ACOUSTIC_STEP * rhs[n]
            )


def sound_two_kernel(sound, base, grads, scale, source_a, source_b, out):
    nodes = sound.shape[1]
    is_flow = on_flow_row()

    @pl.when(is_flow)
    def _():
        out[...] = sound[...]

    @pl.when(jnp.logical_not(is_flow))
    def _():
        total = (source_a[...].astype(F32) + source_b[...].astype(F32)) * scale[0:1, :]
        for h in range(sound.shape[2] // LANES):
            for v, _, new in with_sources(total, columns_of(h), h, nodes, base, grads):
                out[v, :, columns_of(h)] = new


def call(kernel, outs, scratch, operands, cost=None, in_hbm=(), limit=VMEM_LIMIT):
    spaces = [pltpu.HBM if at in in_hbm else pltpu.VMEM for at in range(len(operands))]
    moved = sum(int(np.prod(x.shape)) * x.dtype.itemsize for x in (*operands, *outs))
    return pl.pallas_call(
        kernel,
        out_shape=tuple(outs),
        in_specs=[pl.BlockSpec(memory_space=space) for space in spaces],
        out_specs=tuple([pl.BlockSpec(memory_space=pltpu.VMEM)] * len(outs)),
        scratch_shapes=scratch,
        compiler_params=pltpu.CompilerParams(vmem_limit_bytes=limit),
        cost_estimate=pl.CostEstimate(flops=10**8 if cost is None else cost, bytes_accessed=moved if cost is None else 0, transcendentals=0),
    )(*operands)


def body(
    flow_fields,
    mean_velocity,
    cell_eddy_viscosity,
    tile_links,
    tile_target,
    projector,
    acoustic_state,
    element_face_neighbours,
    face_codes,
):
    groups = lax.axis_size("grp")
    count = lax.axis_size("sfc")
    flow = flow_fields[0]
    mean = mean_velocity[0]
    visc = cell_eddy_viscosity[0]
    links = tile_links[0]
    sound = acoustic_state[0]
    faces, span = element_face_neighbours.shape[1:]
    neighbours = element_face_neighbours.reshape(faces, 1, span)
    codes = face_codes.reshape(faces, 1, span)
    tiles = flow.shape[1]
    _, nodes, elements = sound.shape
    halves = elements // LANES
    block = 4 * nodes
    plan = FlowPlan(tiles)
    shape = jax.ShapeDtypeStruct
    vmem = pltpu.VMEM
    pairs_a = [p for i in range(1, count - 1, 2) for p in ((i, i + 1), (i + 1, i))]
    pairs_b = [p for i in range(0, count - 1, 2) for p in ((i, i + 1), (i + 1, i))]

    edge_rows = 6 * EDGE + EXTRA
    pack_a, pack_b = call(
        pack_kernel,
        [shape((edge_rows, LANES), BF16)] * 2,
        [
            vmem(links.shape, jnp.int32),
            vmem((2, *neighbours.shape), jnp.int32),
            vmem((2, 6 * EDGE, LANES), F32),
            pltpu.SemaphoreType.DMA((2, 6)),
            pltpu.SemaphoreType.DMA((2,)),
        ],
        [flow, visc, links, sound, neighbours, codes],
        in_hbm=(0, 1, 2, 3, 4, 5),
        limit=PACK_LIMIT,
        cost=PACK_COST,
    )
    part_a = lax.ppermute(pack_a, "sfc", pairs_a)
    part_b = lax.ppermute(pack_b, "sfc", pairs_b)

    fields = 5 * LANES
    rows, span = plan.rows, plan.span
    inner_rows = (plan.blocks - 2) * rows
    square = vmem((LANES, LANES), F32)
    packed = vmem((6, tiles, LANES), F32)
    inner_state, inner_high, inner_low, lcol, inner_mats, hits = call(
        inner_kernel,
        [
            shape((inner_rows, fields), F32),
            shape((inner_rows, fields), BF16),
            shape((inner_rows, fields), BF16),
            shape((tiles, LANES), F32),
            shape((plan.blocks - 2, 3 * rows, 2 * span), BF16),
            shape((2 * elements, tiles), BF16),
        ],
        [vmem((tiles, fields), BF16), vmem((tiles, fields), BF16), square],
        [flow, visc, links, tile_target],
    )
    lines = 6 * nodes + EXTRA
    node_rows = vmem((nodes, 8, LANES), F32)
    (
        own_one, next_one, mean_one, base, grads,
        edge_state, edge_high, edge_low, edge_mats, edge_visc,
    ) = call(
        first_kernel,
        [
            shape((lines, elements), F32),
            shape((lines, elements), BF16),
            shape(mean.shape, F32),
            shape(((halves + 2) * block, LANES), F32),
            shape((3, (halves + 2) * block, LANES), F32),
            shape((2 * rows, fields), F32),
            shape((2 * rows, fields), BF16),
            shape((2 * rows, fields), BF16),
            shape((2, 3 * rows, 2 * span), BF16),
            shape((2 * rows, LANES), F32),
        ],
        [
            square,
            vmem((2, span, fields), F32),
            vmem((2, span, fields), BF16),
            vmem((2, span, fields), BF16),
            vmem((HW, fields), BF16),
            packed,
            vmem((lines, tiles), BF16),
            vmem(((halves + 4) * block, LANES), F32),
            vmem((6, 4, 64, LANES), F32),
            vmem((6, (halves + 2) * 64, LANES), F32),
            node_rows,
        ],
        [
            flow, visc, mean, projector, part_a, part_b, sound, neighbours, codes,
            inner_state, inner_high, inner_low, lcol, inner_mats, hits,
        ],
    )

    up = [(i, i + 1) for i in range(count - 1)]

    def climb(x):
        chosen = [(g * count + i, g * count + j) for g in range(groups - 1) for i, j in up]
        return lax.ppermute(x, ("grp", "sfc"), chosen)

    def combined(*xs):
        total = xs[0]
        for x in xs[1:]:
            total = total + x.astype(F32)
        return total.astype(BF16)

    got_one = climb(next_one)
    band = plan.blocks * rows
    velocity = 3 * LANES
    step_one = [inner_state, inner_high, inner_low, inner_mats]
    edges = [edge_state, edge_high, edge_low, edge_mats, edge_visc]
    state_two, mean_two, own_two, next_two = call(
        second_kernel,
        [
            shape((band, velocity), F32),
            shape(mean.shape, F32),
            shape((6 * nodes, elements), F32),
            shape((6 * nodes, elements), BF16),
        ],
        [
            vmem((band, velocity), BF16),
            vmem((band, velocity), BF16),
            vmem((HW, fields), BF16),
            packed,
            vmem((6 * nodes, tiles), BF16),
        ],
        [visc, mean, mean_one, projector, *step_one, hits, *edges],
        cost=SECOND_COST,
    )
    last = (groups - 1) * count
    lines_beside = 6 * nodes // (LANES // HE) + EXTRA

    def borders(sums, row):
        up_border, down_border = call(
            border_kernel, [shape((lines_beside, LANES), BF16)] * 2, [], [sums], cost=0
        )
        start = row * count
        return up_border, [
            lax.ppermute(
                up_border, ("grp", "sfc"), [(start + i, last + i + 1) for i in range(count - 1)]
            ),
            lax.ppermute(
                down_border, ("grp", "sfc"), [(start + i, last + i - 1) for i in range(1, count)]
            ),
        ]

    got_two = climb(next_two)
    sum_one_2 = combined(own_one, got_one)
    one_0_to_1 = lax.ppermute(sum_one_2, "grp", [(0, 1)])
    _, beside_2 = borders(sum_one_2, 2)
    sum_two_1 = combined(own_two, got_two)
    two_0_to_2 = lax.ppermute(sum_two_1, "grp", [(0, 2)])
    one_2_to_3 = lax.ppermute(sum_one_2, "grp", [(2, 3)])
    two_1_to_3 = lax.ppermute(sum_two_1, "grp", [(1, 3)])
    flow_out, mean_out, own_one = call(
        output_kernel,
        [shape(flow.shape, F32), shape(mean.shape, F32), shape(own_one.shape, F32)],
        [vmem((band, fields), F32), vmem((HW, fields), BF16)],
        [flow, visc, mean, state_two, mean_two, *step_one, *edges, sum_two_1, *beside_2, own_one],
        cost=OUTPUT_COST,
    )
    sum_one_1 = combined(own_one, got_one, one_0_to_1)
    one_1_to_3 = lax.ppermute(sum_one_1, "grp", [(1, 3)])
    border, beside_1 = borders(sum_one_1, 1)
    (sum_two_2,) = call(
        gated_sum_kernel,
        [shape(own_two.shape, BF16)],
        [],
        [own_two, got_two, two_0_to_2, border],
        cost=0,
    )
    two_2_to_3 = lax.ppermute(sum_two_2, "grp", [(2, 3)])

    base, grads, scale = call(
        sound_one_kernel,
        [
            shape((halves * block, LANES), F32),
            shape((3, halves * block, LANES), F32),
            shape((8, elements), F32),
        ],
        [
            vmem(((halves + 1) * block, LANES), F32),
            vmem((6, halves + 1, 64, LANES), F32),
            vmem((6, halves * 64, LANES), F32),
            node_rows,
        ],
        [
            base, grads, neighbours, codes, one_2_to_3, one_1_to_3,
            *beside_1, *beside_2, two_1_to_3,
        ],
        cost=SOUND_COST,
    )
    (sound_out,) = call(
        sound_two_kernel,
        [shape(sound.shape, F32)],
        [],
        [sound, base, grads, scale, two_2_to_3, two_1_to_3],
    )
    return flow_out[None], mean_out[None], sound_out[None]


def solution(mesh):
    placed = (
        P("grp", None, "sfc", None),
        P("grp", None, "sfc", None),
        P("grp", "sfc", None),
        P("grp", None, "sfc"),
        P("grp", "sfc"),
        P(),
        P("grp", None, None, "sfc"),
        P("grp", None, "sfc"),
        P("grp", None, "sfc"),
    )
    return jax.shard_map(
        body,
        mesh=mesh,
        in_specs=placed,
        out_specs=(
            P("grp", None, "sfc", None),
            P("grp", None, "sfc", None),
            P("grp", None, None, "sfc"),
        ),
        check_vma=False,
    )
```

```python
import jax
import jax.numpy as jnp
import numpy as np
from jax import lax
from jax.experimental import pallas as pl
from jax.experimental.pallas import tpu as pltpu
from jax.sharding import PartitionSpec as P

HW = 16
HE = 16

ADVECT = 0.1
RELAX = 0.1
PENALTY = 1.5
ACOUSTIC_STEP = 0.08

LANES = 128
EDGE = 3 * HW
NO_LINK = 64
FIELD_ORDER = (1, 2, 3, 0, 4)
ALL_FIELDS = ((0, 2), (2, 4), (4, 5))
BASE = 32.0
EXTRA = 16
PACK_COST, SECOND_COST, OUTPUT_COST, SOUND_COST = 10**10, 10**10, 10**9, 10**9
VMEM_LIMIT = 20 * 1024 * 1024
PACK_LIMIT = 60 * 1024 * 1024

F32 = jnp.float32
BF16 = jnp.bfloat16


def lobatto_matrix():
    points = np.array([-1.0, -1.0 / np.sqrt(5.0), 1.0 / np.sqrt(5.0), 1.0])
    weights = np.array(
        [
            1.0 / np.prod([points[col] - points[other] for other in range(4) if other != col])
            for col in range(4)
        ]
    )
    matrix = np.zeros((4, 4))
    for line in range(4):
        for col in range(4):
            if line != col:
                matrix[line, col] = weights[col] / weights[line] / (points[line] - points[col])
        matrix[line, line] = -matrix[line].sum()
    return matrix.astype(np.float32)


def face_nodes(face):
    axis, level = face // 2, 3 * (face % 2)
    nodes = []
    for second in range(4):
        for first in range(4):
            coords = [first, second]
            coords.insert(axis, level)
            nodes.append(coords[0] + 4 * coords[1] + 16 * coords[2])
    return nodes


def turned_position(turn, position):
    a, b = position % 4, position // 4
    a, b = ((a, b), (3 - b, a), (3 - a, 3 - b), (b, 3 - a))[turn]
    return a + 4 * b


def split_parts(x):
    high = x.astype(BF16)
    return high, (x - high.astype(F32)).astype(BF16)


def dot(a, b):
    return jnp.dot(a, b, preferred_element_type=F32)


def dot_t(a, b):
    return lax.dot_general(a, b, (((1,), (1,)), ((), ())), preferred_element_type=F32)


def on_flow_row():
    return lax.axis_index("grp") < lax.axis_size("grp") - 1


def on_even_column():
    return lax.rem(lax.axis_index("sfc"), 2) == 0


def pack_kernel(
    flow, visc, links, sound, neighbours, codes,
    out_a, out_b, links_in, faces_in, staged, sems, link_sems,
):
    is_flow, even = on_flow_row(), on_even_column()
    tiles = flow.shape[1]
    _, nodes, elements = sound.shape
    outs = (out_a, out_b)

    @pl.when(is_flow)
    def _():
        fetch = pltpu.make_async_copy(links, links_in, link_sems.at[0])
        fetch.start()
        copies = []
        for side in range(2):
            off = pl.multiple_of(jnp.where(even == (side == 0), 0, tiles - EDGE), 8)
            for place, f in enumerate(FIELD_ORDER):
                copies.append(
                    pltpu.make_async_copy(
                        flow.at[f, pl.ds(off, EDGE), :],
                        staged.at[side, pl.ds(place * EDGE, EDGE), :],
                        sems.at[side, place],
                    )
                )
            copies.append(
                pltpu.make_async_copy(
                    visc.at[pl.ds(off, EDGE), :],
                    staged.at[side, pl.ds(5 * EDGE, EDGE), :],
                    sems.at[side, 5],
                )
            )
        for copy in copies:
            copy.start()
        fetch.wait()
        given = links_in[...]
        own = lax.axis_index("sfc") * tiles + lax.broadcasted_iota(jnp.int32, given.shape, 1)
        offset = jnp.where(given < 0, 0, given - own).astype(F32)
        low, high = offset[:, :LANES], offset[:, tiles - LANES :]
        pad = jnp.zeros((EXTRA - 4, LANES), F32)
        for side, (a, b) in enumerate(((low, high), (high, low))):
            block = jnp.concatenate([jnp.where(even, a, b), pad], 0)
            outs[side][6 * EDGE :, :] = block.astype(BF16)
        for copy in copies:
            copy.wait()
        for side in range(2):
            outs[side][: 6 * EDGE, :] = staged[side].astype(BF16)

    @pl.when(jnp.logical_not(is_flow))
    def _():
        copies = []
        for side in range(2):
            off = pl.multiple_of(jnp.where(even == (side == 0), 0, elements - LANES), LANES)
            for v in range(4):
                copies.append(
                    pltpu.make_async_copy(
                        sound.at[v, :, pl.ds(off, LANES)],
                        staged.at[side, pl.ds(v * nodes, nodes), :],
                        sems.at[side, v],
                    )
                )
        for at, ref in enumerate((neighbours, codes)):
            copies.append(pltpu.make_async_copy(ref, faces_in.at[at], link_sems.at[at]))
        for copy in copies:
            copy.start()
        for copy in copies:
            copy.wait()
        first = lax.axis_index("sfc") * elements
        own = first + lax.broadcasted_iota(jnp.int32, (1, elements), 1)
        for face in range(6):
            link = faces_in[0, face]
            offset = jnp.where(link < 0, NO_LINK, link - own).astype(F32)
            for at, row in enumerate((offset, faces_in[1, face].astype(F32))):
                line = 4 * nodes + 6 * at + face
                low, high = row[:, :LANES], row[:, elements - LANES :]
                staged[0, line : line + 1, :] = jnp.where(even, low, high)
                staged[1, line : line + 1, :] = jnp.where(even, high, low)
        used = 4 * nodes + 12
        for side, out in enumerate(outs):
            staged[side, used:, :] = jnp.zeros((staged.shape[1] - used, LANES), F32)
            out[: 6 * EDGE, :] = staged[side].astype(BF16)
            out[6 * EDGE :, :] = jnp.zeros((out.shape[0] - 6 * EDGE, LANES), BF16)


class FlowPlan:
    def __init__(self, tiles):
        self.tiles = tiles
        self.wide = tiles + 2 * EDGE
        self.blocks = 4
        self.rows = (tiles + 4 * HW) // self.blocks
        self.span = self.rows + 2 * HW

    def at(self, b):
        return HW + b * self.rows

    def inner(self):
        return range(1, self.blocks - 1)


def columns_of(place):
    return slice(place * LANES, (place + 1) * LANES)


def rows_between(parts, low, high, columns):
    taken = []
    for start, ref in parts:
        a, b = max(low, start), min(high, start + ref.shape[0])
        if a < b:
            taken.append(ref[a - start : b - start, columns])
    return taken[0] if len(taken) == 1 else jnp.concatenate(taken, 0)


def put(high, low, at, place, value):
    h, l = split_parts(value)
    high[at : at + value.shape[0], columns_of(place)] = h
    low[at : at + value.shape[0], columns_of(place)] = l


def east_west(x):
    return pltpu.roll(x, LANES - 1, 1), pltpu.roll(x, 1, 1)


def link_matrix(plan, offset, mat):
    rows, span = plan.rows, plan.span
    lane = lax.broadcasted_iota(jnp.int32, (rows, 2 * span), 1)
    lane = jnp.where(lane >= span, lane - span, lane)
    place = HW + lax.broadcasted_iota(jnp.int32, (rows, LANES), 0) + offset.astype(jnp.int32)
    hot = [jnp.where(place[:, k : k + 1] == lane, F32(1.0), F32(0.0)) for k in range(4)]
    mat[:rows, :] = (hot[0] + hot[1] + hot[2] + hot[3]).astype(BF16)
    mat[rows : 2 * rows, :] = (hot[0] - hot[1]).astype(BF16)
    mat[2 * rows :, :] = (hot[2] - hot[3]).astype(BF16)


def gathered(plan, mat, high, low, b, columns, at_row):
    at = b * plan.rows
    both = [rows_between(x, at, at + plan.span, columns) for x in (high, low)]
    return dot(mat[at_row:, :], jnp.concatenate(both, 0))


def advance(plan, b, mat, high, low, state, v, places, new_state, new_high, new_low, new_at, split):
    rows = plan.rows
    center = [state(k) for k in range(3)]
    scaled = [(0.5 * ADVECT) * c for c in center]
    for first, last in places:
        got = gathered(plan, mat, high, low, b, slice(first * LANES, last * LANES), 0)
        for place in range(first, last):
            inner = columns_of(place - first)
            total, dy, dz = got[:rows, inner], got[rows : 2 * rows, inner], got[2 * rows :, inner]
            c = center[place] if place < 3 else state(place)
            east, west = east_west(c)
            new = (
                c
                + v * (east + west + total - 6.0 * c)
                - (scaled[0] * (east - west) + scaled[1] * dy + scaled[2] * dz)
            )
            new_state[new_at : new_at + rows, columns_of(place)] = new
            if split:
                put(new_high, new_low, new_at, place, new)


def lamb_block(plan, b, mat, high, low, state, average, average_out, packed):
    rows = plan.rows
    center = [state(k) for k in range(3)]
    got = [
        gathered(plan, mat, high, low, b, slice(0, 2 * LANES), rows),
        gathered(plan, mat, high, low, b, slice(2 * LANES, 3 * LANES), rows),
    ]
    d1, d2, d3 = [], [], []
    for k in range(3):
        east, west = east_west(center[k])
        d1.append((east - west) * 0.5)
        inner = columns_of(k % 2)
        d2.append(got[k // 2][:rows, inner] * 0.5)
        d3.append(got[k // 2][rows:, inner] * 0.5)
    vx = d2[2] - d3[1]
    vy = d3[0] - d1[2]
    vz = d1[1] - d2[0]
    lamb = (
        vy * center[2] - vz * center[1],
        vz * center[0] - vx * center[2],
        vx * center[1] - vy * center[0],
    )
    to = plan.at(b) - EDGE
    low_row, top_row = max(0, -to), min(rows, plan.tiles - to)
    own = slice(to + low_row, to + top_row)
    for i in range(3):
        packed[i, own, :] = lamb[i][low_row:top_row]
        mixed = (1.0 - RELAX) * average[i, own, :] + RELAX * center[i][low_row:top_row]
        average_out[i, own, :] = mixed
        packed[3 + i, own, :] = mixed


def element_sums(projector, packed, hits, pay, own_ref, next_ref):
    nodes = projector.shape[0]
    count, elements = own_ref.shape
    proj_high, proj_low = split_parts(projector[...])
    proj_both = jnp.concatenate(
        [
            jnp.concatenate([proj_high, proj_high], 1),
            jnp.concatenate([proj_low, jnp.zeros_like(proj_low)], 1),
        ],
        0,
    )
    for c in range(6):
        x_high, x_low = split_parts(packed[c])
        main = dot_t(proj_both, jnp.concatenate([x_high, x_low], 1))
        pay[c * nodes : (c + 1) * nodes, :] = (main[:nodes] + main[nodes:]).astype(BF16)
    if count > 6 * nodes:
        pay[6 * nodes :, :] = jnp.ones((count - 6 * nodes, pay.shape[1]), BF16)
    sums = dot_t(pay[...], hits[...])
    if count > 6 * nodes:
        tail = sums[6 * nodes :]
        line = lax.broadcasted_iota(jnp.int32, tail.shape, 0)
        big = jnp.floor(tail * (1.0 / BASE))
        tail = jnp.where(line == 0, tail - BASE * big, jnp.where(line == 1, big, 0.0))
        sums = jnp.concatenate([sums[: 6 * nodes], tail], 0)
    own_ref[...] = sums[:, :elements]
    next_ref[...] = sums[:, elements:].astype(BF16)


def inner_kernel(
    flow, visc, links, target,
    inner_state, inner_high, inner_low, lcol, inner_mats, hits, high0, low0, square,
):
    plan = FlowPlan(flow.shape[1])
    tiles, rows = plan.tiles, plan.rows

    @pl.when(on_flow_row())
    def _():
        column = lax.axis_index("sfc")
        first_tile, first_element = column * tiles, column * (hits.shape[0] // 2)
        for place, f in enumerate(FIELD_ORDER):
            put(high0, low0, 0, place, flow[f])
        square[...] = jnp.zeros_like(square)
        own_tile = first_tile + lax.broadcasted_iota(jnp.int32, links.shape, 1)
        offset = jnp.where(links[...] < 0, 0, links[...] - own_tile).astype(F32)
        for part in range(tiles // LANES):
            square[:4, :] = offset[:, part * LANES : (part + 1) * LANES]
            lcol[part * LANES : (part + 1) * LANES, :] = square[...].T
        local = target[...] - first_element
        hits[...] = jnp.where(
            lax.broadcasted_iota(jnp.int32, hits.shape, 0) == local, F32(1.0), F32(0.0)
        ).astype(BF16)
        for at, b in enumerate(plan.inner()):
            own = slice(plan.at(b) - EDGE, plan.at(b) - EDGE + rows)
            link_matrix(plan, lcol[own, :], inner_mats.at[at])
            advance(
                plan, b, inner_mats.at[at], [(EDGE, high0)], [(EDGE, low0)],
                lambda place, own=own: flow[FIELD_ORDER[place], own, :],
                visc[own, :], ALL_FIELDS, inner_state, inner_high, inner_low, at * rows, True,
            )


def band_parts(plan, edge, inner):
    rows, last = plan.rows, plan.blocks - 1
    return [
        (plan.at(0), edge.at[:rows]),
        (plan.at(1), inner),
        (plan.at(last), edge.at[rows:]),
    ]


def band_state(plan, b, edge, inner):
    at = plan.at(b)
    parts = band_parts(plan, edge, inner)
    return lambda place: rows_between(parts, at, at + plan.rows, columns_of(place))


def closed(plan, parts, zero):
    return [(0, zero), *parts, (plan.wide - HW, zero)]


def mats_of(plan, b, edge_mats, inner_mats):
    if b in plan.inner():
        return inner_mats.at[b - 1]
    return edge_mats.at[0 if b == 0 else 1]


def first_kernel(
    flow, visc, mean, projector, part_a, part_b, sound, neighbours, codes,
    inner_state, inner_high, inner_low, lcol, inner_mats, hits,
    own_one, next_one, mean_one, base, grads, hot_two,
    edge_state, edge_high, edge_low, edge_mats, edge_visc,
    square, state0, high0, low0, zero, packed, pay, rows_of, facing, remote, rhs,
):
    is_flow, even = on_flow_row(), on_even_column()
    plan = FlowPlan(packed.shape[1])
    tiles, rows, span = plan.tiles, plan.rows, plan.span
    own_rows = span - EDGE

    @pl.when(is_flow)
    def _():
        def pick(at, size):
            a, b = part_a[at : at + size, :].astype(F32), part_b[at : at + size, :].astype(F32)
            return jnp.where(even, a, b), jnp.where(even, b, a)

        zero[...] = jnp.zeros_like(zero)
        for place, f in enumerate(FIELD_ORDER):
            before, after = pick(place * EDGE, EDGE)
            ends = (
                jnp.concatenate([before, flow[f, :own_rows, :]], 0),
                jnp.concatenate([flow[f, tiles - own_rows :, :], after], 0),
            )
            for side in range(2):
                state0[side, :, columns_of(place)] = ends[side]
                put(high0.at[side], low0.at[side], 0, place, ends[side])
        before, after = pick(5 * EDGE, EDGE)
        edge_visc[:rows, :] = jnp.concatenate([before[HW:], visc[: rows - EDGE + HW, :]], 0)
        edge_visc[rows:, :] = jnp.concatenate(
            [visc[tiles - (rows - EDGE + HW) :, :], after[: EDGE - HW]], 0
        )
        before, after = pick(6 * EDGE, EXTRA)
        given = []
        for side, block in enumerate((before, after)):
            square[...] = jnp.zeros_like(square)
            square[:EXTRA, :] = block
            turned = square[...].T
            given.append(
                jnp.concatenate([turned[LANES - EDGE + HW :], lcol[: rows - EDGE + HW, :]], 0)
                if side == 0
                else jnp.concatenate(
                    [lcol[tiles - (rows - EDGE + HW) :, :], turned[: EDGE - HW]], 0
                )
            )
        for side, b in enumerate((0, plan.blocks - 1)):
            link_matrix(plan, given[side], edge_mats.at[side])
            advance(
                plan, b, edge_mats.at[side],
                [(b * rows, high0.at[side])], [(b * rows, low0.at[side])],
                lambda place, side=side: state0[side, HW : HW + rows, columns_of(place)],
                edge_visc[side * rows : (side + 1) * rows, :], ALL_FIELDS,
                edge_state, edge_high, edge_low, side * rows, True,
            )
        high1 = closed(plan, band_parts(plan, edge_high, inner_high), zero)
        low1 = closed(plan, band_parts(plan, edge_low, inner_low), zero)
        for b in range(plan.blocks):
            lamb_block(
                plan, b, mats_of(plan, b, edge_mats, inner_mats), high1, low1,
                band_state(plan, b, edge_state, inner_state), mean, mean_one, packed,
            )
        element_sums(projector, packed, hits, pay, own_one, next_one)

    @pl.when(jnp.logical_not(is_flow))
    def _():
        own_one[...] = jnp.zeros_like(own_one)
        next_one[...] = jnp.zeros_like(next_one)
        nodes, elements = sound.shape[1:]
        halves = elements // LANES
        block = 4 * nodes
        for v in range(4):
            for h in range(halves):
                rows_of[h * block + v * nodes : h * block + (v + 1) * nodes, :] = sound[
                    v, :, h * LANES : (h + 1) * LANES
                ]
        a, b = part_a[:block, :].astype(F32), part_b[:block, :].astype(F32)
        before, after = jnp.where(even, a, b), jnp.where(even, b, a)
        lane = lax.broadcasted_iota(jnp.int32, (1, LANES), 1)
        beside = lane < LANES // 2
        rows_of[halves * block : (halves + 1) * block, :] = jnp.where(beside, after, before)
        rows_of[(halves + 1) * block : (halves + 2) * block, :] = jnp.zeros_like(before)
        rows_of[(halves + 2) * block : (halves + 3) * block, :] = before
        rows_of[(halves + 3) * block :, :] = after
        a = part_a[block : block + EXTRA, :].astype(F32)
        b = part_b[block : block + EXTRA, :].astype(F32)
        given = jnp.where(beside, jnp.where(even, b, a), jnp.where(even, a, b)).astype(jnp.int32)
        own_parts = [0, 1, halves + 2, halves + 3]
        first = lax.axis_index("sfc") * elements
        masks = []
        for face in range(6):
            for at, part in enumerate(own_parts):
                facing_rows(rows_of, part * block, nodes, face ^ 1, facing.at[face, at])
            link, code = neighbours[face], codes[face]
            offset, extra_code = given[face : face + 1, :], given[6 + face : 7 + face, :]
            extra = jnp.where(beside, elements + lane, lane - LANES) + offset
            near = jnp.concatenate([link - first, extra], 1)
            valid = jnp.concatenate([link, jnp.where(offset >= NO_LINK, -1, 0)], 1) >= 0
            place = jnp.where(
                near < 0, elements + LANES + near, jnp.where(near < elements, near, near + LANES)
            )
            hot = hot_columns(jnp.where(valid, place, -1), elements + 2 * LANES)
            remote_rows([facing[face, at] for at in range(4)], hot, remote, face)
            near = link - first
            place = jnp.where(near < 0, elements + LANES + near, near)
            hot_two[face] = hot_columns(jnp.where(link < 0, -1, place), elements + LANES)
            masks.append(
                (
                    face_masks(link[:, :LANES], link[:, LANES:], code[:, :LANES], code[:, LANES:]),
                    face_masks(
                        jnp.where(offset >= NO_LINK, -1, 0), jnp.full((1, LANES), -1, jnp.int32),
                        extra_code, extra_code,
                    ),
                )
            )
        for group in range(2):
            start = group * halves * block
            derivatives(rows_of, start, nodes, grads, rhs)
            add_faces(
                rows_of, start, nodes, remote, group * halves * 64, [m[group] for m in masks], rhs
            )
            for n in range(nodes):
                base[pl.ds(start + n, 8, stride=nodes), :] = (
                    node_of(rows_of, start, nodes, n) + ACOUSTIC_STEP * rhs[n]
                )


def second_block(plan, b, carried, visc, places, new_state, new_parts):
    (inner_state, inner_high, inner_low, inner_mats, edge_state, edge_high, edge_low, edge_mats,
     edge_visc, zero) = carried
    rows = plan.rows
    if b in plan.inner():
        v = visc[plan.at(b) - EDGE : plan.at(b) - EDGE + rows, :]
    else:
        v = edge_visc[:rows, :] if b == 0 else edge_visc[rows:, :]
    advance(
        plan, b, mats_of(plan, b, edge_mats, inner_mats),
        closed(plan, band_parts(plan, edge_high, inner_high), zero),
        closed(plan, band_parts(plan, edge_low, inner_low), zero),
        band_state(plan, b, edge_state, inner_state), v, places,
        new_state, *new_parts, b * rows, new_parts[0] is not None,
    )


def second_kernel(
    visc, mean, mean_one, projector,
    inner_state, inner_high, inner_low, inner_mats, hits,
    edge_state, edge_high, edge_low, edge_mats, edge_visc,
    state, mean_two, own_two, next_two,
    high, low, zero, packed, pay,
):
    plan = FlowPlan(packed.shape[1])
    rows = plan.rows
    is_flow = on_flow_row()

    @pl.when(jnp.logical_not(is_flow))
    def _():
        own_two[...] = jnp.zeros_like(own_two)
        next_two[...] = jnp.zeros_like(next_two)

    @pl.when(is_flow)
    def _():
        zero[...] = jnp.zeros_like(zero)
        carried = (
            inner_state, inner_high, inner_low, inner_mats,
            edge_state, edge_high, edge_low, edge_mats, edge_visc, zero,
        )
        for b in range(plan.blocks):
            second_block(plan, b, carried, visc, ((0, 2), (2, 3)), state, (high, low))
        for b in range(plan.blocks):
            lamb_block(
                plan, b, mats_of(plan, b, edge_mats, inner_mats),
                closed(plan, [(HW, high)], zero), closed(plan, [(HW, low)], zero),
                lambda place, b=b: state[b * rows : (b + 1) * rows, columns_of(place)],
                mean_one, mean_two, packed,
            )
        element_sums(projector, packed, hits, pay, own_two, next_two)


def output_kernel(
    flow, visc, mean, state, mean_two,
    inner_state, inner_high, inner_low, inner_mats,
    edge_state, edge_high, edge_low, edge_mats, edge_visc, after, after_up, after_down, own_one,
    flow_out, mean_out, own_one_out, passive, zero,
):
    plan = FlowPlan(flow.shape[1])
    is_flow = on_flow_row()
    own_one_out[...] = own_one[...]

    @pl.when(jnp.logical_not(is_flow))
    def _():
        flow_out[...] = flow[...]
        mean_out[...] = mean[...]

    @pl.when(is_flow)
    def _():
        zero[...] = jnp.zeros_like(zero)
        mean_out[...] = mean_two[...]
        carried = (
            inner_state, inner_high, inner_low, inner_mats,
            edge_state, edge_high, edge_low, edge_mats, edge_visc, zero,
        )
        own = slice(EDGE - HW, EDGE - HW + plan.tiles)
        for place in range(3):
            flow_out[FIELD_ORDER[place]] = state[own, columns_of(place)]
        for b in range(plan.blocks):
            second_block(plan, b, carried, visc, ((3, 5),), passive, (None, None))
        for place in (3, 4):
            flow_out[FIELD_ORDER[place]] = passive[own, columns_of(place)]


def facing_rows(rows_of, base, nodes, face, to):
    axis, level = face // 2, 3 * (face % 2)
    if axis == 0:
        to[...] = rows_of[pl.ds(base + level, 64, stride=4), :]
    elif axis == 1:
        for i in range(4):
            to[pl.ds(i, 16, stride=4), :] = rows_of[pl.ds(base + i + 4 * level, 16, stride=16), :]
    else:
        for v in range(4):
            at = base + v * nodes + 16 * level
            to[v * 16 : (v + 1) * 16, :] = rows_of[at : at + 16, :]


def hot_columns(place, size):
    key = lax.broadcasted_iota(jnp.int32, (size, place.shape[1]), 0)
    return jnp.where(key == place, F32(1.0), F32(0.0)).astype(BF16)


def node_of(rows_of, start, nodes, n):
    return rows_of[pl.ds(start + n, 8, stride=nodes), :]


def remote_rows(parts, hot, remote, face):
    high, low = split_parts(jnp.concatenate(parts, 1))
    got = dot(jnp.concatenate([high, low], 0), hot)
    got = got[:64] + got[64:]
    for h in range(got.shape[1] // LANES):
        remote[face, h * 64 : (h + 1) * 64, :] = got[:, h * LANES : (h + 1) * LANES]


def derivatives(rows_of, start, nodes, grads_out, rhs):
    matrix = lobatto_matrix()
    line = lax.broadcasted_iota(jnp.int32, (8, LANES), 0)
    is_v = [line % 4 == v for v in range(4)]
    node = [node_of(rows_of, start, nodes, n) for n in range(nodes)]
    for n in range(nodes):
        i, j, k = n % 4, n // 4 % 4, n // 16
        lines = (
            [m + 4 * j + 16 * k for m in range(4)],
            [i + 4 * m + 16 * k for m in range(4)],
            [i + 4 * j + 16 * m for m in range(4)],
        )
        grads = []
        for d, at in enumerate((i, j, k)):
            total = None
            for m in range(4):
                if abs(matrix[at, m]) > 1e-12:
                    term = F32(matrix[at, m]) * node[lines[d][m]]
                    total = term if total is None else total + term
            grads.append(total)
            grads_out[d, pl.ds(start + n, 8, stride=nodes), :] = total
        div = sum(pltpu.roll(grads[d], 8 - (1 + d), 0) for d in range(3))
        coupled = jnp.where(is_v[0], div, 0.0)
        for d in range(3):
            coupled = jnp.where(is_v[1 + d], pltpu.roll(grads[d], 1 + d, 0), coupled)
        rhs[n] = -coupled


def face_masks(link_low, link_high, code_low, code_high):
    upper = lax.broadcasted_iota(jnp.int32, (8, LANES), 0) >= 4

    def both(low, high):
        return jnp.where(
            upper, jnp.broadcast_to(high, (8, LANES)), jnp.broadcast_to(low, (8, LANES))
        )

    code = both(code_low, code_high)
    return both(link_low, link_high) >= 0, [code == t for t in range(3)]


def add_faces(rows_of, start, nodes, remote, remote_start, masks, rhs):
    for face in range(6):
        valid, is_turn = masks[face]
        planes = [remote[face, pl.ds(remote_start + p, 8, stride=16), :] for p in range(16)]
        for p, n in enumerate(face_nodes(face)):
            turned = planes[turned_position(3, p)]
            for t in range(3):
                turned = jnp.where(is_turn[t], planes[turned_position(t, p)], turned)
            jump = jnp.where(valid, turned - node_of(rows_of, start, nodes, n), 0.0)
            rhs[n] = rhs[n] + PENALTY * jump


def with_sources(total, columns, block, nodes, base, grads):
    for v in range(4):
        rows = slice(block * 4 * nodes + v * nodes, block * 4 * nodes + (v + 1) * nodes)
        added = total[(v - 1) * nodes : v * nodes, columns] if v else None
        for d in range(3):
            term = total[(3 + d) * nodes : (4 + d) * nodes, columns] * grads[d, rows, :]
            added = term if added is None else added + term
        yield v, rows, base[rows, :] - ACOUSTIC_STEP * added


def gated_sum_kernel(own, *refs):
    *others, _, out = refs

    @pl.when(on_flow_row())
    def _():
        total = own[...]
        for other in others:
            total = total + other[...].astype(F32)
        out[...] = total.astype(BF16)


def border_kernel(sums, up, down):
    nodes_rows = (sums.shape[0] - EXTRA) // (LANES // HE)
    group = lax.broadcasted_iota(jnp.int32, (1, LANES), 1) // HE
    for out, tile, shift in ((up, sums.shape[1] - LANES, HE), (down, 0, 0)):
        columns = slice(tile, tile + LANES)
        total = jnp.zeros((nodes_rows, LANES), F32)
        for i in range(LANES // HE):
            x = sums[i * nodes_rows : (i + 1) * nodes_rows, columns].astype(F32)
            turn = (HE * i + shift) % LANES
            x = pltpu.roll(x, turn, 1) if turn else x
            total = jnp.where(group == i, x, total)
        out[:nodes_rows, :] = total.astype(BF16)
        x = sums[sums.shape[0] - EXTRA :, columns].astype(F32)
        x = pltpu.roll(x, shift, 1) if shift else x
        out[nodes_rows:, :] = jnp.where(group == 0, x, 0.0).astype(BF16)


def border_sums(up, down):
    lines = up.shape[0] - EXTRA
    lane = lax.broadcasted_iota(jnp.int32, (1, LANES), 1)
    parts = []
    for i in range(LANES // HE + 1):
        rows = slice(0, lines) if i < LANES // HE else slice(lines, lines + EXTRA)
        at = HE * (i % (LANES // HE))
        x = pltpu.roll(up[rows], (2 * LANES - HE - at) % LANES, 1)
        y = pltpu.roll(down[rows], (LANES - at) % LANES, 1) if at else down[rows]
        parts.append(jnp.where(lane >= LANES - HE, x, jnp.where(lane < HE, y, 0.0)))
    return jnp.concatenate(parts, 0)


def scaled_sums(total, nodes):
    count = total[6 * nodes : 6 * nodes + 1] + BASE * total[6 * nodes + 1 : 6 * nodes + 2]
    inverse = 1.0 / jnp.maximum(count, 1.0)
    return total[: 6 * nodes] * inverse, inverse


def sound_one_kernel(
    base, grads, hot_two, neighbours, codes, source_a, source_b, up_a, down_a, up_b, down_b, after,
    base_two, grads_two, scale_out, rows_of, facing, remote, rhs,
):
    elements = source_a.shape[1]
    halves = elements // LANES
    nodes = base_two.shape[0] // (4 * halves)
    block = 4 * nodes

    @pl.when(jnp.logical_not(on_flow_row()))
    def _():
        own, inverse = scaled_sums(source_a[...].astype(F32) + source_b[...].astype(F32), nodes)
        scale_out[...] = jnp.broadcast_to(inverse, scale_out.shape)
        extra = border_sums(
            up_a[...].astype(F32) + up_b[...].astype(F32),
            down_a[...].astype(F32) + down_b[...].astype(F32),
        )
        extra, _ = scaled_sums(extra, nodes)
        for h in range(halves + 1):
            total, columns = (own, columns_of(h)) if h < halves else (extra, columns_of(0))
            for _, rows, new in with_sources(total, columns, h, nodes, base, grads):
                rows_of[rows, :] = new
        masks = []
        for face in range(6):
            for part in range(halves + 1):
                facing_rows(rows_of, part * block, nodes, face ^ 1, facing.at[face, part])
            remote_rows(
                [facing[face, part] for part in range(halves + 1)], hot_two[face], remote, face
            )
            link, code = neighbours[face], codes[face]
            masks.append(
                face_masks(link[:, :LANES], link[:, LANES:], code[:, :LANES], code[:, LANES:])
            )
        derivatives(rows_of, 0, nodes, grads_two, rhs)
        add_faces(rows_of, 0, nodes, remote, 0, masks, rhs)
        for n in range(nodes):
            base_two[pl.ds(n, 8, stride=nodes), :] = (
                node_of(rows_of, 0, nodes, n) + ACOUSTIC_STEP * rhs[n]
            )


def sound_two_kernel(sound, base, grads, scale, source_a, source_b, out):
    nodes = sound.shape[1]
    is_flow = on_flow_row()

    @pl.when(is_flow)
    def _():
        out[...] = sound[...]

    @pl.when(jnp.logical_not(is_flow))
    def _():
        total = (source_a[...].astype(F32) + source_b[...].astype(F32)) * scale[0:1, :]
        for h in range(sound.shape[2] // LANES):
            for v, _, new in with_sources(total, columns_of(h), h, nodes, base, grads):
                out[v, :, columns_of(h)] = new


def call(kernel, outs, scratch, operands, cost=None, in_hbm=(), limit=VMEM_LIMIT):
    spaces = [pltpu.HBM if at in in_hbm else pltpu.VMEM for at in range(len(operands))]
    moved = sum(int(np.prod(x.shape)) * x.dtype.itemsize for x in (*operands, *outs))
    return pl.pallas_call(
        kernel,
        out_shape=tuple(outs),
        in_specs=[pl.BlockSpec(memory_space=space) for space in spaces],
        out_specs=tuple([pl.BlockSpec(memory_space=pltpu.VMEM)] * len(outs)),
        scratch_shapes=scratch,
        compiler_params=pltpu.CompilerParams(vmem_limit_bytes=limit),
        cost_estimate=pl.CostEstimate(flops=10**8 if cost is None else cost, bytes_accessed=moved if cost is None else 0, transcendentals=0),
    )(*operands)


def body(
    flow_fields,
    mean_velocity,
    cell_eddy_viscosity,
    tile_links,
    tile_target,
    projector,
    acoustic_state,
    element_face_neighbours,
    face_codes,
):
    groups = lax.axis_size("grp")
    count = lax.axis_size("sfc")
    flow = flow_fields[0]
    mean = mean_velocity[0]
    visc = cell_eddy_viscosity[0]
    links = tile_links[0]
    sound = acoustic_state[0]
    faces, span = element_face_neighbours.shape[1:]
    neighbours = element_face_neighbours.reshape(faces, 1, span)
    codes = face_codes.reshape(faces, 1, span)
    tiles = flow.shape[1]
    _, nodes, elements = sound.shape
    halves = elements // LANES
    block = 4 * nodes
    plan = FlowPlan(tiles)
    shape = jax.ShapeDtypeStruct
    vmem = pltpu.VMEM
    pairs_a = [p for i in range(1, count - 1, 2) for p in ((i, i + 1), (i + 1, i))]
    pairs_b = [p for i in range(0, count - 1, 2) for p in ((i, i + 1), (i + 1, i))]

    edge_rows = 6 * EDGE + EXTRA
    pack_a, pack_b = call(
        pack_kernel,
        [shape((edge_rows, LANES), BF16)] * 2,
        [
            vmem(links.shape, jnp.int32),
            vmem((2, *neighbours.shape), jnp.int32),
            vmem((2, 6 * EDGE, LANES), F32),
            pltpu.SemaphoreType.DMA((2, 6)),
            pltpu.SemaphoreType.DMA((2,)),
        ],
        [flow, visc, links, sound, neighbours, codes],
        in_hbm=(0, 1, 2, 3, 4, 5),
        limit=PACK_LIMIT,
        cost=PACK_COST,
    )
    part_a = lax.ppermute(pack_a, "sfc", pairs_a)
    part_b = lax.ppermute(pack_b, "sfc", pairs_b)

    fields = 5 * LANES
    rows, span = plan.rows, plan.span
    inner_rows = (plan.blocks - 2) * rows
    square = vmem((LANES, LANES), F32)
    packed = vmem((6, tiles, LANES), F32)
    inner_state, inner_high, inner_low, lcol, inner_mats, hits = call(
        inner_kernel,
        [
            shape((inner_rows, fields), F32),
            shape((inner_rows, fields), BF16),
            shape((inner_rows, fields), BF16),
            shape((tiles, LANES), F32),
            shape((plan.blocks - 2, 3 * rows, 2 * span), BF16),
            shape((2 * elements, tiles), BF16),
        ],
        [vmem((tiles, fields), BF16), vmem((tiles, fields), BF16), square],
        [flow, visc, links, tile_target],
    )
    lines = 6 * nodes + EXTRA
    node_rows = vmem((nodes, 8, LANES), F32)
    (
        own_one, next_one, mean_one, base, grads, hot_two,
        edge_state, edge_high, edge_low, edge_mats, edge_visc,
    ) = call(
        first_kernel,
        [
            shape((lines, elements), F32),
            shape((lines, elements), BF16),
            shape(mean.shape, F32),
            shape(((halves + 2) * block, LANES), F32),
            shape((3, (halves + 2) * block, LANES), F32),
            shape((6, elements + LANES, elements), BF16),
            shape((2 * rows, fields), F32),
            shape((2 * rows, fields), BF16),
            shape((2 * rows, fields), BF16),
            shape((2, 3 * rows, 2 * span), BF16),
            shape((2 * rows, LANES), F32),
        ],
        [
            square,
            vmem((2, span, fields), F32),
            vmem((2, span, fields), BF16),
            vmem((2, span, fields), BF16),
            vmem((HW, fields), BF16),
            packed,
            vmem((lines, tiles), BF16),
            vmem(((halves + 4) * block, LANES), F32),
            vmem((6, 4, 64, LANES), F32),
            vmem((6, (halves + 2) * 64, LANES), F32),
            node_rows,
        ],
        [
            flow, visc, mean, projector, part_a, part_b, sound, neighbours, codes,
            inner_state, inner_high, inner_low, lcol, inner_mats, hits,
        ],
    )

    up = [(i, i + 1) for i in range(count - 1)]

    def climb(x):
        chosen = [(g * count + i, g * count + j) for g in range(groups - 1) for i, j in up]
        return lax.ppermute(x, ("grp", "sfc"), chosen)

    def combined(*xs):
        total = xs[0]
        for x in xs[1:]:
            total = total + x.astype(F32)
        return total.astype(BF16)

    got_one = climb(next_one)
    band = plan.blocks * rows
    velocity = 3 * LANES
    step_one = [inner_state, inner_high, inner_low, inner_mats]
    edges = [edge_state, edge_high, edge_low, edge_mats, edge_visc]
    state_two, mean_two, own_two, next_two = call(
        second_kernel,
        [
            shape((band, velocity), F32),
            shape(mean.shape, F32),
            shape((6 * nodes, elements), F32),
            shape((6 * nodes, elements), BF16),
        ],
        [
            vmem((band, velocity), BF16),
            vmem((band, velocity), BF16),
            vmem((HW, fields), BF16),
            packed,
            vmem((6 * nodes, tiles), BF16),
        ],
        [visc, mean, mean_one, projector, *step_one, hits, *edges],
        cost=SECOND_COST,
    )
    last = (groups - 1) * count
    lines_beside = 6 * nodes // (LANES // HE) + EXTRA

    def borders(sums, row):
        up_border, down_border = call(
            border_kernel, [shape((lines_beside, LANES), BF16)] * 2, [], [sums], cost=0
        )
        start = row * count
        return up_border, [
            lax.ppermute(
                up_border, ("grp", "sfc"), [(start + i, last + i + 1) for i in range(count - 1)]
            ),
            lax.ppermute(
                down_border, ("grp", "sfc"), [(start + i, last + i - 1) for i in range(1, count)]
            ),
        ]

    got_two = climb(next_two)
    sum_one_2 = combined(own_one, got_one)
    one_0_to_1 = lax.ppermute(sum_one_2, "grp", [(0, 1)])
    _, beside_2 = borders(sum_one_2, 2)
    sum_two_1 = combined(own_two, got_two)
    two_0_to_2 = lax.ppermute(sum_two_1, "grp", [(0, 2)])
    one_2_to_3 = lax.ppermute(sum_one_2, "grp", [(2, 3)])
    two_1_to_3 = lax.ppermute(sum_two_1, "grp", [(1, 3)])
    flow_out, mean_out, own_one = call(
        output_kernel,
        [shape(flow.shape, F32), shape(mean.shape, F32), shape(own_one.shape, F32)],
        [vmem((band, fields), F32), vmem((HW, fields), BF16)],
        [flow, visc, mean, state_two, mean_two, *step_one, *edges, sum_two_1, *beside_2, own_one],
        cost=OUTPUT_COST,
    )
    sum_one_1 = combined(own_one, got_one, one_0_to_1)
    one_1_to_3 = lax.ppermute(sum_one_1, "grp", [(1, 3)])
    border, beside_1 = borders(sum_one_1, 1)
    (sum_two_2,) = call(
        gated_sum_kernel,
        [shape(own_two.shape, BF16)],
        [],
        [own_two, got_two, two_0_to_2, border],
        cost=0,
    )
    two_2_to_3 = lax.ppermute(sum_two_2, "grp", [(2, 3)])

    base, grads, scale = call(
        sound_one_kernel,
        [
            shape((halves * block, LANES), F32),
            shape((3, halves * block, LANES), F32),
            shape((8, elements), F32),
        ],
        [
            vmem(((halves + 1) * block, LANES), F32),
            vmem((6, halves + 1, 64, LANES), F32),
            vmem((6, halves * 64, LANES), F32),
            node_rows,
        ],
        [
            base, grads, hot_two, neighbours, codes, one_2_to_3, one_1_to_3,
            *beside_1, *beside_2, two_1_to_3,
        ],
        cost=SOUND_COST,
    )
    (sound_out,) = call(
        sound_two_kernel,
        [shape(sound.shape, F32)],
        [],
        [sound, base, grads, scale, two_2_to_3, two_1_to_3],
    )
    return flow_out[None], mean_out[None], sound_out[None]


def solution(mesh):
    placed = (
        P("grp", None, "sfc", None),
        P("grp", None, "sfc", None),
        P("grp", "sfc", None),
        P("grp", None, "sfc"),
        P("grp", "sfc"),
        P(),
        P("grp", None, None, "sfc"),
        P("grp", None, "sfc"),
        P("grp", None, "sfc"),
    )
    return jax.shard_map(
        body,
        mesh=mesh,
        in_specs=placed,
        out_specs=(
            P("grp", None, "sfc", None),
            P("grp", None, "sfc", None),
            P("grp", None, None, "sfc"),
        ),
        check_vma=False,
    )
```

```python
import jax
import jax.numpy as jnp
import numpy as np
from jax import lax
from jax.experimental import pallas as pl
from jax.experimental.pallas import tpu as pltpu
from jax.sharding import PartitionSpec as P

HW = 16
HE = 16

ADVECT = 0.1
RELAX = 0.1
PENALTY = 1.5
ACOUSTIC_STEP = 0.08

LANES = 128
EDGE = 3 * HW
NO_LINK = 64
FIELD_ORDER = (1, 2, 3, 0, 4)
ALL_FIELDS = ((0, 2), (2, 4), (4, 5))
BASE = 32.0
EXTRA = 16
PACK_COST, SECOND_COST, OUTPUT_COST, SOUND_COST = 10**10, 10**10, 10**9, 10**9
VMEM_LIMIT = 20 * 1024 * 1024
PACK_LIMIT = 60 * 1024 * 1024

F32 = jnp.float32
BF16 = jnp.bfloat16


def lobatto_matrix():
    points = np.array([-1.0, -1.0 / np.sqrt(5.0), 1.0 / np.sqrt(5.0), 1.0])
    weights = np.array(
        [
            1.0 / np.prod([points[col] - points[other] for other in range(4) if other != col])
            for col in range(4)
        ]
    )
    matrix = np.zeros((4, 4))
    for line in range(4):
        for col in range(4):
            if line != col:
                matrix[line, col] = weights[col] / weights[line] / (points[line] - points[col])
        matrix[line, line] = -matrix[line].sum()
    return matrix.astype(np.float32)


def face_nodes(face):
    axis, level = face // 2, 3 * (face % 2)
    nodes = []
    for second in range(4):
        for first in range(4):
            coords = [first, second]
            coords.insert(axis, level)
            nodes.append(coords[0] + 4 * coords[1] + 16 * coords[2])
    return nodes


def turned_position(turn, position):
    a, b = position % 4, position // 4
    a, b = ((a, b), (3 - b, a), (3 - a, 3 - b), (b, 3 - a))[turn]
    return a + 4 * b


def split_parts(x):
    high = x.astype(BF16)
    return high, (x - high.astype(F32)).astype(BF16)


def dot(a, b):
    return jnp.dot(a, b, preferred_element_type=F32)


def dot_t(a, b):
    return lax.dot_general(a, b, (((1,), (1,)), ((), ())), preferred_element_type=F32)


def on_flow_row():
    return lax.axis_index("grp") < lax.axis_size("grp") - 1


def on_even_column():
    return lax.rem(lax.axis_index("sfc"), 2) == 0


def pack_kernel(
    flow, visc, links, sound, neighbours, codes,
    out_a, out_b, links_in, faces_in, staged, sems, link_sems,
):
    is_flow, even = on_flow_row(), on_even_column()
    tiles = flow.shape[1]
    _, nodes, elements = sound.shape
    outs = (out_a, out_b)

    @pl.when(is_flow)
    def _():
        fetch = pltpu.make_async_copy(links, links_in, link_sems.at[0])
        fetch.start()
        copies = []
        for side in range(2):
            off = pl.multiple_of(jnp.where(even == (side == 0), 0, tiles - EDGE), 8)
            for place, f in enumerate(FIELD_ORDER):
                copies.append(
                    pltpu.make_async_copy(
                        flow.at[f, pl.ds(off, EDGE), :],
                        staged.at[side, pl.ds(place * EDGE, EDGE), :],
                        sems.at[side, place],
                    )
                )
            copies.append(
                pltpu.make_async_copy(
                    visc.at[pl.ds(off, EDGE), :],
                    staged.at[side, pl.ds(5 * EDGE, EDGE), :],
                    sems.at[side, 5],
                )
            )
        for copy in copies:
            copy.start()
        fetch.wait()
        given = links_in[...]
        own = lax.axis_index("sfc") * tiles + lax.broadcasted_iota(jnp.int32, given.shape, 1)
        offset = jnp.where(given < 0, 0, given - own).astype(F32)
        low, high = offset[:, :LANES], offset[:, tiles - LANES :]
        pad = jnp.zeros((EXTRA - 4, LANES), F32)
        for side, (a, b) in enumerate(((low, high), (high, low))):
            block = jnp.concatenate([jnp.where(even, a, b), pad], 0)
            outs[side][6 * EDGE :, :] = block.astype(BF16)
        for copy in copies:
            copy.wait()
        for side in range(2):
            outs[side][: 6 * EDGE, :] = staged[side].astype(BF16)

    @pl.when(jnp.logical_not(is_flow))
    def _():
        copies = []
        for side in range(2):
            off = pl.multiple_of(jnp.where(even == (side == 0), 0, elements - LANES), LANES)
            for v in range(4):
                copies.append(
                    pltpu.make_async_copy(
                        sound.at[v, :, pl.ds(off, LANES)],
                        staged.at[side, pl.ds(v * nodes, nodes), :],
                        sems.at[side, v],
                    )
                )
        for at, ref in enumerate((neighbours, codes)):
            copies.append(pltpu.make_async_copy(ref, faces_in.at[at], link_sems.at[at]))
        for copy in copies:
            copy.start()
        for copy in copies:
            copy.wait()
        first = lax.axis_index("sfc") * elements
        own = first + lax.broadcasted_iota(jnp.int32, (1, elements), 1)
        for face in range(6):
            link = faces_in[0, face]
            offset = jnp.where(link < 0, NO_LINK, link - own).astype(F32)
            for at, row in enumerate((offset, faces_in[1, face].astype(F32))):
                line = 4 * nodes + 6 * at + face
                low, high = row[:, :LANES], row[:, elements - LANES :]
                staged[0, line : line + 1, :] = jnp.where(even, low, high)
                staged[1, line : line + 1, :] = jnp.where(even, high, low)
        used = 4 * nodes + 12
        for side, out in enumerate(outs):
            staged[side, used:, :] = jnp.zeros((staged.shape[1] - used, LANES), F32)
            out[: 6 * EDGE, :] = staged[side].astype(BF16)
            out[6 * EDGE :, :] = jnp.zeros((out.shape[0] - 6 * EDGE, LANES), BF16)


class FlowPlan:
    def __init__(self, tiles):
        self.tiles = tiles
        self.wide = tiles + 2 * EDGE
        self.blocks = 4
        self.rows = (tiles + 4 * HW) // self.blocks
        self.span = self.rows + 2 * HW

    def at(self, b):
        return HW + b * self.rows

    def inner(self):
        return range(1, self.blocks - 1)


def columns_of(place):
    return slice(place * LANES, (place + 1) * LANES)


def rows_between(parts, low, high, columns):
    taken = []
    for start, ref in parts:
        a, b = max(low, start), min(high, start + ref.shape[0])
        if a < b:
            taken.append(ref[a - start : b - start, columns])
    return taken[0] if len(taken) == 1 else jnp.concatenate(taken, 0)


def put(high, low, at, place, value):
    h, l = split_parts(value)
    high[at : at + value.shape[0], columns_of(place)] = h
    low[at : at + value.shape[0], columns_of(place)] = l


def east_west(x):
    return pltpu.roll(x, LANES - 1, 1), pltpu.roll(x, 1, 1)


def link_matrix(plan, offset, mat):
    rows, span = plan.rows, plan.span
    lane = lax.broadcasted_iota(jnp.int32, (rows, 2 * span), 1)
    lane = jnp.where(lane >= span, lane - span, lane)
    place = HW + lax.broadcasted_iota(jnp.int32, (rows, LANES), 0) + offset.astype(jnp.int32)
    hot = [jnp.where(place[:, k : k + 1] == lane, F32(1.0), F32(0.0)) for k in range(4)]
    mat[:rows, :] = (hot[0] + hot[1] + hot[2] + hot[3]).astype(BF16)
    mat[rows : 2 * rows, :] = (hot[0] - hot[1]).astype(BF16)
    mat[2 * rows :, :] = (hot[2] - hot[3]).astype(BF16)


def gathered(plan, mat, high, low, b, columns, at_row):
    at = b * plan.rows
    both = [rows_between(x, at, at + plan.span, columns) for x in (high, low)]
    return dot(mat[at_row:, :], jnp.concatenate(both, 0))


def advance(plan, b, mat, high, low, state, v, places, new_state, new_high, new_low, new_at, split):
    rows = plan.rows
    center = [state(k) for k in range(3)]
    scaled = [(0.5 * ADVECT) * c for c in center]
    for first, last in places:
        got = gathered(plan, mat, high, low, b, slice(first * LANES, last * LANES), 0)
        for place in range(first, last):
            inner = columns_of(place - first)
            total, dy, dz = got[:rows, inner], got[rows : 2 * rows, inner], got[2 * rows :, inner]
            c = center[place] if place < 3 else state(place)
            east, west = east_west(c)
            new = (
                c
                + v * (east + west + total - 6.0 * c)
                - (scaled[0] * (east - west) + scaled[1] * dy + scaled[2] * dz)
            )
            new_state[new_at : new_at + rows, columns_of(place)] = new
            if split:
                put(new_high, new_low, new_at, place, new)


def lamb_block(plan, b, mat, high, low, state, average, average_out, packed):
    rows = plan.rows
    center = [state(k) for k in range(3)]
    got = [
        gathered(plan, mat, high, low, b, slice(0, 2 * LANES), rows),
        gathered(plan, mat, high, low, b, slice(2 * LANES, 3 * LANES), rows),
    ]
    d1, d2, d3 = [], [], []
    for k in range(3):
        east, west = east_west(center[k])
        d1.append((east - west) * 0.5)
        inner = columns_of(k % 2)
        d2.append(got[k // 2][:rows, inner] * 0.5)
        d3.append(got[k // 2][rows:, inner] * 0.5)
    vx = d2[2] - d3[1]
    vy = d3[0] - d1[2]
    vz = d1[1] - d2[0]
    lamb = (
        vy * center[2] - vz * center[1],
        vz * center[0] - vx * center[2],
        vx * center[1] - vy * center[0],
    )
    to = plan.at(b) - EDGE
    low_row, top_row = max(0, -to), min(rows, plan.tiles - to)
    own = slice(to + low_row, to + top_row)
    for i in range(3):
        packed[i, own, :] = lamb[i][low_row:top_row]
        mixed = (1.0 - RELAX) * average[i, own, :] + RELAX * center[i][low_row:top_row]
        average_out[i, own, :] = mixed
        packed[3 + i, own, :] = mixed


def element_sums(projector, packed, hits, pay, own_ref, next_ref):
    nodes = projector.shape[0]
    count, elements = own_ref.shape
    proj_high, proj_low = split_parts(projector[...])
    proj_both = jnp.concatenate(
        [
            jnp.concatenate([proj_high, proj_high], 1),
            jnp.concatenate([proj_low, jnp.zeros_like(proj_low)], 1),
        ],
        0,
    )
    for c in range(6):
        x_high, x_low = split_parts(packed[c])
        main = dot_t(proj_both, jnp.concatenate([x_high, x_low], 1))
        pay[c * nodes : (c + 1) * nodes, :] = (main[:nodes] + main[nodes:]).astype(BF16)
    if count > 6 * nodes:
        pay[6 * nodes :, :] = jnp.ones((count - 6 * nodes, pay.shape[1]), BF16)
    sums = dot_t(pay[...], hits[...])
    if count > 6 * nodes:
        tail = sums[6 * nodes :]
        line = lax.broadcasted_iota(jnp.int32, tail.shape, 0)
        big = jnp.floor(tail * (1.0 / BASE))
        tail = jnp.where(line == 0, tail - BASE * big, jnp.where(line == 1, big, 0.0))
        sums = jnp.concatenate([sums[: 6 * nodes], tail], 0)
    own_ref[...] = sums[:, :elements]
    next_ref[...] = sums[:, elements:].astype(BF16)


def inner_kernel(
    flow, visc, links, target,
    inner_state, inner_high, inner_low, lcol, inner_mats, hits, high0, low0, square,
):
    plan = FlowPlan(flow.shape[1])
    tiles, rows = plan.tiles, plan.rows

    @pl.when(on_flow_row())
    def _():
        column = lax.axis_index("sfc")
        first_tile, first_element = column * tiles, column * (hits.shape[0] // 2)
        for place, f in enumerate(FIELD_ORDER):
            put(high0, low0, 0, place, flow[f])
        square[...] = jnp.zeros_like(square)
        own_tile = first_tile + lax.broadcasted_iota(jnp.int32, links.shape, 1)
        offset = jnp.where(links[...] < 0, 0, links[...] - own_tile).astype(F32)
        for part in range(tiles // LANES):
            square[:4, :] = offset[:, part * LANES : (part + 1) * LANES]
            lcol[part * LANES : (part + 1) * LANES, :] = square[...].T
        local = target[...] - first_element
        hits[...] = jnp.where(
            lax.broadcasted_iota(jnp.int32, hits.shape, 0) == local, F32(1.0), F32(0.0)
        ).astype(BF16)
        for at, b in enumerate(plan.inner()):
            own = slice(plan.at(b) - EDGE, plan.at(b) - EDGE + rows)
            link_matrix(plan, lcol[own, :], inner_mats.at[at])
            advance(
                plan, b, inner_mats.at[at], [(EDGE, high0)], [(EDGE, low0)],
                lambda place, own=own: flow[FIELD_ORDER[place], own, :],
                visc[own, :], ALL_FIELDS, inner_state, inner_high, inner_low, at * rows, True,
            )


def band_parts(plan, edge, inner):
    rows, last = plan.rows, plan.blocks - 1
    return [
        (plan.at(0), edge.at[:rows]),
        (plan.at(1), inner),
        (plan.at(last), edge.at[rows:]),
    ]


def band_state(plan, b, edge, inner):
    at = plan.at(b)
    parts = band_parts(plan, edge, inner)
    return lambda place: rows_between(parts, at, at + plan.rows, columns_of(place))


def closed(plan, parts, zero):
    return [(0, zero), *parts, (plan.wide - HW, zero)]


def mats_of(plan, b, edge_mats, inner_mats):
    if b in plan.inner():
        return inner_mats.at[b - 1]
    return edge_mats.at[0 if b == 0 else 1]


def first_kernel(
    flow, visc, mean, projector, part_a, part_b, sound, neighbours, codes,
    inner_state, inner_high, inner_low, lcol, inner_mats, hits,
    own_one, next_one, mean_one, base, grads, hot_two,
    edge_state, edge_high, edge_low, edge_mats, edge_visc,
    square, state0, high0, low0, zero, packed, pay, rows_of, facing, remote, rhs,
):
    is_flow, even = on_flow_row(), on_even_column()
    plan = FlowPlan(packed.shape[1])
    tiles, rows, span = plan.tiles, plan.rows, plan.span
    own_rows = span - EDGE

    @pl.when(is_flow)
    def _():
        def pick(at, size):
            a, b = part_a[at : at + size, :].astype(F32), part_b[at : at + size, :].astype(F32)
            return jnp.where(even, a, b), jnp.where(even, b, a)

        zero[...] = jnp.zeros_like(zero)
        for place, f in enumerate(FIELD_ORDER):
            before, after = pick(place * EDGE, EDGE)
            ends = (
                jnp.concatenate([before, flow[f, :own_rows, :]], 0),
                jnp.concatenate([flow[f, tiles - own_rows :, :], after], 0),
            )
            for side in range(2):
                state0[side, :, columns_of(place)] = ends[side]
                put(high0.at[side], low0.at[side], 0, place, ends[side])
        before, after = pick(5 * EDGE, EDGE)
        edge_visc[:rows, :] = jnp.concatenate([before[HW:], visc[: rows - EDGE + HW, :]], 0)
        edge_visc[rows:, :] = jnp.concatenate(
            [visc[tiles - (rows - EDGE + HW) :, :], after[: EDGE - HW]], 0
        )
        before, after = pick(6 * EDGE, EXTRA)
        given = []
        for side, block in enumerate((before, after)):
            square[...] = jnp.zeros_like(square)
            square[:EXTRA, :] = block
            turned = square[...].T
            given.append(
                jnp.concatenate([turned[LANES - EDGE + HW :], lcol[: rows - EDGE + HW, :]], 0)
                if side == 0
                else jnp.concatenate(
                    [lcol[tiles - (rows - EDGE + HW) :, :], turned[: EDGE - HW]], 0
                )
            )
        for side, b in enumerate((0, plan.blocks - 1)):
            link_matrix(plan, given[side], edge_mats.at[side])
            advance(
                plan, b, edge_mats.at[side],
                [(b * rows, high0.at[side])], [(b * rows, low0.at[side])],
                lambda place, side=side: state0[side, HW : HW + rows, columns_of(place)],
                edge_visc[side * rows : (side + 1) * rows, :], ALL_FIELDS,
                edge_state, edge_high, edge_low, side * rows, True,
            )
        high1 = closed(plan, band_parts(plan, edge_high, inner_high), zero)
        low1 = closed(plan, band_parts(plan, edge_low, inner_low), zero)
        for b in range(plan.blocks):
            lamb_block(
                plan, b, mats_of(plan, b, edge_mats, inner_mats), high1, low1,
                band_state(plan, b, edge_state, inner_state), mean, mean_one, packed,
            )
        element_sums(projector, packed, hits, pay, own_one, next_one)

    @pl.when(jnp.logical_not(is_flow))
    def _():
        own_one[...] = jnp.zeros_like(own_one)
        next_one[...] = jnp.zeros_like(next_one)
        nodes, elements = sound.shape[1:]
        halves = elements // LANES
        block = 4 * nodes
        for v in range(4):
            for h in range(halves):
                rows_of[h * block + v * nodes : h * block + (v + 1) * nodes, :] = sound[
                    v, :, h * LANES : (h + 1) * LANES
                ]
        a, b = part_a[:block, :].astype(F32), part_b[:block, :].astype(F32)
        before, after = jnp.where(even, a, b), jnp.where(even, b, a)
        lane = lax.broadcasted_iota(jnp.int32, (1, LANES), 1)
        beside = lane < LANES // 2
        rows_of[halves * block : (halves + 1) * block, :] = jnp.where(beside, after, before)
        rows_of[(halves + 1) * block : (halves + 2) * block, :] = jnp.zeros_like(before)
        rows_of[(halves + 2) * block : (halves + 3) * block, :] = before
        rows_of[(halves + 3) * block :, :] = after
        a = part_a[block : block + EXTRA, :].astype(F32)
        b = part_b[block : block + EXTRA, :].astype(F32)
        given = jnp.where(beside, jnp.where(even, b, a), jnp.where(even, a, b)).astype(jnp.int32)
        own_parts = [0, 1, halves + 2, halves + 3]
        first = lax.axis_index("sfc") * elements
        masks = []
        for face in range(6):
            for at, part in enumerate(own_parts):
                facing_rows(rows_of, part * block, nodes, face ^ 1, facing.at[face, at])
            link, code = neighbours[face], codes[face]
            offset, extra_code = given[face : face + 1, :], given[6 + face : 7 + face, :]
            extra = jnp.where(beside, elements + lane, lane - LANES) + offset
            near = jnp.concatenate([link - first, extra], 1)
            valid = jnp.concatenate([link, jnp.where(offset >= NO_LINK, -1, 0)], 1) >= 0
            place = jnp.where(
                near < 0, elements + LANES + near, jnp.where(near < elements, near, near + LANES)
            )
            hot = hot_columns(jnp.where(valid, place, -1), elements + 2 * LANES)
            remote_rows([facing[face, at] for at in range(4)], hot, remote, face)
            near = link - first
            place = jnp.where(near < 0, elements + LANES + near, near)
            hot_two[face] = hot_columns(jnp.where(link < 0, -1, place), elements + LANES)
            masks.append(
                (
                    face_masks(link[:, :LANES], link[:, LANES:], code[:, :LANES], code[:, LANES:]),
                    face_masks(
                        jnp.where(offset >= NO_LINK, -1, 0), jnp.full((1, LANES), -1, jnp.int32),
                        extra_code, extra_code,
                    ),
                )
            )
        for group in range(2):
            start = group * halves * block
            derivatives(rows_of, start, nodes, grads)
            rhs[...] = jnp.zeros_like(rhs)
            add_faces(
                rows_of, start, nodes, remote, group * halves * 64, [m[group] for m in masks], rhs
            )
            for n in range(nodes):
                base[pl.ds(start + n, 8, stride=nodes), :] = (
                    node_of(rows_of, start, nodes, n) + ACOUSTIC_STEP * rhs[n]
                )


def second_block(plan, b, carried, visc, places, new_state, new_parts):
    (inner_state, inner_high, inner_low, inner_mats, edge_state, edge_high, edge_low, edge_mats,
     edge_visc, zero) = carried
    rows = plan.rows
    if b in plan.inner():
        v = visc[plan.at(b) - EDGE : plan.at(b) - EDGE + rows, :]
    else:
        v = edge_visc[:rows, :] if b == 0 else edge_visc[rows:, :]
    advance(
        plan, b, mats_of(plan, b, edge_mats, inner_mats),
        closed(plan, band_parts(plan, edge_high, inner_high), zero),
        closed(plan, band_parts(plan, edge_low, inner_low), zero),
        band_state(plan, b, edge_state, inner_state), v, places,
        new_state, *new_parts, b * rows, new_parts[0] is not None,
    )


def second_kernel(
    visc, mean, mean_one, projector,
    inner_state, inner_high, inner_low, inner_mats, hits,
    edge_state, edge_high, edge_low, edge_mats, edge_visc,
    state, mean_two, own_two, next_two,
    high, low, zero, packed, pay,
):
    plan = FlowPlan(packed.shape[1])
    rows = plan.rows
    is_flow = on_flow_row()

    @pl.when(jnp.logical_not(is_flow))
    def _():
        own_two[...] = jnp.zeros_like(own_two)
        next_two[...] = jnp.zeros_like(next_two)

    @pl.when(is_flow)
    def _():
        zero[...] = jnp.zeros_like(zero)
        carried = (
            inner_state, inner_high, inner_low, inner_mats,
            edge_state, edge_high, edge_low, edge_mats, edge_visc, zero,
        )
        for b in range(plan.blocks):
            second_block(plan, b, carried, visc, ((0, 2), (2, 3)), state, (high, low))
        for b in range(plan.blocks):
            lamb_block(
                plan, b, mats_of(plan, b, edge_mats, inner_mats),
                closed(plan, [(HW, high)], zero), closed(plan, [(HW, low)], zero),
                lambda place, b=b: state[b * rows : (b + 1) * rows, columns_of(place)],
                mean_one, mean_two, packed,
            )
        element_sums(projector, packed, hits, pay, own_two, next_two)


def output_kernel(
    flow, visc, mean, state, mean_two,
    inner_state, inner_high, inner_low, inner_mats,
    edge_state, edge_high, edge_low, edge_mats, edge_visc, after, after_up, after_down, own_one,
    flow_out, mean_out, own_one_out, passive, zero,
):
    plan = FlowPlan(flow.shape[1])
    is_flow = on_flow_row()
    own_one_out[...] = own_one[...]

    @pl.when(jnp.logical_not(is_flow))
    def _():
        flow_out[...] = flow[...]
        mean_out[...] = mean[...]

    @pl.when(is_flow)
    def _():
        zero[...] = jnp.zeros_like(zero)
        mean_out[...] = mean_two[...]
        carried = (
            inner_state, inner_high, inner_low, inner_mats,
            edge_state, edge_high, edge_low, edge_mats, edge_visc, zero,
        )
        own = slice(EDGE - HW, EDGE - HW + plan.tiles)
        for place in range(3):
            flow_out[FIELD_ORDER[place]] = state[own, columns_of(place)]
        for b in range(plan.blocks):
            second_block(plan, b, carried, visc, ((3, 5),), passive, (None, None))
        for place in (3, 4):
            flow_out[FIELD_ORDER[place]] = passive[own, columns_of(place)]


def facing_rows(rows_of, base, nodes, face, to):
    axis, level = face // 2, 3 * (face % 2)
    if axis == 0:
        to[...] = rows_of[pl.ds(base + level, 64, stride=4), :]
    elif axis == 1:
        for i in range(4):
            to[pl.ds(i, 16, stride=4), :] = rows_of[pl.ds(base + i + 4 * level, 16, stride=16), :]
    else:
        for v in range(4):
            at = base + v * nodes + 16 * level
            to[v * 16 : (v + 1) * 16, :] = rows_of[at : at + 16, :]


def hot_columns(place, size):
    key = lax.broadcasted_iota(jnp.int32, (size, place.shape[1]), 0)
    return jnp.where(key == place, F32(1.0), F32(0.0)).astype(BF16)


def node_of(rows_of, start, nodes, n):
    return rows_of[pl.ds(start + n, 8, stride=nodes), :]


def remote_rows(parts, hot, remote, face):
    high, low = split_parts(jnp.concatenate(parts, 1))
    got = dot(jnp.concatenate([high, low], 0), hot)
    got = got[:64] + got[64:]
    for h in range(got.shape[1] // LANES):
        remote[face, h * 64 : (h + 1) * 64, :] = got[:, h * LANES : (h + 1) * LANES]


def derivatives(rows_of, start, nodes, grads_out):
    matrix = lobatto_matrix()
    node = [node_of(rows_of, start, nodes, n) for n in range(nodes)]
    for n in range(nodes):
        i, j, k = n % 4, n // 4 % 4, n // 16
        lines = (
            [m + 4 * j + 16 * k for m in range(4)],
            [i + 4 * m + 16 * k for m in range(4)],
            [i + 4 * j + 16 * m for m in range(4)],
        )
        for d, at in enumerate((i, j, k)):
            total = None
            for m in range(4):
                if abs(matrix[at, m]) > 1e-12:
                    term = F32(matrix[at, m]) * node[lines[d][m]]
                    total = term if total is None else total + term
            grads_out[d, pl.ds(start + n, 8, stride=nodes), :] = total


def face_masks(link_low, link_high, code_low, code_high):
    upper = lax.broadcasted_iota(jnp.int32, (8, LANES), 0) >= 4

    def both(low, high):
        return jnp.where(
            upper, jnp.broadcast_to(high, (8, LANES)), jnp.broadcast_to(low, (8, LANES))
        )

    code = both(code_low, code_high)
    return both(link_low, link_high) >= 0, [code == t for t in range(3)]


def add_faces(rows_of, start, nodes, remote, remote_start, masks, rhs):
    for face in range(6):
        valid, is_turn = masks[face]
        planes = [remote[face, pl.ds(remote_start + p, 8, stride=16), :] for p in range(16)]
        for p, n in enumerate(face_nodes(face)):
            turned = planes[turned_position(3, p)]
            for t in range(3):
                turned = jnp.where(is_turn[t], planes[turned_position(t, p)], turned)
            jump = jnp.where(valid, turned - node_of(rows_of, start, nodes, n), 0.0)
            rhs[n] = rhs[n] + PENALTY * jump


def with_sources(total, columns, block, nodes, base, grads):
    def rows_at(v):
        return slice((block * 4 + v) * nodes, (block * 4 + v + 1) * nodes)

    for v in range(4):
        rows = rows_at(v)
        if v:
            added = grads[v - 1, rows_at(0), :] + total[(v - 1) * nodes : v * nodes, columns]
        else:
            added = sum(grads[d, rows_at(1 + d), :] for d in range(3))
        for d in range(3):
            added = added + total[(3 + d) * nodes : (4 + d) * nodes, columns] * grads[d, rows, :]
        yield v, rows, base[rows, :] - ACOUSTIC_STEP * added


def gated_sum_kernel(own, *refs):
    *others, _, out = refs

    @pl.when(on_flow_row())
    def _():
        total = own[...]
        for other in others:
            total = total + other[...].astype(F32)
        out[...] = total.astype(BF16)


def border_kernel(sums, up, down):
    nodes_rows = (sums.shape[0] - EXTRA) // (LANES // HE)
    group = lax.broadcasted_iota(jnp.int32, (1, LANES), 1) // HE
    for out, tile, shift in ((up, sums.shape[1] - LANES, HE), (down, 0, 0)):
        columns = slice(tile, tile + LANES)
        total = jnp.zeros((nodes_rows, LANES), F32)
        for i in range(LANES // HE):
            x = sums[i * nodes_rows : (i + 1) * nodes_rows, columns].astype(F32)
            turn = (HE * i + shift) % LANES
            x = pltpu.roll(x, turn, 1) if turn else x
            total = jnp.where(group == i, x, total)
        out[:nodes_rows, :] = total.astype(BF16)
        x = sums[sums.shape[0] - EXTRA :, columns].astype(F32)
        x = pltpu.roll(x, shift, 1) if shift else x
        out[nodes_rows:, :] = jnp.where(group == 0, x, 0.0).astype(BF16)


def border_sums(up, down):
    lines = up.shape[0] - EXTRA
    lane = lax.broadcasted_iota(jnp.int32, (1, LANES), 1)
    parts = []
    for i in range(LANES // HE + 1):
        rows = slice(0, lines) if i < LANES // HE else slice(lines, lines + EXTRA)
        at = HE * (i % (LANES // HE))
        x = pltpu.roll(up[rows], (2 * LANES - HE - at) % LANES, 1)
        y = pltpu.roll(down[rows], (LANES - at) % LANES, 1) if at else down[rows]
        parts.append(jnp.where(lane >= LANES - HE, x, jnp.where(lane < HE, y, 0.0)))
    return jnp.concatenate(parts, 0)


def scaled_sums(total, nodes):
    count = total[6 * nodes : 6 * nodes + 1] + BASE * total[6 * nodes + 1 : 6 * nodes + 2]
    inverse = 1.0 / jnp.maximum(count, 1.0)
    return total[: 6 * nodes] * inverse, inverse


def sound_one_kernel(
    base, grads, hot_two, neighbours, codes, source_a, source_b, up_a, down_a, up_b, down_b, after,
    base_two, grads_two, scale_out, rows_of, facing, remote, rhs,
):
    elements = source_a.shape[1]
    halves = elements // LANES
    nodes = base_two.shape[0] // (4 * halves)
    block = 4 * nodes

    @pl.when(jnp.logical_not(on_flow_row()))
    def _():
        own, inverse = scaled_sums(source_a[...].astype(F32) + source_b[...].astype(F32), nodes)
        scale_out[...] = jnp.broadcast_to(inverse, scale_out.shape)
        extra = border_sums(
            up_a[...].astype(F32) + up_b[...].astype(F32),
            down_a[...].astype(F32) + down_b[...].astype(F32),
        )
        extra, _ = scaled_sums(extra, nodes)
        for h in range(halves + 1):
            total, columns = (own, columns_of(h)) if h < halves else (extra, columns_of(0))
            for _, rows, new in with_sources(total, columns, h, nodes, base, grads):
                rows_of[rows, :] = new
        masks = []
        for face in range(6):
            for part in range(halves + 1):
                facing_rows(rows_of, part * block, nodes, face ^ 1, facing.at[face, part])
            remote_rows(
                [facing[face, part] for part in range(halves + 1)], hot_two[face], remote, face
            )
            link, code = neighbours[face], codes[face]
            masks.append(
                face_masks(link[:, :LANES], link[:, LANES:], code[:, :LANES], code[:, LANES:])
            )
        derivatives(rows_of, 0, nodes, grads_two)
        rhs[...] = jnp.zeros_like(rhs)
        add_faces(rows_of, 0, nodes, remote, 0, masks, rhs)
        for n in range(nodes):
            base_two[pl.ds(n, 8, stride=nodes), :] = (
                node_of(rows_of, 0, nodes, n) + ACOUSTIC_STEP * rhs[n]
            )


def sound_two_kernel(sound, base, grads, scale, source_a, source_b, out):
    nodes = sound.shape[1]
    is_flow = on_flow_row()

    @pl.when(is_flow)
    def _():
        out[...] = sound[...]

    @pl.when(jnp.logical_not(is_flow))
    def _():
        total = (source_a[...].astype(F32) + source_b[...].astype(F32)) * scale[0:1, :]
        for h in range(sound.shape[2] // LANES):
            for v, _, new in with_sources(total, columns_of(h), h, nodes, base, grads):
                out[v, :, columns_of(h)] = new


def call(kernel, outs, scratch, operands, cost=None, in_hbm=(), limit=VMEM_LIMIT):
    spaces = [pltpu.HBM if at in in_hbm else pltpu.VMEM for at in range(len(operands))]
    moved = sum(int(np.prod(x.shape)) * x.dtype.itemsize for x in (*operands, *outs))
    return pl.pallas_call(
        kernel,
        out_shape=tuple(outs),
        in_specs=[pl.BlockSpec(memory_space=space) for space in spaces],
        out_specs=tuple([pl.BlockSpec(memory_space=pltpu.VMEM)] * len(outs)),
        scratch_shapes=scratch,
        compiler_params=pltpu.CompilerParams(vmem_limit_bytes=limit),
        cost_estimate=pl.CostEstimate(flops=10**8 if cost is None else cost, bytes_accessed=moved if cost is None else 0, transcendentals=0),
    )(*operands)


def body(
    flow_fields,
    mean_velocity,
    cell_eddy_viscosity,
    tile_links,
    tile_target,
    projector,
    acoustic_state,
    element_face_neighbours,
    face_codes,
):
    groups = lax.axis_size("grp")
    count = lax.axis_size("sfc")
    flow = flow_fields[0]
    mean = mean_velocity[0]
    visc = cell_eddy_viscosity[0]
    links = tile_links[0]
    sound = acoustic_state[0]
    faces, span = element_face_neighbours.shape[1:]
    neighbours = element_face_neighbours.reshape(faces, 1, span)
    codes = face_codes.reshape(faces, 1, span)
    tiles = flow.shape[1]
    _, nodes, elements = sound.shape
    halves = elements // LANES
    block = 4 * nodes
    plan = FlowPlan(tiles)
    shape = jax.ShapeDtypeStruct
    vmem = pltpu.VMEM
    pairs_a = [p for i in range(1, count - 1, 2) for p in ((i, i + 1), (i + 1, i))]
    pairs_b = [p for i in range(0, count - 1, 2) for p in ((i, i + 1), (i + 1, i))]

    edge_rows = 6 * EDGE + EXTRA
    pack_a, pack_b = call(
        pack_kernel,
        [shape((edge_rows, LANES), BF16)] * 2,
        [
            vmem(links.shape, jnp.int32),
            vmem((2, *neighbours.shape), jnp.int32),
            vmem((2, 6 * EDGE, LANES), F32),
            pltpu.SemaphoreType.DMA((2, 6)),
            pltpu.SemaphoreType.DMA((2,)),
        ],
        [flow, visc, links, sound, neighbours, codes],
        in_hbm=(0, 1, 2, 3, 4, 5),
        limit=PACK_LIMIT,
        cost=PACK_COST,
    )
    part_a = lax.ppermute(pack_a, "sfc", pairs_a)
    part_b = lax.ppermute(pack_b, "sfc", pairs_b)

    fields = 5 * LANES
    rows, span = plan.rows, plan.span
    inner_rows = (plan.blocks - 2) * rows
    square = vmem((LANES, LANES), F32)
    packed = vmem((6, tiles, LANES), F32)
    inner_state, inner_high, inner_low, lcol, inner_mats, hits = call(
        inner_kernel,
        [
            shape((inner_rows, fields), F32),
            shape((inner_rows, fields), BF16),
            shape((inner_rows, fields), BF16),
            shape((tiles, LANES), F32),
            shape((plan.blocks - 2, 3 * rows, 2 * span), BF16),
            shape((2 * elements, tiles), BF16),
        ],
        [vmem((tiles, fields), BF16), vmem((tiles, fields), BF16), square],
        [flow, visc, links, tile_target],
    )
    lines = 6 * nodes + EXTRA
    node_rows = vmem((nodes, 8, LANES), F32)
    (
        own_one, next_one, mean_one, base, grads, hot_two,
        edge_state, edge_high, edge_low, edge_mats, edge_visc,
    ) = call(
        first_kernel,
        [
            shape((lines, elements), F32),
            shape((lines, elements), BF16),
            shape(mean.shape, F32),
            shape(((halves + 2) * block, LANES), F32),
            shape((3, (halves + 2) * block, LANES), F32),
            shape((6, elements + LANES, elements), BF16),
            shape((2 * rows, fields), F32),
            shape((2 * rows, fields), BF16),
            shape((2 * rows, fields), BF16),
            shape((2, 3 * rows, 2 * span), BF16),
            shape((2 * rows, LANES), F32),
        ],
        [
            square,
            vmem((2, span, fields), F32),
            vmem((2, span, fields), BF16),
            vmem((2, span, fields), BF16),
            vmem((HW, fields), BF16),
            packed,
            vmem((lines, tiles), BF16),
            vmem(((halves + 4) * block, LANES), F32),
            vmem((6, 4, 64, LANES), F32),
            vmem((6, (halves + 2) * 64, LANES), F32),
            node_rows,
        ],
        [
            flow, visc, mean, projector, part_a, part_b, sound, neighbours, codes,
            inner_state, inner_high, inner_low, lcol, inner_mats, hits,
        ],
    )

    up = [(i, i + 1) for i in range(count - 1)]

    def climb(x):
        chosen = [(g * count + i, g * count + j) for g in range(groups - 1) for i, j in up]
        return lax.ppermute(x, ("grp", "sfc"), chosen)

    def combined(*xs):
        total = xs[0]
        for x in xs[1:]:
            total = total + x.astype(F32)
        return total.astype(BF16)

    got_one = climb(next_one)
    band = plan.blocks * rows
    velocity = 3 * LANES
    step_one = [inner_state, inner_high, inner_low, inner_mats]
    edges = [edge_state, edge_high, edge_low, edge_mats, edge_visc]
    state_two, mean_two, own_two, next_two = call(
        second_kernel,
        [
            shape((band, velocity), F32),
            shape(mean.shape, F32),
            shape((6 * nodes, elements), F32),
            shape((6 * nodes, elements), BF16),
        ],
        [
            vmem((band, velocity), BF16),
            vmem((band, velocity), BF16),
            vmem((HW, fields), BF16),
            packed,
            vmem((6 * nodes, tiles), BF16),
        ],
        [visc, mean, mean_one, projector, *step_one, hits, *edges],
        cost=SECOND_COST,
    )
    last = (groups - 1) * count
    lines_beside = 6 * nodes // (LANES // HE) + EXTRA

    def borders(sums, row):
        up_border, down_border = call(
            border_kernel, [shape((lines_beside, LANES), BF16)] * 2, [], [sums], cost=0
        )
        start = row * count
        return up_border, [
            lax.ppermute(
                up_border, ("grp", "sfc"), [(start + i, last + i + 1) for i in range(count - 1)]
            ),
            lax.ppermute(
                down_border, ("grp", "sfc"), [(start + i, last + i - 1) for i in range(1, count)]
            ),
        ]

    got_two = climb(next_two)
    sum_one_2 = combined(own_one, got_one)
    one_0_to_1 = lax.ppermute(sum_one_2, "grp", [(0, 1)])
    _, beside_2 = borders(sum_one_2, 2)
    sum_two_1 = combined(own_two, got_two)
    two_0_to_2 = lax.ppermute(sum_two_1, "grp", [(0, 2)])
    one_2_to_3 = lax.ppermute(sum_one_2, "grp", [(2, 3)])
    two_1_to_3 = lax.ppermute(sum_two_1, "grp", [(1, 3)])
    flow_out, mean_out, own_one = call(
        output_kernel,
        [shape(flow.shape, F32), shape(mean.shape, F32), shape(own_one.shape, F32)],
        [vmem((band, fields), F32), vmem((HW, fields), BF16)],
        [flow, visc, mean, state_two, mean_two, *step_one, *edges, sum_two_1, *beside_2, own_one],
        cost=OUTPUT_COST,
    )
    sum_one_1 = combined(own_one, got_one, one_0_to_1)
    one_1_to_3 = lax.ppermute(sum_one_1, "grp", [(1, 3)])
    border, beside_1 = borders(sum_one_1, 1)
    (sum_two_2,) = call(
        gated_sum_kernel,
        [shape(own_two.shape, BF16)],
        [],
        [own_two, got_two, two_0_to_2, border],
        cost=0,
    )
    two_2_to_3 = lax.ppermute(sum_two_2, "grp", [(2, 3)])

    base, grads, scale = call(
        sound_one_kernel,
        [
            shape((halves * block, LANES), F32),
            shape((3, halves * block, LANES), F32),
            shape((8, elements), F32),
        ],
        [
            vmem(((halves + 1) * block, LANES), F32),
            vmem((6, halves + 1, 64, LANES), F32),
            vmem((6, halves * 64, LANES), F32),
            node_rows,
        ],
        [
            base, grads, hot_two, neighbours, codes, one_2_to_3, one_1_to_3,
            *beside_1, *beside_2, two_1_to_3,
        ],
        cost=SOUND_COST,
    )
    (sound_out,) = call(
        sound_two_kernel,
        [shape(sound.shape, F32)],
        [],
        [sound, base, grads, scale, two_2_to_3, two_1_to_3],
    )
    return flow_out[None], mean_out[None], sound_out[None]


def solution(mesh):
    placed = (
        P("grp", None, "sfc", None),
        P("grp", None, "sfc", None),
        P("grp", "sfc", None),
        P("grp", None, "sfc"),
        P("grp", "sfc"),
        P(),
        P("grp", None, None, "sfc"),
        P("grp", None, "sfc"),
        P("grp", None, "sfc"),
    )
    return jax.shard_map(
        body,
        mesh=mesh,
        in_specs=placed,
        out_specs=(
            P("grp", None, "sfc", None),
            P("grp", None, "sfc", None),
            P("grp", None, None, "sfc"),
        ),
        check_vma=False,
    )
```

```python
import jax
import jax.numpy as jnp
import numpy as np
from jax import lax
from jax.experimental import pallas as pl
from jax.experimental.pallas import tpu as pltpu
from jax.sharding import PartitionSpec as P

HW = 16
HE = 16

ADVECT = 0.1
RELAX = 0.1
PENALTY = 1.5
ACOUSTIC_STEP = 0.08

LANES = 128
EDGE = 3 * HW
NO_LINK = 64
FIELD_ORDER = (1, 2, 3, 0, 4)
ALL_FIELDS = ((0, 2), (2, 4), (4, 5))
BASE = 32.0
EXTRA = 16
PACK_COST, SECOND_COST, OUTPUT_COST, SOUND_COST = 10**10, 10**10, 10**9, 10**9
VMEM_LIMIT = 20 * 1024 * 1024
PACK_LIMIT = 60 * 1024 * 1024

F32 = jnp.float32
BF16 = jnp.bfloat16


def lobatto_matrix():
    points = np.array([-1.0, -1.0 / np.sqrt(5.0), 1.0 / np.sqrt(5.0), 1.0])
    weights = np.array(
        [
            1.0 / np.prod([points[col] - points[other] for other in range(4) if other != col])
            for col in range(4)
        ]
    )
    matrix = np.zeros((4, 4))
    for line in range(4):
        for col in range(4):
            if line != col:
                matrix[line, col] = weights[col] / weights[line] / (points[line] - points[col])
        matrix[line, line] = -matrix[line].sum()
    return matrix.astype(np.float32)


def face_nodes(face):
    axis, level = face // 2, 3 * (face % 2)
    nodes = []
    for second in range(4):
        for first in range(4):
            coords = [first, second]
            coords.insert(axis, level)
            nodes.append(coords[0] + 4 * coords[1] + 16 * coords[2])
    return nodes


def turned_position(turn, position):
    a, b = position % 4, position // 4
    a, b = ((a, b), (3 - b, a), (3 - a, 3 - b), (b, 3 - a))[turn]
    return a + 4 * b


def split_parts(x):
    high = x.astype(BF16)
    return high, (x - high.astype(F32)).astype(BF16)


def dot(a, b):
    return jnp.dot(a, b, preferred_element_type=F32)


def dot_t(a, b):
    return lax.dot_general(a, b, (((1,), (1,)), ((), ())), preferred_element_type=F32)


def on_flow_row():
    return lax.axis_index("grp") < lax.axis_size("grp") - 1


def on_even_column():
    return lax.rem(lax.axis_index("sfc"), 2) == 0


def pack_kernel(
    flow, visc, links, sound, neighbours, codes,
    out_a, out_b, links_in, faces_in, staged, sems, link_sems,
):
    is_flow, even = on_flow_row(), on_even_column()
    tiles = flow.shape[1]
    _, nodes, elements = sound.shape
    outs = (out_a, out_b)

    @pl.when(is_flow)
    def _():
        fetch = pltpu.make_async_copy(links, links_in, link_sems.at[0])
        fetch.start()
        copies = []
        for side in range(2):
            off = pl.multiple_of(jnp.where(even == (side == 0), 0, tiles - EDGE), 8)
            for place, f in enumerate(FIELD_ORDER):
                copies.append(
                    pltpu.make_async_copy(
                        flow.at[f, pl.ds(off, EDGE), :],
                        staged.at[side, pl.ds(place * EDGE, EDGE), :],
                        sems.at[side, place],
                    )
                )
            copies.append(
                pltpu.make_async_copy(
                    visc.at[pl.ds(off, EDGE), :],
                    staged.at[side, pl.ds(5 * EDGE, EDGE), :],
                    sems.at[side, 5],
                )
            )
        for copy in copies:
            copy.start()
        fetch.wait()
        given = links_in[...]
        own = lax.axis_index("sfc") * tiles + lax.broadcasted_iota(jnp.int32, given.shape, 1)
        offset = jnp.where(given < 0, 0, given - own).astype(F32)
        low, high = offset[:, :LANES], offset[:, tiles - LANES :]
        pad = jnp.zeros((EXTRA - 4, LANES), F32)
        for side, (a, b) in enumerate(((low, high), (high, low))):
            block = jnp.concatenate([jnp.where(even, a, b), pad], 0)
            outs[side][6 * EDGE :, :] = block.astype(BF16)
        for copy in copies:
            copy.wait()
        for side in range(2):
            outs[side][: 6 * EDGE, :] = staged[side].astype(BF16)

    @pl.when(jnp.logical_not(is_flow))
    def _():
        copies = []
        for side in range(2):
            off = pl.multiple_of(jnp.where(even == (side == 0), 0, elements - LANES), LANES)
            for v in range(4):
                copies.append(
                    pltpu.make_async_copy(
                        sound.at[v, :, pl.ds(off, LANES)],
                        staged.at[side, pl.ds(v * nodes, nodes), :],
                        sems.at[side, v],
                    )
                )
        for at, ref in enumerate((neighbours, codes)):
            copies.append(pltpu.make_async_copy(ref, faces_in.at[at], link_sems.at[at]))
        for copy in copies:
            copy.start()
        for copy in copies:
            copy.wait()
        first = lax.axis_index("sfc") * elements
        own = first + lax.broadcasted_iota(jnp.int32, (1, elements), 1)
        for face in range(6):
            link = faces_in[0, face]
            offset = jnp.where(link < 0, NO_LINK, link - own).astype(F32)
            for at, row in enumerate((offset, faces_in[1, face].astype(F32))):
                line = 4 * nodes + 6 * at + face
                low, high = row[:, :LANES], row[:, elements - LANES :]
                staged[0, line : line + 1, :] = jnp.where(even, low, high)
                staged[1, line : line + 1, :] = jnp.where(even, high, low)
        used = 4 * nodes + 12
        for side, out in enumerate(outs):
            staged[side, used:, :] = jnp.zeros((staged.shape[1] - used, LANES), F32)
            out[: 6 * EDGE, :] = staged[side].astype(BF16)
            out[6 * EDGE :, :] = jnp.zeros((out.shape[0] - 6 * EDGE, LANES), BF16)


class FlowPlan:
    def __init__(self, tiles):
        self.tiles = tiles
        self.wide = tiles + 2 * EDGE
        self.blocks = 4
        self.rows = (tiles + 4 * HW) // self.blocks
        self.span = self.rows + 2 * HW

    def at(self, b):
        return HW + b * self.rows

    def inner(self):
        return range(1, self.blocks - 1)


def columns_of(place):
    return slice(place * LANES, (place + 1) * LANES)


def rows_between(parts, low, high, columns):
    taken = []
    for start, ref in parts:
        a, b = max(low, start), min(high, start + ref.shape[0])
        if a < b:
            taken.append(ref[a - start : b - start, columns])
    return taken[0] if len(taken) == 1 else jnp.concatenate(taken, 0)


def put(high, low, at, place, value):
    h, l = split_parts(value)
    high[at : at + value.shape[0], columns_of(place)] = h
    low[at : at + value.shape[0], columns_of(place)] = l


def east_west(x):
    return pltpu.roll(x, LANES - 1, 1), pltpu.roll(x, 1, 1)


def link_matrix(plan, offset, mat):
    rows, span = plan.rows, plan.span
    lane = lax.broadcasted_iota(jnp.int32, (rows, 2 * span), 1)
    lane = jnp.where(lane >= span, lane - span, lane)
    place = HW + lax.broadcasted_iota(jnp.int32, (rows, LANES), 0) + offset.astype(jnp.int32)
    hot = [jnp.where(place[:, k : k + 1] == lane, F32(1.0), F32(0.0)) for k in range(4)]
    mat[:rows, :] = (hot[0] + hot[1] + hot[2] + hot[3]).astype(BF16)
    mat[rows : 2 * rows, :] = (hot[0] - hot[1]).astype(BF16)
    mat[2 * rows :, :] = (hot[2] - hot[3]).astype(BF16)


def gathered(plan, mat, high, low, b, columns, at_row):
    at = b * plan.rows
    both = [rows_between(x, at, at + plan.span, columns) for x in (high, low)]
    return dot(mat[at_row:, :], jnp.concatenate(both, 0))


def advance(plan, b, mat, high, low, state, v, places, new_state, new_high, new_low, new_at, split):
    rows = plan.rows
    center = [state(k) for k in range(3)]
    scaled = [(0.5 * ADVECT) * c for c in center]
    for first, last in places:
        got = gathered(plan, mat, high, low, b, slice(first * LANES, last * LANES), 0)
        for place in range(first, last):
            inner = columns_of(place - first)
            total, dy, dz = got[:rows, inner], got[rows : 2 * rows, inner], got[2 * rows :, inner]
            c = center[place] if place < 3 else state(place)
            east, west = east_west(c)
            new = (
                c
                + v * (east + west + total - 6.0 * c)
                - (scaled[0] * (east - west) + scaled[1] * dy + scaled[2] * dz)
            )
            new_state[new_at : new_at + rows, columns_of(place)] = new
            if split:
                put(new_high, new_low, new_at, place, new)


def lamb_block(plan, b, mat, high, low, state, average, average_out, packed):
    rows = plan.rows
    center = [state(k) for k in range(3)]
    got = [
        gathered(plan, mat, high, low, b, slice(0, 2 * LANES), rows),
        gathered(plan, mat, high, low, b, slice(2 * LANES, 3 * LANES), rows),
    ]
    d1, d2, d3 = [], [], []
    for k in range(3):
        east, west = east_west(center[k])
        d1.append((east - west) * 0.5)
        inner = columns_of(k % 2)
        d2.append(got[k // 2][:rows, inner] * 0.5)
        d3.append(got[k // 2][rows:, inner] * 0.5)
    vx = d2[2] - d3[1]
    vy = d3[0] - d1[2]
    vz = d1[1] - d2[0]
    lamb = (
        vy * center[2] - vz * center[1],
        vz * center[0] - vx * center[2],
        vx * center[1] - vy * center[0],
    )
    to = plan.at(b) - EDGE
    low_row, top_row = max(0, -to), min(rows, plan.tiles - to)
    own = slice(to + low_row, to + top_row)
    for i in range(3):
        packed[i, own, :] = lamb[i][low_row:top_row]
        mixed = (1.0 - RELAX) * average[i, own, :] + RELAX * center[i][low_row:top_row]
        average_out[i, own, :] = mixed
        packed[3 + i, own, :] = mixed


def element_sums(projector, packed, hits, pay, own_ref, next_ref):
    nodes = projector.shape[0]
    count, elements = own_ref.shape
    proj_high, proj_low = split_parts(projector[...])
    proj_both = jnp.concatenate(
        [
            jnp.concatenate([proj_high, proj_high], 1),
            jnp.concatenate([proj_low, jnp.zeros_like(proj_low)], 1),
        ],
        0,
    )
    for c in range(6):
        x_high, x_low = split_parts(packed[c])
        main = dot_t(proj_both, jnp.concatenate([x_high, x_low], 1))
        pay[c * nodes : (c + 1) * nodes, :] = (main[:nodes] + main[nodes:]).astype(BF16)
    if count > 6 * nodes:
        pay[6 * nodes :, :] = jnp.ones((count - 6 * nodes, pay.shape[1]), BF16)
    sums = dot_t(pay[...], hits[...])
    if count > 6 * nodes:
        tail = sums[6 * nodes :]
        line = lax.broadcasted_iota(jnp.int32, tail.shape, 0)
        big = jnp.floor(tail * (1.0 / BASE))
        tail = jnp.where(line == 0, tail - BASE * big, jnp.where(line == 1, big, 0.0))
        sums = jnp.concatenate([sums[: 6 * nodes], tail], 0)
    own_ref[...] = sums[:, :elements]
    next_ref[...] = sums[:, elements:].astype(BF16)


def inner_kernel(
    flow, visc, links, target,
    inner_state, inner_high, inner_low, lcol, inner_mats, hits, high0, low0, square,
):
    plan = FlowPlan(flow.shape[1])
    tiles, rows = plan.tiles, plan.rows

    @pl.when(on_flow_row())
    def _():
        column = lax.axis_index("sfc")
        first_tile, first_element = column * tiles, column * (hits.shape[0] // 2)
        for place, f in enumerate(FIELD_ORDER):
            put(high0, low0, 0, place, flow[f])
        square[...] = jnp.zeros_like(square)
        own_tile = first_tile + lax.broadcasted_iota(jnp.int32, links.shape, 1)
        offset = jnp.where(links[...] < 0, 0, links[...] - own_tile).astype(F32)
        for part in range(tiles // LANES):
            square[:4, :] = offset[:, part * LANES : (part + 1) * LANES]
            lcol[part * LANES : (part + 1) * LANES, :] = square[...].T
        local = target[...] - first_element
        hits[...] = jnp.where(
            lax.broadcasted_iota(jnp.int32, hits.shape, 0) == local, F32(1.0), F32(0.0)
        ).astype(BF16)
        for at, b in enumerate(plan.inner()):
            own = slice(plan.at(b) - EDGE, plan.at(b) - EDGE + rows)
            link_matrix(plan, lcol[own, :], inner_mats.at[at])
            advance(
                plan, b, inner_mats.at[at], [(EDGE, high0)], [(EDGE, low0)],
                lambda place, own=own: flow[FIELD_ORDER[place], own, :],
                visc[own, :], ALL_FIELDS, inner_state, inner_high, inner_low, at * rows, True,
            )


def band_parts(plan, edge, inner):
    rows, last = plan.rows, plan.blocks - 1
    return [
        (plan.at(0), edge.at[:rows]),
        (plan.at(1), inner),
        (plan.at(last), edge.at[rows:]),
    ]


def band_state(plan, b, edge, inner):
    at = plan.at(b)
    parts = band_parts(plan, edge, inner)
    return lambda place: rows_between(parts, at, at + plan.rows, columns_of(place))


def closed(plan, parts, zero):
    return [(0, zero), *parts, (plan.wide - HW, zero)]


def mats_of(plan, b, edge_mats, inner_mats):
    if b in plan.inner():
        return inner_mats.at[b - 1]
    return edge_mats.at[0 if b == 0 else 1]


def first_kernel(
    flow, visc, mean, projector, part_a, part_b, sound, neighbours, codes,
    inner_state, inner_high, inner_low, lcol, inner_mats, hits,
    own_one, next_one, mean_one, base, grads, hot_two,
    edge_state, edge_high, edge_low, edge_mats, edge_visc,
    square, state0, high0, low0, zero, packed, pay, rows_of, facing, remote, rhs,
):
    is_flow, even = on_flow_row(), on_even_column()
    plan = FlowPlan(packed.shape[1])
    tiles, rows, span = plan.tiles, plan.rows, plan.span
    own_rows = span - EDGE

    @pl.when(is_flow)
    def _():
        def pick(at, size):
            a, b = part_a[at : at + size, :].astype(F32), part_b[at : at + size, :].astype(F32)
            return jnp.where(even, a, b), jnp.where(even, b, a)

        zero[...] = jnp.zeros_like(zero)
        for place, f in enumerate(FIELD_ORDER):
            before, after = pick(place * EDGE, EDGE)
            ends = (
                jnp.concatenate([before, flow[f, :own_rows, :]], 0),
                jnp.concatenate([flow[f, tiles - own_rows :, :], after], 0),
            )
            for side in range(2):
                state0[side, :, columns_of(place)] = ends[side]
                put(high0.at[side], low0.at[side], 0, place, ends[side])
        before, after = pick(5 * EDGE, EDGE)
        edge_visc[:rows, :] = jnp.concatenate([before[HW:], visc[: rows - EDGE + HW, :]], 0)
        edge_visc[rows:, :] = jnp.concatenate(
            [visc[tiles - (rows - EDGE + HW) :, :], after[: EDGE - HW]], 0
        )
        before, after = pick(6 * EDGE, EXTRA)
        given = []
        for side, block in enumerate((before, after)):
            square[...] = jnp.zeros_like(square)
            square[:EXTRA, :] = block
            turned = square[...].T
            given.append(
                jnp.concatenate([turned[LANES - EDGE + HW :], lcol[: rows - EDGE + HW, :]], 0)
                if side == 0
                else jnp.concatenate(
                    [lcol[tiles - (rows - EDGE + HW) :, :], turned[: EDGE - HW]], 0
                )
            )
        for side, b in enumerate((0, plan.blocks - 1)):
            link_matrix(plan, given[side], edge_mats.at[side])
            advance(
                plan, b, edge_mats.at[side],
                [(b * rows, high0.at[side])], [(b * rows, low0.at[side])],
                lambda place, side=side: state0[side, HW : HW + rows, columns_of(place)],
                edge_visc[side * rows : (side + 1) * rows, :], ALL_FIELDS,
                edge_state, edge_high, edge_low, side * rows, True,
            )
        high1 = closed(plan, band_parts(plan, edge_high, inner_high), zero)
        low1 = closed(plan, band_parts(plan, edge_low, inner_low), zero)
        for b in range(plan.blocks):
            lamb_block(
                plan, b, mats_of(plan, b, edge_mats, inner_mats), high1, low1,
                band_state(plan, b, edge_state, inner_state), mean, mean_one, packed,
            )
        element_sums(projector, packed, hits, pay, own_one, next_one)

    @pl.when(jnp.logical_not(is_flow))
    def _():
        own_one[...] = jnp.zeros_like(own_one)
        next_one[...] = jnp.zeros_like(next_one)
        nodes, elements = sound.shape[1:]
        halves = elements // LANES
        block = 4 * nodes
        for v in range(4):
            for h in range(halves):
                rows_of[h * block + v * nodes : h * block + (v + 1) * nodes, :] = sound[
                    v, :, h * LANES : (h + 1) * LANES
                ]
        a, b = part_a[:block, :].astype(F32), part_b[:block, :].astype(F32)
        before, after = jnp.where(even, a, b), jnp.where(even, b, a)
        lane = lax.broadcasted_iota(jnp.int32, (1, LANES), 1)
        beside = lane < LANES // 2
        rows_of[halves * block : (halves + 1) * block, :] = jnp.where(beside, after, before)
        rows_of[(halves + 1) * block : (halves + 2) * block, :] = jnp.zeros_like(before)
        rows_of[(halves + 2) * block : (halves + 3) * block, :] = before
        rows_of[(halves + 3) * block :, :] = after
        a = part_a[block : block + EXTRA, :].astype(F32)
        b = part_b[block : block + EXTRA, :].astype(F32)
        given = jnp.where(beside, jnp.where(even, b, a), jnp.where(even, a, b)).astype(jnp.int32)
        own_parts = [0, 1, halves + 2, halves + 3]
        first = lax.axis_index("sfc") * elements
        masks = []
        for face in range(6):
            for at, part in enumerate(own_parts):
                facing_rows(rows_of, part * block, nodes, face ^ 1, facing.at[face, at])
            link, code = neighbours[face], codes[face]
            offset, extra_code = given[face : face + 1, :], given[6 + face : 7 + face, :]
            extra = jnp.where(beside, elements + lane, lane - LANES) + offset
            near = jnp.concatenate([link - first, extra], 1)
            valid = jnp.concatenate([link, jnp.where(offset >= NO_LINK, -1, 0)], 1) >= 0
            place = jnp.where(
                near < 0, elements + LANES + near, jnp.where(near < elements, near, near + LANES)
            )
            hot = hot_columns(jnp.where(valid, place, -1), elements + 2 * LANES)
            remote_rows([facing[face, at] for at in range(4)], hot, remote, face)
            near = link - first
            place = jnp.where(near < 0, elements + LANES + near, near)
            hot_two[face] = hot_columns(jnp.where(link < 0, -1, place), elements + LANES)
            masks.append(
                (
                    face_masks(link[:, :LANES], link[:, LANES:], code[:, :LANES], code[:, LANES:]),
                    face_masks(
                        jnp.where(offset >= NO_LINK, -1, 0), jnp.full((1, LANES), -1, jnp.int32),
                        extra_code, extra_code,
                    ),
                )
            )
        for group in range(2):
            start = group * halves * block
            derivatives(rows_of, start, nodes, grads)
            rhs[...] = jnp.zeros_like(rhs)
            add_faces(
                rows_of, start, nodes, remote, group * halves * 64, [m[group] for m in masks], rhs
            )
            for n in range(nodes):
                base[pl.ds(start + n, 8, stride=nodes), :] = (
                    node_of(rows_of, start, nodes, n) + ACOUSTIC_STEP * rhs[n]
                )


def second_block(plan, b, carried, visc, places, new_state, new_parts):
    (inner_state, inner_high, inner_low, inner_mats, edge_state, edge_high, edge_low, edge_mats,
     edge_visc, zero) = carried
    rows = plan.rows
    if b in plan.inner():
        v = visc[plan.at(b) - EDGE : plan.at(b) - EDGE + rows, :]
    else:
        v = edge_visc[:rows, :] if b == 0 else edge_visc[rows:, :]
    advance(
        plan, b, mats_of(plan, b, edge_mats, inner_mats),
        closed(plan, band_parts(plan, edge_high, inner_high), zero),
        closed(plan, band_parts(plan, edge_low, inner_low), zero),
        band_state(plan, b, edge_state, inner_state), v, places,
        new_state, *new_parts, b * rows, new_parts[0] is not None,
    )


def second_kernel(
    visc, mean, mean_one, projector,
    inner_state, inner_high, inner_low, inner_mats, hits,
    edge_state, edge_high, edge_low, edge_mats, edge_visc,
    state, mean_two, own_two, next_two,
    high, low, zero, packed, pay,
):
    plan = FlowPlan(packed.shape[1])
    rows = plan.rows
    is_flow = on_flow_row()

    @pl.when(jnp.logical_not(is_flow))
    def _():
        own_two[...] = jnp.zeros_like(own_two)
        next_two[...] = jnp.zeros_like(next_two)

    @pl.when(is_flow)
    def _():
        zero[...] = jnp.zeros_like(zero)
        carried = (
            inner_state, inner_high, inner_low, inner_mats,
            edge_state, edge_high, edge_low, edge_mats, edge_visc, zero,
        )
        for b in range(plan.blocks):
            second_block(plan, b, carried, visc, ((0, 2), (2, 3)), state, (high, low))
        for b in range(plan.blocks):
            lamb_block(
                plan, b, mats_of(plan, b, edge_mats, inner_mats),
                closed(plan, [(HW, high)], zero), closed(plan, [(HW, low)], zero),
                lambda place, b=b: state[b * rows : (b + 1) * rows, columns_of(place)],
                mean_one, mean_two, packed,
            )
        element_sums(projector, packed, hits, pay, own_two, next_two)


def output_kernel(
    flow, visc, state,
    inner_state, inner_high, inner_low, inner_mats,
    edge_state, edge_high, edge_low, edge_mats, edge_visc, after, after_up, after_down, own_one,
    flow_out, own_one_out, passive, zero,
):
    plan = FlowPlan(flow.shape[1])
    is_flow = on_flow_row()
    own_one_out[...] = own_one[...]

    @pl.when(jnp.logical_not(is_flow))
    def _():
        flow_out[...] = flow[...]

    @pl.when(is_flow)
    def _():
        zero[...] = jnp.zeros_like(zero)
        carried = (
            inner_state, inner_high, inner_low, inner_mats,
            edge_state, edge_high, edge_low, edge_mats, edge_visc, zero,
        )
        own = slice(EDGE - HW, EDGE - HW + plan.tiles)
        for place in range(3):
            flow_out[FIELD_ORDER[place]] = state[own, columns_of(place)]
        for b in range(plan.blocks):
            second_block(plan, b, carried, visc, ((3, 5),), passive, (None, None))
        for place in (3, 4):
            flow_out[FIELD_ORDER[place]] = passive[own, columns_of(place)]


def mean_kernel(mean, mean_two, after, mean_out):
    is_flow = on_flow_row()

    @pl.when(is_flow)
    def _():
        mean_out[...] = mean_two[...]

    @pl.when(jnp.logical_not(is_flow))
    def _():
        mean_out[...] = mean[...]


def facing_rows(rows_of, base, nodes, face, to):
    axis, level = face // 2, 3 * (face % 2)
    if axis == 0:
        to[...] = rows_of[pl.ds(base + level, 64, stride=4), :]
    elif axis == 1:
        for i in range(4):
            to[pl.ds(i, 16, stride=4), :] = rows_of[pl.ds(base + i + 4 * level, 16, stride=16), :]
    else:
        for v in range(4):
            at = base + v * nodes + 16 * level
            to[v * 16 : (v + 1) * 16, :] = rows_of[at : at + 16, :]


def hot_columns(place, size):
    key = lax.broadcasted_iota(jnp.int32, (size, place.shape[1]), 0)
    return jnp.where(key == place, F32(1.0), F32(0.0)).astype(BF16)


def node_of(rows_of, start, nodes, n):
    return rows_of[pl.ds(start + n, 8, stride=nodes), :]


def remote_rows(parts, hot, remote, face):
    high, low = split_parts(jnp.concatenate(parts, 1))
    got = dot(jnp.concatenate([high, low], 0), hot)
    got = got[:64] + got[64:]
    for h in range(got.shape[1] // LANES):
        remote[face, h * 64 : (h + 1) * 64, :] = got[:, h * LANES : (h + 1) * LANES]


def derivatives(rows_of, start, nodes, grads_out):
    matrix = lobatto_matrix()
    node = [node_of(rows_of, start, nodes, n) for n in range(nodes)]
    for n in range(nodes):
        i, j, k = n % 4, n // 4 % 4, n // 16
        lines = (
            [m + 4 * j + 16 * k for m in range(4)],
            [i + 4 * m + 16 * k for m in range(4)],
            [i + 4 * j + 16 * m for m in range(4)],
        )
        for d, at in enumerate((i, j, k)):
            total = None
            for m in range(4):
                if abs(matrix[at, m]) > 1e-12:
                    term = F32(matrix[at, m]) * node[lines[d][m]]
                    total = term if total is None else total + term
            grads_out[d, pl.ds(start + n, 8, stride=nodes), :] = total


def face_masks(link_low, link_high, code_low, code_high):
    upper = lax.broadcasted_iota(jnp.int32, (8, LANES), 0) >= 4

    def both(low, high):
        return jnp.where(
            upper, jnp.broadcast_to(high, (8, LANES)), jnp.broadcast_to(low, (8, LANES))
        )

    code = both(code_low, code_high)
    return both(link_low, link_high) >= 0, [code == t for t in range(3)]


def add_faces(rows_of, start, nodes, remote, remote_start, masks, rhs):
    for face in range(6):
        valid, is_turn = masks[face]
        planes = [remote[face, pl.ds(remote_start + p, 8, stride=16), :] for p in range(16)]
        for p, n in enumerate(face_nodes(face)):
            turned = planes[turned_position(3, p)]
            for t in range(3):
                turned = jnp.where(is_turn[t], planes[turned_position(t, p)], turned)
            jump = jnp.where(valid, turned - node_of(rows_of, start, nodes, n), 0.0)
            rhs[n] = rhs[n] + PENALTY * jump


def with_sources(total, columns, block, nodes, base, grads):
    def rows_at(v):
        return slice((block * 4 + v) * nodes, (block * 4 + v + 1) * nodes)

    for v in range(4):
        rows = rows_at(v)
        if v:
            added = grads[v - 1, rows_at(0), :] + total[(v - 1) * nodes : v * nodes, columns]
        else:
            added = sum(grads[d, rows_at(1 + d), :] for d in range(3))
        for d in range(3):
            added = added + total[(3 + d) * nodes : (4 + d) * nodes, columns] * grads[d, rows, :]
        yield v, rows, base[rows, :] - ACOUSTIC_STEP * added


def gated_sum_kernel(own, *refs):
    *others, _, out = refs

    @pl.when(on_flow_row())
    def _():
        total = own[...]
        for other in others:
            total = total + other[...].astype(F32)
        out[...] = total.astype(BF16)


def border_kernel(sums, up, down):
    nodes_rows = (sums.shape[0] - EXTRA) // (LANES // HE)
    group = lax.broadcasted_iota(jnp.int32, (1, LANES), 1) // HE
    for out, tile, shift in ((up, sums.shape[1] - LANES, HE), (down, 0, 0)):
        columns = slice(tile, tile + LANES)
        total = jnp.zeros((nodes_rows, LANES), F32)
        for i in range(LANES // HE):
            x = sums[i * nodes_rows : (i + 1) * nodes_rows, columns].astype(F32)
            turn = (HE * i + shift) % LANES
            x = pltpu.roll(x, turn, 1) if turn else x
            total = jnp.where(group == i, x, total)
        out[:nodes_rows, :] = total.astype(BF16)
        x = sums[sums.shape[0] - EXTRA :, columns].astype(F32)
        x = pltpu.roll(x, shift, 1) if shift else x
        out[nodes_rows:, :] = jnp.where(group == 0, x, 0.0).astype(BF16)


def border_sums(up, down):
    lines = up.shape[0] - EXTRA
    lane = lax.broadcasted_iota(jnp.int32, (1, LANES), 1)
    parts = []
    for i in range(LANES // HE + 1):
        rows = slice(0, lines) if i < LANES // HE else slice(lines, lines + EXTRA)
        at = HE * (i % (LANES // HE))
        x = pltpu.roll(up[rows], (2 * LANES - HE - at) % LANES, 1)
        y = pltpu.roll(down[rows], (LANES - at) % LANES, 1) if at else down[rows]
        parts.append(jnp.where(lane >= LANES - HE, x, jnp.where(lane < HE, y, 0.0)))
    return jnp.concatenate(parts, 0)


def scaled_sums(total, nodes):
    count = total[6 * nodes : 6 * nodes + 1] + BASE * total[6 * nodes + 1 : 6 * nodes + 2]
    inverse = 1.0 / jnp.maximum(count, 1.0)
    return total[: 6 * nodes] * inverse, inverse


def sound_one_kernel(
    base, grads, hot_two, neighbours, codes, source_a, source_b, up_a, down_a, up_b, down_b, after,
    base_two, grads_two, scale_out, rows_of, facing, remote, rhs,
):
    elements = source_a.shape[1]
    halves = elements // LANES
    nodes = base_two.shape[0] // (4 * halves)
    block = 4 * nodes

    @pl.when(jnp.logical_not(on_flow_row()))
    def _():
        own, inverse = scaled_sums(source_a[...].astype(F32) + source_b[...].astype(F32), nodes)
        scale_out[...] = jnp.broadcast_to(inverse, scale_out.shape)
        extra = border_sums(
            up_a[...].astype(F32) + up_b[...].astype(F32),
            down_a[...].astype(F32) + down_b[...].astype(F32),
        )
        extra, _ = scaled_sums(extra, nodes)
        for h in range(halves + 1):
            total, columns = (own, columns_of(h)) if h < halves else (extra, columns_of(0))
            for _, rows, new in with_sources(total, columns, h, nodes, base, grads):
                rows_of[rows, :] = new
        masks = []
        for face in range(6):
            for part in range(halves + 1):
                facing_rows(rows_of, part * block, nodes, face ^ 1, facing.at[face, part])
            remote_rows(
                [facing[face, part] for part in range(halves + 1)], hot_two[face], remote, face
            )
            link, code = neighbours[face], codes[face]
            masks.append(
                face_masks(link[:, :LANES], link[:, LANES:], code[:, :LANES], code[:, LANES:])
            )
        derivatives(rows_of, 0, nodes, grads_two)
        rhs[...] = jnp.zeros_like(rhs)
        add_faces(rows_of, 0, nodes, remote, 0, masks, rhs)
        for n in range(nodes):
            base_two[pl.ds(n, 8, stride=nodes), :] = (
                node_of(rows_of, 0, nodes, n) + ACOUSTIC_STEP * rhs[n]
            )


def sound_two_kernel(sound, base, grads, scale, source_a, source_b, out):
    nodes = sound.shape[1]
    is_flow = on_flow_row()

    @pl.when(is_flow)
    def _():
        out[...] = sound[...]

    @pl.when(jnp.logical_not(is_flow))
    def _():
        total = (source_a[...].astype(F32) + source_b[...].astype(F32)) * scale[0:1, :]
        for h in range(sound.shape[2] // LANES):
            for v, _, new in with_sources(total, columns_of(h), h, nodes, base, grads):
                out[v, :, columns_of(h)] = new


def call(kernel, outs, scratch, operands, cost=None, in_hbm=(), limit=VMEM_LIMIT):
    spaces = [pltpu.HBM if at in in_hbm else pltpu.VMEM for at in range(len(operands))]
    moved = sum(int(np.prod(x.shape)) * x.dtype.itemsize for x in (*operands, *outs))
    return pl.pallas_call(
        kernel,
        out_shape=tuple(outs),
        in_specs=[pl.BlockSpec(memory_space=space) for space in spaces],
        out_specs=tuple([pl.BlockSpec(memory_space=pltpu.VMEM)] * len(outs)),
        scratch_shapes=scratch,
        compiler_params=pltpu.CompilerParams(vmem_limit_bytes=limit),
        cost_estimate=pl.CostEstimate(flops=10**8 if cost is None else cost, bytes_accessed=moved if cost is None else 0, transcendentals=0),
    )(*operands)


def body(
    flow_fields,
    mean_velocity,
    cell_eddy_viscosity,
    tile_links,
    tile_target,
    projector,
    acoustic_state,
    element_face_neighbours,
    face_codes,
):
    groups = lax.axis_size("grp")
    count = lax.axis_size("sfc")
    flow = flow_fields[0]
    mean = mean_velocity[0]
    visc = cell_eddy_viscosity[0]
    links = tile_links[0]
    sound = acoustic_state[0]
    faces, span = element_face_neighbours.shape[1:]
    neighbours = element_face_neighbours.reshape(faces, 1, span)
    codes = face_codes.reshape(faces, 1, span)
    tiles = flow.shape[1]
    _, nodes, elements = sound.shape
    halves = elements // LANES
    block = 4 * nodes
    plan = FlowPlan(tiles)
    shape = jax.ShapeDtypeStruct
    vmem = pltpu.VMEM
    pairs_a = [p for i in range(1, count - 1, 2) for p in ((i, i + 1), (i + 1, i))]
    pairs_b = [p for i in range(0, count - 1, 2) for p in ((i, i + 1), (i + 1, i))]

    edge_rows = 6 * EDGE + EXTRA
    pack_a, pack_b = call(
        pack_kernel,
        [shape((edge_rows, LANES), BF16)] * 2,
        [
            vmem(links.shape, jnp.int32),
            vmem((2, *neighbours.shape), jnp.int32),
            vmem((2, 6 * EDGE, LANES), F32),
            pltpu.SemaphoreType.DMA((2, 6)),
            pltpu.SemaphoreType.DMA((2,)),
        ],
        [flow, visc, links, sound, neighbours, codes],
        in_hbm=(0, 1, 2, 3, 4, 5),
        limit=PACK_LIMIT,
        cost=PACK_COST,
    )
    part_a = lax.ppermute(pack_a, "sfc", pairs_a)
    part_b = lax.ppermute(pack_b, "sfc", pairs_b)

    fields = 5 * LANES
    rows, span = plan.rows, plan.span
    inner_rows = (plan.blocks - 2) * rows
    square = vmem((LANES, LANES), F32)
    packed = vmem((6, tiles, LANES), F32)
    inner_state, inner_high, inner_low, lcol, inner_mats, hits = call(
        inner_kernel,
        [
            shape((inner_rows, fields), F32),
            shape((inner_rows, fields), BF16),
            shape((inner_rows, fields), BF16),
            shape((tiles, LANES), F32),
            shape((plan.blocks - 2, 3 * rows, 2 * span), BF16),
            shape((2 * elements, tiles), BF16),
        ],
        [vmem((tiles, fields), BF16), vmem((tiles, fields), BF16), square],
        [flow, visc, links, tile_target],
    )
    lines = 6 * nodes + EXTRA
    node_rows = vmem((nodes, 8, LANES), F32)
    (
        own_one, next_one, mean_one, base, grads, hot_two,
        edge_state, edge_high, edge_low, edge_mats, edge_visc,
    ) = call(
        first_kernel,
        [
            shape((lines, elements), F32),
            shape((lines, elements), BF16),
            shape(mean.shape, F32),
            shape(((halves + 2) * block, LANES), F32),
            shape((3, (halves + 2) * block, LANES), F32),
            shape((6, elements + LANES, elements), BF16),
            shape((2 * rows, fields), F32),
            shape((2 * rows, fields), BF16),
            shape((2 * rows, fields), BF16),
            shape((2, 3 * rows, 2 * span), BF16),
            shape((2 * rows, LANES), F32),
        ],
        [
            square,
            vmem((2, span, fields), F32),
            vmem((2, span, fields), BF16),
            vmem((2, span, fields), BF16),
            vmem((HW, fields), BF16),
            packed,
            vmem((lines, tiles), BF16),
            vmem(((halves + 4) * block, LANES), F32),
            vmem((6, 4, 64, LANES), F32),
            vmem((6, (halves + 2) * 64, LANES), F32),
            node_rows,
        ],
        [
            flow, visc, mean, projector, part_a, part_b, sound, neighbours, codes,
            inner_state, inner_high, inner_low, lcol, inner_mats, hits,
        ],
    )

    up = [(i, i + 1) for i in range(count - 1)]

    def climb(x):
        chosen = [(g * count + i, g * count + j) for g in range(groups - 1) for i, j in up]
        return lax.ppermute(x, ("grp", "sfc"), chosen)

    def combined(*xs):
        total = xs[0]
        for x in xs[1:]:
            total = total + x.astype(F32)
        return total.astype(BF16)

    got_one = climb(next_one)
    band = plan.blocks * rows
    velocity = 3 * LANES
    step_one = [inner_state, inner_high, inner_low, inner_mats]
    edges = [edge_state, edge_high, edge_low, edge_mats, edge_visc]
    state_two, mean_two, own_two, next_two = call(
        second_kernel,
        [
            shape((band, velocity), F32),
            shape(mean.shape, F32),
            shape((6 * nodes, elements), F32),
            shape((6 * nodes, elements), BF16),
        ],
        [
            vmem((band, velocity), BF16),
            vmem((band, velocity), BF16),
            vmem((HW, fields), BF16),
            packed,
            vmem((6 * nodes, tiles), BF16),
        ],
        [visc, mean, mean_one, projector, *step_one, hits, *edges],
        cost=SECOND_COST,
    )
    last = (groups - 1) * count
    lines_beside = 6 * nodes // (LANES // HE) + EXTRA

    def borders(sums, row):
        up_border, down_border = call(
            border_kernel, [shape((lines_beside, LANES), BF16)] * 2, [], [sums], cost=0
        )
        start = row * count
        return up_border, [
            lax.ppermute(
                up_border, ("grp", "sfc"), [(start + i, last + i + 1) for i in range(count - 1)]
            ),
            lax.ppermute(
                down_border, ("grp", "sfc"), [(start + i, last + i - 1) for i in range(1, count)]
            ),
        ]

    got_two = climb(next_two)
    sum_one_2 = combined(own_one, got_one)
    one_0_to_1 = lax.ppermute(sum_one_2, "grp", [(0, 1)])
    _, beside_2 = borders(sum_one_2, 2)
    sum_two_1 = combined(own_two, got_two)
    two_0_to_2 = lax.ppermute(sum_two_1, "grp", [(0, 2)])
    one_2_to_3 = lax.ppermute(sum_one_2, "grp", [(2, 3)])
    (sum_two_1,) = call(
        gated_sum_kernel,
        [shape(own_two.shape, BF16)],
        [],
        [own_two, got_two, sum_two_1],
        cost=0,
    )
    two_1_to_3 = lax.ppermute(sum_two_1, "grp", [(1, 3)])
    flow_out, own_one = call(
        output_kernel,
        [shape(flow.shape, F32), shape(own_one.shape, F32)],
        [vmem((band, fields), F32), vmem((HW, fields), BF16)],
        [flow, visc, state_two, *step_one, *edges, sum_two_1, *beside_2, own_one],
        cost=OUTPUT_COST,
    )
    sum_one_1 = combined(own_one, got_one, one_0_to_1)
    one_1_to_3 = lax.ppermute(sum_one_1, "grp", [(1, 3)])
    border, beside_1 = borders(sum_one_1, 1)
    (sum_two_2,) = call(
        gated_sum_kernel,
        [shape(own_two.shape, BF16)],
        [],
        [own_two, got_two, two_0_to_2, border],
        cost=0,
    )
    (mean_out,) = call(
        mean_kernel, [shape(mean.shape, F32)], [], [mean, mean_two, sum_two_2], cost=0
    )
    two_2_to_3 = lax.ppermute(sum_two_2, "grp", [(2, 3)])

    base, grads, scale = call(
        sound_one_kernel,
        [
            shape((halves * block, LANES), F32),
            shape((3, halves * block, LANES), F32),
            shape((8, elements), F32),
        ],
        [
            vmem(((halves + 1) * block, LANES), F32),
            vmem((6, halves + 1, 64, LANES), F32),
            vmem((6, halves * 64, LANES), F32),
            node_rows,
        ],
        [
            base, grads, hot_two, neighbours, codes, one_2_to_3, one_1_to_3,
            *beside_1, *beside_2, two_1_to_3,
        ],
        cost=SOUND_COST,
    )
    (sound_out,) = call(
        sound_two_kernel,
        [shape(sound.shape, F32)],
        [],
        [sound, base, grads, scale, two_2_to_3, two_1_to_3],
    )
    return flow_out[None], mean_out[None], sound_out[None]


def solution(mesh):
    placed = (
        P("grp", None, "sfc", None),
        P("grp", None, "sfc", None),
        P("grp", "sfc", None),
        P("grp", None, "sfc"),
        P("grp", "sfc"),
        P(),
        P("grp", None, None, "sfc"),
        P("grp", None, "sfc"),
        P("grp", None, "sfc"),
    )
    return jax.shard_map(
        body,
        mesh=mesh,
        in_specs=placed,
        out_specs=(
            P("grp", None, "sfc", None),
            P("grp", None, "sfc", None),
            P("grp", None, None, "sfc"),
        ),
        check_vma=False,
    )
```
